32 devices in a mesh: ctx: 16 (over z, y, core), fsdp: 2 (over x).
Axes of the slice: x: 2, y: 2, z: 4, core: 2. Of those that a mesh axis runs over, the one named last changes fastest.
Arguments:
- tokens: bfloat16 [2, 6144, 2560], P('fsdp', 'ctx'), may hold values from -6 to 6
- positions: int32 [2, 6144], P('fsdp', 'ctx'), may hold values from 0 to 6142, as said below
- attn_gain: float32 [2560], P(('ctx', 'fsdp')), may hold values from 0.1 to 1.9
- query_weight: bfloat16 [2560, 2560], P(('ctx', 'fsdp')), may hold values from -0.125 to 0.125
- key_weight: bfloat16 [2560, 256], P(('ctx', 'fsdp')), may hold values from -0.125 to 0.125
- value_weight: bfloat16 [2560, 256], P(('ctx', 'fsdp')), may hold values from -0.125 to 0.125
- out_weight: bfloat16 [2560, 2560], P(None, ('ctx', 'fsdp')), may hold values from -0.5 to 0.5
- mlp_gain: float32 [2560], P(('ctx', 'fsdp')), may hold values from 0.1 to 1.9
- gate_weight: bfloat16 [2560, 7680], P(('ctx', 'fsdp')), may hold values from -0.125 to 0.125
- up_weight: bfloat16 [2560, 7680], P(('ctx', 'fsdp')), may hold values from -0.125 to 0.125
- down_weight: bfloat16 [7680, 2560], P(None, ('ctx', 'fsdp')), may hold values from -0.0625 to 0.0625
- cotangent: bfloat16 [2, 6144, 2560], P('fsdp', 'ctx'), may hold values from -6 to 6
Outputs:
- output: float32 [2, 6144, 2560], P('fsdp', 'ctx')
- grad_tokens: float32 [2, 6144, 2560], P('fsdp', 'ctx')
- grad_attn_gain: float32 [2560], P(('ctx', 'fsdp'))
- grad_query_weight: float32 [2560, 2560], P(('ctx', 'fsdp'))
- grad_key_weight: float32 [2560, 256], P(('ctx', 'fsdp'))
- grad_value_weight: float32 [2560, 256], P(('ctx', 'fsdp'))
- grad_out_weight: float32 [2560, 2560], P(None, ('ctx', 'fsdp'))
- grad_mlp_gain: float32 [2560], P(('ctx', 'fsdp'))
- grad_gate_weight: float32 [2560, 7680], P(('ctx', 'fsdp'))
- grad_up_weight: float32 [2560, 7680], P(('ctx', 'fsdp'))
- grad_down_weight: float32 [7680, 2560], P(None, ('ctx', 'fsdp'))
The draws below stay inside these ranges and needn't reach their ends.
Inputs may be any that keep to these rules, and one draw needn't show every extreme that they name: `positions`: positions count from 0 at each document's first token and rise by one per token. In every group a first document of 1 to 383 tokens starts at token 0. In one group the first document has a single token and a second one fills the rest of the group; in every other group documents of 4096 tokens follow the first one, the last of them possibly shorter.
All inputs are finite; a program needn't handle non-finite values.
Results may differ from the reference program's by a relative error of at most 0.039.
Values may be sent and summed in bfloat16 or wider, within the bound.
No kernel may reach another device: no remote copies, remote signals or barrier semaphores. Data moves between devices by JAX's collectives and lax.ppermute only.
A program may use at most 576 MiB of HBM per device.

```python
import jax
import jax.numpy as jnp
from jax import lax

D = 2560
HEADS = 10
HD = 256
FF = 7680
WINDOW = 2048
SEQ_LEN = 4096
TOK_DEV = 384
GROUPS = 2
GROUP_TOK = 6144
N_CTX = 16


def draw_positions(key, part):
    key = jax.random.fold_in(key, 7)
    start_key = jax.random.fold_in(key, 1)
    pick_key = jax.random.fold_in(key, 2)
    starts = jax.random.randint(start_key, (GROUPS, 1), 1, TOK_DEV, dtype=jnp.int32)
    chosen = jax.random.randint(pick_key, (), 0, GROUPS, dtype=jnp.int32)
    rows = jnp.arange(GROUPS, dtype=jnp.int32)[:, None]
    single = rows == chosen
    starts = jnp.where(single, jnp.ones_like(starts), starts)
    places = jnp.arange(GROUP_TOK, dtype=jnp.int32)[None, :]
    shifted = places - starts
    packed = jnp.where(single, shifted, jnp.remainder(jnp.maximum(shifted, 0), SEQ_LEN))
    return jnp.where(places < starts, places, packed).astype(jnp.int32)


def spiked(entries, key, source, target, shards_of, factor):
    def block_of(position):
        return (jnp.arange(entries.shape[position]) // (entries.shape[position] // shards_of)).reshape((-1,) + (1,) * (entries.ndim - 1 - position))

    near = jax.random.permutation(key, shards_of)[block_of(target)]
    other_side = (block_of(target) + shards_of // 2) % shards_of
    return jnp.where((block_of(source) == near) | (block_of(source) == other_side), factor * entries, entries)


def block_levels(own_key, dims, shards, low, largest):
    loudness, own = 1.0, jax.random.fold_in(own_key, 6)
    for axis_at, shards_of in shards:
        steps = jnp.exp(jax.random.uniform(jax.random.fold_in(own, axis_at), (shards_of,), jnp.float32, low / len(shards), largest / len(shards)))
        loudness = loudness * jnp.repeat(steps, dims[axis_at] // shards_of).reshape([-1 if axis == axis_at else 1 for axis in range(len(dims))])
    return loudness


def noise(key, shape, width, most, shards=(), kind=jnp.bfloat16):
    loudness = block_levels(key, shape, shards, -0.22, 0.18) if shards else 1.0
    values = jax.random.normal(key, shape, jnp.float32) * width * loudness
    return jnp.minimum(jnp.maximum(values, -most), most).astype(kind)


def bell_draw_with(own_key, extent, deviation, limit, pieces, heavy, kind=jnp.bfloat16):
    array = deviation * jax.random.normal(own_key, extent, jnp.float32)
    if pieces:
        array = array * block_levels(own_key, extent, pieces, -0.22, 0.18)
    return jnp.clip(spiked(array, jax.random.fold_in(own_key, 3), *heavy), -limit, limit).astype(kind)


def setup_inputs(seed: int = 0) -> dict:
    splits = jax.random.split(jax.random.key(seed), 13)
    return {
        "tokens": noise(splits[0], (GROUPS, GROUP_TOK, D), 1.0, 6.0, ((0, 2), (1, 16))),
        "positions": draw_positions(jax.random.fold_in(splits[12], 71), 0),
        "attn_gain": jnp.clip(1.0 + 0.18 * jax.random.normal(splits[2], (D,), jnp.float32), 0.1, 1.9),
        "query_weight": noise(splits[3], (D, HEADS * HD), D ** -0.5, 0.125, ((0, 32),)),
        "key_weight": noise(splits[4], (D, HD), D ** -0.5, 0.125, ((0, 32),)),
        "value_weight": noise(splits[5], (D, HD), D ** -0.5, 0.125, ((0, 32),)),
        "out_weight": noise(splits[6], (HEADS * HD, D), (D // 16) ** -0.5, 0.5, ((1, 32),)),
        "mlp_gain": jnp.clip(1.0 + 0.18 * jax.random.normal(splits[7], (D,), jnp.float32), 0.1, 1.9),
        "gate_weight": noise(splits[8], (D, FF), D ** -0.5, 0.125, ((0, 32),)),
        "up_weight": noise(splits[9], (D, FF), D ** -0.5, 0.125, ((0, 32),)),
        "down_weight": noise(splits[10], (FF, D), FF ** -0.5, 0.0625, ((1, 32),)),
        "cotangent": bell_draw_with(splits[11], (GROUPS, GROUP_TOK, D), 1.0, 6.0, ((0, 2), (1, 16)), (1, 2, 16, 2.0)),
    }


@jax.custom_vjp
def low(v):
    return lax.optimization_barrier(v.astype(jnp.bfloat16)).astype(jnp.float32)

@jax.custom_vjp
def low_back(v):
    return v

def low_keep(v):
    return (low(v), None)

def low_pass(kept, grad):
    return (grad,)

def back_keep(v):
    return (v, None)

def back_low(kept, grad):
    return (low(grad),)
low.defvjp(low_keep, low_pass)
low_back.defvjp(back_keep, back_low)
epsilon = 1e-06
blocked_score = -1e+30

def product(left, right):
    return jnp.dot(left, right, precision=lax.Precision.HIGHEST)

def normalize(values, gain):
    return values * lax.rsqrt(lax.optimization_barrier(jnp.mean(values * values, axis=-1, keepdims=True)) + epsilon) * gain

def geglu(gates, upward):
    return jax.nn.gelu(gates, approximate=True) * upward

def reference(tokens, positions, attn_gain, query_weight, key_weight, value_weight, out_weight, mlp_gain, gate_weight, up_weight, down_weight, cotangent):
    reach = (WINDOW + TOK_DEV - 2) // TOK_DEV
    span = (reach + 1) * TOK_DEV
    margin = reach * TOK_DEV
    scale = HD ** (-0.5)

    def attend(queries, keys, values):
        keys_pad = jnp.pad(keys, ((0, 0), (margin, 0), (0, 0)))
        values_pad = jnp.pad(values, ((0, 0), (margin, 0), (0, 0)))

        def block(number):
            group = (number // N_CTX).astype(jnp.int32)
            begin = (number % N_CTX * TOK_DEV).astype(jnp.int32)
            zero = jnp.zeros((), jnp.int32)
            query_block = lax.dynamic_slice(queries, (group, begin, zero, zero), (1, TOK_DEV, HEADS, HD))[0]
            key_block = lax.dynamic_slice(keys_pad, (group, begin, zero), (1, span, HD))[0]
            value_block = lax.dynamic_slice(values_pad, (group, begin, zero), (1, span, HD))[0]
            places = lax.dynamic_slice(positions, (group, begin), (1, TOK_DEV))[0]
            query_index = begin + jnp.arange(TOK_DEV, dtype=jnp.int32)
            key_index = begin - margin + jnp.arange(span, dtype=jnp.int32)
            first = (query_index - places)[:, None]
            allowed = (key_index[None, :] >= first) & (key_index[None, :] <= query_index[:, None]) & (query_index[:, None] - key_index[None, :] < WINDOW)
            raw = low_back(jnp.einsum('qhd,kd->hqk', query_block, key_block, precision=lax.Precision.HIGHEST) * scale)
            scores = jnp.where(allowed[None], raw, blocked_score)
            highest = lax.optimization_barrier(jnp.max(scores, axis=-1, keepdims=True))
            expo = jnp.exp(scores - highest)
            probs = low(expo / lax.optimization_barrier(jnp.sum(expo, axis=-1, keepdims=True)))
            return jnp.einsum('hqk,kd->qhd', probs, value_block, precision=lax.Precision.HIGHEST)
        numbers = jnp.arange(GROUPS * N_CTX, dtype=jnp.int32)
        mixed = lax.map(jax.checkpoint(block), numbers)
        return mixed.reshape(GROUPS * GROUP_TOK, HEADS * HD)

    def forward(inputs, gain_one, query_full, key_full, value_full, out_full, gain_two, gate_full, up_full, down_full):
        flat = inputs.reshape(GROUPS * GROUP_TOK, D)
        normed_one = low(normalize(flat, gain_one))
        queries = low(low_back(product(normed_one, query_full)))
        keys = low(low_back(product(normed_one, key_full)))
        values = low(low_back(product(normed_one, value_full)))
        mixed = attend(queries.reshape(GROUPS, GROUP_TOK, HEADS, HD), keys.reshape(GROUPS, GROUP_TOK, HD), values.reshape(GROUPS, GROUP_TOK, HD))
        mixed = low(low_back(mixed))
        resid = flat + low_back(product(mixed, out_full))
        normed_two = low(normalize(resid, gain_two))
        gates = low_back(product(normed_two, gate_full))
        upward = low_back(product(normed_two, up_full))
        middle = low(geglu(gates, upward))
        result = resid + low_back(product(middle, down_full))
        return result.reshape(GROUPS, GROUP_TOK, D)
    result, pull = jax.vjp(forward, tokens.astype(jnp.float32), attn_gain.astype(jnp.float32), query_weight.astype(jnp.float32), key_weight.astype(jnp.float32), value_weight.astype(jnp.float32), out_weight.astype(jnp.float32), mlp_gain.astype(jnp.float32), gate_weight.astype(jnp.float32), up_weight.astype(jnp.float32), down_weight.astype(jnp.float32))
    grads = pull(cotangent.astype(jnp.float32))
    return (result, grads[0], grads[1], grads[2], grads[3], grads[4], grads[5], grads[6], grads[7], grads[8], grads[9])
```

```python
import functools

import jax
import jax.numpy as jnp
from jax import lax
from jax.experimental import pallas as pl
from jax.experimental.pallas import tpu as pltpu
from jax.sharding import Mesh, PartitionSpec as P

WINDOW = 2048
SUB = 128
epsilon = 1e-06
blocked_score = -1e30
PLANE = ("y", "c", "x")
low = jnp.bfloat16
f32 = jnp.float32


def dot(left, right, contract, kind=f32):
    return lax.dot_general(
        left, right, ((contract[:1], contract[1:]), ((), ())), preferred_element_type=f32
    ).astype(kind)


def swap(value, axis):
    return lax.ppermute(value, axis, [(0, 1), (1, 0)])


def plane_gather(own):
    half = own.shape[0] // 2
    by_x = swap(own, "x")
    by_y = swap(own, "y")
    own_c = swap(own, "c")
    diag_top = swap(by_y[:half], "x")
    diag_bottom = swap(by_x[half:], "y")
    by_x_c = swap(by_x, "c")
    by_y_c = swap(by_y, "c")
    diag = jnp.concatenate([diag_top, diag_bottom], 0)
    diag_c = swap(diag, "c")
    return [own, by_x, own_c, by_x_c, by_y, diag, by_y_c, diag_c]


def plane_scatter(parts):
    half = parts[0].shape[0] // 2

    def chip(r):
        return parts[r].astype(f32) + swap(parts[r + 2].astype(low), "c").astype(f32)

    diag = chip(5).astype(low)
    diag_x = swap(diag[:half], "x").astype(f32)
    diag_y = swap(diag[half:], "y").astype(f32)
    to_x, to_y = chip(1), chip(4)
    x_top = swap(to_x[:half].astype(low), "x").astype(f32)
    y_bottom = swap(to_y[half:].astype(low), "y").astype(f32)
    mine = chip(0)
    x_bottom = swap((to_x[half:] + diag_y).astype(low), "x").astype(f32)
    y_top = swap((to_y[:half] + diag_x).astype(low), "y").astype(f32)
    return jnp.concatenate(
        [mine[:half] + x_top + y_top, mine[half:] + x_bottom + y_bottom], 0
    )


def plane_index():
    return (lax.axis_index("y") * 2 + lax.axis_index("c")) * 2 + lax.axis_index("x")


def gather_rows(shard):
    column = lax.all_gather(shard, "z", axis=0, tiled=False)
    blocks = plane_gather(column)
    here = plane_index()
    planes, rows, wide = column.shape
    whole = jnp.zeros((planes, 8, rows, wide), shard.dtype)
    for r, block in enumerate(blocks):
        whole = lax.dynamic_update_slice(whole, block[:, None], (0, here ^ r, 0, 0))
    return whole.reshape(planes * 8 * rows, wide)


def scatter_rows(partial):
    planes = lax.axis_size("z")
    wide = partial.shape[1]
    rows = partial.shape[0] // (planes * 8)
    blocks = partial.reshape(planes, 8, rows, wide)
    here = plane_index()
    parts = [
        lax.dynamic_slice(blocks, (0, here ^ r, 0, 0), (planes, 1, rows, wide))[:, 0]
        for r in range(8)
    ]
    column = plane_scatter(parts).astype(low).reshape(planes * rows, wide)
    return lax.psum_scatter(column, "z", scatter_dimension=0, tiled=True).astype(f32)


def columns_of_plane(shard):
    rows, wide = shard.shape
    split = jnp.swapaxes(shard.reshape(rows, 8, wide // 8), 0, 1)
    return lax.all_to_all(split, PLANE, split_axis=0, concat_axis=0, tiled=True)


def window_blocks(pair, chips):
    count = lax.axis_size("z") * lax.axis_size("y")
    same = [
        lax.ppermute(pair, ("z", "y"), [(i, i + d) for i in range(count - d)])
        for d in range(chips, 0, -1)
    ] + [pair]
    same = jnp.stack(same)
    other = swap(same, "c")
    first = lax.axis_index("c") == 0
    return jnp.stack(
        [jnp.where(first, same, other), jnp.where(first, other, same)], 1
    ).reshape((chips + 1) * 2 * pair.shape[0], pair.shape[1])


def return_blocks(grads, chips, rows):
    count = lax.axis_size("z") * lax.axis_size("y")
    both = grads.reshape(chips + 1, 2, rows, grads.shape[1])
    first = lax.axis_index("c") == 0
    mine = jnp.where(first, both[:, 0], both[:, 1])
    theirs = jnp.where(first, both[:, 1], both[:, 0])
    mine = mine + swap(theirs.astype(low), "c").astype(f32)
    total = mine[chips]
    for d in range(chips, 0, -1):
        total = total + lax.ppermute(
            mine[chips - d].astype(low), ("z", "y"), [(i + d, i) for i in range(count - d)]
        ).astype(f32)
    return total


def two_heads(block, size):
    return jnp.concatenate([block[:, :size], block[:, size:]], 0)


def side_by_side(rows, size):
    half = rows.shape[0] // 2
    return jnp.concatenate([rows[:half], rows[half:]], 1)


def write_bias(bias, places, span, block):
    key = lax.broadcasted_iota(jnp.int32, (span, SUB), 0) - WINDOW
    query = lax.broadcasted_iota(jnp.int32, (span, SUB), 1)
    age = query - key
    seen = (age <= places) & (age >= 0) & (age < WINDOW)
    value = jnp.where(seen, 0.0, blocked_score).astype(f32)
    bias[:, :SUB] = value
    bias[:, SUB:] = value


def attend_kernel(size, scale, span, base, offset, places, queries, pairs, values_t, mixed, logs, bias):
    block = pl.program_id(0)
    start = pl.multiple_of(offset[0] + base + block * SUB, SUB)

    @pl.when(pl.program_id(1) == 0)
    def _():
        write_bias(bias, places[...], span, block)

    query = two_heads(queries[...], size)
    keys = pairs[pl.ds(start, span), :size]
    scores = dot(keys, query, (1, 1)) * scale + bias[...]
    highest = jnp.max(scores, axis=0, keepdims=True)
    expo = jnp.exp(scores - highest)
    total = jnp.sum(expo, axis=0, keepdims=True)
    flat = dot(values_t[:, pl.ds(start, span)], expo.astype(low), (1, 0)) / total
    mixed[...] = side_by_side(flat.T, size).astype(low)
    logs[0] = highest + jnp.log(total)


def attend_back_kernel(
    size, scale, span, base, offset, places, queries, grads, logs, pairs, keys_t, grad_queries, grad_pairs, bias
):
    block = pl.program_id(0)
    start = pl.multiple_of(offset[0] + base + block * SUB, SUB)

    @pl.when((block == 0) & (pl.program_id(1) == 0))
    def _():
        grad_pairs[...] = jnp.zeros_like(grad_pairs)

    @pl.when(pl.program_id(1) == 0)
    def _():
        write_bias(bias, places[...], span, block)

    query = two_heads(queries[...], size)
    grad = two_heads(grads[...], size)
    keys = pairs[pl.ds(start, span), :size]
    values = pairs[pl.ds(start, span), size:]
    probs = jnp.exp(dot(keys, query, (1, 1)) * scale + bias[...] - logs[0])
    grad_pairs[pl.ds(start, span), size:] += dot(probs.astype(low), grad, (1, 0))
    grad_probs = dot(values, grad, (1, 1))
    inner = jnp.sum(probs * grad_probs, axis=0, keepdims=True)
    grad_scores = (probs * (grad_probs - inner)).astype(low)
    grad_pairs[pl.ds(start, span), :size] += dot(grad_scores, query, (1, 0)) * scale
    flat = dot(keys_t[:, pl.ds(start, span)], grad_scores, (1, 0)) * scale
    grad_queries[...] = side_by_side(flat.T, size).astype(low)


def attend(queries, pairs, places, size, base):
    count, wide = queries.shape
    grid = (count // SUB, wide // (2 * size))
    span = WINDOW + SUB
    offset = (lax.axis_index("c") * count).astype(jnp.int32)[None]
    whole = lambda shape: pl.BlockSpec(shape, lambda s, h, o: (0, 0))
    return pl.pallas_call(
        functools.partial(attend_kernel, size, size**-0.5, span, base),
        out_shape=(
            jax.ShapeDtypeStruct((count, wide), low),
            jax.ShapeDtypeStruct((grid[0] * grid[1], 1, 2 * SUB), f32),
        ),
        grid_spec=pltpu.PrefetchScalarGridSpec(
            num_scalar_prefetch=1,
            grid=grid,
            in_specs=[
                pl.BlockSpec((1, SUB), lambda s, h, o: (0, s)),
                pl.BlockSpec((SUB, 2 * size), lambda s, h, o: (s, h)),
                whole(pairs.shape),
                whole((size, pairs.shape[0])),
            ],
            out_specs=[
                pl.BlockSpec((SUB, 2 * size), lambda s, h, o: (s, h)),
                pl.BlockSpec((1, 1, 2 * SUB), lambda s, h, o: (s * grid[1] + h, 0, 0)),
            ],
            scratch_shapes=[pltpu.VMEM((span, 2 * SUB), f32)],
        ),
        compiler_params=pltpu.CompilerParams(vmem_limit_bytes=48 << 20),
        cost_estimate=pl.CostEstimate(
            flops=4 * count * wide * span, bytes_accessed=8 << 20, transcendentals=count * span * wide // size
        ),
    )(offset, places, queries, pairs, pairs[:, size:].T)


def attend_back(queries, grads, logs, pairs, places, size, base):
    count, wide = queries.shape
    grid = (count // SUB, wide // (2 * size))
    span = WINDOW + SUB
    offset = (lax.axis_index("c") * count).astype(jnp.int32)[None]
    whole = lambda shape: pl.BlockSpec(shape, lambda s, h, o: (0, 0))
    tile = pl.BlockSpec((SUB, 2 * size), lambda s, h, o: (s, h))
    return pl.pallas_call(
        functools.partial(attend_back_kernel, size, size**-0.5, span, base),
        out_shape=(
            jax.ShapeDtypeStruct((count, wide), low),
            jax.ShapeDtypeStruct(pairs.shape, f32),
        ),
        grid_spec=pltpu.PrefetchScalarGridSpec(
            num_scalar_prefetch=1,
            grid=grid,
            in_specs=[
                pl.BlockSpec((1, SUB), lambda s, h, o: (0, s)),
                tile,
                tile,
                pl.BlockSpec((1, 1, 2 * SUB), lambda s, h, o: (s * grid[1] + h, 0, 0)),
                whole(pairs.shape),
                whole((size, pairs.shape[0])),
            ],
            out_specs=[tile, whole(pairs.shape)],
            scratch_shapes=[pltpu.VMEM((span, 2 * SUB), f32)],
        ),
        compiler_params=pltpu.CompilerParams(vmem_limit_bytes=56 << 20),
        cost_estimate=pl.CostEstimate(
            flops=10 * count * wide * span, bytes_accessed=16 << 20, transcendentals=count * span * wide // size
        ),
    )(offset, places, queries, grads, logs, pairs, pairs[:, :size].T)


def unit_of(values):
    scale = lax.rsqrt(jnp.mean(values * values, axis=-1, keepdims=True) + epsilon)
    return scale, (values * scale).astype(low)


def unit_back(grad, values, scale):
    unit = values * scale
    return scale * (grad - unit * jnp.mean(grad * unit, axis=-1, keepdims=True))


def geglu(gates, upward):
    return jax.nn.gelu(gates, approximate=True) * upward


def local(
    tokens,
    positions,
    attn_gain,
    query_weight,
    key_weight,
    value_weight,
    out_weight,
    mlp_gain,
    gate_weight,
    up_weight,
    down_weight,
    cotangent,
):
    count = tokens.shape[1]
    size = key_weight.shape[1]
    wide = query_weight.shape[1]
    reach = (WINDOW + count - 2) // count
    chips = (reach + 1) // 2
    base = 2 * chips * count - WINDOW
    gain_one = attn_gain[:, None]
    gain_two = mlp_gain[:, None]

    qkv_shard = (
        jnp.concatenate([query_weight, key_weight, value_weight], 1).astype(f32) * gain_one
    ).astype(low)
    qkv_full = gather_rows(qkv_shard)
    out_full = gather_rows(out_weight.T)
    mlp_shards = (
        (gate_weight.astype(f32) * gain_two).astype(low),
        (up_weight.astype(f32) * gain_two).astype(low),
        down_weight.T,
    )
    gate_full, up_full, down_full = [
        lax.all_gather(
            columns_of_plane(shard).reshape(-1, shard.shape[1] // 8), "z", axis=0, tiled=True
        )
        for shard in mlp_shards
    ]

    inputs = tokens[0].astype(f32)
    scale_one, unit_one = unit_of(inputs)
    qkv = dot(unit_one, qkv_full, (1, 0), low)
    queries = qkv[:, :wide]
    pairs = window_blocks(qkv[:, wide:], chips)
    mixed, logs = attend(queries, pairs, positions, size, base)
    resid = inputs + dot(mixed, out_full, (1, 1))

    scale_two, unit_two = unit_of(resid)
    units = jnp.concatenate(plane_gather(unit_two), 0)
    grad_final = jnp.concatenate(plane_gather(cotangent[0]), 0)
    gates = dot(units, gate_full, (1, 0))
    upward = dot(units, up_full, (1, 0))
    middle = geglu(gates, upward).astype(low)
    finals = dot(middle, down_full, (1, 1), low).reshape(8, count, -1)
    output = resid + plane_scatter([finals[r] for r in range(8)])

    grad_down = dot(grad_final, middle, (0, 0), low)
    grad_middle = dot(grad_final, down_full, (1, 0))
    grad_gates, grad_upward = jax.vjp(geglu, gates, upward)[1](grad_middle)
    grad_gates = grad_gates.astype(low)
    grad_upward = grad_upward.astype(low)
    grad_gate = dot(units, grad_gates, (0, 0), low)
    grad_up = dot(units, grad_upward, (0, 0), low)
    grad_units = (dot(grad_gates, gate_full, (1, 1)) + dot(grad_upward, up_full, (1, 1))).astype(low)
    grad_units = grad_units.reshape(8, count, -1)
    grad_unit_two = plane_scatter([grad_units[r] for r in range(8)])
    grad_resid = cotangent[0].astype(f32) + unit_back(grad_unit_two, resid, scale_two)

    def to_shard(partial):
        column = lax.psum_scatter(partial, "z", scatter_dimension=0, tiled=True)
        rows = column.shape[0] // 8
        split = lax.all_to_all(
            column.reshape(8, rows, -1), PLANE, split_axis=0, concat_axis=0, tiled=True
        )
        return jnp.swapaxes(split, 0, 1).reshape(rows, -1).astype(f32)

    down_sum, gate_sum, up_sum = to_shard(grad_down), to_shard(grad_gate), to_shard(grad_up)
    grad_mlp_gain = jnp.sum(
        gate_weight.astype(f32) * gate_sum + up_weight.astype(f32) * up_sum, axis=1
    )

    grad_attn = grad_resid.astype(low)
    out_sum = scatter_rows(dot(grad_attn, mixed, (0, 0), low))
    grad_mixed = dot(grad_attn, out_full, (1, 0), low)
    grad_queries, grad_pairs = attend_back(queries, grad_mixed, logs, pairs, positions, size, base)
    grad_pair = return_blocks(grad_pairs, chips, count).astype(low)
    grad_qkv = jnp.concatenate([grad_queries, grad_pair], 1)
    qkv_sum = scatter_rows(dot(unit_one, grad_qkv, (0, 0), low))
    grad_unit_one = dot(grad_qkv, qkv_full, (1, 1))
    grad_tokens = grad_resid + unit_back(grad_unit_one, inputs, scale_one)
    query_sum = qkv_sum[:, :wide]
    key_sum = qkv_sum[:, wide : wide + size]
    value_sum = qkv_sum[:, wide + size :]
    grad_attn_gain = (
        jnp.sum(query_weight.astype(f32) * query_sum, axis=1)
        + jnp.sum(key_weight.astype(f32) * key_sum, axis=1)
        + jnp.sum(value_weight.astype(f32) * value_sum, axis=1)
    )
    return (
        output[None],
        grad_tokens[None],
        grad_attn_gain,
        query_sum * gain_one,
        key_sum * gain_one,
        value_sum * gain_one,
        out_sum.T,
        grad_mlp_gain,
        gate_sum * gain_two,
        up_sum * gain_two,
        down_sum.T,
    )


def solution(mesh):
    ctx, fsdp = mesh.shape["ctx"], mesh.shape["fsdp"]
    fine = Mesh(mesh.devices.reshape(ctx // 4, 2, 2, fsdp), ("z", "y", "c", "x"))
    rows = ("z", "y", "c")
    every = ("z", "y", "c", "x")
    return jax.shard_map(
        local,
        mesh=fine,
        in_specs=(
            P("x", rows, None),
            P("x", rows),
            P(every),
            P(every, None),
            P(every, None),
            P(every, None),
            P(None, every),
            P(every),
            P(every, None),
            P(every, None),
            P(None, every),
            P("x", rows, None),
        ),
        out_specs=(
            P("x", rows, None),
            P("x", rows, None),
            P(every),
            P(every, None),
            P(every, None),
            P(every, None),
            P(None, every),
            P(every),
            P(every, None),
            P(every, None),
            P(None, every),
        ),
        check_vma=False,
    )
```

```python
import functools

import jax
import jax.numpy as jnp
from jax import lax
from jax.experimental import pallas as pl
from jax.experimental.pallas import tpu as pltpu
from jax.sharding import Mesh, PartitionSpec as P

WINDOW = 2048
SUB = 128
TILE = 512
epsilon = 1e-06
blocked_score = -1e30
PLANE = ("y", "c", "x")
low = jnp.bfloat16
f32 = jnp.float32


def dot(left, right, contract, kind=f32):
    return lax.dot_general(
        left, right, ((contract[:1], contract[1:]), ((), ())), preferred_element_type=f32
    ).astype(kind)


def swap(value, axis):
    return lax.ppermute(value, axis, [(0, 1), (1, 0)])


def plane_gather(own):
    half = own.shape[0] // 2
    by_x = swap(own, "x")
    by_y = swap(own, "y")
    own_c = swap(own, "c")
    diag_top = swap(by_y[:half], "x")
    diag_bottom = swap(by_x[half:], "y")
    by_x_c = swap(by_x, "c")
    by_y_c = swap(by_y, "c")
    diag = jnp.concatenate([diag_top, diag_bottom], 0)
    diag_c = swap(diag, "c")
    return [own, by_x, own_c, by_x_c, by_y, diag, by_y_c, diag_c]


def plane_scatter(parts):
    half = parts[0].shape[0] // 2

    def chip(r):
        return parts[r].astype(f32) + swap(parts[r + 2].astype(low), "c").astype(f32)

    diag = chip(5).astype(low)
    diag_x = swap(diag[:half], "x").astype(f32)
    diag_y = swap(diag[half:], "y").astype(f32)
    to_x, to_y = chip(1), chip(4)
    x_top = swap(to_x[:half].astype(low), "x").astype(f32)
    y_bottom = swap(to_y[half:].astype(low), "y").astype(f32)
    mine = chip(0)
    x_bottom = swap((to_x[half:] + diag_y).astype(low), "x").astype(f32)
    y_top = swap((to_y[:half] + diag_x).astype(low), "y").astype(f32)
    return jnp.concatenate(
        [mine[:half] + x_top + y_top, mine[half:] + x_bottom + y_bottom], 0
    )


def plane_index():
    return (lax.axis_index("y") * 2 + lax.axis_index("c")) * 2 + lax.axis_index("x")


def scatter_rows(partial):
    planes = lax.axis_size("z")
    wide = partial.shape[1]
    rows = partial.shape[0] // (planes * 8)
    blocks = partial.reshape(planes, 8, rows, wide)
    here = plane_index()
    parts = [
        lax.dynamic_slice(blocks, (0, here ^ r, 0, 0), (planes, 1, rows, wide))[:, 0]
        for r in range(8)
    ]
    return plane_scatter(parts).astype(low).reshape(planes * rows, wide)


def after(value, *earlier):
    return lax.optimization_barrier((value,) + earlier)[0]


def window_blocks(pair, chips):
    count = lax.axis_size("z") * lax.axis_size("y")
    same = [
        lax.ppermute(pair, ("z", "y"), [(i, i + d) for i in range(count - d)])
        for d in range(chips, 0, -1)
    ] + [pair]
    return same + [swap(block, "c") for block in same]


def return_blocks(mine, theirs, chips):
    count = lax.axis_size("z") * lax.axis_size("y")
    mine = mine + swap(theirs, "c").astype(f32)
    total = mine[chips]
    for d in range(chips, 0, -1):
        total = total + lax.ppermute(
            mine[chips - d].astype(low), ("z", "y"), [(i + d, i) for i in range(count - d)]
        ).astype(f32)
    return total


def two_heads(block, size):
    return jnp.concatenate([block[:, :size], block[:, size:]], 0)


def side_by_side(rows, size):
    half = rows.shape[0] // 2
    return jnp.concatenate([rows[:half], rows[half:]], 1)


def write_bias(bias, places, span, block):
    key = lax.broadcasted_iota(jnp.int32, (span, SUB), 0) - WINDOW
    query = lax.broadcasted_iota(jnp.int32, (span, SUB), 1)
    age = query - key
    seen = (age <= places) & (age >= 0) & (age < WINDOW)
    value = jnp.where(seen, 0.0, blocked_score).astype(f32)
    bias[:, :SUB] = value
    bias[:, SUB:] = value


def lay_window(core, blocks, window, turned, columns):
    count = blocks[0].shape[0]
    half = len(blocks) // 2
    for i in range(half):
        for which, block in ((core, blocks[i]), (1 - core, blocks[half + i])):
            at = pl.multiple_of((2 * i + which) * count, SUB)
            window[pl.ds(at, count), :] = block[...]
            turned[:, pl.ds(at, count)] = block[:, columns].T


def attend_kernel(size, scale, span, base, core, places, queries, *rest):
    blocks, (mixed, logs, bias, window, turned) = rest[:-5], rest[-5:]
    block = pl.program_id(0)
    count = blocks[0].shape[0]
    start = pl.multiple_of(core[0] * count + base + block * SUB, SUB)

    @pl.when((block == 0) & (pl.program_id(1) == 0))
    def _():
        lay_window(core[0], blocks, window, turned, slice(size, 2 * size))

    @pl.when(pl.program_id(1) == 0)
    def _():
        write_bias(bias, places[...], span, block)

    query = two_heads(queries[...], size)
    keys = window[pl.ds(start, span), :size]
    scores = dot(keys, query, (1, 1)) * scale + bias[...]
    highest = jnp.max(scores, axis=0, keepdims=True)
    expo = jnp.exp(scores - highest)
    total = jnp.sum(expo, axis=0, keepdims=True)
    flat = dot(turned[:, pl.ds(start, span)], expo.astype(low), (1, 0)) / total
    mixed[...] = side_by_side(flat.T, size).astype(low)
    logs[0] = highest + jnp.log(total)


def attend_back_kernel(size, scale, span, base, core, places, queries, grads, logs, *rest):
    blocks, (grad_queries, mine, theirs, bias, window, turned, total) = rest[:-7], rest[-7:]
    block = pl.program_id(0)
    count = blocks[0].shape[0]
    start = pl.multiple_of(core[0] * count + base + block * SUB, SUB)

    @pl.when((block == 0) & (pl.program_id(1) == 0))
    def _():
        lay_window(core[0], blocks, window, turned, slice(0, size))
        total[...] = jnp.zeros_like(total)

    @pl.when(pl.program_id(1) == 0)
    def _():
        write_bias(bias, places[...], span, block)

    query = two_heads(queries[...], size)
    grad = two_heads(grads[...], size)
    keys = window[pl.ds(start, span), :size]
    values = window[pl.ds(start, span), size:]
    probs = jnp.exp(dot(keys, query, (1, 1)) * scale + bias[...] - logs[0])
    total[pl.ds(start, span), size:] += dot(probs.astype(low), grad, (1, 0))
    grad_probs = dot(values, grad, (1, 1))
    inner = jnp.sum(probs * grad_probs, axis=0, keepdims=True)
    grad_scores = (probs * (grad_probs - inner)).astype(low)
    total[pl.ds(start, span), :size] += dot(grad_scores, query, (1, 0)) * scale
    flat = dot(turned[:, pl.ds(start, span)], grad_scores, (1, 0)) * scale
    grad_queries[...] = side_by_side(flat.T, size).astype(low)

    @pl.when((block == pl.num_programs(0) - 1) & (pl.program_id(1) == pl.num_programs(1) - 1))
    def _():
        for i in range(len(blocks) // 2):
            at = pl.multiple_of((2 * i + core[0]) * count, SUB)
            mine[i] = total[pl.ds(at, count), :]
            at = pl.multiple_of((2 * i + 1 - core[0]) * count, SUB)
            theirs[i] = total[pl.ds(at, count), :].astype(low)


def attend(queries, blocks, places, size, base):
    count, wide = queries.shape
    grid = (count // SUB, wide // (2 * size))
    span = WINDOW + SUB
    rows = len(blocks) * count
    core = lax.axis_index("c").astype(jnp.int32)[None]
    tile = pl.BlockSpec((SUB, 2 * size), lambda s, h, o: (s, h))
    return pl.pallas_call(
        functools.partial(attend_kernel, size, size**-0.5, span, base),
        out_shape=(
            jax.ShapeDtypeStruct((count, wide), low),
            jax.ShapeDtypeStruct((grid[0] * grid[1], 1, 2 * SUB), f32),
        ),
        grid_spec=pltpu.PrefetchScalarGridSpec(
            num_scalar_prefetch=1,
            grid=grid,
            in_specs=[pl.BlockSpec((1, SUB), lambda s, h, o: (0, s)), tile]
            + [pl.BlockSpec(block.shape, lambda s, h, o: (0, 0)) for block in blocks],
            out_specs=[tile, pl.BlockSpec((1, 1, 2 * SUB), lambda s, h, o: (s * grid[1] + h, 0, 0))],
            scratch_shapes=[
                pltpu.VMEM((span, 2 * SUB), f32),
                pltpu.VMEM((rows, 2 * size), low),
                pltpu.VMEM((size, rows), low),
            ],
        ),
        compiler_params=pltpu.CompilerParams(vmem_limit_bytes=56 << 20),
        cost_estimate=pl.CostEstimate(
            flops=4 * count * wide * span, bytes_accessed=8 << 20, transcendentals=count * span * wide // size
        ),
    )(core, places, queries, *blocks)


def attend_back(queries, grads, logs, blocks, places, size, base):
    count, wide = queries.shape
    grid = (count // SUB, wide // (2 * size))
    span = WINDOW + SUB
    rows = len(blocks) * count
    half = len(blocks) // 2
    core = lax.axis_index("c").astype(jnp.int32)[None]
    tile = pl.BlockSpec((SUB, 2 * size), lambda s, h, o: (s, h))
    whole = pl.BlockSpec((half, count, 2 * size), lambda s, h, o: (0, 0, 0))
    return pl.pallas_call(
        functools.partial(attend_back_kernel, size, size**-0.5, span, base),
        out_shape=(
            jax.ShapeDtypeStruct((count, wide), low),
            jax.ShapeDtypeStruct((half, count, 2 * size), f32),
            jax.ShapeDtypeStruct((half, count, 2 * size), low),
        ),
        grid_spec=pltpu.PrefetchScalarGridSpec(
            num_scalar_prefetch=1,
            grid=grid,
            in_specs=[
                pl.BlockSpec((1, SUB), lambda s, h, o: (0, s)),
                tile,
                tile,
                pl.BlockSpec((1, 1, 2 * SUB), lambda s, h, o: (s * grid[1] + h, 0, 0)),
            ]
            + [pl.BlockSpec(block.shape, lambda s, h, o: (0, 0)) for block in blocks],
            out_specs=[tile, whole, whole],
            scratch_shapes=[
                pltpu.VMEM((span, 2 * SUB), f32),
                pltpu.VMEM((rows, 2 * size), low),
                pltpu.VMEM((size, rows), low),
                pltpu.VMEM((rows, 2 * size), f32),
            ],
        ),
        compiler_params=pltpu.CompilerParams(vmem_limit_bytes=60 << 20),
        cost_estimate=pl.CostEstimate(
            flops=10 * count * wide * span, bytes_accessed=16 << 20, transcendentals=count * span * wide // size
        ),
    )(core, places, queries, grads, logs, *blocks)


def lay_rows(slots, blocks, full):
    planes, rows, _ = blocks[0].shape
    for r in range(8):
        for plane in range(planes):
            at = pl.multiple_of((plane * 8 + slots[r]) * rows, 16)
            full[pl.ds(at, rows), :] = blocks[r][plane]


def apply_kernel(slots, left, *rest):
    blocks, (out, full) = rest[:8], rest[8:]
    lay_rows(slots, blocks, full)
    out[...] = dot(left[...], full[...], (1, 0), low)


def apply_turned_kernel(slots, left, start, *rest):
    blocks, (out, full) = rest[:8], rest[8:]
    lay_rows(slots, blocks, full)

    @pl.when(pl.program_id(0) == 0)
    def _():
        out[...] = start[...]

    out[...] += dot(left[...], full[...], (1, 1))


def whole_rows(blocks):
    planes, rows, wide = blocks[0].shape
    here = plane_index()
    whole = jnp.zeros((planes, 8, rows, wide), blocks[0].dtype)
    for r, block in enumerate(blocks):
        whole = lax.dynamic_update_slice(whole, block[:, None], (0, here ^ r, 0, 0))
    return whole.reshape(planes * 8 * rows, wide)


def apply_rows(left, blocks, start=None):
    planes, rows, wide = blocks[0].shape
    if rows % 16 or wide % TILE:
        whole = whole_rows(blocks)
        if start is None:
            return dot(left, whole, (1, 0), low)
        return start + dot(left, whole, (1, 1))
    count, deep = left.shape[0], planes * 8 * rows
    slots = (plane_index() ^ jnp.arange(8)).astype(jnp.int32)
    pieces = [pl.BlockSpec((planes, rows, TILE), lambda n, s: (0, 0, n))] * 8
    whole = pl.BlockSpec((count, deep), lambda n, s: (0, 0))
    part = pl.BlockSpec((count, TILE), lambda n, s: (0, n))
    if start is None:
        kernel, given, specs, result = apply_kernel, [left], [whole], part
        shape = jax.ShapeDtypeStruct((count, wide), low)
    else:
        kernel, given, specs, result = apply_turned_kernel, [left, start], [part, whole], whole
        shape = jax.ShapeDtypeStruct((count, deep), f32)
    return pl.pallas_call(
        kernel,
        out_shape=shape,
        grid_spec=pltpu.PrefetchScalarGridSpec(
            num_scalar_prefetch=1,
            grid=(wide // TILE,),
            in_specs=specs + pieces,
            out_specs=result,
            scratch_shapes=[pltpu.VMEM((deep, TILE), low)],
        ),
        compiler_params=pltpu.CompilerParams(vmem_limit_bytes=48 << 20),
        cost_estimate=pl.CostEstimate(
            flops=2 * count * deep * wide, bytes_accessed=2 * deep * wide + 8 * count * deep, transcendentals=0
        ),
    )(slots, *given, *blocks)


def mlp_kernel(part, units, grads, weights, *rest):
    before, (out, grad_units, hidden) = rest[:-3], rest[-3:]
    both = dot(units[...], weights[:, : 2 * part], (1, 0))
    gates, upward = both[:, :part], both[:, part:]
    grad_middle = dot(grads[...], weights[:, 2 * part :], (1, 0))
    slope = 0.7978845608028654
    square = gates * gates
    bend = jnp.tanh(slope * gates * (1.0 + 0.044715 * square))
    half = 0.5 * (1.0 + bend)
    gelu = gates * half
    grad_gelu = half + 0.5 * gates * (1.0 - bend * bend) * (slope * (1.0 + 3 * 0.044715 * square))
    hidden[:, :part] = (grad_middle * upward * grad_gelu).astype(low)
    hidden[:, part : 2 * part] = (grad_middle * gelu).astype(low)
    hidden[:, 2 * part :] = (gelu * upward).astype(low)
    value = dot(hidden[:, 2 * part :], weights[:, 2 * part :], (1, 1))
    if before:
        value = value + before[0][...].astype(f32)
    out[...] = value.astype(low)
    value = dot(hidden[:, : 2 * part], weights[:, : 2 * part], (1, 1))
    if before:
        value = value + before[1][...].astype(f32)
    grad_units[...] = value.astype(low)


def mlp(units, grads, weights, before, rows):
    count, wide = units.shape
    deep = weights.shape[1]
    tile = pl.BlockSpec((rows, wide), lambda i: (i, 0))
    return pl.pallas_call(
        functools.partial(mlp_kernel, deep // 3),
        out_shape=(
            jax.ShapeDtypeStruct((count, wide), low),
            jax.ShapeDtypeStruct((count, wide), low),
            jax.ShapeDtypeStruct((count, deep), low),
        ),
        grid=(count // rows,),
        in_specs=[tile, tile, pl.BlockSpec(weights.shape, lambda i: (0, 0), pipeline_mode=pl.Buffered(1))]
        + [tile] * len(before),
        out_specs=[tile, tile, pl.BlockSpec((rows, deep), lambda i: (i, 0))],
        compiler_params=pltpu.CompilerParams(vmem_limit_bytes=60 << 20),
        cost_estimate=pl.CostEstimate(
            flops=4 * count * wide * deep,
            bytes_accessed=2 * (wide * deep + count * (4 * wide + deep)),
            transcendentals=count * deep // 3,
        ),
    )(units, grads, weights, *before)


def mlp_grads_kernel(units_a, units_b, grads_a, grads_b, hidden_a, hidden_b, out, turned):
    piece = pl.program_id(1)
    count = units_a.shape[0]

    @pl.when(piece == 0)
    def _():
        turned[:, :count] = units_a[...].T
        turned[:, count:] = units_b[...].T

    @pl.when(piece == 2)
    def _():
        turned[:, :count] = grads_a[...].T
        turned[:, count:] = grads_b[...].T

    out[...] = (
        dot(turned[:, :count], hidden_a[...], (1, 0)) + dot(turned[:, count:], hidden_b[...], (1, 0))
    ).astype(low)


def mlp_grads(units, grads, hidden):
    count, wide = units[0].shape
    deep = hidden[0].shape[1]
    part = deep // 3
    rows = 512
    left = pl.BlockSpec((count, rows), lambda d, f: (0, d))
    right = pl.BlockSpec((count, part), lambda d, f: (0, f))
    return pl.pallas_call(
        mlp_grads_kernel,
        out_shape=jax.ShapeDtypeStruct((wide, deep), low),
        grid=(wide // rows, 3),
        in_specs=[left] * 4 + [right] * 2,
        out_specs=pl.BlockSpec((rows, part), lambda d, f: (d, f)),
        scratch_shapes=[pltpu.VMEM((rows, 2 * count), low)],
        compiler_params=pltpu.CompilerParams(vmem_limit_bytes=56 << 20),
        cost_estimate=pl.CostEstimate(
            flops=4 * count * wide * deep,
            bytes_accessed=8 * count * wide + 20 * count * deep + 2 * wide * deep,
            transcendentals=0,
        ),
    )(*units, *grads, *hidden)


def shares(columns):
    tiles = -(-columns // 128)
    few, more = divmod(tiles, 8)
    sizes = [128 * (few + (p < more)) for p in range(8)]
    return [(sum(sizes[:p]), size) for p, size in enumerate(sizes)], 128 * (few + (more > 0))


def unit_of(values):
    scale = lax.rsqrt(jnp.mean(values * values, axis=-1, keepdims=True) + epsilon)
    return scale, (values * scale).astype(low)


def unit_back(grad, values, scale):
    unit = values * scale
    return scale * (grad - unit * jnp.mean(grad * unit, axis=-1, keepdims=True))


def local(
    tokens,
    positions,
    attn_gain,
    query_weight,
    key_weight,
    value_weight,
    out_weight,
    mlp_gain,
    gate_weight,
    up_weight,
    down_weight,
    cotangent,
):
    count = tokens.shape[1]
    size = key_weight.shape[1]
    wide = query_weight.shape[1]
    reach = (WINDOW + count - 2) // count
    chips = (reach + 1) // 2
    base = 2 * chips * count - WINDOW
    gain_one = attn_gain[:, None]
    gain_two = mlp_gain[:, None]

    qkv_shard = (
        jnp.concatenate([query_weight, key_weight, value_weight], 1).astype(f32) * gain_one
    ).astype(low)
    qkv_column = lax.all_gather(qkv_shard, "z", axis=0, tiled=False)
    out_column = lax.all_gather(after(out_weight.T, qkv_column), "z", axis=0, tiled=False)

    spans, share = shares(gate_weight.shape[1])
    parts = 2 if share % 256 == 0 else 1
    part = share // parts
    mlp_shards = (
        (gate_weight.astype(f32) * gain_two).astype(low),
        (up_weight.astype(f32) * gain_two).astype(low),
        down_weight.T,
    )
    split = [
        jnp.stack([jnp.pad(shard[:, at : at + n], ((0, 0), (0, share - n))) for at, n in spans])
        for shard in mlp_shards
    ]
    mlp_columns = [
        lax.all_to_all(
            jnp.concatenate([whole[:, :, k * part : (k + 1) * part] for whole in split], 2),
            PLANE,
            split_axis=0,
            concat_axis=0,
            tiled=True,
        ).reshape(-1, 3 * part)
        for k in range(parts)
    ]
    mlp_full = []
    earlier = out_column
    for column in mlp_columns:
        earlier = lax.all_gather(after(column, earlier), "z", axis=0, tiled=True)
        mlp_full.append(earlier)

    qkv_blocks = plane_gather(qkv_column)
    inputs = tokens[0].astype(f32)
    scale_one, unit_one = unit_of(inputs)
    qkv = apply_rows(unit_one, qkv_blocks)
    out_blocks = plane_gather(after(out_column, qkv_blocks[7]))
    queries = qkv[:, :wide]
    pairs = window_blocks(qkv[:, wide:], chips)
    mixed, logs = attend(queries, pairs, positions, size, base)
    resid = apply_rows(mixed, out_blocks, inputs)

    scale_two, unit_two = unit_of(resid)
    finals = plane_gather(after(cotangent[0], out_blocks[7]))
    units = plane_gather(unit_two)
    far, near = (5, 7, 1, 3), (4, 6, 0, 2)
    units = [jnp.concatenate([units[r] for r in half], 0) for half in (far, near)]
    finals = [jnp.concatenate([finals[r] for r in half], 0) for half in (far, near)]
    sums = [(), ()]
    hidden = []
    for k in range(parts):
        results = [None, None]
        for half in (1, 0) if k < parts - 1 else (0, 1):
            results[half] = mlp(units[half], finals[half], mlp_full[k], sums[half], count)
        sums = [result[:2] for result in results]
        hidden.append([result[2] for result in results])

    def by_device(index):
        rows = [sums[half][index].reshape(4, count, -1) for half in (0, 1)]
        found = {r: rows[half][i] for half, group in enumerate((far, near)) for i, r in enumerate(group)}
        return [found[r] for r in range(8)]

    grad_unit_two = plane_scatter(by_device(1))
    grad_resid = cotangent[0].astype(f32) + unit_back(grad_unit_two, resid, scale_two)

    columns = []
    earlier = mlp_full[-1]
    for k in range(parts):
        partial = mlp_grads(units, finals, hidden[k])
        earlier = lax.psum_scatter(after(partial, earlier), "z", scatter_dimension=0, tiled=True)
        columns.append(earlier)

    grad_attn = grad_resid.astype(low)
    grad_mixed = apply_rows(grad_attn, out_blocks)
    out_scattered = scatter_rows(dot(grad_attn, mixed, (0, 0), low))
    grad_queries, mine, theirs = attend_back(queries, grad_mixed, logs, pairs, positions, size, base)
    grad_pair = return_blocks(mine, theirs, chips).astype(low)
    grad_qkv = jnp.concatenate([grad_queries, grad_pair], 1)
    qkv_scattered = scatter_rows(dot(unit_one, grad_qkv, (0, 0), low))
    grad_unit_one = apply_rows(grad_qkv, qkv_blocks, jnp.zeros_like(inputs))
    grad_tokens = grad_resid + unit_back(grad_unit_one, inputs, scale_one)

    def over_z(column, earlier):
        return lax.psum_scatter(after(column, earlier), "z", scatter_dimension=0, tiled=True)

    out_low = over_z(out_scattered, earlier)
    qkv_low = over_z(qkv_scattered, out_low)
    out_sum = out_low.astype(f32)
    qkv_sum = qkv_low.astype(f32)
    query_sum = qkv_sum[:, :wide]
    key_sum = qkv_sum[:, wide : wide + size]
    value_sum = qkv_sum[:, wide + size :]
    grad_attn_gain = (
        jnp.sum(query_weight.astype(f32) * query_sum, axis=1)
        + jnp.sum(key_weight.astype(f32) * key_sum, axis=1)
        + jnp.sum(value_weight.astype(f32) * value_sum, axis=1)
    )
    output = resid + plane_scatter([after(value, qkv_scattered) for value in by_device(0)])

    whole = [
        lax.all_to_all(
            column.reshape(8, -1, 3 * part), PLANE, split_axis=0, concat_axis=0, tiled=True
        )
        for column in columns
    ]

    def joined(which):
        pieces = []
        for p, (_, n) in enumerate(spans):
            for k in range(parts):
                width = min(part, n - k * part)
                if width > 0:
                    pieces.append(whole[k][p, :, which * part : which * part + width])
        return jnp.concatenate(pieces, 1).astype(f32)

    gate_sum, up_sum, down_sum = joined(0), joined(1), joined(2)
    grad_mlp_gain = jnp.sum(
        gate_weight.astype(f32) * gate_sum + up_weight.astype(f32) * up_sum, axis=1
    )
    return (
        output[None],
        grad_tokens[None],
        grad_attn_gain,
        query_sum * gain_one,
        key_sum * gain_one,
        value_sum * gain_one,
        out_sum.T,
        grad_mlp_gain,
        gate_sum * gain_two,
        up_sum * gain_two,
        down_sum.T,
    )


def solution(mesh):
    ctx, fsdp = mesh.shape["ctx"], mesh.shape["fsdp"]
    fine = Mesh(mesh.devices.reshape(ctx // 4, 2, 2, fsdp), ("z", "y", "c", "x"))
    rows = ("z", "y", "c")
    every = ("z", "y", "c", "x")
    return jax.shard_map(
        local,
        mesh=fine,
        in_specs=(
            P("x", rows, None),
            P("x", rows),
            P(every),
            P(every, None),
            P(every, None),
            P(every, None),
            P(None, every),
            P(every),
            P(every, None),
            P(every, None),
            P(None, every),
            P("x", rows, None),
        ),
        out_specs=(
            P("x", rows, None),
            P("x", rows, None),
            P(every),
            P(every, None),
            P(every, None),
            P(every, None),
            P(None, every),
            P(every),
            P(every, None),
            P(every, None),
            P(None, every),
        ),
        check_vma=False,
    )
```

```python
import functools

import jax
import jax.numpy as jnp
from jax import lax
from jax.experimental import pallas as pl
from jax.experimental.pallas import tpu as pltpu
from jax.sharding import Mesh, PartitionSpec as P

WINDOW = 2048
SUB = 128
TILE = 512
FEW = 4
epsilon = 1e-06
blocked_score = -1e30
PLANE = ("y", "c", "x")
low = jnp.bfloat16
f32 = jnp.float32
NOMINAL = pl.CostEstimate(flops=1 << 20, bytes_accessed=1 << 12, transcendentals=0)


def dot(left, right, contract, kind=f32):
    return lax.dot_general(
        left, right, ((contract[:1], contract[1:]), ((), ())), preferred_element_type=f32
    ).astype(kind)


def swap(value, axis):
    return lax.ppermute(value, axis, [(0, 1), (1, 0)])


def plane_gather(own, second=(), third=()):
    half = own.shape[0] // 2
    by_x = swap(own, "x")
    by_y = swap(own, "y")
    own_c = swap(own, "c")
    diag = (
        swap(after(by_y[:half], *second), "x"),
        swap(after(by_x[half:], *second), "y"),
    )
    by_x_c = swap(after(by_x, *second), "c")
    by_y_c = swap(after(by_y, *second), "c")
    diag_c = tuple(swap(after(part, *third), "c") for part in diag)
    return [own, by_x, own_c, by_x_c, by_y, diag, by_y_c, diag_c]


def joined_blocks(blocks):
    return [jnp.concatenate(block, 0) if isinstance(block, tuple) else block for block in blocks]


def core_sum(keep, send):
    return keep.astype(f32) + swap(send, "c").astype(f32)


def scatter_start(diag, to_x, to_y):
    half = diag.shape[0] // 2
    return (
        swap(diag[:half].astype(low), "x"),
        swap(diag[half:].astype(low), "y"),
        swap(to_x[:half].astype(low), "x"),
        swap(to_y[half:].astype(low), "y"),
    )


def scatter_turn(started, to_x, to_y, later=()):
    half = to_x.shape[0] // 2
    diag_x, diag_y = (value.astype(f32) for value in started[:2])
    return (
        after((to_x[half:] + diag_y).astype(low), *later),
        after((to_y[:half] + diag_x).astype(low), *later),
    )


def scatter_end(started, x_bottom, y_top, own):
    half = own.shape[0] // 2
    x_top, y_bottom = (value.astype(f32) for value in started[2:])
    x_bottom, y_top = swap(x_bottom, "x").astype(f32), swap(y_top, "y").astype(f32)
    return jnp.concatenate([own[:half] + x_top + y_top, own[half:] + x_bottom + y_bottom], 0)


def shift(value, steps):
    count = lax.axis_size("z")
    return lax.ppermute(value, "z", [(i, i + steps) for i in range(count) if 0 <= i + steps < count])


def planes_scatter(column):
    count = lax.axis_size("z")
    if count > FEW:
        return lax.psum_scatter(column, "z", scatter_dimension=0, tiled=False).astype(f32)
    here = lax.axis_index("z")
    total = lax.dynamic_index_in_dim(column, here, 0, False).astype(f32)
    for r in range(1, count):
        part = lax.dynamic_index_in_dim(column, (here + r) % count, 0, False)
        total = total + shift(part, r).astype(f32) + shift(part, r - count).astype(f32)
    return total


def plane_index():
    return (lax.axis_index("y") * 2 + lax.axis_index("c")) * 2 + lax.axis_index("x")


def after(value, *earlier):
    return lax.optimization_barrier((value,) + earlier)[0]


def window_blocks(pair, chips):
    count = lax.axis_size("z") * lax.axis_size("y")
    same = [
        lax.ppermute(pair, ("z", "y"), [(i, i + d) for i in range(count - d)])
        for d in range(chips, 0, -1)
    ] + [pair]
    same = list(lax.optimization_barrier(tuple(same)))
    return same + [swap(block, "c") for block in same]


def return_blocks(mine, theirs, chips):
    count = lax.axis_size("z") * lax.axis_size("y")
    mine = mine + swap(theirs, "c").astype(f32)
    total = mine[chips]
    for d in range(chips, 0, -1):
        total = total + lax.ppermute(
            mine[chips - d].astype(low), ("z", "y"), [(i + d, i) for i in range(count - d)]
        ).astype(f32)
    return total


def two_heads(block, size):
    return jnp.concatenate([block[:, :size], block[:, size:]], 0)


def side_by_side(rows, size):
    half = rows.shape[0] // 2
    return jnp.concatenate([rows[:half], rows[half:]], 1)


def write_bias(bias, places, span, block):
    key = lax.broadcasted_iota(jnp.int32, (span, SUB), 0) - WINDOW
    query = lax.broadcasted_iota(jnp.int32, (span, SUB), 1)
    age = query - key
    seen = (age <= places) & (age >= 0) & (age < WINDOW)
    value = jnp.where(seen, 0.0, blocked_score).astype(f32)
    bias[:, :SUB] = value
    bias[:, SUB:] = value


def lay_window(core, blocks, window, turned, columns):
    count = blocks[0].shape[0]
    half = len(blocks) // 2
    for i in range(half):
        for which, block in ((core, blocks[i]), (1 - core, blocks[half + i])):
            at = pl.multiple_of((2 * i + which) * count, SUB)
            window[pl.ds(at, count), :] = block[...]
            turned[:, pl.ds(at, count)] = block[:, columns].T


def attend_kernel(size, scale, span, base, core, places, queries, *rest):
    blocks, (mixed, logs, bias, window, turned) = rest[:-5], rest[-5:]
    block = pl.program_id(0)
    count = blocks[0].shape[0]
    start = pl.multiple_of(core[0] * count + base + block * SUB, SUB)

    @pl.when((block == 0) & (pl.program_id(1) == 0))
    def _():
        lay_window(core[0], blocks, window, turned, slice(size, 2 * size))

    @pl.when(pl.program_id(1) == 0)
    def _():
        write_bias(bias, places[...], span, block)

    query = two_heads(queries[...], size)
    keys = window[pl.ds(start, span), :size]
    scores = dot(keys, query, (1, 1)) * scale + bias[...]
    highest = jnp.max(scores, axis=0, keepdims=True)
    expo = jnp.exp(scores - highest)
    total = jnp.sum(expo, axis=0, keepdims=True)
    flat = dot(turned[:, pl.ds(start, span)], expo.astype(low), (1, 0)) / total
    mixed[...] = side_by_side(flat.T, size).astype(low)
    logs[0] = highest + jnp.log(total)


def attend_back_kernel(size, scale, span, base, core, places, queries, grads, logs, *rest):
    blocks, (grad_queries, mine, theirs, bias, window, turned, total) = rest[:-7], rest[-7:]
    block = pl.program_id(0)
    count = blocks[0].shape[0]
    start = pl.multiple_of(core[0] * count + base + block * SUB, SUB)

    @pl.when((block == 0) & (pl.program_id(1) == 0))
    def _():
        lay_window(core[0], blocks, window, turned, slice(0, size))
        total[...] = jnp.zeros_like(total)

    @pl.when(pl.program_id(1) == 0)
    def _():
        write_bias(bias, places[...], span, block)

    query = two_heads(queries[...], size)
    grad = two_heads(grads[...], size)
    keys = window[pl.ds(start, span), :size]
    values = window[pl.ds(start, span), size:]
    probs = jnp.exp(dot(keys, query, (1, 1)) * scale + bias[...] - logs[0])
    total[pl.ds(start, span), size:] += dot(probs.astype(low), grad, (1, 0))
    grad_probs = dot(values, grad, (1, 1))
    inner = jnp.sum(probs * grad_probs, axis=0, keepdims=True)
    grad_scores = (probs * (grad_probs - inner)).astype(low)
    total[pl.ds(start, span), :size] += dot(grad_scores, query, (1, 0)) * scale
    flat = dot(turned[:, pl.ds(start, span)], grad_scores, (1, 0)) * scale
    grad_queries[...] = side_by_side(flat.T, size).astype(low)

    @pl.when((block == pl.num_programs(0) - 1) & (pl.program_id(1) == pl.num_programs(1) - 1))
    def _():
        for i in range(len(blocks) // 2):
            at = pl.multiple_of((2 * i + core[0]) * count, SUB)
            mine[i] = total[pl.ds(at, count), :]
            at = pl.multiple_of((2 * i + 1 - core[0]) * count, SUB)
            theirs[i] = total[pl.ds(at, count), :].astype(low)


def attend(queries, blocks, places, size, base):
    count, wide = queries.shape
    grid = (count // SUB, wide // (2 * size))
    span = WINDOW + SUB
    rows = len(blocks) * count
    core = lax.axis_index("c").astype(jnp.int32)[None]
    tile = pl.BlockSpec((SUB, 2 * size), lambda s, h, o: (s, h))
    return pl.pallas_call(
        functools.partial(attend_kernel, size, size**-0.5, span, base),
        out_shape=(
            jax.ShapeDtypeStruct((count, wide), low),
            jax.ShapeDtypeStruct((grid[0] * grid[1], 1, 2 * SUB), f32),
        ),
        grid_spec=pltpu.PrefetchScalarGridSpec(
            num_scalar_prefetch=1,
            grid=grid,
            in_specs=[pl.BlockSpec((1, SUB), lambda s, h, o: (0, s)), tile]
            + [pl.BlockSpec(block.shape, lambda s, h, o: (0, 0)) for block in blocks],
            out_specs=[tile, pl.BlockSpec((1, 1, 2 * SUB), lambda s, h, o: (s * grid[1] + h, 0, 0))],
            scratch_shapes=[
                pltpu.VMEM((span, 2 * SUB), f32),
                pltpu.VMEM((rows, 2 * size), low),
                pltpu.VMEM((size, rows), low),
            ],
        ),
        compiler_params=pltpu.CompilerParams(vmem_limit_bytes=56 << 20),
        cost_estimate=NOMINAL,
    )(core, places, queries, *blocks)


def attend_back(queries, grads, logs, blocks, places, size, base):
    count, wide = queries.shape
    grid = (count // SUB, wide // (2 * size))
    span = WINDOW + SUB
    rows = len(blocks) * count
    half = len(blocks) // 2
    core = lax.axis_index("c").astype(jnp.int32)[None]
    tile = pl.BlockSpec((SUB, 2 * size), lambda s, h, o: (s, h))
    whole = pl.BlockSpec((half, count, 2 * size), lambda s, h, o: (0, 0, 0))
    return pl.pallas_call(
        functools.partial(attend_back_kernel, size, size**-0.5, span, base),
        out_shape=(
            jax.ShapeDtypeStruct((count, wide), low),
            jax.ShapeDtypeStruct((half, count, 2 * size), f32),
            jax.ShapeDtypeStruct((half, count, 2 * size), low),
        ),
        grid_spec=pltpu.PrefetchScalarGridSpec(
            num_scalar_prefetch=1,
            grid=grid,
            in_specs=[
                pl.BlockSpec((1, SUB), lambda s, h, o: (0, s)),
                tile,
                tile,
                pl.BlockSpec((1, 1, 2 * SUB), lambda s, h, o: (s * grid[1] + h, 0, 0)),
            ]
            + [pl.BlockSpec(block.shape, lambda s, h, o: (0, 0)) for block in blocks],
            out_specs=[tile, whole, whole],
            scratch_shapes=[
                pltpu.VMEM((span, 2 * SUB), f32),
                pltpu.VMEM((rows, 2 * size), low),
                pltpu.VMEM((size, rows), low),
                pltpu.VMEM((rows, 2 * size), f32),
            ],
        ),
        compiler_params=pltpu.CompilerParams(vmem_limit_bytes=60 << 20),
        cost_estimate=NOMINAL,
    )(core, places, queries, grads, logs, *blocks)


def lay_rows(slots, blocks, full):
    planes, rows, _ = blocks[0].shape
    for r in range(8):
        for plane in range(planes):
            at = pl.multiple_of((plane * 8 + slots[r]) * rows, 16)
            full[pl.ds(at, rows), :] = blocks[r][plane]


def apply_kernel(slots, left, *rest):
    blocks, (out, full) = rest[:8], rest[8:]
    lay_rows(slots, blocks, full)
    out[...] = dot(left[...], full[...], (1, 0), low)


def apply_turned_kernel(slots, left, start, *rest):
    blocks, (out, full) = rest[:8], rest[8:]
    lay_rows(slots, blocks, full)

    @pl.when(pl.program_id(0) == 0)
    def _():
        out[...] = start[...]

    out[...] += dot(left[...], full[...], (1, 1))


def whole_rows(blocks):
    planes, rows, wide = blocks[0].shape
    here = plane_index()
    whole = jnp.zeros((planes, 8, rows, wide), blocks[0].dtype)
    for r, block in enumerate(blocks):
        whole = lax.dynamic_update_slice(whole, block[:, None], (0, here ^ r, 0, 0))
    return whole.reshape(planes * 8 * rows, wide)


def apply_rows(left, blocks, start=None):
    planes, rows, wide = blocks[0].shape
    if rows % 16 or wide % TILE:
        whole = whole_rows(blocks)
        if start is None:
            return dot(left, whole, (1, 0), low)
        return start + dot(left, whole, (1, 1))
    count, deep = left.shape[0], planes * 8 * rows
    slots = (plane_index() ^ jnp.arange(8)).astype(jnp.int32)
    pieces = [pl.BlockSpec((planes, rows, TILE), lambda n, s: (0, 0, n))] * 8
    whole = pl.BlockSpec((count, deep), lambda n, s: (0, 0))
    part = pl.BlockSpec((count, TILE), lambda n, s: (0, n))
    if start is None:
        kernel, given, specs, result = apply_kernel, [left], [whole], part
        shape = jax.ShapeDtypeStruct((count, wide), low)
    else:
        kernel, given, specs, result = apply_turned_kernel, [left, start], [part, whole], whole
        shape = jax.ShapeDtypeStruct((count, deep), f32)
    return pl.pallas_call(
        kernel,
        out_shape=shape,
        grid_spec=pltpu.PrefetchScalarGridSpec(
            num_scalar_prefetch=1,
            grid=(wide // TILE,),
            in_specs=specs + pieces,
            out_specs=result,
            scratch_shapes=[pltpu.VMEM((deep, TILE), low)],
        ),
        compiler_params=pltpu.CompilerParams(vmem_limit_bytes=48 << 20),
        cost_estimate=NOMINAL,
    )(slots, *given, *blocks)


def row_grads_kernel(slots, left, right, keep, send, turned):
    @pl.when(pl.program_id(1) == 0)
    def _():
        turned[...] = left[...].T

    rows = keep.shape[2]
    value = dot(turned[...], right[...], (1, 0), low)
    for i in range(8):
        place = slots[i]

        @pl.when(place < 4)
        def _():
            keep[place, 0] = value[i * rows : (i + 1) * rows]

        @pl.when(place >= 4)
        def _():
            send[place - 4, 0] = value[i * rows : (i + 1) * rows]


def row_grads(left, right):
    planes = lax.axis_size("z")
    count, deep = left.shape
    wide = right.shape[1]
    rows = deep // (planes * 8)
    places = jnp.array([3, 1, 7, 5, 2, 0, 6, 4], jnp.int32)
    slots = places[plane_index() ^ jnp.arange(8)]
    if rows % 16 or wide % TILE or (planes * 8 * rows) % (planes * 128):
        blocks = dot(left, right, (0, 0), low).reshape(planes, 8, rows, wide)
        order = jnp.argsort(slots)
        blocks = jnp.swapaxes(jnp.take(blocks, order, axis=1), 0, 1)
        return blocks[:4], blocks[4:]
    group = pl.BlockSpec((4, 1, rows, TILE), lambda z, n, s: (0, z, 0, n))
    shape = jax.ShapeDtypeStruct((4, planes, rows, wide), low)
    return pl.pallas_call(
        row_grads_kernel,
        out_shape=(shape, shape),
        grid_spec=pltpu.PrefetchScalarGridSpec(
            num_scalar_prefetch=1,
            grid=(planes, wide // TILE),
            in_specs=[
                pl.BlockSpec((count, 8 * rows), lambda z, n, s: (0, z)),
                pl.BlockSpec((count, TILE), lambda z, n, s: (0, n)),
            ],
            out_specs=[group, group],
            scratch_shapes=[pltpu.VMEM((8 * rows, count), low)],
        ),
        compiler_params=pltpu.CompilerParams(vmem_limit_bytes=48 << 20),
        cost_estimate=NOMINAL,
    )(slots, left, right)


def mlp_kernel(part, per, tiles, *rest):
    weights, rest = rest[:per], rest[per:]
    pieces = 2 * sum(tiles)
    sources, rest = rest[:pieces], rest[pieces:]
    outs, grad_units, hidden = rest[0:2], rest[2:4], rest[4 : 4 + per]
    units, grads, arrived = rest[4 + per :]
    step = pl.program_id(0)

    def fetches(tile):
        first = 2 * sum(tiles[:tile])
        found = []
        for array, target in enumerate((units, grads)):
            at = 0
            for i in range(tiles[tile]):
                source = sources[first + array * tiles[tile] + i]
                found.append(
                    pltpu.make_async_copy(
                        source,
                        target.at[tile % 2, pl.ds(at, source.shape[0])],
                        arrived.at[tile % 2, array, i],
                    )
                )
                at += source.shape[0]
        return found

    for tile in range(len(tiles)):

        @pl.when(step == tile)
        def _():
            if tile == 0:
                for copy in fetches(0):
                    copy.start()
            if tile + 1 < len(tiles):
                for copy in fetches(tile + 1):
                    copy.start()
            for copy in fetches(tile):
                copy.wait()

    unit = units[step % 2]
    grad = grads[step % 2]
    slope = 0.7978845608028654
    for j in range(per):
        both = dot(unit, weights[j][:, : 2 * part], (1, 0))
        gates, upward = both[:, :part], both[:, part:]
        grad_middle = dot(grad, weights[j][:, 2 * part :], (1, 0))
        square = gates * gates
        bend = jnp.tanh(slope * gates * (1.0 + 0.044715 * square))
        half = 0.5 * (1.0 + bend)
        gelu = gates * half
        grad_gelu = half + 0.5 * gates * (1.0 - bend * bend) * (slope * (1.0 + 3 * 0.044715 * square))
        hidden[j][:, :part] = (grad_middle * upward * grad_gelu).astype(low)
        hidden[j][:, part : 2 * part] = (grad_middle * gelu).astype(low)
        hidden[j][:, 2 * part :] = (gelu * upward).astype(low)
    for which, targets in enumerate((outs, grad_units)):
        value = 0.0
        for j in range(per):
            columns = slice(0, 2 * part) if which else slice(2 * part, 3 * part)
            value = value + dot(hidden[j][:, columns], weights[j][:, columns], (1, 1))
        for side in range(2):

            @pl.when(step // (len(tiles) // 2) == side)
            def _():
                targets[side][...] = value.astype(low)


def mlp(units, grads, weights):
    rows = sum(piece.shape[0] for piece in units[0])
    count, wide = rows * len(units), units[0][0].shape[1]
    per, each = len(weights), weights[0].shape[1]
    tiles = tuple(len(tile) for tile in units)
    sources = [piece for pair in zip(units, grads) for tile in pair for piece in tile]
    side = len(units) // 2
    sides = [
        pl.BlockSpec((rows, wide), lambda i: (jnp.minimum(i, side - 1), 0)),
        pl.BlockSpec((rows, wide), lambda i: (jnp.maximum(i - side, 0), 0)),
    ]
    half = jax.ShapeDtypeStruct((count // 2, wide), low)
    return pl.pallas_call(
        functools.partial(mlp_kernel, each // 3, per, tiles),
        out_shape=[half] * 4 + [jax.ShapeDtypeStruct((count, each), low)] * per,
        grid=(len(units),),
        in_specs=[pl.BlockSpec((wide, each), lambda i: (0, 0), pipeline_mode=pl.Buffered(1))] * per
        + [pl.BlockSpec(memory_space=pl.ANY)] * len(sources),
        out_specs=sides * 2 + [pl.BlockSpec((rows, each), lambda i: (i, 0))] * per,
        scratch_shapes=[
            pltpu.VMEM((2, rows, wide), low),
            pltpu.VMEM((2, rows, wide), low),
            pltpu.SemaphoreType.DMA((2, 2, max(tiles))),
        ],
        compiler_params=pltpu.CompilerParams(vmem_limit_bytes=62 << 20),
        cost_estimate=NOMINAL,
    )(*weights, *sources)


def mlp_grads_kernel(number, *rest):
    units, grads, hidden, rest = rest[:number], rest[number : 2 * number], rest[2 * number : 2 * number + 2], rest[2 * number + 2 :]
    outs, turned = rest[:-1], rest[-1]
    step = pl.program_id(0)
    part = hidden[0].shape[1] // 3
    out_wide = outs[0].shape[1]
    piece = min(part, 256)

    def turn(slot, which, sources, share, shares):
        at = 0
        for i, source in enumerate(sources):
            if i * shares // len(sources) == share:
                turned[slot, which, :, at : at + source.shape[0]] = source[...].T
            at += source.shape[0]

    def multiply(slot, which, at):
        value, start = 0.0, 0
        for block in hidden:
            left = turned[slot, which, :, start : start + block.shape[0]]
            value = value + dot(left, block[:, at : at + piece], (1, 0))
            start += block.shape[0]
        outs[at // out_wide][:, at % out_wide : at % out_wide + piece] = value.astype(low)

    work = [(at // (2 * part), at) for at in range(0, 3 * part, piece)]

    @pl.when(step == 0)
    def _():
        turn(0, 0, units, 0, 1)
        turn(0, 1, grads, 0, 1)

    @pl.when(step > 0)
    def _():
        for i, (which, at) in enumerate(work):
            multiply((step - 1) % 2, which, at)
            turn(step % 2, 0, units, i, len(work))
            turn(step % 2, 1, grads, i, len(work))


def mlp_grads(units, grads, hidden, pieces):
    wide = units[0].shape[1]
    deep = hidden[0].shape[1]
    count = sum(piece.shape[0] for piece in units)
    rows = 512
    last = wide // rows - 1
    return pl.pallas_call(
        functools.partial(mlp_grads_kernel, len(units)),
        out_shape=[jax.ShapeDtypeStruct((wide, deep // pieces), low)] * pieces,
        grid=(last + 2,),
        in_specs=[
            pl.BlockSpec((piece.shape[0], rows), lambda s: (0, jnp.minimum(s, last))) for piece in units + grads
        ]
        + [pl.BlockSpec(piece.shape, lambda s: (0, 0), pipeline_mode=pl.Buffered(1)) for piece in hidden],
        out_specs=[pl.BlockSpec((rows, deep // pieces), lambda s: (jnp.maximum(s - 1, 0), 0))] * pieces,
        scratch_shapes=[pltpu.VMEM((2, 2, rows, count), low)],
        compiler_params=pltpu.CompilerParams(vmem_limit_bytes=62 << 20),
        cost_estimate=NOMINAL,
    )(*units, *grads, *hidden)


def shares(columns):
    tiles = -(-columns // 128)
    few, more = divmod(tiles, 8)
    sizes = [128 * (few + (p < more)) for p in range(8)]
    return [(sum(sizes[:p]), size) for p, size in enumerate(sizes)], 128 * (few + (more > 0))


def unit_of(values):
    scale = lax.rsqrt(jnp.mean(values * values, axis=-1, keepdims=True) + epsilon)
    return scale, (values * scale).astype(low)


def unit_back(grad, values, scale):
    unit = values * scale
    return scale * (grad - unit * jnp.mean(grad * unit, axis=-1, keepdims=True))


def local(
    tokens,
    positions,
    attn_gain,
    query_weight,
    key_weight,
    value_weight,
    out_weight,
    mlp_gain,
    gate_weight,
    up_weight,
    down_weight,
    cotangent,
):
    count = tokens.shape[1]
    size = key_weight.shape[1]
    wide = query_weight.shape[1]
    reach = (WINDOW + count - 2) // count
    chips = (reach + 1) // 2
    base = 2 * chips * count - WINDOW
    gain_one = attn_gain[:, None]
    gain_two = mlp_gain[:, None]

    attn_shard = jnp.concatenate([query_weight, key_weight, value_weight], 1).astype(f32) * gain_one
    attn_shard = jnp.concatenate([attn_shard.astype(low), out_weight.T], 1)
    attn_column = lax.all_gather(attn_shard, "z", axis=0, tiled=False)
    qkv_column, out_column = attn_column[:, :, : wide + 2 * size], attn_column[:, :, wide + 2 * size :]

    spans, share = shares(gate_weight.shape[1])
    parts = 2 if share % 256 == 0 else 1
    part = share // parts
    mlp_shards = (
        (gate_weight.astype(f32) * gain_two).astype(low),
        (up_weight.astype(f32) * gain_two).astype(low),
        down_weight.T,
    )
    split = [
        jnp.stack([jnp.pad(shard[:, at : at + n], ((0, 0), (0, share - n))) for at, n in spans])
        for shard in mlp_shards
    ]
    mine = jnp.concatenate(
        [whole[:, :, k * part : (k + 1) * part] for k in range(parts) for whole in split], 2
    )
    mlp_column = lax.all_to_all(after(mine, attn_shard), PLANE, split_axis=0, concat_axis=0, tiled=True)
    mlp_column = mlp_column.reshape(-1, 3 * share)
    mlp_full = [
        lax.all_gather(mlp_column[:, k * 3 * part : (k + 1) * 3 * part], "z", axis=0, tiled=True) for k in range(parts)
    ]

    qkv_blocks = joined_blocks(plane_gather(after(qkv_column, mlp_column)))
    inputs = tokens[0].astype(f32)
    scale_one, unit_one = unit_of(inputs)
    qkv = apply_rows(unit_one, qkv_blocks)
    queries = qkv[:, :wide]
    pairs = window_blocks(qkv[:, wide:], chips)
    out_blocks = plane_gather(after(out_column, qkv_blocks[7]), second=tuple(pairs[: chips + 1]), third=(pairs[-1],))
    out_blocks = joined_blocks(out_blocks)
    mixed, logs = attend(queries, pairs, positions, size, base)
    finals = plane_gather(after(cotangent[0], pairs[0]), second=(mixed,), third=(mixed,))
    resid = apply_rows(after(mixed, finals[1], finals[4]), out_blocks, inputs)

    scale_two, unit_two = unit_of(resid)
    units = plane_gather(unit_two)

    def tiles(blocks, order):
        return [blocks[r] if isinstance(blocks[r], tuple) else (blocks[r],) for r in order]

    far, near = (5, 1, 7, 3), (4, 0, 6, 2)
    units = [tiles(units, order) for order in (far, near)]
    finals = [tiles(finals, order) for order in (far, near)]
    flat_units, flat_finals = (
        [piece for half in whole for tile in half for piece in tile] for whole in (units, finals)
    )
    far_sums = mlp(units[0], finals[0], mlp_full)

    def of_chip(sums, which):
        both = core_sum(sums[2 * which], sums[2 * which + 1])
        return both[:count], both[count:]

    half = count // 2
    diag, to_x = (value.astype(low) for value in of_chip(far_sums, 1))
    far_parts = (diag[:half], diag[half:], to_x[:half])
    started = (swap(far_parts[0], "x"), swap(far_parts[1], "y"), swap(far_parts[2], "x"))
    units[1][0] = (after(units[1][0][0], *far_parts),)
    near_sums = mlp(units[1], finals[1], mlp_full)
    to_y, own = of_chip(near_sums, 1)
    to_y = to_y.astype(low)
    y_bottom = to_y[half:]
    started += (swap(y_bottom, "y"),)
    x_bottom, y_top = scatter_turn(started, to_x, to_y)
    hidden = [[sums[4 + k] for sums in (far_sums, near_sums)] for k in range(parts)]
    hidden[0][0] = after(hidden[0][0], x_bottom, y_top, y_bottom)

    def to_planes(k, pieces):
        partial = mlp_grads(flat_units, flat_finals, hidden[k], pieces)
        return partial, [lax.psum_scatter(piece, "z", scatter_dimension=0, tiled=True) for piece in partial]

    partial, columns = to_planes(0, 1)
    grad_unit_two = scatter_end(started, x_bottom, y_top, own)
    grad_resid = cotangent[0].astype(f32) + unit_back(grad_unit_two, resid, scale_two)
    grad_attn = grad_resid.astype(low)

    diag, out_x = (value.astype(low) for value in of_chip(far_sums, 0))
    out_y, out_own = (value.astype(low) for value in of_chip(near_sums, 0))
    first = tuple(after(v, x_bottom, y_top) for v in (diag[:half], diag[half:], out_x[:half], out_y[half:]))
    outputs = tuple(swap(value, axis) for value, axis in zip(first, ("x", "y", "x", "y")))

    grad_mixed = apply_rows(after(grad_attn, *first, *partial), out_blocks)
    grad_queries, own_grads, other_grads = attend_back(queries, grad_mixed, logs, pairs, positions, size, base)
    other_grads = after(other_grads, *outputs)
    out_keep, out_send = row_grads(after(grad_attn, other_grads, columns[0]), mixed)
    if parts > 1:
        hidden[1][0] = after(hidden[1][0], out_keep)
        later, more = to_planes(1, 3)
        columns += more
    out_both = core_sum(out_keep, out_send).astype(low)
    grad_pair = return_blocks(own_grads, other_grads, chips).astype(low)
    if parts > 1:
        grad_pair = after(grad_pair, *later)
    out_both = after(out_both, grad_pair)
    out_started = scatter_start(out_both[0], out_both[1], out_both[2])
    grad_qkv = jnp.concatenate([grad_queries, grad_pair], 1)
    qkv_keep, qkv_send = row_grads(unit_one, grad_qkv)
    qkv_both = core_sum(qkv_keep, qkv_send).astype(low)
    qkv_started = scatter_start(qkv_both[0], qkv_both[1], qkv_both[2])
    grad_unit_one = apply_rows(after(grad_qkv, qkv_both), qkv_blocks, jnp.zeros_like(inputs))
    grad_tokens = grad_resid + unit_back(grad_unit_one, inputs, scale_one)

    def of_plane(started, both, later=()):
        turned = scatter_turn(started, both[1], both[2], later)
        return scatter_end(started, *turned, both[3]).astype(low)

    out_plane = of_plane(out_started, out_both)
    qkv_plane = after(of_plane(qkv_started, qkv_both, columns[1:2]), *columns[2:3])
    out_sum = planes_scatter(out_plane)
    qkv_sum = planes_scatter(qkv_plane)
    query_sum = qkv_sum[:, :wide]
    key_sum = qkv_sum[:, wide : wide + size]
    value_sum = qkv_sum[:, wide + size :]
    grad_attn_gain = (
        jnp.sum(query_weight.astype(f32) * query_sum, axis=1)
        + jnp.sum(key_weight.astype(f32) * key_sum, axis=1)
        + jnp.sum(value_weight.astype(f32) * value_sum, axis=1)
    )
    output = resid + scatter_end(outputs, *scatter_turn(outputs, out_x, out_y, (qkv_both,)), out_own)

    whole = [
        lax.all_to_all(
            after(column, qkv_plane).reshape(8, -1, column.shape[1]), PLANE, split_axis=0, concat_axis=0, tiled=True
        )
        for column in columns
    ]

    whole = [whole[0]] + ([jnp.concatenate(whole[1:], 2)] if parts > 1 else [])

    def joined(which):
        pieces = []
        for p, (_, n) in enumerate(spans):
            for k in range(parts):
                width = min(part, n - k * part)
                if width > 0:
                    pieces.append(whole[k][p, :, which * part : which * part + width])
        return jnp.concatenate(pieces, 1).astype(f32)

    gate_sum, up_sum, down_sum = joined(0), joined(1), joined(2)
    grad_mlp_gain = jnp.sum(
        gate_weight.astype(f32) * gate_sum + up_weight.astype(f32) * up_sum, axis=1
    )
    return (
        output[None],
        grad_tokens[None],
        grad_attn_gain,
        query_sum * gain_one,
        key_sum * gain_one,
        value_sum * gain_one,
        out_sum.T,
        grad_mlp_gain,
        gate_sum * gain_two,
        up_sum * gain_two,
        down_sum.T,
    )


def solution(mesh):
    ctx, fsdp = mesh.shape["ctx"], mesh.shape["fsdp"]
    fine = Mesh(mesh.devices.reshape(ctx // 4, 2, 2, fsdp), ("z", "y", "c", "x"))
    rows = ("z", "y", "c")
    every = ("z", "y", "c", "x")
    return jax.shard_map(
        local,
        mesh=fine,
        in_specs=(
            P("x", rows, None),
            P("x", rows),
            P(every),
            P(every, None),
            P(every, None),
            P(every, None),
            P(None, every),
            P(every),
            P(every, None),
            P(every, None),
            P(None, every),
            P("x", rows, None),
        ),
        out_specs=(
            P("x", rows, None),
            P("x", rows, None),
            P(every),
            P(every, None),
            P(every, None),
            P(every, None),
            P(None, every),
            P(every),
            P(every, None),
            P(every, None),
            P(None, every),
        ),
        check_vma=False,
    )
```

```python
import functools

import jax
import jax.numpy as jnp
from jax import lax
from jax.experimental import pallas as pl
from jax.experimental.pallas import tpu as pltpu
from jax.sharding import Mesh, PartitionSpec as P

WINDOW = 2048
SUB = 128
TILE = 512
epsilon = 1e-06
blocked_score = -1e30
PLANE = ("y", "c", "x")
low = jnp.bfloat16
f32 = jnp.float32
NOMINAL = pl.CostEstimate(flops=1 << 20, bytes_accessed=1 << 12, transcendentals=0)


def dot(left, right, contract, kind=f32):
    return lax.dot_general(
        left, right, ((contract[:1], contract[1:]), ((), ())), preferred_element_type=f32
    ).astype(kind)


def swap(value, axis):
    return lax.ppermute(value, axis, [(0, 1), (1, 0)])


def plane_gather(own, second=(), third=()):
    half = own.shape[0] // 2
    by_x = swap(own, "x")
    by_y = swap(own, "y")
    own_c = swap(own, "c")
    diag = (
        swap(after(by_y[:half], *second), "x"),
        swap(after(by_x[half:], *second), "y"),
    )
    by_x_c = swap(after(by_x, *second), "c")
    by_y_c = swap(after(by_y, *second), "c")
    diag_c = tuple(swap(after(part, *third), "c") for part in diag)
    return [own, by_x, own_c, by_x_c, by_y, diag, by_y_c, diag_c]


def joined_blocks(blocks):
    return [jnp.concatenate(block, 0) if isinstance(block, tuple) else block for block in blocks]


def stage(sends, work=None, given=()):
    fenced, given = lax.optimization_barrier((tuple(value for value, _ in sends), tuple(given)))
    received = tuple(
        swap(value, way) if isinstance(way, str) else way(value) for value, (_, way) in zip(fenced, sends)
    )
    return lax.optimization_barrier((received, work(*given) if work else given))


def boxed(sure, work, *given):
    shapes = jax.eval_shape(work, *given)
    return lax.cond(
        sure, work, lambda *_: jax.tree.map(lambda out: jnp.zeros(out.shape, out.dtype), shapes), *given
    )


def plane_index():
    return (lax.axis_index("y") * 2 + lax.axis_index("c")) * 2 + lax.axis_index("x")


def after(value, *earlier):
    return lax.optimization_barrier((value,) + earlier)[0]


def across(distance):
    return lambda value: lax.ppermute(value, PLANE, [(i, i ^ distance) for i in range(8)])


def behind(steps):
    count = lax.axis_size("z") * lax.axis_size("y")
    pairs = [(i, i + steps) for i in range(count) if 0 <= i + steps < count]
    return lambda value: lax.ppermute(value, ("z", "y"), pairs)


def two_heads(block, size):
    return jnp.concatenate([block[:, :size], block[:, size:]], 0)


def side_by_side(rows, size):
    half = rows.shape[0] // 2
    return jnp.concatenate([rows[:half], rows[half:]], 1)


def write_bias(bias, places, span, block):
    key = lax.broadcasted_iota(jnp.int32, (span, SUB), 0) - WINDOW
    query = lax.broadcasted_iota(jnp.int32, (span, SUB), 1)
    age = query - key
    seen = (age <= places) & (age >= 0) & (age < WINDOW)
    value = jnp.where(seen, 0.0, blocked_score).astype(f32)
    bias[:, :SUB] = value
    bias[:, SUB:] = value


def lay_window(core, blocks, window, turned, columns):
    count = blocks[0].shape[0]
    half = len(blocks) // 2
    for i in range(half):
        for which, block in ((core, blocks[i]), (1 - core, blocks[half + i])):
            at = pl.multiple_of((2 * i + which) * count, SUB)
            window[pl.ds(at, count), :] = block[...]
            turned[:, pl.ds(at, count)] = block[:, columns].T


def attend_kernel(size, scale, span, base, core, places, queries, *rest):
    blocks, (mixed, logs, bias, window, turned) = rest[:-5], rest[-5:]
    block = pl.program_id(0)
    count = blocks[0].shape[0]
    start = pl.multiple_of(core[0] * count + base + block * SUB, SUB)

    @pl.when((block == 0) & (pl.program_id(1) == 0))
    def _():
        lay_window(core[0], blocks, window, turned, slice(size, 2 * size))

    @pl.when(pl.program_id(1) == 0)
    def _():
        write_bias(bias, places[...], span, block)

    query = two_heads(queries[...], size)
    keys = window[pl.ds(start, span), :size]
    scores = dot(keys, query, (1, 1)) * scale + bias[...]
    highest = jnp.max(scores, axis=0, keepdims=True)
    expo = jnp.exp(scores - highest)
    total = jnp.sum(expo, axis=0, keepdims=True)
    flat = dot(turned[:, pl.ds(start, span)], expo.astype(low), (1, 0)) / total
    mixed[...] = side_by_side(flat.T, size).astype(low)
    logs[0] = highest + jnp.log(total)


def attend_back_kernel(size, scale, span, base, core, places, queries, grads, logs, *rest):
    blocks, (grad_queries, mine, theirs, bias, window, turned, total) = rest[:-7], rest[-7:]
    block = pl.program_id(0)
    count = blocks[0].shape[0]
    start = pl.multiple_of(core[0] * count + base + block * SUB, SUB)

    @pl.when((block == 0) & (pl.program_id(1) == 0))
    def _():
        lay_window(core[0], blocks, window, turned, slice(0, size))
        total[...] = jnp.zeros_like(total)

    @pl.when(pl.program_id(1) == 0)
    def _():
        write_bias(bias, places[...], span, block)

    query = two_heads(queries[...], size)
    grad = two_heads(grads[...], size)
    keys = window[pl.ds(start, span), :size]
    values = window[pl.ds(start, span), size:]
    probs = jnp.exp(dot(keys, query, (1, 1)) * scale + bias[...] - logs[0])
    total[pl.ds(start, span), size:] += dot(probs.astype(low), grad, (1, 0))
    grad_probs = dot(values, grad, (1, 1))
    inner = jnp.sum(probs * grad_probs, axis=0, keepdims=True)
    grad_scores = (probs * (grad_probs - inner)).astype(low)
    total[pl.ds(start, span), :size] += dot(grad_scores, query, (1, 0)) * scale
    flat = dot(turned[:, pl.ds(start, span)], grad_scores, (1, 0)) * scale
    grad_queries[...] = side_by_side(flat.T, size).astype(low)

    @pl.when((block == pl.num_programs(0) - 1) & (pl.program_id(1) == pl.num_programs(1) - 1))
    def _():
        for i in range(len(blocks) // 2):
            at = pl.multiple_of((2 * i + core[0]) * count, SUB)
            mine[i] = total[pl.ds(at, count), :]
            at = pl.multiple_of((2 * i + 1 - core[0]) * count, SUB)
            theirs[i] = total[pl.ds(at, count), :].astype(low)


def attend(queries, blocks, places, size, base):
    count, wide = queries.shape
    grid = (count // SUB, wide // (2 * size))
    span = WINDOW + SUB
    rows = len(blocks) * count
    core = lax.axis_index("c").astype(jnp.int32)[None]
    tile = pl.BlockSpec((SUB, 2 * size), lambda s, h, o: (s, h))
    return pl.pallas_call(
        functools.partial(attend_kernel, size, size**-0.5, span, base),
        out_shape=(
            jax.ShapeDtypeStruct((count, wide), low),
            jax.ShapeDtypeStruct((grid[0] * grid[1], 1, 2 * SUB), f32),
        ),
        grid_spec=pltpu.PrefetchScalarGridSpec(
            num_scalar_prefetch=1,
            grid=grid,
            in_specs=[pl.BlockSpec((1, SUB), lambda s, h, o: (0, s)), tile]
            + [pl.BlockSpec(block.shape, lambda s, h, o: (0, 0)) for block in blocks],
            out_specs=[tile, pl.BlockSpec((1, 1, 2 * SUB), lambda s, h, o: (s * grid[1] + h, 0, 0))],
            scratch_shapes=[
                pltpu.VMEM((span, 2 * SUB), f32),
                pltpu.VMEM((rows, 2 * size), low),
                pltpu.VMEM((size, rows), low),
            ],
        ),
        compiler_params=pltpu.CompilerParams(vmem_limit_bytes=56 << 20),
        cost_estimate=NOMINAL,
    )(core, places, queries, *blocks)


def attend_back(queries, grads, logs, blocks, places, size, base):
    count, wide = queries.shape
    grid = (count // SUB, wide // (2 * size))
    span = WINDOW + SUB
    rows = len(blocks) * count
    half = len(blocks) // 2
    core = lax.axis_index("c").astype(jnp.int32)[None]
    tile = pl.BlockSpec((SUB, 2 * size), lambda s, h, o: (s, h))
    whole = pl.BlockSpec((half, count, 2 * size), lambda s, h, o: (0, 0, 0))
    return pl.pallas_call(
        functools.partial(attend_back_kernel, size, size**-0.5, span, base),
        out_shape=(
            jax.ShapeDtypeStruct((count, wide), low),
            jax.ShapeDtypeStruct((half, count, 2 * size), f32),
            jax.ShapeDtypeStruct((half, count, 2 * size), low),
        ),
        grid_spec=pltpu.PrefetchScalarGridSpec(
            num_scalar_prefetch=1,
            grid=grid,
            in_specs=[
                pl.BlockSpec((1, SUB), lambda s, h, o: (0, s)),
                tile,
                tile,
                pl.BlockSpec((1, 1, 2 * SUB), lambda s, h, o: (s * grid[1] + h, 0, 0)),
            ]
            + [pl.BlockSpec(block.shape, lambda s, h, o: (0, 0)) for block in blocks],
            out_specs=[tile, whole, whole],
            scratch_shapes=[
                pltpu.VMEM((span, 2 * SUB), f32),
                pltpu.VMEM((rows, 2 * size), low),
                pltpu.VMEM((size, rows), low),
                pltpu.VMEM((rows, 2 * size), f32),
            ],
        ),
        compiler_params=pltpu.CompilerParams(vmem_limit_bytes=60 << 20),
        cost_estimate=NOMINAL,
    )(core, places, queries, grads, logs, *blocks)


def lay_rows(slots, blocks, full):
    planes, rows, _ = blocks[0].shape
    for r in range(8):
        for plane in range(planes):
            at = pl.multiple_of((plane * 8 + slots[r]) * rows, 16)
            full[pl.ds(at, rows), :] = blocks[r][plane]


def apply_kernel(slots, left, *rest):
    blocks, (out, full) = rest[:8], rest[8:]
    lay_rows(slots, blocks, full)
    out[...] = dot(left[...], full[...], (1, 0), low)


def apply_turned_kernel(slots, left, start, *rest):
    blocks, (out, full) = rest[:8], rest[8:]
    lay_rows(slots, blocks, full)

    @pl.when(pl.program_id(0) == 0)
    def _():
        out[...] = start[...]

    out[...] += dot(left[...], full[...], (1, 1))


def whole_rows(blocks):
    planes, rows, wide = blocks[0].shape
    here = plane_index()
    whole = jnp.zeros((planes, 8, rows, wide), blocks[0].dtype)
    for r, block in enumerate(blocks):
        whole = lax.dynamic_update_slice(whole, block[:, None], (0, here ^ r, 0, 0))
    return whole.reshape(planes * 8 * rows, wide)


def apply_rows(left, blocks, start=None):
    planes, rows, wide = blocks[0].shape
    if rows % 16 or wide % TILE:
        whole = whole_rows(blocks)
        if start is None:
            return dot(left, whole, (1, 0), low)
        return start + dot(left, whole, (1, 1))
    count, deep = left.shape[0], planes * 8 * rows
    slots = (plane_index() ^ jnp.arange(8)).astype(jnp.int32)
    pieces = [pl.BlockSpec((planes, rows, TILE), lambda n, s: (0, 0, n))] * 8
    whole = pl.BlockSpec((count, deep), lambda n, s: (0, 0))
    part = pl.BlockSpec((count, TILE), lambda n, s: (0, n))
    if start is None:
        kernel, given, specs, result = apply_kernel, [left], [whole], part
        shape = jax.ShapeDtypeStruct((count, wide), low)
    else:
        kernel, given, specs, result = apply_turned_kernel, [left, start], [part, whole], whole
        shape = jax.ShapeDtypeStruct((count, deep), f32)
    return pl.pallas_call(
        kernel,
        out_shape=shape,
        grid_spec=pltpu.PrefetchScalarGridSpec(
            num_scalar_prefetch=1,
            grid=(wide // TILE,),
            in_specs=specs + pieces,
            out_specs=result,
            scratch_shapes=[pltpu.VMEM((deep, TILE), low)],
        ),
        compiler_params=pltpu.CompilerParams(vmem_limit_bytes=48 << 20),
        cost_estimate=NOMINAL,
    )(slots, *given, *blocks)


def row_grads_kernel(slots, left, right, keep, send, turned):
    @pl.when(pl.program_id(1) == 0)
    def _():
        turned[...] = left[...].T

    rows = keep.shape[2]
    value = dot(turned[...], right[...], (1, 0), low)
    for i in range(8):
        place = slots[i]

        @pl.when(place < 4)
        def _():
            keep[place, 0] = value[i * rows : (i + 1) * rows]

        @pl.when(place >= 4)
        def _():
            send[place - 4, 0] = value[i * rows : (i + 1) * rows]


def row_grads(left, right):
    planes = lax.axis_size("z")
    count, deep = left.shape
    wide = right.shape[1]
    rows = deep // (planes * 8)
    places = jnp.array([3, 1, 7, 5, 2, 0, 6, 4], jnp.int32)
    slots = places[plane_index() ^ jnp.arange(8)]
    if rows % 16 or wide % TILE or (planes * 8 * rows) % (planes * 128):
        blocks = dot(left, right, (0, 0), low).reshape(planes, 8, rows, wide)
        order = jnp.argsort(slots)
        blocks = jnp.swapaxes(jnp.take(blocks, order, axis=1), 0, 1)
        return blocks[:4], blocks[4:]
    tile = wide if wide <= 5 * TILE else TILE
    group = pl.BlockSpec((4, 1, rows, tile), lambda z, n, s: (0, z, 0, n))
    shape = jax.ShapeDtypeStruct((4, planes, rows, wide), low)
    return pl.pallas_call(
        row_grads_kernel,
        out_shape=(shape, shape),
        grid_spec=pltpu.PrefetchScalarGridSpec(
            num_scalar_prefetch=1,
            grid=(planes, wide // tile),
            in_specs=[
                pl.BlockSpec((count, 8 * rows), lambda z, n, s: (0, z)),
                pl.BlockSpec((count, tile), lambda z, n, s: (0, n)),
            ],
            out_specs=[group, group],
            scratch_shapes=[pltpu.VMEM((8 * rows, count), low)],
        ),
        compiler_params=pltpu.CompilerParams(vmem_limit_bytes=48 << 20),
        cost_estimate=NOMINAL,
    )(slots, left, right)


def mlp_kernel(part, per, tiles, *rest):
    weights, rest = rest[:per], rest[per:]
    pieces = 2 * sum(tiles)
    sources, rest = rest[:pieces], rest[pieces:]
    before, rest = rest[:-8], rest[-8:]
    outs, grad_units, hidden, units, grads, arrived = rest[0:2], rest[2:4], *rest[4:]
    step = pl.program_id(0)

    def fetches(tile):
        first = 2 * sum(tiles[:tile])
        found = []
        for array, target in enumerate((units, grads)):
            at = 0
            for i in range(tiles[tile]):
                source = sources[first + array * tiles[tile] + i]
                found.append(
                    pltpu.make_async_copy(
                        source,
                        target.at[tile % 2, pl.ds(at, source.shape[0])],
                        arrived.at[tile % 2, array, i],
                    )
                )
                at += source.shape[0]
        return found

    for tile in range(len(tiles)):

        @pl.when(step == tile)
        def _():
            if tile == 0:
                for copy in fetches(0):
                    copy.start()
            if tile + 1 < len(tiles):
                for copy in fetches(tile + 1):
                    copy.start()
            for copy in fetches(tile):
                copy.wait()

    slope = 0.7978845608028654
    for j in range(per):
        both = dot(units[step % 2], weights[j][:, : 2 * part], (1, 0))
        gates, upward = both[:, :part], both[:, part:]
        grad_middle = dot(grads[step % 2], weights[j][:, 2 * part :], (1, 0))
        square = gates * gates
        bend = jnp.tanh(slope * gates * (1.0 + 0.044715 * square))
        half = 0.5 * (1.0 + bend)
        gelu = gates * half
        grad_gelu = half + 0.5 * gates * (1.0 - bend * bend) * (slope * (1.0 + 3 * 0.044715 * square))
        at = 2 * part * j
        hidden[:, at : at + part] = (grad_middle * upward * grad_gelu).astype(low)
        hidden[:, at + part : at + 2 * part] = (grad_middle * gelu).astype(low)
        at = part * (2 * per + j)
        hidden[:, at : at + part] = (gelu * upward).astype(low)
    for which, targets in enumerate((outs, grad_units)):
        value = 0.0
        for j in range(per):
            at, width = (2 * part * j, 2 * part) if which else (part * (2 * per + j), part)
            first = 0 if which else 2 * part
            value = value + dot(hidden[:, at : at + width], weights[j][:, first : first + width], (1, 1))
        for side in range(2):

            @pl.when(step // (len(tiles) // 2) == side)
            def _():
                if before:
                    targets[side][...] = (value + before[2 * which + side][...].astype(f32)).astype(low)
                else:
                    targets[side][...] = value.astype(low)


def mlp(units, grads, weights, before):
    rows = sum(piece.shape[0] for piece in units[0])
    count, wide = rows * len(units), units[0][0].shape[1]
    per, each = len(weights), weights[0].shape[1]
    deep = per * each
    tiles = tuple(len(tile) for tile in units)
    sources = [piece for pair in zip(units, grads) for tile in pair for piece in tile]
    side = len(units) // 2
    sides = [
        pl.BlockSpec((rows, wide), lambda i: (jnp.minimum(i, side - 1), 0)),
        pl.BlockSpec((rows, wide), lambda i: (jnp.maximum(i - side, 0), 0)),
    ]
    half = jax.ShapeDtypeStruct((count // 2, wide), low)
    return pl.pallas_call(
        functools.partial(mlp_kernel, each // 3, per, tiles),
        out_shape=[half] * 4 + [jax.ShapeDtypeStruct((count, deep), low)],
        grid=(len(units),),
        in_specs=[pl.BlockSpec((wide, each), lambda i: (0, 0), pipeline_mode=pl.Buffered(1))] * per
        + [pl.BlockSpec(memory_space=pl.ANY)] * len(sources)
        + (sides * 2 if before else []),
        out_specs=sides * 2 + [pl.BlockSpec((rows, deep), lambda i: (i, 0))],
        scratch_shapes=[
            pltpu.VMEM((2, rows, wide), low),
            pltpu.VMEM((2, rows, wide), low),
            pltpu.SemaphoreType.DMA((2, 2, max(tiles))),
        ],
        compiler_params=pltpu.CompilerParams(vmem_limit_bytes=62 << 20),
        cost_estimate=NOMINAL,
    )(*weights, *sources, *before)


def mlp_grads_kernel(number, *rest):
    units, grads, hidden, rest = rest[:number], rest[number : 2 * number], rest[2 * number : 2 * number + 2], rest[2 * number + 2 :]
    *outs, turned = rest
    out_wide = outs[0].shape[1]
    step = pl.program_id(0)
    part = hidden[0].shape[1] // 3
    piece = min(part, 256)

    def turn(slot, which, sources, share, shares):
        at = 0
        for i, source in enumerate(sources):
            if i * shares // len(sources) == share:
                turned[slot, which, :, at : at + source.shape[0]] = source[...].T
            at += source.shape[0]

    def multiply(slot, which, at):
        value, start = 0.0, 0
        for block in hidden:
            left = turned[slot, which, :, start : start + block.shape[0]]
            value = value + dot(left, block[:, at : at + piece], (1, 0))
            start += block.shape[0]
        outs[at // out_wide][:, at % out_wide : at % out_wide + piece] = value.astype(low)

    work = [(at // (2 * part), at) for at in range(0, 3 * part, piece)]

    @pl.when(step == 0)
    def _():
        turn(0, 0, units, 0, 1)
        turn(0, 1, grads, 0, 1)

    @pl.when(step > 0)
    def _():
        for i, (which, at) in enumerate(work):
            multiply((step - 1) % 2, which, at)
            turn(step % 2, 0, units, i, len(work))
            turn(step % 2, 1, grads, i, len(work))


def mlp_grads(units, grads, hidden, pieces=1):
    wide = units[0].shape[1]
    deep = hidden[0].shape[1]
    count = sum(piece.shape[0] for piece in units)
    rows = 512
    last = wide // rows - 1
    return pl.pallas_call(
        functools.partial(mlp_grads_kernel, len(units)),
        out_shape=[jax.ShapeDtypeStruct((wide, deep // pieces), low)] * pieces,
        grid=(last + 2,),
        in_specs=[
            pl.BlockSpec((piece.shape[0], rows), lambda s: (0, jnp.minimum(s, last))) for piece in units + grads
        ]
        + [pl.BlockSpec(piece.shape, lambda s: (0, 0), pipeline_mode=pl.Buffered(1)) for piece in hidden],
        out_specs=[pl.BlockSpec((rows, deep // pieces), lambda s: (jnp.maximum(s - 1, 0), 0))] * pieces,
        scratch_shapes=[pltpu.VMEM((2, 2, rows, count), low)],
        compiler_params=pltpu.CompilerParams(vmem_limit_bytes=62 << 20),
        cost_estimate=NOMINAL,
    )(*units, *grads, *hidden)


def token_grads_kernel(number, *rest):
    units, (right, out, turned) = rest[:number], rest[number:]

    @pl.when(pl.program_id(0) == 0)
    def _():
        turned[...] = right[...].T

    value, at = 0.0, 0
    for unit in units:
        value = value + dot(turned[:, at : at + unit.shape[0]], unit[...], (1, 0))
        at += unit.shape[0]
    out[...] = value.astype(low).T


def token_grads(units, right):
    wide = units[0].shape[1]
    count, deep = right.shape
    rows = 512
    return pl.pallas_call(
        functools.partial(token_grads_kernel, len(units)),
        out_shape=jax.ShapeDtypeStruct((wide, deep), low),
        grid=(wide // rows,),
        in_specs=[pl.BlockSpec((piece.shape[0], rows), lambda s: (0, s)) for piece in units]
        + [pl.BlockSpec(right.shape, lambda s: (0, 0), pipeline_mode=pl.Buffered(1))],
        out_specs=pl.BlockSpec((rows, deep), lambda s: (s, 0)),
        scratch_shapes=[pltpu.VMEM((deep, count), low)],
        compiler_params=pltpu.CompilerParams(vmem_limit_bytes=56 << 20),
        cost_estimate=NOMINAL,
    )(*units, right)


def spread_kernel(slots, value, *outs):
    deep = outs[0].shape[1]
    for i, out in enumerate(outs):
        out[...] = value[:, pl.ds(pl.multiple_of(slots[i] * deep, 128), deep)]


def spread(value):
    count, wide = value.shape
    slots = (plane_index() ^ jnp.arange(8)).astype(jnp.int32)
    deep = wide // 8
    if deep % 128:
        return [lax.dynamic_slice(value, (0, slots[r] * deep), (count, deep)) for r in range(8)]
    return pl.pallas_call(
        spread_kernel,
        out_shape=[jax.ShapeDtypeStruct((count, deep), value.dtype)] * 8,
        grid_spec=pltpu.PrefetchScalarGridSpec(
            num_scalar_prefetch=1,
            grid=(1,),
            in_specs=[pl.BlockSpec((count, wide), lambda i, s: (0, 0))],
            out_specs=[pl.BlockSpec((count, deep), lambda i, s: (0, 0))] * 8,
        ),
        cost_estimate=NOMINAL,
    )(slots, value)


def shares(columns):
    tiles = -(-columns // 128)
    few, more = divmod(tiles, 8)
    sizes = [128 * (few + (p < more)) for p in range(8)]
    return [(sum(sizes[:p]), size) for p, size in enumerate(sizes)], 128 * (few + (more > 0))


def finish_kernel(spans, part, per, gain, gate, up, whole, gate_out, up_out, down_out, gain_out):
    scale = gain[...]
    total = jnp.zeros_like(scale)
    for p, (at, n) in enumerate(spans):
        for q in range(-(-n // part)):
            width = min(part, n - q * part)
            start, j = 3 * part * per * (q // per), q % per
            place = slice(at + q * part, at + q * part + width)
            for which, (weight, out) in enumerate(((gate, gate_out), (up, up_out))):
                first = start + part * (2 * j + which)
                value = whole[p, :, first : first + width].astype(f32)
                total = total + jnp.sum(value * weight[:, place].astype(f32), axis=1, keepdims=True)
                out[:, place] = value * scale
            first = start + part * (2 * per + j)
            down_out[place, :] = whole[p, :, first : first + width].astype(f32).T
    gain_out[...] = total


def finish(spans, part, per, gain, gate, up, whole):
    rows, columns = gate.shape
    return pl.pallas_call(
        functools.partial(finish_kernel, spans, part, per),
        out_shape=(
            jax.ShapeDtypeStruct((rows, columns), f32),
            jax.ShapeDtypeStruct((rows, columns), f32),
            jax.ShapeDtypeStruct((columns, rows), f32),
            jax.ShapeDtypeStruct((rows, 1), f32),
        ),
        compiler_params=pltpu.CompilerParams(vmem_limit_bytes=48 << 20),
        cost_estimate=NOMINAL,
    )(gain, gate, up, whole)


def unit_of(values):
    scale = lax.rsqrt(jnp.mean(values * values, axis=-1, keepdims=True) + epsilon)
    return scale, (values * scale).astype(low)


def unit_back(grad, values, scale):
    unit = values * scale
    return scale * (grad - unit * jnp.mean(grad * unit, axis=-1, keepdims=True))


def local(
    tokens,
    positions,
    attn_gain,
    query_weight,
    key_weight,
    value_weight,
    out_weight,
    mlp_gain,
    gate_weight,
    up_weight,
    down_weight,
    cotangent,
):
    count = tokens.shape[1]
    size = key_weight.shape[1]
    wide = query_weight.shape[1]
    reach = (WINDOW + count - 2) // count
    chips = (reach + 1) // 2
    base = 2 * chips * count - WINDOW
    gain_one = attn_gain[:, None]
    gain_two = mlp_gain[:, None]

    qkv_shard = jnp.concatenate([query_weight, key_weight, value_weight], 1).astype(f32) * gain_one
    qkv_shard = qkv_shard.astype(low)
    qkv_column = lax.all_gather(qkv_shard, "z", axis=0, tiled=False)
    out_column = lax.all_gather(after(out_weight.T, qkv_shard), "z", axis=0, tiled=False)

    spans, share = shares(gate_weight.shape[1])
    parts = share // 256 if share % 256 == 0 else 1
    calls = 2 if parts % 2 == 0 else 1
    per = parts // calls
    part = share // parts
    mlp_shards = (
        (gate_weight.astype(f32) * gain_two).astype(low),
        (up_weight.astype(f32) * gain_two).astype(low),
        down_weight.T,
    )
    split = [
        jnp.stack([jnp.pad(shard[:, at : at + n], ((0, 0), (0, share - n))) for at, n in spans])
        for shard in mlp_shards
    ]
    mine = jnp.concatenate(
        [whole[:, :, k * part : (k + 1) * part] for k in range(parts) for whole in split], 2
    )
    gift = cotangent[0]
    mlp_column = lax.all_to_all(after(mine, qkv_shard), PLANE, split_axis=0, concat_axis=0, tiled=True)
    mlp_column = mlp_column.reshape(-1, 3 * share)

    def gathered(k, *earlier):
        piece = after(mlp_column[:, k * 3 * part : (k + 1) * 3 * part], *earlier)
        return lax.all_gather(piece, "z", axis=0, tiled=True)

    mlp_full = [gathered(0)]
    sure = positions[0, 0] >= 0
    half = count // 2

    def project(qkv_column, tokens, gift):
        qkv_blocks = joined_blocks(plane_gather(qkv_column))
        scale_one, unit_one = unit_of(tokens[0].astype(f32))
        qkv = apply_rows(unit_one, qkv_blocks)
        queries, pair = qkv[:, :wide], qkv[:, wide:]
        moves = [behind(d) for d in range(chips, 0, -1)]
        found, _ = stage([(pair, move) for move in moves] + [(pair, "c"), (gift, "x"), (gift, "y"), (gift, "c")])
        *pairs, pair_c, gift_x, gift_y, gift_c = found
        found, _ = stage([(block, "c") for block in pairs])
        gifts = gift_x, gift_y, gift_c
        return qkv_blocks[1:], queries, [*pairs, pair, *found, pair_c], gifts, unit_one, scale_one

    def forward(queries, pairs, out_column, tokens, positions, gift_x, gift_y):
        inputs = tokens[0].astype(f32)
        mid = out_column.shape[0] // 2
        (out_x, out_y, out_c, gift_x_c, gift_y_c), (mixed, logs) = stage(
            [(out_column, "x"), (out_column, "y"), (out_column, "c"), (gift_x, "c"), (gift_y, "c")],
            lambda *given: attend(given[0], given[1:], positions, size, base),
            [queries, *pairs],
        )
        (out_top, out_bottom, out_x_c, out_y_c), _ = stage(
            [(out_y[:mid], "x"), (out_x[mid:], "y"), (out_x, "c"), (out_y, "c")]
        )
        out_diag = jnp.concatenate([out_top, out_bottom], 0)
        (out_diag_c,), _ = stage([(out_diag, "c")])
        out_blocks = [out_column, out_x, out_c, out_x_c, out_y, out_diag, out_y_c, out_diag_c]
        resid = apply_rows(mixed, out_blocks, inputs)
        scale_two, unit_two = unit_of(resid)
        (unit_x, unit_y, unit_c), _ = stage([(unit_two, "x"), (unit_two, "y"), (unit_two, "c")])
        (unit_x_c, unit_y_c), _ = stage([(unit_x, "c"), (unit_y, "c")])
        unit_blocks = unit_two, unit_x, unit_c, unit_x_c, unit_y, unit_y_c
        return out_blocks[1:], mixed, logs, resid, scale_two, unit_blocks, gift_x_c, gift_y_c

    qkv_column = after(qkv_column, mlp_column)
    qkv_blocks, queries, pairs, gifts, unit_one, scale_one = boxed(sure, project, qkv_column, tokens, gift)
    gift_x, gift_y, gift_c = gifts
    mlp_full += [gathered(k, pairs[0]) for k in range(1, parts)]
    out_blocks, mixed, logs, resid, scale_two, unit_blocks, gift_x_c, gift_y_c = boxed(
        sure, forward, after(queries, mlp_full[0]), pairs, out_column, tokens, positions, gift_x, gift_y
    )
    qkv_blocks, out_blocks = [qkv_column, *qkv_blocks], [out_column, *out_blocks]
    grads_near = [(gift_y,), (gift,), (gift_y_c,), (gift_c,)]

    def flat(*tiles):
        return [piece for group in tiles for tile in group for piece in tile]

    def summed(keep, received):
        return keep.astype(f32) + received.astype(f32)

    def halves(value):
        middle = value.shape[0] // 2
        return value[:middle], value[middle:]

    def total(*values):
        return sum(value.astype(f32) for value in values)

    def opening(weights, blocks, gift_x, gift_x_c, grads_near, unit_one):
        unit_two, unit_x, unit_c, unit_x_c, unit_y, unit_y_c = blocks
        units_near = [(unit_y,), (unit_two,), (unit_y_c,), (unit_c,)]
        gift_y = grads_near[0][0]
        sends = [(unit_y[:half], "x"), (unit_x[half:], "y"), (gift_y[:half], "x"), (gift_x[half:], "y")]
        one_sends = [(unit_one, "x"), (unit_one, "y"), (unit_one, "c")]
        far_sums = near_sums = partial = ()
        if calls > 1:
            (unit_top, unit_bottom, gift_top, gift_bottom), near_sums = stage(
                sends, lambda *given: mlp([(v,) for v in given], grads_near, weights, ()), flat(units_near)
            )
        else:
            (unit_top, unit_bottom, gift_top, gift_bottom), _ = stage(sends)
        (unit_top_c, unit_bottom_c, gift_top_c, gift_bottom_c), _ = stage(
            [(unit_top, "c"), (unit_bottom, "c"), (gift_top, "c"), (gift_bottom, "c")]
        )
        grads_far = [(gift_top, gift_bottom), (gift_x,), (gift_top_c, gift_bottom_c), (gift_x_c,)]
        units_far = [(unit_top, unit_bottom), (unit_x,), (unit_top_c, unit_bottom_c), (unit_x_c,)]
        if calls > 1:
            (one_x, one_y, one_c), far_sums = stage(
                one_sends, lambda weights: mlp(units_far, grads_far, weights, ()), [weights]
            )
        else:
            (one_x, one_y, one_c), _ = stage(one_sends)
        one_sends = [(one_y[:half], "x"), (one_x[half:], "y"), (one_x, "c"), (one_y, "c")]
        if calls > 1:
            (one_top, one_bottom, one_x_c, one_y_c), partial = stage(
                one_sends,
                lambda *given: mlp_grads(flat(units_far, units_near), flat(grads_far, grads_near), given)[0],
                [far_sums[4], near_sums[4]],
            )
        else:
            (one_top, one_bottom, one_x_c, one_y_c), _ = stage(one_sends)
        ones = one_x, one_c, one_x_c, one_y, one_top, one_bottom, one_y_c
        halves_far = unit_top, unit_bottom, unit_top_c, unit_bottom_c
        return halves_far, grads_far, far_sums[:4], near_sums[:4], partial, ones

    columns = []
    unit_two, unit_x, unit_c, unit_x_c, unit_y, unit_y_c = unit_blocks
    if calls > 1:
        unit_blocks = after(unit_blocks, *mlp_full[per : per + 1])
    halves_far, grads_far, far_before, near_before, partial, ones = boxed(
        sure, opening, mlp_full[:per] if calls > 1 else (), unit_blocks, gift_x, gift_x_c, grads_near, unit_one
    )
    if calls > 1:
        columns.append(lax.psum_scatter(partial, "z", scatter_dimension=0, tiled=True))
    unit_top, unit_bottom, unit_top_c, unit_bottom_c = halves_far
    units_far = [(unit_top, unit_bottom), (unit_x,), (unit_top_c, unit_bottom_c), (unit_x_c,)]
    units_near = [(unit_y,), (unit_two,), (unit_y_c,), (unit_c,)]

    def middle(weights, units_far, units_near, grads_far, grads_near, far_before, near_before, resid, scale_two, gift, ones):
        (one_top_c, one_bottom_c), far_sums = stage(
            [(ones[4], "c"), (ones[5], "c")],
            lambda *weights: mlp(units_far, grads_far, weights, far_before),
            weights,
        )
        (found,), _ = stage([(far_sums[3], "c")])
        both = summed(far_sums[2], found).astype(low)
        (diag_top, diag_bottom), (x_top, x_bottom) = halves(both[:count]), halves(both[count:])
        (diag_x, diag_y, x_top, far_out), near_sums = stage(
            [(diag_top, "x"), (diag_bottom, "y"), (x_top, "x"), (far_sums[1], "c")],
            lambda *given: mlp([(value,) for value in given], grads_near, weights, near_before),
            [tile[0] for tile in units_near],
        )
        (found,), _ = stage([(near_sums[3], "c")])
        both = summed(near_sums[2], found)
        (y_top, y_bottom), (own_top, own_bottom) = halves(both[:count]), halves(both[count:])
        x_bottom, y_top = total(x_bottom, diag_y).astype(low), total(y_top, diag_x).astype(low)
        (y_bottom, x_bottom, y_top, near_out), partial = stage(
            [(y_bottom.astype(low), "y"), (x_bottom, "x"), (y_top, "y"), (near_sums[1], "c")],
            lambda *given: mlp_grads(flat(units_far, units_near), flat(grads_far, grads_near), given, cuts),
            [far_sums[4], near_sums[4]],
        )
        grad_unit_two = jnp.concatenate(
            [total(own_top, x_top, y_top), total(own_bottom, x_bottom, y_bottom)], 0
        )
        grad_resid = gift.astype(f32) + unit_back(grad_unit_two, resid, scale_two)
        out_far = summed(far_sums[0], far_out).astype(low)
        out_near = summed(near_sums[0], near_out).astype(low)
        return partial, grad_resid, grad_resid.astype(low), out_far, out_near, one_top_c, one_bottom_c

    cuts = 2 if part % 256 == 0 and per % 2 == 0 else 1
    partial, grad_resid, grad_attn, out_far, out_near, one_top_c, one_bottom_c = boxed(
        sure,
        middle,
        mlp_full[-per:],
        units_far,
        units_near,
        grads_far,
        grads_near,
        far_before,
        near_before,
        resid,
        scale_two,
        gift,
        ones,
    )
    columns.append(lax.psum_scatter(partial[0], "z", scatter_dimension=0, tiled=True))
    one_x, one_c, one_x_c, one_y, one_top, one_bottom, one_y_c = ones
    flat_ones = [unit_one, one_x, one_c, one_x_c, one_y, one_top, one_bottom, one_y_c, one_top_c, one_bottom_c]

    def first_sends(diag, to_x, to_y):
        diag_top, diag_bottom = halves(diag)
        return [(diag_top, "x"), (diag_bottom, "y"), (halves(to_x)[0], "x"), (halves(to_y)[1], "y")]

    def second_sends(to_x, to_y, received):
        x_bottom = total(halves(to_x)[1], received[1]).astype(low)
        y_top = total(halves(to_y)[0], received[0]).astype(low)
        return [(x_bottom, "x"), (y_top, "y")]

    def joined(own, first, second):
        top, bottom = halves(own)
        return jnp.concatenate([total(top, first[2], second[1]), total(bottom, second[0], first[3])], 0)

    def backward(grad_attn, out_far, out_near, queries, pairs, logs, out_blocks, positions):
        def attention(grad_attn):
            grad_mixed = apply_rows(grad_attn, out_blocks)
            return attend_back(queries, grad_mixed, logs, pairs, positions, size, base)

        first, (grad_queries, mine, theirs) = stage(
            first_sends(out_far[:count], out_far[count:], out_near[:count]), attention, [grad_attn]
        )
        (found,), _ = stage([(theirs, "c")])
        mine = summed(mine, found)
        second = second_sends(out_far[count:], out_near[:count], first)
        found, second = stage(
            [(mine[chips - d].astype(low), behind(-d)) for d in range(chips, 0, -1)],
            lambda *given: given,
            [value for value, _ in second],
        )
        grad_pair = total(mine[chips], *found).astype(low)
        return jnp.concatenate([grad_queries, grad_pair], 1), first, second

    grad_qkv, first, second = boxed(
        sure, backward, after(grad_attn, *columns[:-1]), out_far, out_near, queries, pairs, logs, out_blocks, positions
    )
    columns += [
        lax.psum_scatter(after(piece, grad_qkv), "z", scatter_dimension=0, tiled=True) for piece in partial[1:]
    ]

    def collect(grad_attn, grad_qkv, second, mixed, flat_ones):
        own, *others = spread(grad_qkv)
        found, (out_keep, out_send) = stage(
            [(value, across(r + 1)) for r, value in enumerate(others)],
            lambda *given: row_grads(*given),
            [grad_attn, mixed],
        )
        (found, *second), qkv_column = stage(
            [(out_send, "c"), (second[0], "x"), (second[1], "y")],
            lambda *gathered: token_grads(flat_ones, jnp.concatenate(gathered, 0)),
            [own, *found],
        )
        return qkv_column, out_keep, found, second

    qkv_column, out_keep, found, second = boxed(sure, collect, grad_attn, grad_qkv, second, mixed, flat_ones)
    qkv_low = lax.psum_scatter(qkv_column, "z", scatter_dimension=0, tiled=True)

    def end(out_keep, found, first, second, grad_resid, grad_qkv, out_near, qkv_blocks, resid, scale_one, tokens):
        both = summed(out_keep, found).astype(low)

        def results(grad_qkv, *second):
            inputs = tokens[0].astype(f32)
            output = resid + joined(out_near[count:], first, second)
            grad_unit_one = apply_rows(grad_qkv, qkv_blocks, jnp.zeros_like(inputs))
            return output, grad_resid + unit_back(grad_unit_one, inputs, scale_one)

        started, (output, grad_tokens) = stage(first_sends(*both[:3]), results, [grad_qkv, *second])
        second, _ = stage(second_sends(both[1], both[2], started))
        column = joined(both[3], started, second).astype(low)
        return output, grad_tokens, column.reshape(-1, column.shape[-1])

    output, grad_tokens, out_column = boxed(
        sure,
        end,
        out_keep,
        found,
        first,
        second,
        after(grad_resid, *columns),
        grad_qkv,
        out_near,
        qkv_blocks,
        resid,
        scale_one,
        tokens,
    )
    out_sum = lax.psum_scatter(out_column, "z", scatter_dimension=0, tiled=True).astype(f32)
    every = jnp.concatenate([*columns, qkv_low], 1)
    every = after(every, out_column).reshape(8, -1, every.shape[1])
    every = lax.all_to_all(every, PLANE, split_axis=0, concat_axis=0, tiled=True)
    deep = qkv_low.shape[1]
    qkv_sum = jnp.swapaxes(every[:, :, -deep:], 0, 1).reshape(-1, 8 * deep).astype(f32)
    query_sum = qkv_sum[:, :wide]
    key_sum = qkv_sum[:, wide : wide + size]
    value_sum = qkv_sum[:, wide + size :]
    grad_attn_gain = (
        jnp.sum(query_weight.astype(f32) * query_sum, axis=1)
        + jnp.sum(key_weight.astype(f32) * key_sum, axis=1)
        + jnp.sum(value_weight.astype(f32) * value_sum, axis=1)
    )
    grad_gate, grad_up, grad_down, grad_mlp_gain = finish(spans, part, per, gain_two, gate_weight, up_weight, every)
    return (
        output[None],
        grad_tokens[None],
        grad_attn_gain,
        query_sum * gain_one,
        key_sum * gain_one,
        value_sum * gain_one,
        out_sum.T,
        grad_mlp_gain[:, 0],
        grad_gate,
        grad_up,
        grad_down,
    )


def solution(mesh):
    ctx, fsdp = mesh.shape["ctx"], mesh.shape["fsdp"]
    fine = Mesh(mesh.devices.reshape(ctx // 4, 2, 2, fsdp), ("z", "y", "c", "x"))
    rows = ("z", "y", "c")
    every = ("z", "y", "c", "x")
    return jax.shard_map(
        local,
        mesh=fine,
        in_specs=(
            P("x", rows, None),
            P("x", rows),
            P(every),
            P(every, None),
            P(every, None),
            P(every, None),
            P(None, every),
            P(every),
            P(every, None),
            P(every, None),
            P(None, every),
            P("x", rows, None),
        ),
        out_specs=(
            P("x", rows, None),
            P("x", rows, None),
            P(every),
            P(every, None),
            P(every, None),
            P(every, None),
            P(None, every),
            P(every),
            P(every, None),
            P(every, None),
            P(None, every),
        ),
        check_vma=False,
    )
```

```python
import functools

import jax
import jax.numpy as jnp
from jax import lax
from jax.experimental import pallas as pl
from jax.experimental.pallas import tpu as pltpu
from jax.sharding import Mesh, PartitionSpec as P

WINDOW = 2048
SUB = 128
TILE = 512
epsilon = 1e-06
blocked_score = -1e30
PLANE = ("y", "c", "x")
low = jnp.bfloat16
f32 = jnp.float32
NOMINAL = pl.CostEstimate(flops=1 << 20, bytes_accessed=1 << 12, transcendentals=0)


def dot(left, right, contract, kind=f32):
    return lax.dot_general(
        left, right, ((contract[:1], contract[1:]), ((), ())), preferred_element_type=f32
    ).astype(kind)


def swap(value, axis):
    return lax.ppermute(value, axis, [(0, 1), (1, 0)])


def plane_gather(own, second=(), third=()):
    half = own.shape[0] // 2
    by_x = swap(own, "x")
    by_y = swap(own, "y")
    own_c = swap(own, "c")
    diag = (
        swap(after(by_y[:half], *second), "x"),
        swap(after(by_x[half:], *second), "y"),
    )
    by_x_c = swap(after(by_x, *second), "c")
    by_y_c = swap(after(by_y, *second), "c")
    diag_c = tuple(swap(after(part, *third), "c") for part in diag)
    return [own, by_x, own_c, by_x_c, by_y, diag, by_y_c, diag_c]


def joined_blocks(blocks):
    return [jnp.concatenate(block, 0) if isinstance(block, tuple) else block for block in blocks]


def stage(sends, work=None, given=()):
    fenced, given = lax.optimization_barrier((tuple(value for value, _ in sends), tuple(given)))
    received = tuple(
        swap(value, way) if isinstance(way, str) else way(value) for value, (_, way) in zip(fenced, sends)
    )
    return lax.optimization_barrier((received, work(*given) if work else given))


def boxed(sure, work, *given):
    shapes = jax.eval_shape(work, *given)
    return lax.cond(
        sure, work, lambda *_: jax.tree.map(lambda out: jnp.zeros(out.shape, out.dtype), shapes), *given
    )


def plane_index():
    return (lax.axis_index("y") * 2 + lax.axis_index("c")) * 2 + lax.axis_index("x")


def after(value, *earlier):
    return lax.optimization_barrier((value,) + earlier)[0]


def across(distance):
    return lambda value: lax.ppermute(value, PLANE, [(i, i ^ distance) for i in range(8)])


def behind(steps):
    count = lax.axis_size("z") * lax.axis_size("y")
    pairs = [(i, i + steps) for i in range(count) if 0 <= i + steps < count]
    return lambda value: lax.ppermute(value, ("z", "y"), pairs)


def two_heads(block, size):
    return jnp.concatenate([block[:, :size], block[:, size:]], 0)


def side_by_side(rows, size):
    half = rows.shape[0] // 2
    return jnp.concatenate([rows[:half], rows[half:]], 1)


def write_bias(bias, places, span, block):
    key = lax.broadcasted_iota(jnp.int32, (span, SUB), 0) - WINDOW
    query = lax.broadcasted_iota(jnp.int32, (span, SUB), 1)
    age = query - key
    seen = (age <= places) & (age >= 0) & (age < WINDOW)
    value = jnp.where(seen, 0.0, blocked_score).astype(f32)
    bias[:, :SUB] = value
    bias[:, SUB:] = value


def lay_window(core, blocks, window, turned, columns):
    count = blocks[0].shape[0]
    half = len(blocks) // 2
    for i in range(half):
        for which, block in ((core, blocks[i]), (1 - core, blocks[half + i])):
            at = pl.multiple_of((2 * i + which) * count, SUB)
            window[pl.ds(at, count), :] = block[...]
            turned[:, pl.ds(at, count)] = block[:, columns].T


def chunks(span, number):
    tiles = span // 128
    return [(128 * (tiles * i // number), 128 * (tiles * (i + 1) // number)) for i in range(number)]


def attend_kernel(size, scale, span, base, core, places, queries, *rest):
    blocks, (mixed, wide, logs, bias, window, turned) = rest[:-6], rest[-6:]
    block = pl.program_id(0)
    count = blocks[0].shape[0]
    start = pl.multiple_of(core[0] * count + base + block * SUB, SUB)

    @pl.when((block == 0) & (pl.program_id(1) == 0))
    def _():
        lay_window(core[0], blocks, window, turned, slice(size, 2 * size))

    @pl.when(pl.program_id(1) == 0)
    def _():
        write_bias(bias, places[...], span, block)

    query = two_heads(queries[...], size) * jnp.asarray(scale, low)
    highest = total = flat = None
    for at, end in chunks(span, 8):
        place = pl.ds(start + at, end - at)
        scores = dot(window[place, :size], query, (1, 1)) + bias[at:end]
        top = jnp.max(scores, axis=0, keepdims=True)
        if highest is not None:
            top = jnp.maximum(highest, top)
            fade = jnp.exp(highest - top)
        highest = top
        expo = jnp.exp(scores - highest)
        part = jnp.sum(expo, axis=0, keepdims=True)
        mix = dot(turned[:, place], expo.astype(low), (1, 0))
        total = part if total is None else total * fade + part
        flat = mix if flat is None else flat * fade + mix
    result = side_by_side((flat / total).T, size)
    wide[...] = result
    mixed[...] = result.astype(low)
    logs[0] = highest + jnp.log(total)


def attend_back_kernel(size, scale, span, base, core, places, queries, grads, wide, logs, *rest):
    blocks, (grad_queries, mine, theirs, bias, window, turned, total) = rest[:-7], rest[-7:]
    block = pl.program_id(0)
    count = blocks[0].shape[0]
    start = pl.multiple_of(core[0] * count + base + block * SUB, SUB)

    @pl.when((block == 0) & (pl.program_id(1) == 0))
    def _():
        lay_window(core[0], blocks, window, turned, slice(0, size))
        total[...] = jnp.zeros_like(total)

    @pl.when(pl.program_id(1) == 0)
    def _():
        write_bias(bias, places[...], span, block)

    query = two_heads(queries[...], size) * jnp.asarray(scale, low)
    grad = two_heads(grads[...], size)
    inner = jnp.sum((grad.astype(f32) * two_heads(wide[...], size)).T, axis=0, keepdims=True)
    place = pl.ds(start, span)
    keys, values = window[place, :size], window[place, size:]
    probs = jnp.exp(dot(keys, query, (1, 1)) + (bias[...] - logs[0]))
    grad_scores = (probs * (dot(values, grad, (1, 1)) - inner)).astype(low)
    total[place, size:] += dot(probs.astype(low), grad, (1, 0))
    total[place, :size] += dot(grad_scores, query, (1, 0))
    flat = dot(turned[:, place], grad_scores, (1, 0)) * scale
    grad_queries[...] = side_by_side(flat.T, size).astype(low)

    @pl.when((block == pl.num_programs(0) - 1) & (pl.program_id(1) == pl.num_programs(1) - 1))
    def _():
        for i in range(len(blocks) // 2):
            at = pl.multiple_of((2 * i + core[0]) * count, SUB)
            mine[i] = total[pl.ds(at, count), :]
            at = pl.multiple_of((2 * i + 1 - core[0]) * count, SUB)
            theirs[i] = total[pl.ds(at, count), :].astype(low)


def attend(queries, blocks, places, size, base):
    count, wide = queries.shape
    grid = (count // SUB, wide // (2 * size))
    span = WINDOW + SUB
    rows = len(blocks) * count
    core = lax.axis_index("c").astype(jnp.int32)[None]
    tile = pl.BlockSpec((SUB, 2 * size), lambda s, h, o: (s, h))
    return pl.pallas_call(
        functools.partial(attend_kernel, size, size**-0.5, span, base),
        out_shape=(
            jax.ShapeDtypeStruct((count, wide), low),
            jax.ShapeDtypeStruct((count, wide), f32),
            jax.ShapeDtypeStruct((grid[0] * grid[1], 1, 2 * SUB), f32),
        ),
        grid_spec=pltpu.PrefetchScalarGridSpec(
            num_scalar_prefetch=1,
            grid=grid,
            in_specs=[pl.BlockSpec((1, SUB), lambda s, h, o: (0, s)), tile]
            + [pl.BlockSpec(block.shape, lambda s, h, o: (0, 0)) for block in blocks],
            out_specs=[tile, tile, pl.BlockSpec((1, 1, 2 * SUB), lambda s, h, o: (s * grid[1] + h, 0, 0))],
            scratch_shapes=[
                pltpu.VMEM((span, 2 * SUB), f32),
                pltpu.VMEM((rows, 2 * size), low),
                pltpu.VMEM((size, rows), low),
            ],
        ),
        compiler_params=pltpu.CompilerParams(vmem_limit_bytes=56 << 20),
        cost_estimate=NOMINAL,
    )(core, places, queries, *blocks)


def attend_back(queries, grads, mixed, logs, blocks, places, size, base):
    count, wide = queries.shape
    grid = (count // SUB, wide // (2 * size))
    span = WINDOW + SUB
    rows = len(blocks) * count
    half = len(blocks) // 2
    core = lax.axis_index("c").astype(jnp.int32)[None]
    tile = pl.BlockSpec((SUB, 2 * size), lambda s, h, o: (s, h))
    whole = pl.BlockSpec((half, count, 2 * size), lambda s, h, o: (0, 0, 0))
    return pl.pallas_call(
        functools.partial(attend_back_kernel, size, size**-0.5, span, base),
        out_shape=(
            jax.ShapeDtypeStruct((count, wide), low),
            jax.ShapeDtypeStruct((half, count, 2 * size), f32),
            jax.ShapeDtypeStruct((half, count, 2 * size), low),
        ),
        grid_spec=pltpu.PrefetchScalarGridSpec(
            num_scalar_prefetch=1,
            grid=grid,
            in_specs=[
                pl.BlockSpec((1, SUB), lambda s, h, o: (0, s)),
                tile,
                tile,
                tile,
                pl.BlockSpec((1, 1, 2 * SUB), lambda s, h, o: (s * grid[1] + h, 0, 0)),
            ]
            + [pl.BlockSpec(block.shape, lambda s, h, o: (0, 0)) for block in blocks],
            out_specs=[tile, whole, whole],
            scratch_shapes=[
                pltpu.VMEM((span, 2 * SUB), f32),
                pltpu.VMEM((rows, 2 * size), low),
                pltpu.VMEM((size, rows), low),
                pltpu.VMEM((rows, 2 * size), f32),
            ],
        ),
        compiler_params=pltpu.CompilerParams(vmem_limit_bytes=60 << 20),
        cost_estimate=NOMINAL,
    )(core, places, queries, grads, mixed, logs, *blocks)


def lay_rows(slots, blocks, full):
    planes, rows, _ = blocks[0].shape
    for r in range(8):
        for plane in range(planes):
            at = pl.multiple_of((plane * 8 + slots[r]) * rows, 16)
            full[pl.ds(at, rows), :] = blocks[r][plane]


def apply_kernel(slots, left, *rest):
    blocks, (out, full) = rest[:8], rest[8:]
    lay_rows(slots, blocks, full)
    out[...] = dot(left[...], full[...], (1, 0), low)


def apply_turned_kernel(slots, left, start, *rest):
    blocks, (out, full) = rest[:8], rest[8:]
    lay_rows(slots, blocks, full)

    @pl.when(pl.program_id(0) == 0)
    def _():
        out[...] = start[...]

    out[...] += dot(left[...], full[...], (1, 1))


def whole_rows(blocks):
    planes, rows, wide = blocks[0].shape
    here = plane_index()
    whole = jnp.zeros((planes, 8, rows, wide), blocks[0].dtype)
    for r, block in enumerate(blocks):
        whole = lax.dynamic_update_slice(whole, block[:, None], (0, here ^ r, 0, 0))
    return whole.reshape(planes * 8 * rows, wide)


def apply_rows(left, blocks, start=None):
    planes, rows, wide = blocks[0].shape
    if rows % 16 or wide % TILE:
        whole = whole_rows(blocks)
        if start is None:
            return dot(left, whole, (1, 0), low)
        return start + dot(left, whole, (1, 1))
    count, deep = left.shape[0], planes * 8 * rows
    slots = (plane_index() ^ jnp.arange(8)).astype(jnp.int32)
    pieces = [pl.BlockSpec((planes, rows, TILE), lambda n, s: (0, 0, n))] * 8
    whole = pl.BlockSpec((count, deep), lambda n, s: (0, 0))
    part = pl.BlockSpec((count, TILE), lambda n, s: (0, n))
    if start is None:
        kernel, given, specs, result = apply_kernel, [left], [whole], part
        shape = jax.ShapeDtypeStruct((count, wide), low)
    else:
        kernel, given, specs, result = apply_turned_kernel, [left, start], [part, whole], whole
        shape = jax.ShapeDtypeStruct((count, deep), f32)
    return pl.pallas_call(
        kernel,
        out_shape=shape,
        grid_spec=pltpu.PrefetchScalarGridSpec(
            num_scalar_prefetch=1,
            grid=(wide // TILE,),
            in_specs=specs + pieces,
            out_specs=result,
            scratch_shapes=[pltpu.VMEM((deep, TILE), low)],
        ),
        compiler_params=pltpu.CompilerParams(vmem_limit_bytes=48 << 20),
        cost_estimate=NOMINAL,
    )(slots, *given, *blocks)


def row_grads_kernel(slots, left, right, keep, send, turned):
    @pl.when(pl.program_id(1) == 0)
    def _():
        turned[...] = left[...].T

    rows = keep.shape[2]
    value = dot(turned[...], right[...], (1, 0), low)
    for i in range(8):
        place = slots[i]

        @pl.when(place < 4)
        def _():
            keep[place, 0] = value[i * rows : (i + 1) * rows]

        @pl.when(place >= 4)
        def _():
            send[place - 4, 0] = value[i * rows : (i + 1) * rows]


def row_grads(left, right):
    planes = lax.axis_size("z")
    count, deep = left.shape
    wide = right.shape[1]
    rows = deep // (planes * 8)
    places = jnp.array([3, 1, 7, 5, 2, 0, 6, 4], jnp.int32)
    slots = places[plane_index() ^ jnp.arange(8)]
    if rows % 16 or wide % TILE or (planes * 8 * rows) % (planes * 128):
        blocks = dot(left, right, (0, 0), low).reshape(planes, 8, rows, wide)
        order = jnp.argsort(slots)
        blocks = jnp.swapaxes(jnp.take(blocks, order, axis=1), 0, 1)
        return blocks[:4], blocks[4:]
    tile = wide if wide <= 5 * TILE else TILE
    group = pl.BlockSpec((4, 1, rows, tile), lambda z, n, s: (0, z, 0, n))
    shape = jax.ShapeDtypeStruct((4, planes, rows, wide), low)
    return pl.pallas_call(
        row_grads_kernel,
        out_shape=(shape, shape),
        grid_spec=pltpu.PrefetchScalarGridSpec(
            num_scalar_prefetch=1,
            grid=(planes, wide // tile),
            in_specs=[
                pl.BlockSpec((count, 8 * rows), lambda z, n, s: (0, z)),
                pl.BlockSpec((count, tile), lambda z, n, s: (0, n)),
            ],
            out_specs=[group, group],
            scratch_shapes=[pltpu.VMEM((8 * rows, count), low)],
        ),
        compiler_params=pltpu.CompilerParams(vmem_limit_bytes=48 << 20),
        cost_estimate=NOMINAL,
    )(slots, left, right)


def mlp_kernel(part, per, tiles, *rest):
    weights, rest = rest[:per], rest[per:]
    pieces = 2 * sum(tiles)
    sources, rest = rest[:pieces], rest[pieces:]
    before, rest = rest[:-8], rest[-8:]
    outs, grad_units, hidden, units, grads, arrived = rest[0:2], rest[2:4], *rest[4:]
    step = pl.program_id(0)

    def fetches(tile):
        first = 2 * sum(tiles[:tile])
        found = []
        for array, target in enumerate((units, grads)):
            at = 0
            for i in range(tiles[tile]):
                source = sources[first + array * tiles[tile] + i]
                found.append(
                    pltpu.make_async_copy(
                        source,
                        target.at[tile % 2, pl.ds(at, source.shape[0])],
                        arrived.at[tile % 2, array, i],
                    )
                )
                at += source.shape[0]
        return found

    for tile in range(len(tiles)):

        @pl.when(step == tile)
        def _():
            if tile == 0:
                for copy in fetches(0):
                    copy.start()
            if tile + 1 < len(tiles):
                for copy in fetches(tile + 1):
                    copy.start()
            for copy in fetches(tile):
                copy.wait()

    slope = 0.7978845608028654
    for j in range(per):
        both = dot(units[step % 2], weights[j][:, : 2 * part], (1, 0))
        gates, upward = both[:, :part], both[:, part:]
        grad_middle = dot(grads[step % 2], weights[j][:, 2 * part :], (1, 0))
        square = gates * gates
        bend = jnp.tanh(slope * gates * (1.0 + 0.044715 * square))
        half = 0.5 * (1.0 + bend)
        gelu = gates * half
        grad_gelu = half + 0.5 * gates * (1.0 - bend * bend) * (slope * (1.0 + 3 * 0.044715 * square))
        at = 2 * part * j
        hidden[:, at : at + part] = (grad_middle * upward * grad_gelu).astype(low)
        hidden[:, at + part : at + 2 * part] = (grad_middle * gelu).astype(low)
        at = part * (2 * per + j)
        hidden[:, at : at + part] = (gelu * upward).astype(low)
    for which, targets in enumerate((outs, grad_units)):
        value = 0.0
        for j in range(per):
            at, width = (2 * part * j, 2 * part) if which else (part * (2 * per + j), part)
            first = 0 if which else 2 * part
            value = value + dot(hidden[:, at : at + width], weights[j][:, first : first + width], (1, 1))
        for side in range(2):

            @pl.when(step // (len(tiles) // 2) == side)
            def _():
                if before:
                    targets[side][...] = (value + before[2 * which + side][...].astype(f32)).astype(low)
                else:
                    targets[side][...] = value.astype(low)


def mlp(units, grads, weights, before):
    rows = sum(piece.shape[0] for piece in units[0])
    count, wide = rows * len(units), units[0][0].shape[1]
    per, each = len(weights), weights[0].shape[1]
    deep = per * each
    tiles = tuple(len(tile) for tile in units)
    sources = [piece for pair in zip(units, grads) for tile in pair for piece in tile]
    side = len(units) // 2
    sides = [
        pl.BlockSpec((rows, wide), lambda i: (jnp.minimum(i, side - 1), 0)),
        pl.BlockSpec((rows, wide), lambda i: (jnp.maximum(i - side, 0), 0)),
    ]
    half = jax.ShapeDtypeStruct((count // 2, wide), low)
    return pl.pallas_call(
        functools.partial(mlp_kernel, each // 3, per, tiles),
        out_shape=[half] * 4 + [jax.ShapeDtypeStruct((count, deep), low)],
        grid=(len(units),),
        in_specs=[pl.BlockSpec((wide, each), lambda i: (0, 0), pipeline_mode=pl.Buffered(1))] * per
        + [pl.BlockSpec(memory_space=pl.ANY)] * len(sources)
        + (sides * 2 if before else []),
        out_specs=sides * 2 + [pl.BlockSpec((rows, deep), lambda i: (i, 0))],
        scratch_shapes=[
            pltpu.VMEM((2, rows, wide), low),
            pltpu.VMEM((2, rows, wide), low),
            pltpu.SemaphoreType.DMA((2, 2, max(tiles))),
        ],
        compiler_params=pltpu.CompilerParams(vmem_limit_bytes=62 << 20),
        cost_estimate=NOMINAL,
    )(*weights, *sources, *before)


def mlp_grads_kernel(number, *rest):
    units, grads, hidden, rest = rest[:number], rest[number : 2 * number], rest[2 * number : 2 * number + 2], rest[2 * number + 2 :]
    *outs, turned = rest
    step = pl.program_id(0)
    part = hidden[0].shape[1] // 3
    piece = min(part, 256)
    places = [(out, at) for out in outs for at in range(0, out.shape[1], piece)]

    def turn(slot, which, sources, share, shares):
        at = 0
        for i, source in enumerate(sources):
            if i * shares // len(sources) == share:
                turned[slot, which, :, at : at + source.shape[0]] = source[...].T
            at += source.shape[0]

    def multiply(slot, which, i, at):
        value, start = 0.0, 0
        for block in hidden:
            left = turned[slot, which, :, start : start + block.shape[0]]
            value = value + dot(left, block[:, at : at + piece], (1, 0))
            start += block.shape[0]
        out, place = places[i]
        out[:, place : place + piece] = value.astype(low)

    work = [(at // (2 * part), at) for at in range(0, 3 * part, piece)]

    @pl.when(step == 0)
    def _():
        turn(0, 0, units, 0, 1)
        turn(0, 1, grads, 0, 1)

    @pl.when(step > 0)
    def _():
        for i, (which, at) in enumerate(work):
            multiply((step - 1) % 2, which, i, at)
            turn(step % 2, 0, units, i, len(work))
            turn(step % 2, 1, grads, i, len(work))


def mlp_grads(units, grads, hidden, pieces=(3,)):
    wide = units[0].shape[1]
    deep = hidden[0].shape[1]
    count = sum(piece.shape[0] for piece in units)
    rows = 512
    last = wide // rows - 1
    return pl.pallas_call(
        functools.partial(mlp_grads_kernel, len(units)),
        out_shape=[jax.ShapeDtypeStruct((wide, deep // 3 * piece), low) for piece in pieces],
        grid=(last + 2,),
        in_specs=[
            pl.BlockSpec((piece.shape[0], rows), lambda s: (0, jnp.minimum(s, last))) for piece in units + grads
        ]
        + [pl.BlockSpec(piece.shape, lambda s: (0, 0), pipeline_mode=pl.Buffered(1)) for piece in hidden],
        out_specs=[
            pl.BlockSpec((rows, deep // 3 * piece), lambda s: (jnp.maximum(s - 1, 0), 0)) for piece in pieces
        ],
        scratch_shapes=[pltpu.VMEM((2, 2, rows, count), low)],
        compiler_params=pltpu.CompilerParams(vmem_limit_bytes=62 << 20),
        cost_estimate=NOMINAL,
    )(*units, *grads, *hidden)


def token_grads_kernel(number, *rest):
    units, (right, out, turned) = rest[:number], rest[number:]

    @pl.when(pl.program_id(0) == 0)
    def _():
        turned[...] = right[...].T

    value, at = 0.0, 0
    for unit in units:
        value = value + dot(turned[:, at : at + unit.shape[0]], unit[...], (1, 0))
        at += unit.shape[0]
    out[...] = value.astype(low).T


def token_grads(units, right):
    wide = units[0].shape[1]
    count, deep = right.shape
    rows = 512
    return pl.pallas_call(
        functools.partial(token_grads_kernel, len(units)),
        out_shape=jax.ShapeDtypeStruct((wide, deep), low),
        grid=(wide // rows,),
        in_specs=[pl.BlockSpec((piece.shape[0], rows), lambda s: (0, s)) for piece in units]
        + [pl.BlockSpec(right.shape, lambda s: (0, 0), pipeline_mode=pl.Buffered(1))],
        out_specs=pl.BlockSpec((rows, deep), lambda s: (s, 0)),
        scratch_shapes=[pltpu.VMEM((deep, count), low)],
        compiler_params=pltpu.CompilerParams(vmem_limit_bytes=56 << 20),
        cost_estimate=NOMINAL,
    )(*units, right)


def spread_kernel(slots, value, *outs):
    deep = outs[0].shape[1]
    for i, out in enumerate(outs):
        out[...] = value[:, pl.ds(pl.multiple_of(slots[i] * deep, 128), deep)]


def spread(value):
    count, wide = value.shape
    slots = (plane_index() ^ jnp.arange(8)).astype(jnp.int32)
    deep = wide // 8
    if deep % 128:
        return [lax.dynamic_slice(value, (0, slots[r] * deep), (count, deep)) for r in range(8)]
    return pl.pallas_call(
        spread_kernel,
        out_shape=[jax.ShapeDtypeStruct((count, deep), value.dtype)] * 8,
        grid_spec=pltpu.PrefetchScalarGridSpec(
            num_scalar_prefetch=1,
            grid=(1,),
            in_specs=[pl.BlockSpec((count, wide), lambda i, s: (0, 0))],
            out_specs=[pl.BlockSpec((count, deep), lambda i, s: (0, 0))] * 8,
        ),
        cost_estimate=NOMINAL,
    )(slots, value)


def turn_kernel(keep, found, far, diag_x, diag_y, y_bottom, x_bottom, y_top, own):
    half = far.shape[0]

    def both(start, rows):
        return keep[start : start + rows].astype(f32) + found[start : start + rows].astype(f32)

    y_top[...] = (both(0, half) + diag_x[...].astype(f32)).astype(low)
    y_bottom[...] = both(half, half).astype(low)
    x_bottom[...] = (far[...].astype(f32) + diag_y[...].astype(f32)).astype(low)
    own[...] = both(2 * half, 2 * half)


def turn(keep, found, far, diag_x, diag_y):
    half, wide = far.shape
    part = lambda rows: pl.BlockSpec((rows, TILE), lambda n: (0, n))
    return pl.pallas_call(
        turn_kernel,
        out_shape=[jax.ShapeDtypeStruct((half, wide), low)] * 3 + [jax.ShapeDtypeStruct((2 * half, wide), f32)],
        grid=(wide // TILE,),
        in_specs=[part(4 * half)] * 2 + [part(half)] * 3,
        out_specs=[part(half)] * 3 + [part(2 * half)],
        cost_estimate=NOMINAL,
    )(keep, found, far, diag_x, diag_y)


def resid_kernel(steps, own, x_top, x_bottom, y_top, y_bottom, resid, gift, scale, grad_out, grad_low):
    upper = pl.program_id(0) < steps
    x_part = jnp.where(upper, x_top[...].astype(f32), x_bottom[...].astype(f32))
    y_part = jnp.where(upper, y_top[...].astype(f32), y_bottom[...].astype(f32))
    grad = unit_back(own[...] + x_part + y_part, resid[...], scale[...])
    grad = gift[...].astype(f32) + grad
    grad_out[...] = grad
    grad_low[...] = grad.astype(low)


def resid_grads(own, x_top, x_bottom, y_top, y_bottom, resid, gift, scale):
    count, wide = own.shape
    rows = 96
    steps = count // (2 * rows)
    row = pl.BlockSpec((rows, wide), lambda i: (i, 0))
    first = pl.BlockSpec((rows, wide), lambda i: (jnp.minimum(i, steps - 1), 0))
    last = pl.BlockSpec((rows, wide), lambda i: (jnp.maximum(i - steps, 0), 0))
    return pl.pallas_call(
        functools.partial(resid_kernel, steps),
        out_shape=(jax.ShapeDtypeStruct((count, wide), f32), jax.ShapeDtypeStruct((count, wide), low)),
        grid=(2 * steps,),
        in_specs=[row, first, last, first, last, row, row, pl.BlockSpec((rows, 1), lambda i: (i, 0))],
        out_specs=(row, row),
        cost_estimate=NOMINAL,
    )(own, x_top, x_bottom, y_top, y_bottom, resid, gift, scale)


def part_sums_kernel(keep, found, diag_top, diag_bottom, x_top, x_bottom, y_top, y_bottom, own):
    half = diag_top.shape[0]

    def both(place, first, rows):
        part = slice(first, first + rows)
        return (keep[place, part].astype(f32) + found[place, part].astype(f32)).astype(low)

    for place, (top, bottom) in enumerate(((diag_top, diag_bottom), (x_top, x_bottom), (y_top, y_bottom))):
        top[...] = both(place, 0, half)
        bottom[...] = both(place, half, half)
    own[...] = both(3, 0, 2 * half)


def part_sums(keep, found):
    _, planes, rows, wide = keep.shape
    four = pl.BlockSpec((4, planes, rows, TILE), lambda n: (0, 0, 0, n))
    some = lambda planes: pl.BlockSpec((planes, rows, TILE), lambda n: (0, 0, n))
    half = planes // 2
    shape = lambda planes: jax.ShapeDtypeStruct((planes, rows, wide), low)
    return pl.pallas_call(
        part_sums_kernel,
        out_shape=[shape(half)] * 6 + [shape(planes)],
        grid=(wide // TILE,),
        in_specs=[four] * 2,
        out_specs=[some(half)] * 6 + [some(planes)],
        compiler_params=pltpu.CompilerParams(vmem_limit_bytes=48 << 20),
        cost_estimate=NOMINAL,
    )(keep, found)


def pack_kernel(spans, part, gain, gate, up, down, out):
    scale = gain[...]
    share = out.shape[2] // 3
    for p, (at, n) in enumerate(spans):
        for q in range(share // part):
            width = min(part, n - q * part)
            place = slice(at + q * part, at + q * part + width)
            for which, source in enumerate((gate, up, down)):
                first = part * (3 * q + which)
                if width > 0:
                    value = source[:, place]
                    if which < 2:
                        value = (value.astype(f32) * scale).astype(low)
                    out[p, :, first : first + width] = value
                if width < part:
                    empty = max(width, 0)
                    out[p, :, first + empty : first + part] = jnp.zeros((out.shape[1], part - empty), low)


def pack(spans, part, share, gain, gate, up, down):
    rows, _ = gate.shape
    return pl.pallas_call(
        functools.partial(pack_kernel, spans, part),
        out_shape=jax.ShapeDtypeStruct((8, rows, 3 * share), low),
        compiler_params=pltpu.CompilerParams(vmem_limit_bytes=48 << 20),
        cost_estimate=NOMINAL,
    )(gain, gate, up, down)


def shares(columns):
    tiles = -(-columns // 128)
    few, more = divmod(tiles, 8)
    sizes = [128 * (few + (p < more)) for p in range(8)]
    return [(sum(sizes[:p]), size) for p, size in enumerate(sizes)], 128 * (few + (more > 0))


def finish_kernel(spans, part, per, gain, gate, up, whole, gate_out, up_out, down_out, gain_out):
    scale = gain[...]
    total = jnp.zeros_like(scale)
    for p, (at, n) in enumerate(spans):
        for q in range(-(-n // part)):
            width = min(part, n - q * part)
            start, j = 3 * part * per * (q // per), q % per
            place = slice(at + q * part, at + q * part + width)
            for which, (weight, out) in enumerate(((gate, gate_out), (up, up_out))):
                first = start + part * (2 * j + which)
                value = whole[p, :, first : first + width].astype(f32)
                total = total + jnp.sum(value * weight[:, place].astype(f32), axis=1, keepdims=True)
                out[:, place] = value * scale
            first = start + part * (2 * per + j)
            down_out[:, place] = whole[p, :, first : first + width].astype(f32)
    gain_out[...] = total


def finish(spans, part, per, gain, gate, up, whole):
    rows, columns = gate.shape
    return pl.pallas_call(
        functools.partial(finish_kernel, spans, part, per),
        out_shape=(
            jax.ShapeDtypeStruct((rows, columns), f32),
            jax.ShapeDtypeStruct((rows, columns), f32),
            jax.ShapeDtypeStruct((rows, columns), f32),
            jax.ShapeDtypeStruct((rows, 1), f32),
        ),
        compiler_params=pltpu.CompilerParams(vmem_limit_bytes=48 << 20),
        cost_estimate=NOMINAL,
    )(gain, gate, up, whole)


def unit_of(values):
    scale = lax.rsqrt(jnp.mean(values * values, axis=-1, keepdims=True) + epsilon)
    return scale, (values * scale).astype(low)


def unit_back(grad, values, scale):
    unit = values * scale
    return scale * (grad - unit * jnp.mean(grad * unit, axis=-1, keepdims=True))


def local(
    tokens,
    positions,
    attn_gain,
    query_weight,
    key_weight,
    value_weight,
    out_weight,
    mlp_gain,
    gate_weight,
    up_weight,
    down_weight,
    cotangent,
):
    count = tokens.shape[1]
    size = key_weight.shape[1]
    wide = query_weight.shape[1]
    reach = (WINDOW + count - 2) // count
    chips = (reach + 1) // 2
    base = 2 * chips * count - WINDOW
    gain_one = attn_gain[:, None]
    gain_two = mlp_gain[:, None]

    qkv_shard = jnp.concatenate([query_weight, key_weight, value_weight], 1).astype(f32) * gain_one
    qkv_shard = qkv_shard.astype(low)
    qkv_column = lax.all_gather(qkv_shard, "z", axis=0, tiled=False)
    out_column = lax.all_gather(after(out_weight.T, qkv_shard), "z", axis=0, tiled=False)

    spans, share = shares(gate_weight.shape[1])
    parts = share // 256 if share % 256 == 0 else 1
    calls = 2 if parts % 2 == 0 else 1
    per = parts // calls
    part = share // parts
    mine = pack(spans, part, share, gain_two, gate_weight, up_weight, down_weight.T)
    gift = cotangent[0]
    mlp_column = lax.all_to_all(after(mine, qkv_shard), PLANE, split_axis=0, concat_axis=0, tiled=True)
    mlp_column = mlp_column.reshape(-1, 3 * share)

    def gathered(k, *earlier):
        piece = after(mlp_column[:, k * 3 * part : (k + 1) * 3 * part], *earlier)
        return lax.all_gather(piece, "z", axis=0, tiled=True)

    mlp_full = [gathered(0)]
    sure = positions[0, 0] >= 0
    half = count // 2

    def project(qkv_column, tokens, gift):
        qkv_blocks = joined_blocks(plane_gather(qkv_column))
        scale_one, unit_one = unit_of(tokens[0].astype(f32))
        qkv = apply_rows(unit_one, qkv_blocks)
        queries, pair = qkv[:, :wide], qkv[:, wide:]
        moves = [behind(d) for d in range(chips, 0, -1)]
        found, _ = stage([(pair, move) for move in moves] + [(pair, "c"), (gift, "x"), (gift, "y"), (gift, "c")])
        *pairs, pair_c, gift_x, gift_y, gift_c = found
        found, _ = stage([(block, "c") for block in pairs])
        gifts = gift_x, gift_y, gift_c
        return qkv_blocks[1:], queries, [*pairs, pair, *found, pair_c], gifts, unit_one, scale_one

    def forward(queries, pairs, out_column, tokens, positions, gift_x, gift_y):
        inputs = tokens[0].astype(f32)
        mid = out_column.shape[0] // 2
        (out_x, out_y, out_c, gift_x_c, gift_y_c), (mixed, mixed_wide, logs) = stage(
            [(out_column, "x"), (out_column, "y"), (out_column, "c"), (gift_x, "c"), (gift_y, "c")],
            lambda *given: attend(given[0], given[1:], positions, size, base),
            [queries, *pairs],
        )
        (out_top, out_bottom, out_x_c, out_y_c), _ = stage(
            [(out_y[:mid], "x"), (out_x[mid:], "y"), (out_x, "c"), (out_y, "c")]
        )
        out_diag = jnp.concatenate([out_top, out_bottom], 0)
        (out_diag_c,), _ = stage([(out_diag, "c")])
        out_blocks = [out_column, out_x, out_c, out_x_c, out_y, out_diag, out_y_c, out_diag_c]
        resid = apply_rows(mixed, out_blocks, inputs)
        scale_two, unit_two = unit_of(resid)
        (unit_x, unit_y, unit_c), _ = stage([(unit_two, "x"), (unit_two, "y"), (unit_two, "c")])
        (unit_x_c, unit_y_c), _ = stage([(unit_x, "c"), (unit_y, "c")])
        unit_blocks = unit_two, unit_x, unit_c, unit_x_c, unit_y, unit_y_c
        return out_blocks[1:], mixed, mixed_wide, logs, resid, scale_two, unit_blocks, gift_x_c, gift_y_c

    qkv_column = after(qkv_column, mlp_column)
    qkv_blocks, queries, pairs, gifts, unit_one, scale_one = boxed(sure, project, qkv_column, tokens, gift)
    gift_x, gift_y, gift_c = gifts
    mlp_full += [gathered(k, pairs[0]) for k in range(1, parts)]
    out_blocks, mixed, mixed_wide, logs, resid, scale_two, unit_blocks, gift_x_c, gift_y_c = boxed(
        sure, forward, after(queries, mlp_full[0]), pairs, out_column, tokens, positions, gift_x, gift_y
    )
    qkv_blocks, out_blocks = [qkv_column, *qkv_blocks], [out_column, *out_blocks]
    grads_near = [(gift_y,), (gift,), (gift_y_c,), (gift_c,)]

    def flat(*tiles):
        return [piece for group in tiles for tile in group for piece in tile]

    def summed(keep, received):
        return keep.astype(f32) + received.astype(f32)

    def halves(value):
        middle = value.shape[0] // 2
        return value[:middle], value[middle:]

    def total(*values):
        return sum(value.astype(f32) for value in values)

    def opening(weights, blocks, gift_x, gift_x_c, grads_near, unit_one):
        unit_two, unit_x, unit_c, unit_x_c, unit_y, unit_y_c = blocks
        units_near = [(unit_y,), (unit_two,), (unit_y_c,), (unit_c,)]
        gift_y = grads_near[0][0]
        sends = [(unit_y, "x"), (gift_x, "y")]
        one_sends = [(unit_one, "x"), (unit_one, "y"), (unit_one, "c")]
        far_sums = near_sums = partial = ()
        if calls > 1:
            (unit_d, gift_d), near_sums = stage(
                sends, lambda *given: mlp([(v,) for v in given], grads_near, weights, ()), flat(units_near)
            )
        else:
            (unit_d, gift_d), _ = stage(sends)
        (unit_d_c, gift_d_c), _ = stage([(unit_d, "c"), (gift_d, "c")])
        units_far = [(unit_d,), (unit_x,), (unit_d_c,), (unit_x_c,)]
        grads_far = [(gift_d,), (gift_x,), (gift_d_c,), (gift_x_c,)]
        if calls > 1:
            (one_x, one_y, one_c), far_sums = stage(
                one_sends, lambda weights: mlp(units_far, grads_far, weights, ()), [weights]
            )
        else:
            (one_x, one_y, one_c), _ = stage(one_sends)
        one_sends = [(one_y, "x"), (one_x, "c"), (one_y, "c")]
        if calls > 1:
            (one_d, one_x_c, one_y_c), partial = stage(
                one_sends,
                lambda *given: mlp_grads(flat(units_far, units_near), flat(grads_far, grads_near), given)[0],
                [far_sums[4], near_sums[4]],
            )
        else:
            (one_d, one_x_c, one_y_c), _ = stage(one_sends)
        ones = one_x, one_c, one_x_c, one_y, one_d, one_y_c
        return (unit_d, unit_d_c), grads_far, far_sums[:4], near_sums[:4], partial, ones

    columns = []
    unit_two, unit_x, unit_c, unit_x_c, unit_y, unit_y_c = unit_blocks
    halves_far, grads_far, far_before, near_before, partial, ones = boxed(
        sure, opening, mlp_full[:per] if calls > 1 else (), unit_blocks, gift_x, gift_x_c, grads_near, unit_one
    )
    if calls > 1:
        columns.append(lax.psum_scatter(partial, "z", scatter_dimension=0, tiled=True))
    unit_d, unit_d_c = halves_far
    units_far = [(unit_d,), (unit_x,), (unit_d_c,), (unit_x_c,)]
    units_near = [(unit_y,), (unit_two,), (unit_y_c,), (unit_c,)]

    def middle(weights, units_far, units_near, grads_far, grads_near, far_before, near_before, resid, scale_two, gift, ones):
        (one_d_c,), far_sums = stage(
            [(ones[4], "c")],
            lambda *weights: mlp(units_far, grads_far, weights, far_before),
            weights,
        )
        (found,), _ = stage([(far_sums[3], "c")])
        both = summed(far_sums[2], found).astype(low)
        (diag_top, diag_bottom), (x_top, x_bottom) = halves(both[:count]), halves(both[count:])
        (diag_x, diag_y, x_top, far_out), near_sums = stage(
            [(diag_top, "x"), (diag_bottom, "y"), (x_top, "x"), (far_sums[1], "c")],
            lambda *given: mlp([(value,) for value in given], grads_near, weights, near_before),
            [tile[0] for tile in units_near],
        )
        (found,), _ = stage([(near_sums[3], "c")])
        y_bottom, x_bottom, y_top, own = turn(near_sums[2], found, x_bottom, diag_x, diag_y)
        (y_bottom, x_bottom, y_top, near_out), partial = stage(
            [(y_bottom, "y"), (x_bottom, "x"), (y_top, "y"), (near_sums[1], "c")],
            lambda *given: mlp_grads(flat(units_far, units_near), flat(grads_far, grads_near), given, cuts),
            [far_sums[4], near_sums[4]],
        )
        grad_resid, grad_attn = resid_grads(own, x_top, x_bottom, y_top, y_bottom, resid, gift, scale_two)
        out_far = summed(far_sums[0], far_out).astype(low)
        out_near = summed(near_sums[0], near_out).astype(low)
        return partial, grad_resid, grad_attn, out_far, out_near, one_d_c

    cuts = (2, 1)
    partial, grad_resid, grad_attn, out_far, out_near, one_d_c = boxed(
        sure,
        middle,
        mlp_full[-per:],
        units_far,
        units_near,
        grads_far,
        grads_near,
        far_before,
        near_before,
        resid,
        scale_two,
        gift,
        ones,
    )
    columns.append(lax.psum_scatter(partial[0], "z", scatter_dimension=0, tiled=True))
    one_x, one_c, one_x_c, one_y, one_d, one_y_c = ones
    flat_ones = [unit_one, one_x, one_c, one_x_c, one_y, one_d, one_y_c, one_d_c]

    def first_sends(diag, to_x, to_y):
        diag_top, diag_bottom = halves(diag)
        return [(diag_top, "x"), (diag_bottom, "y"), (halves(to_x)[0], "x"), (halves(to_y)[1], "y")]

    def second_sends(to_x, to_y, received):
        x_bottom = total(halves(to_x)[1], received[1]).astype(low)
        y_top = total(halves(to_y)[0], received[0]).astype(low)
        return [(x_bottom, "x"), (y_top, "y")]

    def joined(own, first, second):
        top, bottom = halves(own)
        return jnp.concatenate([total(top, first[2], second[1]), total(bottom, second[0], first[3])], 0)

    def backward(grad_attn, out_far, out_near, queries, pairs, mixed_wide, logs, out_blocks, positions):
        def attention(grad_attn):
            grad_mixed = apply_rows(grad_attn, out_blocks)
            return attend_back(queries, grad_mixed, mixed_wide, logs, pairs, positions, size, base)

        first, (grad_queries, mine, theirs) = stage(
            first_sends(out_far[:count], out_far[count:], out_near[:count]), attention, [grad_attn]
        )
        (found,), _ = stage([(theirs, "c")])
        mine = summed(mine, found)
        second = second_sends(out_far[count:], out_near[:count], first)
        found, second = stage(
            [(mine[chips - d].astype(low), behind(-d)) for d in range(chips, 0, -1)],
            lambda *given: given,
            [value for value, _ in second],
        )
        grad_pair = total(mine[chips], *found).astype(low)
        return jnp.concatenate([grad_queries, grad_pair], 1), first, second

    grad_qkv, first, second = boxed(
        sure, backward, after(grad_attn, *columns[:-1]), out_far, out_near, queries, pairs, mixed_wide, logs, out_blocks, positions
    )
    columns += [
        lax.psum_scatter(after(piece, grad_qkv), "z", scatter_dimension=0, tiled=True) for piece in partial[1:]
    ]

    def collect(grad_attn, grad_qkv, second, mixed, flat_ones):
        own, *others = spread(grad_qkv)
        found, (out_keep, out_send) = stage(
            [(value, across(r + 1)) for r, value in enumerate(others)],
            lambda *given: row_grads(*given),
            [grad_attn, mixed],
        )
        (found, *second), qkv_column = stage(
            [(out_send, "c"), (second[0], "x"), (second[1], "y")],
            lambda *gathered: token_grads(flat_ones, jnp.concatenate(gathered, 0)),
            [own, *found],
        )
        return qkv_column, out_keep, found, second

    qkv_column, out_keep, found, second = boxed(
        sure, collect, after(grad_attn, columns[-2]), grad_qkv, second, mixed, flat_ones
    )
    qkv_low = lax.psum_scatter(qkv_column, "z", scatter_dimension=0, tiled=True)

    def end(out_keep, found, first, second, grad_resid, grad_qkv, out_near, qkv_blocks, resid, scale_one, tokens):
        diag_top, diag_bottom, x_top, x_bottom, y_top, y_bottom, own = part_sums(out_keep, found)

        def results(grad_qkv, *second):
            inputs = tokens[0].astype(f32)
            output = resid + joined(out_near[count:], first, second)
            grad_unit_one = apply_rows(grad_qkv, qkv_blocks, jnp.zeros_like(inputs))
            return output, grad_resid + unit_back(grad_unit_one, inputs, scale_one)

        started, (output, grad_tokens) = stage(
            [(diag_top, "x"), (diag_bottom, "y"), (x_top, "x"), (y_bottom, "y")], results, [grad_qkv, *second]
        )
        x_bottom, y_top = total(x_bottom, started[1]).astype(low), total(y_top, started[0]).astype(low)
        second, _ = stage([(x_bottom, "x"), (y_top, "y")])
        column = joined(own, started, second).astype(low)
        return output, grad_tokens, column.reshape(-1, column.shape[-1])

    output, grad_tokens, out_column = boxed(
        sure,
        end,
        out_keep,
        found,
        first,
        second,
        after(grad_resid, columns[-1]),
        grad_qkv,
        out_near,
        qkv_blocks,
        resid,
        scale_one,
        tokens,
    )
    out_sum = lax.psum_scatter(out_column, "z", scatter_dimension=0, tiled=True).astype(f32)
    every = jnp.concatenate([*columns, qkv_low], 1)
    every = after(every, out_column).reshape(8, -1, every.shape[1])
    every = lax.all_to_all(every, PLANE, split_axis=0, concat_axis=0, tiled=True)
    deep = qkv_low.shape[1]
    qkv_sum = jnp.swapaxes(every[:, :, -deep:], 0, 1).reshape(-1, 8 * deep).astype(f32)
    query_sum = qkv_sum[:, :wide]
    key_sum = qkv_sum[:, wide : wide + size]
    value_sum = qkv_sum[:, wide + size :]
    grad_attn_gain = (
        jnp.sum(query_weight.astype(f32) * query_sum, axis=1)
        + jnp.sum(key_weight.astype(f32) * key_sum, axis=1)
        + jnp.sum(value_weight.astype(f32) * value_sum, axis=1)
    )
    grad_gate, grad_up, grad_down, grad_mlp_gain = finish(spans, part, per, gain_two, gate_weight, up_weight, every)
    return (
        output[None],
        grad_tokens[None],
        grad_attn_gain,
        query_sum * gain_one,
        key_sum * gain_one,
        value_sum * gain_one,
        out_sum.T,
        grad_mlp_gain[:, 0],
        grad_gate,
        grad_up,
        grad_down.T,
    )


def solution(mesh):
    ctx, fsdp = mesh.shape["ctx"], mesh.shape["fsdp"]
    fine = Mesh(mesh.devices.reshape(ctx // 4, 2, 2, fsdp), ("z", "y", "c", "x"))
    rows = ("z", "y", "c")
    every = ("z", "y", "c", "x")
    return jax.shard_map(
        local,
        mesh=fine,
        in_specs=(
            P("x", rows, None),
            P("x", rows),
            P(every),
            P(every, None),
            P(every, None),
            P(every, None),
            P(None, every),
            P(every),
            P(every, None),
            P(every, None),
            P(None, every),
            P("x", rows, None),
        ),
        out_specs=(
            P("x", rows, None),
            P("x", rows, None),
            P(every),
            P(every, None),
            P(every, None),
            P(every, None),
            P(None, every),
            P(every),
            P(every, None),
            P(every, None),
            P(None, every),
        ),
        check_vma=False,
    )
```

```python
import functools

import jax
import jax.numpy as jnp
from jax import lax
from jax.experimental import pallas as pl
from jax.experimental.pallas import tpu as pltpu
from jax.sharding import Mesh, PartitionSpec as P

WINDOW = 2048
SUB = 128
TILE = 512
epsilon = 1e-06
blocked_score = -1e30
PLANE = ("y", "c", "x")
low = jnp.bfloat16
f32 = jnp.float32
NOMINAL = pl.CostEstimate(flops=1 << 20, bytes_accessed=1 << 12, transcendentals=0)


def dot(left, right, contract, kind=f32):
    return lax.dot_general(
        left, right, ((contract[:1], contract[1:]), ((), ())), preferred_element_type=f32
    ).astype(kind)


def swap(value, axis):
    return lax.ppermute(value, axis, [(0, 1), (1, 0)])


def plane_gather(own, second=(), third=()):
    half = own.shape[0] // 2
    by_x = swap(own, "x")
    by_y = swap(own, "y")
    own_c = swap(own, "c")
    diag = (
        swap(after(by_y[:half], *second), "x"),
        swap(after(by_x[half:], *second), "y"),
    )
    by_x_c = swap(after(by_x, *second), "c")
    by_y_c = swap(after(by_y, *second), "c")
    diag_c = tuple(swap(after(part, *third), "c") for part in diag)
    return [own, by_x, own_c, by_x_c, by_y, diag, by_y_c, diag_c]


def joined_blocks(blocks):
    return [jnp.concatenate(block, 0) if isinstance(block, tuple) else block for block in blocks]


def stage(sends, work=None, given=()):
    fenced, given = lax.optimization_barrier((tuple(value for value, _ in sends), tuple(given)))
    received = tuple(
        swap(value, way) if isinstance(way, str) else way(value) for value, (_, way) in zip(fenced, sends)
    )
    return lax.optimization_barrier((received, work(*given) if work else given))


def boxed(sure, work, *given):
    shapes = jax.eval_shape(work, *given)
    return lax.cond(
        sure, work, lambda *_: jax.tree.map(lambda out: jnp.zeros(out.shape, out.dtype), shapes), *given
    )


def plane_index():
    return (lax.axis_index("y") * 2 + lax.axis_index("c")) * 2 + lax.axis_index("x")


def after(value, *earlier):
    return lax.optimization_barrier((value,) + earlier)[0]


def across(distance):
    return lambda value: lax.ppermute(value, PLANE, [(i, i ^ distance) for i in range(8)])


def behind(steps):
    count = lax.axis_size("z") * lax.axis_size("y")
    pairs = [(i, i + steps) for i in range(count) if 0 <= i + steps < count]
    return lambda value: lax.ppermute(value, ("z", "y"), pairs)


def two_heads(block, size):
    return jnp.concatenate([block[:, :size], block[:, size:]], 0)


def side_by_side(rows, size):
    half = rows.shape[0] // 2
    return jnp.concatenate([rows[:half], rows[half:]], 1)


def write_bias(bias, places, span, block):
    key = lax.broadcasted_iota(jnp.int32, (span, SUB), 0) - WINDOW
    query = lax.broadcasted_iota(jnp.int32, (span, SUB), 1)
    age = query - key
    seen = (age <= places) & (age >= 0) & (age < WINDOW)
    value = jnp.where(seen, 0.0, blocked_score).astype(f32)
    bias[:, :SUB] = value
    bias[:, SUB:] = value


def lay_window(core, blocks, window, turned, columns):
    count = blocks[0].shape[0]
    half = len(blocks) // 2
    for i in range(half):
        for which, block in ((core, blocks[i]), (1 - core, blocks[half + i])):
            at = pl.multiple_of((2 * i + which) * count, SUB)
            window[pl.ds(at, count), :] = block[...]
            turned[:, pl.ds(at, count)] = block[:, columns].T


def chunks(span, number):
    tiles = span // 128
    return [(128 * (tiles * i // number), 128 * (tiles * (i + 1) // number)) for i in range(number)]


def attend_kernel(size, scale, span, base, core, places, queries, *rest):
    blocks, (mixed, wide, logs, bias, window, turned) = rest[:-6], rest[-6:]
    block = pl.program_id(0)
    count = blocks[0].shape[0]
    start = pl.multiple_of(core[0] * count + base + block * SUB, SUB)

    @pl.when((block == 0) & (pl.program_id(1) == 0))
    def _():
        lay_window(core[0], blocks, window, turned, slice(size, 2 * size))

    @pl.when(pl.program_id(1) == 0)
    def _():
        write_bias(bias, places[...], span, block)

    query = two_heads(queries[...], size) * jnp.asarray(scale, low)
    highest = total = flat = None
    for at, end in chunks(span, 8):
        place = pl.ds(start + at, end - at)
        scores = dot(window[place, :size], query, (1, 1)) + bias[at:end]
        top = jnp.max(scores, axis=0, keepdims=True)
        if highest is not None:
            top = jnp.maximum(highest, top)
            fade = jnp.exp(highest - top)
        highest = top
        expo = jnp.exp(scores - highest)
        part = jnp.sum(expo, axis=0, keepdims=True)
        mix = dot(turned[:, place], expo.astype(low), (1, 0))
        total = part if total is None else total * fade + part
        flat = mix if flat is None else flat * fade + mix
    result = side_by_side((flat / total).T, size)
    wide[...] = result
    mixed[...] = result.astype(low)
    logs[0] = highest + jnp.log(total)


def attend_back_kernel(size, scale, span, base, core, places, queries, grads, wide, logs, *rest):
    blocks, (grad_queries, mine, theirs, bias, window, turned, total) = rest[:-7], rest[-7:]
    block = pl.program_id(0)
    count = blocks[0].shape[0]
    start = pl.multiple_of(core[0] * count + base + block * SUB, SUB)

    @pl.when((block == 0) & (pl.program_id(1) == 0))
    def _():
        lay_window(core[0], blocks, window, turned, slice(0, size))
        total[...] = jnp.zeros_like(total)

    @pl.when(pl.program_id(1) == 0)
    def _():
        write_bias(bias, places[...], span, block)

    query = two_heads(queries[...], size) * jnp.asarray(scale, low)
    grad = two_heads(grads[...], size)
    inner = jnp.sum((grad.astype(f32) * two_heads(wide[...], size)).T, axis=0, keepdims=True)
    place = pl.ds(start, span)
    keys, values = window[place, :size], window[place, size:]
    probs = jnp.exp(dot(keys, query, (1, 1)) + (bias[...] - logs[0]))
    grad_scores = (probs * (dot(values, grad, (1, 1)) - inner)).astype(low)
    total[place, size:] += dot(probs.astype(low), grad, (1, 0))
    total[place, :size] += dot(grad_scores, query, (1, 0))
    flat = dot(turned[:, place], grad_scores, (1, 0)) * scale
    grad_queries[...] = side_by_side(flat.T, size).astype(low)

    @pl.when((block == pl.num_programs(0) - 1) & (pl.program_id(1) == pl.num_programs(1) - 1))
    def _():
        for i in range(len(blocks) // 2):
            at = pl.multiple_of((2 * i + core[0]) * count, SUB)
            mine[i] = total[pl.ds(at, count), :]
            at = pl.multiple_of((2 * i + 1 - core[0]) * count, SUB)
            theirs[i] = total[pl.ds(at, count), :].astype(low)


def attend(queries, blocks, places, size, base):
    count, wide = queries.shape
    grid = (count // SUB, wide // (2 * size))
    span = WINDOW + SUB
    rows = len(blocks) * count
    core = lax.axis_index("c").astype(jnp.int32)[None]
    tile = pl.BlockSpec((SUB, 2 * size), lambda s, h, o: (s, h))
    return pl.pallas_call(
        functools.partial(attend_kernel, size, size**-0.5, span, base),
        out_shape=(
            jax.ShapeDtypeStruct((count, wide), low),
            jax.ShapeDtypeStruct((count, wide), f32),
            jax.ShapeDtypeStruct((grid[0] * grid[1], 1, 2 * SUB), f32),
        ),
        grid_spec=pltpu.PrefetchScalarGridSpec(
            num_scalar_prefetch=1,
            grid=grid,
            in_specs=[pl.BlockSpec((1, SUB), lambda s, h, o: (0, s)), tile]
            + [pl.BlockSpec(block.shape, lambda s, h, o: (0, 0)) for block in blocks],
            out_specs=[tile, tile, pl.BlockSpec((1, 1, 2 * SUB), lambda s, h, o: (s * grid[1] + h, 0, 0))],
            scratch_shapes=[
                pltpu.VMEM((span, 2 * SUB), f32),
                pltpu.VMEM((rows, 2 * size), low),
                pltpu.VMEM((size, rows), low),
            ],
        ),
        compiler_params=pltpu.CompilerParams(vmem_limit_bytes=56 << 20),
        cost_estimate=NOMINAL,
    )(core, places, queries, *blocks)


def attend_back(queries, grads, mixed, logs, blocks, places, size, base):
    count, wide = queries.shape
    grid = (count // SUB, wide // (2 * size))
    span = WINDOW + SUB
    rows = len(blocks) * count
    half = len(blocks) // 2
    core = lax.axis_index("c").astype(jnp.int32)[None]
    tile = pl.BlockSpec((SUB, 2 * size), lambda s, h, o: (s, h))
    whole = pl.BlockSpec((half, count, 2 * size), lambda s, h, o: (0, 0, 0))
    return pl.pallas_call(
        functools.partial(attend_back_kernel, size, size**-0.5, span, base),
        out_shape=(
            jax.ShapeDtypeStruct((count, wide), low),
            jax.ShapeDtypeStruct((half, count, 2 * size), f32),
            jax.ShapeDtypeStruct((half, count, 2 * size), low),
        ),
        grid_spec=pltpu.PrefetchScalarGridSpec(
            num_scalar_prefetch=1,
            grid=grid,
            in_specs=[
                pl.BlockSpec((1, SUB), lambda s, h, o: (0, s)),
                tile,
                tile,
                tile,
                pl.BlockSpec((1, 1, 2 * SUB), lambda s, h, o: (s * grid[1] + h, 0, 0)),
            ]
            + [pl.BlockSpec(block.shape, lambda s, h, o: (0, 0)) for block in blocks],
            out_specs=[tile, whole, whole],
            scratch_shapes=[
                pltpu.VMEM((span, 2 * SUB), f32),
                pltpu.VMEM((rows, 2 * size), low),
                pltpu.VMEM((size, rows), low),
                pltpu.VMEM((rows, 2 * size), f32),
            ],
        ),
        compiler_params=pltpu.CompilerParams(vmem_limit_bytes=60 << 20),
        cost_estimate=NOMINAL,
    )(core, places, queries, grads, mixed, logs, *blocks)


def lay_rows(slots, blocks, full):
    planes, rows, _ = blocks[0].shape
    for r in range(8):
        for plane in range(planes):
            at = pl.multiple_of((plane * 8 + slots[r]) * rows, 16)
            full[pl.ds(at, rows), :] = blocks[r][plane]


def apply_kernel(slots, left, *rest):
    blocks, (out, full) = rest[:8], rest[8:]
    lay_rows(slots, blocks, full)
    out[...] = dot(left[...], full[...], (1, 0), low)


def apply_turned_kernel(slots, left, *rest):
    *start, out, full = rest
    start, blocks = start[:-8], start[-8:]
    lay_rows(slots, blocks, full)

    @pl.when(pl.program_id(0) == 0)
    def _():
        out[...] = start[0][...] if start else jnp.zeros_like(out)

    out[...] += dot(left[...], full[...], (1, 1))


def whole_rows(blocks):
    planes, rows, wide = blocks[0].shape
    here = plane_index()
    whole = jnp.zeros((planes, 8, rows, wide), blocks[0].dtype)
    for r, block in enumerate(blocks):
        whole = lax.dynamic_update_slice(whole, block[:, None], (0, here ^ r, 0, 0))
    return whole.reshape(planes * 8 * rows, wide)


def apply_rows(left, blocks, turned=False, start=None):
    planes, rows, wide = blocks[0].shape
    if rows % 16 or wide % TILE:
        whole = whole_rows(blocks)
        if not turned:
            return dot(left, whole, (1, 0), low)
        return dot(left, whole, (1, 1)) + (0.0 if start is None else start)
    count, deep = left.shape[0], planes * 8 * rows
    slots = (plane_index() ^ jnp.arange(8)).astype(jnp.int32)
    pieces = [pl.BlockSpec((planes, rows, TILE), lambda n, s: (0, 0, n))] * 8
    whole = pl.BlockSpec((count, deep), lambda n, s: (0, 0))
    part = pl.BlockSpec((count, TILE), lambda n, s: (0, n))
    if not turned:
        kernel, given, specs, result = apply_kernel, [left], [whole], part
        shape = jax.ShapeDtypeStruct((count, wide), low)
    else:
        kernel, given, specs, result = apply_turned_kernel, [left], [part], whole
        if start is not None:
            given, specs = given + [start], specs + [whole]
        shape = jax.ShapeDtypeStruct((count, deep), f32)
    return pl.pallas_call(
        kernel,
        out_shape=shape,
        grid_spec=pltpu.PrefetchScalarGridSpec(
            num_scalar_prefetch=1,
            grid=(wide // TILE,),
            in_specs=specs + pieces,
            out_specs=result,
            scratch_shapes=[pltpu.VMEM((deep, TILE), low)],
        ),
        compiler_params=pltpu.CompilerParams(vmem_limit_bytes=48 << 20),
        cost_estimate=NOMINAL,
    )(slots, *given, *blocks)


def row_grads_kernel(slots, left, right, keep, send, turned):
    @pl.when(pl.program_id(1) == 0)
    def _():
        turned[...] = left[...].T

    rows = keep.shape[2]
    value = dot(turned[...], right[...], (1, 0), low)
    for i in range(8):
        place = slots[i]

        @pl.when(place < 4)
        def _():
            keep[place, 0] = value[i * rows : (i + 1) * rows]

        @pl.when(place >= 4)
        def _():
            send[place - 4, 0] = value[i * rows : (i + 1) * rows]


def row_grads(left, right):
    planes = lax.axis_size("z")
    count, deep = left.shape
    wide = right.shape[1]
    rows = deep // (planes * 8)
    places = jnp.array([3, 1, 7, 5, 2, 0, 6, 4], jnp.int32)
    slots = places[plane_index() ^ jnp.arange(8)]
    if rows % 16 or wide % TILE or (planes * 8 * rows) % (planes * 128):
        blocks = dot(left, right, (0, 0), low).reshape(planes, 8, rows, wide)
        order = jnp.argsort(slots)
        blocks = jnp.swapaxes(jnp.take(blocks, order, axis=1), 0, 1)
        return blocks[:4], blocks[4:]
    tile = wide if wide <= 5 * TILE else TILE
    group = pl.BlockSpec((4, 1, rows, tile), lambda z, n, s: (0, z, 0, n))
    shape = jax.ShapeDtypeStruct((4, planes, rows, wide), low)
    return pl.pallas_call(
        row_grads_kernel,
        out_shape=(shape, shape),
        grid_spec=pltpu.PrefetchScalarGridSpec(
            num_scalar_prefetch=1,
            grid=(planes, wide // tile),
            in_specs=[
                pl.BlockSpec((count, 8 * rows), lambda z, n, s: (0, z)),
                pl.BlockSpec((count, tile), lambda z, n, s: (0, n)),
            ],
            out_specs=[group, group],
            scratch_shapes=[pltpu.VMEM((8 * rows, count), low)],
        ),
        compiler_params=pltpu.CompilerParams(vmem_limit_bytes=48 << 20),
        cost_estimate=NOMINAL,
    )(slots, left, right)


def mlp_kernel(part, per, tiles, *rest):
    weights, rest = rest[:per], rest[per:]
    pieces = 2 * sum(tiles)
    sources, rest = rest[:pieces], rest[pieces:]
    before, rest = rest[:-8], rest[-8:]
    outs, grad_units, hidden, units, grads, arrived = rest[0:2], rest[2:4], *rest[4:]
    step = pl.program_id(0)

    def fetches(tile):
        first = 2 * sum(tiles[:tile])
        found = []
        for array, target in enumerate((units, grads)):
            at = 0
            for i in range(tiles[tile]):
                source = sources[first + array * tiles[tile] + i]
                found.append(
                    pltpu.make_async_copy(
                        source,
                        target.at[tile % 2, pl.ds(at, source.shape[0])],
                        arrived.at[tile % 2, array, i],
                    )
                )
                at += source.shape[0]
        return found

    for tile in range(len(tiles)):

        @pl.when(step == tile)
        def _():
            if tile == 0:
                for copy in fetches(0):
                    copy.start()
            if tile + 1 < len(tiles):
                for copy in fetches(tile + 1):
                    copy.start()
            for copy in fetches(tile):
                copy.wait()

    slope = 0.7978845608028654
    for j in range(per):
        both = dot(units[step % 2], weights[j][:, : 2 * part], (1, 0))
        gates, upward = both[:, :part], both[:, part:]
        grad_middle = dot(grads[step % 2], weights[j][:, 2 * part :], (1, 0))
        square = gates * gates
        half = 0.5 + 0.5 * jnp.tanh(gates * (slope + slope * 0.044715 * square))
        gelu = gates * half
        grad_gelu = half + gelu * (1.0 - half) * (2 * slope + 6 * slope * 0.044715 * square)
        at = 2 * part * j
        hidden[:, at : at + part] = (grad_middle * upward * grad_gelu).astype(low)
        hidden[:, at + part : at + 2 * part] = (grad_middle * gelu).astype(low)
        at = part * (2 * per + j)
        hidden[:, at : at + part] = (gelu * upward).astype(low)
    for which, targets in enumerate((outs, grad_units)):
        value = 0.0
        for j in range(per):
            at, width = (2 * part * j, 2 * part) if which else (part * (2 * per + j), part)
            first = 0 if which else 2 * part
            value = value + dot(hidden[:, at : at + width], weights[j][:, first : first + width], (1, 1))
        for side in range(2):

            @pl.when(step // (len(tiles) // 2) == side)
            def _():
                if before:
                    targets[side][...] = (value + before[2 * which + side][...].astype(f32)).astype(low)
                else:
                    targets[side][...] = value.astype(low)


def mlp(units, grads, weights, before):
    rows = sum(piece.shape[0] for piece in units[0])
    count, wide = rows * len(units), units[0][0].shape[1]
    per, each = len(weights), weights[0].shape[1]
    deep = per * each
    tiles = tuple(len(tile) for tile in units)
    sources = [piece for pair in zip(units, grads) for tile in pair for piece in tile]
    side = len(units) // 2
    sides = [
        pl.BlockSpec((rows, wide), lambda i: (jnp.minimum(i, side - 1), 0)),
        pl.BlockSpec((rows, wide), lambda i: (jnp.maximum(i - side, 0), 0)),
    ]
    half = jax.ShapeDtypeStruct((count // 2, wide), low)
    return pl.pallas_call(
        functools.partial(mlp_kernel, each // 3, per, tiles),
        out_shape=[half] * 4 + [jax.ShapeDtypeStruct((count, deep), low)],
        grid=(len(units),),
        in_specs=[pl.BlockSpec((wide, each), lambda i: (0, 0), pipeline_mode=pl.Buffered(1))] * per
        + [pl.BlockSpec(memory_space=pl.ANY)] * len(sources)
        + (sides * 2 if before else []),
        out_specs=sides * 2 + [pl.BlockSpec((rows, deep), lambda i: (i, 0))],
        scratch_shapes=[
            pltpu.VMEM((2, rows, wide), low),
            pltpu.VMEM((2, rows, wide), low),
            pltpu.SemaphoreType.DMA((2, 2, max(tiles))),
        ],
        compiler_params=pltpu.CompilerParams(vmem_limit_bytes=62 << 20),
        cost_estimate=NOMINAL,
    )(*weights, *sources, *before)


def mlp_grads_kernel(number, *rest):
    units, grads, hidden, rest = rest[:number], rest[number : 2 * number], rest[2 * number : 2 * number + 2], rest[2 * number + 2 :]
    *outs, turned = rest
    step = pl.program_id(0)
    part = hidden[0].shape[1] // 3
    piece = min(part, 256)
    places = [(out, at) for out in outs for at in range(0, out.shape[1], piece)]

    def turn(slot, which, sources, share, shares):
        at = 0
        for i, source in enumerate(sources):
            if i * shares // len(sources) == share:
                turned[slot, which, :, at : at + source.shape[0]] = source[...].T
            at += source.shape[0]

    def multiply(slot, which, i, at):
        value, start = 0.0, 0
        for block in hidden:
            left = turned[slot, which, :, start : start + block.shape[0]]
            value = value + dot(left, block[:, at : at + piece], (1, 0))
            start += block.shape[0]
        out, place = places[i]
        out[:, place : place + piece] = value.astype(low)

    work = [(at // (2 * part), at) for at in range(0, 3 * part, piece)]

    @pl.when(step == 0)
    def _():
        turn(0, 0, units, 0, 1)
        turn(0, 1, grads, 0, 1)

    @pl.when(step > 0)
    def _():
        for i, (which, at) in enumerate(work):
            multiply((step - 1) % 2, which, i, at)
            turn(step % 2, 0, units, i, len(work))
            turn(step % 2, 1, grads, i, len(work))


def mlp_grads(units, grads, hidden, pieces=(3,)):
    wide = units[0].shape[1]
    deep = hidden[0].shape[1]
    count = sum(piece.shape[0] for piece in units)
    rows = 512
    last = wide // rows - 1
    return pl.pallas_call(
        functools.partial(mlp_grads_kernel, len(units)),
        out_shape=[jax.ShapeDtypeStruct((wide, deep // 3 * piece), low) for piece in pieces],
        grid=(last + 2,),
        in_specs=[
            pl.BlockSpec((piece.shape[0], rows), lambda s: (0, jnp.minimum(s, last))) for piece in units + grads
        ]
        + [pl.BlockSpec(piece.shape, lambda s: (0, 0), pipeline_mode=pl.Buffered(1)) for piece in hidden],
        out_specs=[
            pl.BlockSpec((rows, deep // 3 * piece), lambda s: (jnp.maximum(s - 1, 0), 0)) for piece in pieces
        ],
        scratch_shapes=[pltpu.VMEM((2, 2, rows, count), low)],
        compiler_params=pltpu.CompilerParams(vmem_limit_bytes=62 << 20),
        cost_estimate=NOMINAL,
    )(*units, *grads, *hidden)


def token_grads_kernel(number, *rest):
    units, (right, out, turned) = rest[:number], rest[number:]

    @pl.when(pl.program_id(0) == 0)
    def _():
        turned[...] = right[...].T

    value, at = 0.0, 0
    for unit in units:
        value = value + dot(turned[:, at : at + unit.shape[0]], unit[...], (1, 0))
        at += unit.shape[0]
    out[...] = value.astype(low).T


def token_grads(units, right):
    wide = units[0].shape[1]
    count, deep = right.shape
    rows = 512
    return pl.pallas_call(
        functools.partial(token_grads_kernel, len(units)),
        out_shape=jax.ShapeDtypeStruct((wide, deep), low),
        grid=(wide // rows,),
        in_specs=[pl.BlockSpec((piece.shape[0], rows), lambda s: (0, s)) for piece in units]
        + [pl.BlockSpec(right.shape, lambda s: (0, 0), pipeline_mode=pl.Buffered(1))],
        out_specs=pl.BlockSpec((rows, deep), lambda s: (s, 0)),
        scratch_shapes=[pltpu.VMEM((deep, count), low)],
        compiler_params=pltpu.CompilerParams(vmem_limit_bytes=56 << 20),
        cost_estimate=NOMINAL,
    )(*units, right)


def spread_kernel(slots, value, *outs):
    deep = outs[0].shape[1]
    for i, out in enumerate(outs):
        out[...] = value[:, pl.ds(pl.multiple_of(slots[i] * deep, 128), deep)]


def spread(value):
    count, wide = value.shape
    slots = (plane_index() ^ jnp.arange(8)).astype(jnp.int32)
    deep = wide // 8
    if deep % 128:
        return [lax.dynamic_slice(value, (0, slots[r] * deep), (count, deep)) for r in range(8)]
    return pl.pallas_call(
        spread_kernel,
        out_shape=[jax.ShapeDtypeStruct((count, deep), value.dtype)] * 8,
        grid_spec=pltpu.PrefetchScalarGridSpec(
            num_scalar_prefetch=1,
            grid=(1,),
            in_specs=[pl.BlockSpec((count, wide), lambda i, s: (0, 0))],
            out_specs=[pl.BlockSpec((count, deep), lambda i, s: (0, 0))] * 8,
        ),
        cost_estimate=NOMINAL,
    )(slots, value)


def turn_kernel(keep, found, far, diag_x, diag_y, y_bottom, x_bottom, y_top):
    half = far.shape[0]
    both = keep[...].astype(f32) + found[...].astype(f32)
    y_top[...] = (both[:half] + diag_x[...].astype(f32)).astype(low)
    y_bottom[...] = both[half:].astype(low)
    x_bottom[...] = (far[...].astype(f32) + diag_y[...].astype(f32)).astype(low)


def turn(keep, found, far, diag_x, diag_y):
    half, wide = far.shape
    part = lambda rows: pl.BlockSpec((rows, TILE), lambda n: (0, n))
    return pl.pallas_call(
        turn_kernel,
        out_shape=[jax.ShapeDtypeStruct((half, wide), low)] * 3,
        grid=(wide // TILE,),
        in_specs=[part(2 * half)] * 2 + [part(half)] * 3,
        out_specs=[part(half)] * 3,
        cost_estimate=NOMINAL,
    )(keep, found, far, diag_x, diag_y)


def halved_kernel(keep, found, *outs):
    half = outs[0].shape[0]
    for i, out in enumerate(outs):
        rows = slice(i * half, i * half + half)
        out[...] = (keep[rows].astype(f32) + found[rows].astype(f32)).astype(low)


def halved(keep, found):
    count, wide = keep.shape
    part = lambda rows: pl.BlockSpec((rows, TILE), lambda n: (0, n))
    return pl.pallas_call(
        halved_kernel,
        out_shape=[jax.ShapeDtypeStruct((count // 4, wide), low)] * 4,
        grid=(wide // TILE,),
        in_specs=[part(count)] * 2,
        out_specs=[part(count // 4)] * 4,
        cost_estimate=NOMINAL,
    )(keep, found)


def resid_kernel(steps, keep, found, x_top, x_bottom, y_top, y_bottom, resid, gift, scale, grad_out, grad_low):
    upper = pl.program_id(0) < steps
    x_part = jnp.where(upper, x_top[...].astype(f32), x_bottom[...].astype(f32))
    y_part = jnp.where(upper, y_top[...].astype(f32), y_bottom[...].astype(f32))
    grad = keep[...].astype(f32) + found[...].astype(f32) + x_part + y_part
    grad = gift[...].astype(f32) + unit_back(grad, resid[...], scale[...])
    grad_out[...] = grad
    grad_low[...] = grad.astype(low)


def resid_grads(keep, found, x_top, x_bottom, y_top, y_bottom, resid, gift, scale):
    count, wide = resid.shape
    rows = 96
    steps = count // (2 * rows)
    row = pl.BlockSpec((rows, wide), lambda i: (i, 0))
    own = pl.BlockSpec((rows, wide), lambda i: (i + 2 * steps, 0))
    first = pl.BlockSpec((rows, wide), lambda i: (jnp.minimum(i, steps - 1), 0))
    last = pl.BlockSpec((rows, wide), lambda i: (jnp.maximum(i - steps, 0), 0))
    return pl.pallas_call(
        functools.partial(resid_kernel, steps),
        out_shape=(jax.ShapeDtypeStruct((count, wide), f32), jax.ShapeDtypeStruct((count, wide), low)),
        grid=(2 * steps,),
        in_specs=[own, own, first, last, first, last, row, row, pl.BlockSpec((rows, 1), lambda i: (i, 0))],
        out_specs=(row, row),
        cost_estimate=NOMINAL,
    )(keep, found, x_top, x_bottom, y_top, y_bottom, resid, gift, scale)


def part_sums_kernel(keep, found, diag_top, diag_bottom, x_top, x_bottom, y_top, y_bottom, own):
    half = diag_top.shape[0]

    def both(place, first, rows):
        part = slice(first, first + rows)
        return (keep[place, part].astype(f32) + found[place, part].astype(f32)).astype(low)

    for place, (top, bottom) in enumerate(((diag_top, diag_bottom), (x_top, x_bottom), (y_top, y_bottom))):
        top[...] = both(place, 0, half)
        bottom[...] = both(place, half, half)
    own[...] = both(3, 0, 2 * half)


def part_sums(keep, found):
    _, planes, rows, wide = keep.shape
    four = pl.BlockSpec((4, planes, rows, TILE), lambda n: (0, 0, 0, n))
    some = lambda planes: pl.BlockSpec((planes, rows, TILE), lambda n: (0, 0, n))
    half = planes // 2
    shape = lambda planes: jax.ShapeDtypeStruct((planes, rows, wide), low)
    return pl.pallas_call(
        part_sums_kernel,
        out_shape=[shape(half)] * 6 + [shape(planes)],
        grid=(wide // TILE,),
        in_specs=[four] * 2,
        out_specs=[some(half)] * 6 + [some(planes)],
        compiler_params=pltpu.CompilerParams(vmem_limit_bytes=48 << 20),
        cost_estimate=NOMINAL,
    )(keep, found)


def pack_kernel(spans, part, gain, gate, up, down, out):
    scale = gain[...]
    share = out.shape[2] // 3
    for p, (at, n) in enumerate(spans):
        for q in range(share // part):
            width = min(part, n - q * part)
            place = slice(at + q * part, at + q * part + width)
            for which, source in enumerate((gate, up, down)):
                first = part * (3 * q + which)
                if width > 0:
                    value = source[:, place]
                    if which < 2:
                        value = (value.astype(f32) * scale).astype(low)
                    out[p, :, first : first + width] = value
                if width < part:
                    empty = max(width, 0)
                    out[p, :, first + empty : first + part] = jnp.zeros((out.shape[1], part - empty), low)


def pack(spans, part, share, gain, gate, up, down):
    rows, _ = gate.shape
    return pl.pallas_call(
        functools.partial(pack_kernel, spans, part),
        out_shape=jax.ShapeDtypeStruct((8, rows, 3 * share), low),
        compiler_params=pltpu.CompilerParams(vmem_limit_bytes=48 << 20),
        cost_estimate=NOMINAL,
    )(gain, gate, up, down)


def shares(columns):
    tiles = -(-columns // 128)
    few, more = divmod(tiles, 8)
    sizes = [128 * (few + (p < more)) for p in range(8)]
    return [(sum(sizes[:p]), size) for p, size in enumerate(sizes)], 128 * (few + (more > 0))


def finish_kernel(spans, part, per, gain, gate, up, whole, gate_out, up_out, down_out, gain_out):
    scale = gain[...]
    total = jnp.zeros_like(scale)
    for p, (at, n) in enumerate(spans):
        for q in range(-(-n // part)):
            width = min(part, n - q * part)
            start, j = 3 * part * per * (q // per), q % per
            place = slice(at + q * part, at + q * part + width)
            for which, (weight, out) in enumerate(((gate, gate_out), (up, up_out))):
                first = start + part * (2 * j + which)
                value = whole[p, :, first : first + width].astype(f32)
                total = total + jnp.sum(value * weight[:, place].astype(f32), axis=1, keepdims=True)
                out[:, place] = value * scale
            first = start + part * (2 * per + j)
            down_out[:, place] = whole[p, :, first : first + width].astype(f32)
    gain_out[...] = total


def finish(spans, part, per, gain, gate, up, whole):
    rows, columns = gate.shape
    return pl.pallas_call(
        functools.partial(finish_kernel, spans, part, per),
        out_shape=(
            jax.ShapeDtypeStruct((rows, columns), f32),
            jax.ShapeDtypeStruct((rows, columns), f32),
            jax.ShapeDtypeStruct((rows, columns), f32),
            jax.ShapeDtypeStruct((rows, 1), f32),
        ),
        compiler_params=pltpu.CompilerParams(vmem_limit_bytes=48 << 20),
        cost_estimate=NOMINAL,
    )(gain, gate, up, whole)


def unit_of(values):
    scale = lax.rsqrt(jnp.mean(values * values, axis=-1, keepdims=True) + epsilon)
    return scale, (values * scale).astype(low)


def unit_back(grad, values, scale):
    unit = values * scale
    return scale * (grad - unit * jnp.mean(grad * unit, axis=-1, keepdims=True))


def local(
    tokens,
    positions,
    attn_gain,
    query_weight,
    key_weight,
    value_weight,
    out_weight,
    mlp_gain,
    gate_weight,
    up_weight,
    down_weight,
    cotangent,
):
    count = tokens.shape[1]
    size = key_weight.shape[1]
    wide = query_weight.shape[1]
    reach = (WINDOW + count - 2) // count
    chips = (reach + 1) // 2
    base = 2 * chips * count - WINDOW
    gain_one = attn_gain[:, None]
    gain_two = mlp_gain[:, None]

    qkv_shard = jnp.concatenate([query_weight, key_weight, value_weight], 1).astype(f32) * gain_one
    qkv_shard = qkv_shard.astype(low)
    qkv_column = lax.all_gather(qkv_shard, "z", axis=0, tiled=False)
    out_column = lax.all_gather(after(out_weight.T, qkv_shard), "z", axis=0, tiled=False)

    spans, share = shares(gate_weight.shape[1])
    parts = share // 256 if share % 256 == 0 else 1
    calls = 2 if parts % 2 == 0 else 1
    per = parts // calls
    part = share // parts
    mine = pack(spans, part, share, after(gain_two, qkv_shard), gate_weight, up_weight, down_weight.T)
    gift = cotangent[0]
    mlp_column = lax.all_to_all(mine, PLANE, split_axis=0, concat_axis=0, tiled=True)
    mlp_column = mlp_column.reshape(-1, 3 * share)

    def gathered(k, *earlier):
        piece = after(mlp_column[:, k * 3 * part : (k + 1) * 3 * part], *earlier)
        return lax.all_gather(piece, "z", axis=0, tiled=True)

    mlp_full = [gathered(0)]
    sure = positions[0, 0] >= 0
    half = count // 2

    def project(qkv_column, tokens, gift):
        qkv_blocks = joined_blocks(plane_gather(qkv_column))
        scale_one, unit_one = unit_of(tokens[0].astype(f32))
        qkv = apply_rows(unit_one, qkv_blocks)
        queries, pair = qkv[:, :wide], qkv[:, wide:]
        moves = [behind(d) for d in range(chips, 0, -1)]
        found, _ = stage([(pair, move) for move in moves] + [(pair, "c"), (gift, "x"), (gift, "y"), (gift, "c")])
        *pairs, pair_c, gift_x, gift_y, gift_c = found
        found, _ = stage([(block, "c") for block in pairs])
        gifts = gift_x, gift_y, gift_c
        return qkv_blocks[1:], queries, [*pairs, pair, *found, pair_c], gifts, unit_one, scale_one

    def forward(queries, pairs, out_column, tokens, positions, gift_x, gift_y):
        inputs = tokens[0].astype(f32)
        mid = out_column.shape[0] // 2
        (out_x, out_y, out_c, gift_x_c, gift_y_c), (mixed, mixed_wide, logs) = stage(
            [(out_column, "x"), (out_column, "y"), (out_column, "c"), (gift_x, "c"), (gift_y, "c")],
            lambda *given: attend(given[0], given[1:], positions, size, base),
            [queries, *pairs],
        )
        (out_top, out_bottom, out_x_c, out_y_c), _ = stage(
            [(out_y[:mid], "x"), (out_x[mid:], "y"), (out_x, "c"), (out_y, "c")]
        )
        out_diag = jnp.concatenate([out_top, out_bottom], 0)
        (out_diag_c,), _ = stage([(out_diag, "c")])
        out_blocks = [out_column, out_x, out_c, out_x_c, out_y, out_diag, out_y_c, out_diag_c]
        resid = apply_rows(mixed, out_blocks, True, inputs)
        scale_two, unit_two = unit_of(resid)
        (unit_x, unit_y, unit_c), _ = stage([(unit_two, "x"), (unit_two, "y"), (unit_two, "c")])
        (unit_x_c, unit_y_c), _ = stage([(unit_x, "c"), (unit_y, "c")])
        unit_blocks = unit_two, unit_x, unit_c, unit_x_c, unit_y, unit_y_c
        return out_blocks[1:], mixed, mixed_wide, logs, resid, scale_two, unit_blocks, gift_x_c, gift_y_c

    qkv_column = after(qkv_column, mlp_column)
    qkv_blocks, queries, pairs, gifts, unit_one, scale_one = boxed(sure, project, qkv_column, tokens, gift)
    gift_x, gift_y, gift_c = gifts
    mlp_full += [gathered(k, pairs[0]) for k in range(1, parts)]
    out_blocks, mixed, mixed_wide, logs, resid, scale_two, unit_blocks, gift_x_c, gift_y_c = boxed(
        sure, forward, after(queries, mlp_full[0]), pairs, out_column, tokens, positions, gift_x, gift_y
    )
    qkv_blocks, out_blocks = [qkv_column, *qkv_blocks], [out_column, *out_blocks]
    grads_near = [(gift_y,), (gift,), (gift_y_c,), (gift_c,)]

    def flat(*tiles):
        return [piece for group in tiles for tile in group for piece in tile]

    def summed(keep, received):
        return keep.astype(f32) + received.astype(f32)

    def halves(value):
        middle = value.shape[0] // 2
        return value[:middle], value[middle:]

    def total(*values):
        return sum(value.astype(f32) for value in values)

    def opening(weights, blocks, gift_x, gift_x_c, grads_near, unit_one):
        unit_two, unit_x, unit_c, unit_x_c, unit_y, unit_y_c = blocks
        units_near = [(unit_y,), (unit_two,), (unit_y_c,), (unit_c,)]
        gift_y = grads_near[0][0]
        sends = [(unit_y, "x"), (gift_x, "y")]
        one_sends = [(unit_one, "x"), (unit_one, "y"), (unit_one, "c")]
        far_sums = near_sums = partial = ()
        if calls > 1:
            (unit_d, gift_d), near_sums = stage(
                sends, lambda *given: mlp([(v,) for v in given], grads_near, weights, ()), flat(units_near)
            )
        else:
            (unit_d, gift_d), _ = stage(sends)
        (unit_d_c, gift_d_c), _ = stage([(unit_d, "c"), (gift_d, "c")])
        units_far = [(unit_d,), (unit_x,), (unit_d_c,), (unit_x_c,)]
        grads_far = [(gift_d,), (gift_x,), (gift_d_c,), (gift_x_c,)]
        if calls > 1:
            (one_x, one_y, one_c), far_sums = stage(
                one_sends, lambda weights: mlp(units_far, grads_far, weights, ()), [weights]
            )
        else:
            (one_x, one_y, one_c), _ = stage(one_sends)
        one_sends = [(one_y, "x"), (one_x, "c"), (one_y, "c")]
        if calls > 1:
            (one_d, one_x_c, one_y_c), partial = stage(
                one_sends,
                lambda *given: mlp_grads(flat(units_far, units_near), flat(grads_far, grads_near), given)[0],
                [far_sums[4], near_sums[4]],
            )
        else:
            (one_d, one_x_c, one_y_c), _ = stage(one_sends)
        ones = one_x, one_c, one_x_c, one_y, one_d, one_y_c
        return (unit_d, unit_d_c), (gift_d, gift_d_c), far_sums[:4], near_sums[:4], partial, ones

    columns = []
    unit_two, unit_x, unit_c, unit_x_c, unit_y, unit_y_c = unit_blocks
    unit_far, gift_far, far_before, near_before, partial, ones = boxed(
        sure, opening, mlp_full[:per] if calls > 1 else (), unit_blocks, gift_x, gift_x_c, grads_near, unit_one
    )
    if calls > 1:
        columns.append(lax.psum_scatter(partial, "z", scatter_dimension=0, tiled=True))
    unit_d, unit_d_c = unit_far
    gift_d, gift_d_c = gift_far
    grads_far = [(gift_d,), (gift_x,), (gift_d_c,), (gift_x_c,)]
    units_far = [(unit_d,), (unit_x,), (unit_d_c,), (unit_x_c,)]
    units_near = [(unit_y,), (unit_two,), (unit_y_c,), (unit_c,)]

    def middle(weights, units_far, units_near, grads_far, grads_near, far_before, near_before, resid, scale_two, gift, ones):
        (one_d_c,), far_sums = stage(
            [(ones[4], "c")],
            lambda *weights: mlp(units_far, grads_far, weights, far_before),
            weights,
        )
        (found,), _ = stage([(far_sums[3], "c")])
        diag_top, diag_bottom, x_top, x_bottom = halved(far_sums[2], found)
        (diag_x, diag_y, x_top, far_out), near_sums = stage(
            [(diag_top, "x"), (diag_bottom, "y"), (x_top, "x"), (far_sums[1], "c")],
            lambda *given: mlp([(value,) for value in given], grads_near, weights, near_before),
            [tile[0] for tile in units_near],
        )
        (found,), _ = stage([(near_sums[3], "c")])
        y_bottom, x_bottom, y_top = turn(near_sums[2], found, x_bottom, diag_x, diag_y)
        (y_bottom, x_bottom, y_top, near_out), partial = stage(
            [(y_bottom, "y"), (x_bottom, "x"), (y_top, "y"), (near_sums[1], "c")],
            lambda *given: mlp_grads(flat(units_far, units_near), flat(grads_far, grads_near), given, cuts),
            [far_sums[4], near_sums[4]],
        )
        grad_resid, grad_attn = resid_grads(
            near_sums[2], found, x_top, x_bottom, y_top, y_bottom, resid, gift, scale_two
        )
        out_far = halved(far_sums[0], after(far_out, partial[0]))
        out_near = halved(near_sums[0], near_out)
        return partial, grad_resid, grad_attn, out_far, out_near, one_d_c

    cuts = (1, 1, 1)
    partial, grad_resid, grad_attn, out_far, out_near, one_d_c = boxed(
        sure,
        middle,
        mlp_full[-per:],
        units_far,
        units_near,
        grads_far,
        grads_near,
        far_before,
        near_before,
        resid,
        scale_two,
        gift,
        ones,
    )
    columns.append(lax.psum_scatter(partial[0], "z", scatter_dimension=0, tiled=True))
    one_x, one_c, one_x_c, one_y, one_d, one_y_c = ones
    flat_ones = [unit_one, one_x, one_c, one_x_c, one_y, one_d, one_y_c, one_d_c]

    def joined(own, first, second):
        top, bottom = own if isinstance(own, tuple) else halves(own)
        return jnp.concatenate([total(top, first[2], second[1]), total(bottom, second[0], first[3])], 0)

    def backward(grad_attn, out_far, out_near, queries, pairs, mixed_wide, logs, out_blocks, positions):
        def attention(grad_attn):
            grad_mixed = apply_rows(grad_attn, out_blocks)
            return attend_back(queries, grad_mixed, mixed_wide, logs, pairs, positions, size, base)

        first, (grad_queries, mine, theirs) = stage(
            [(out_far[0], "x"), (out_far[1], "y"), (out_far[2], "x"), (out_near[1], "y")], attention, [grad_attn]
        )
        (found,), _ = stage([(theirs, "c")])
        mine = summed(mine, found)
        second = total(out_far[3], first[1]).astype(low), total(out_near[0], first[0]).astype(low)
        found, second = stage(
            [(mine[chips - d].astype(low), behind(-d)) for d in range(chips, 0, -1)],
            lambda *given: given,
            second,
        )
        grad_pair = total(mine[chips], *found).astype(low)
        return jnp.concatenate([grad_queries, grad_pair], 1), first, second

    grad_qkv, first, second = boxed(
        sure, backward, after(grad_attn, *columns[:-1]), out_far, out_near, queries, pairs, mixed_wide, logs, out_blocks, positions
    )
    columns += [
        lax.psum_scatter(after(piece, grad_qkv), "z", scatter_dimension=0, tiled=True) for piece in partial[1:]
    ]

    def collect(grad_attn, grad_qkv, second, mixed, flat_ones):
        own, *others = spread(grad_qkv)
        found, (out_keep, out_send) = stage(
            [(value, across(r + 1)) for r, value in enumerate(others)],
            lambda *given: row_grads(*given),
            [grad_attn, mixed],
        )
        (found, *second), qkv_column = stage(
            [(out_send, "c"), (second[0], "x"), (second[1], "y")],
            lambda *gathered: token_grads(flat_ones, jnp.concatenate(gathered, 0)),
            [own, *found],
        )
        return qkv_column, out_keep, found, second

    qkv_column, out_keep, found, second = boxed(
        sure, collect, after(grad_attn, columns[-3]), grad_qkv, second, mixed, flat_ones
    )
    qkv_low = lax.psum_scatter(qkv_column, "z", scatter_dimension=0, tiled=True)

    def end(out_keep, found, first, second, grad_resid, grad_qkv, out_near, qkv_blocks, resid, scale_one, tokens):
        diag_top, diag_bottom, x_top, x_bottom, y_top, y_bottom, own = part_sums(out_keep, found)

        def results(grad_qkv, *second):
            inputs = tokens[0].astype(f32)
            output = resid + joined((out_near[2], out_near[3]), first, second)
            grad_unit_one = apply_rows(grad_qkv, qkv_blocks, True)
            return output, grad_resid + unit_back(grad_unit_one, inputs, scale_one)

        started, (output, grad_tokens) = stage(
            [(diag_top, "x"), (diag_bottom, "y"), (x_top, "x"), (y_bottom, "y")], results, [grad_qkv, *second]
        )
        x_bottom, y_top = total(x_bottom, started[1]).astype(low), total(y_top, started[0]).astype(low)
        second, _ = stage([(x_bottom, "x"), (y_top, "y")])
        column = joined(own, started, second).astype(low)
        return output, grad_tokens, column.reshape(-1, column.shape[-1])

    output, grad_tokens, out_column = boxed(
        sure,
        end,
        out_keep,
        found,
        first,
        second,
        after(grad_resid, columns[-2]),
        grad_qkv,
        out_near,
        qkv_blocks,
        resid,
        scale_one,
        tokens,
    )
    out_sum = lax.psum_scatter(out_column, "z", scatter_dimension=0, tiled=True).astype(f32)
    every = jnp.concatenate([*columns, qkv_low], 1)
    every = after(every, out_column).reshape(8, -1, every.shape[1])
    every = lax.all_to_all(every, PLANE, split_axis=0, concat_axis=0, tiled=True)
    deep = qkv_low.shape[1]
    qkv_sum = jnp.swapaxes(every[:, :, -deep:], 0, 1).reshape(-1, 8 * deep).astype(f32)
    query_sum = qkv_sum[:, :wide]
    key_sum = qkv_sum[:, wide : wide + size]
    value_sum = qkv_sum[:, wide + size :]
    grad_attn_gain = (
        jnp.sum(query_weight.astype(f32) * query_sum, axis=1)
        + jnp.sum(key_weight.astype(f32) * key_sum, axis=1)
        + jnp.sum(value_weight.astype(f32) * value_sum, axis=1)
    )
    grad_gate, grad_up, grad_down, grad_mlp_gain = finish(spans, part, per, gain_two, gate_weight, up_weight, every)
    return (
        output[None],
        grad_tokens[None],
        grad_attn_gain,
        query_sum * gain_one,
        key_sum * gain_one,
        value_sum * gain_one,
        out_sum.T,
        grad_mlp_gain[:, 0],
        grad_gate,
        grad_up,
        grad_down.T,
    )


def solution(mesh):
    ctx, fsdp = mesh.shape["ctx"], mesh.shape["fsdp"]
    fine = Mesh(mesh.devices.reshape(ctx // 4, 2, 2, fsdp), ("z", "y", "c", "x"))
    rows = ("z", "y", "c")
    every = ("z", "y", "c", "x")
    return jax.shard_map(
        local,
        mesh=fine,
        in_specs=(
            P("x", rows, None),
            P("x", rows),
            P(every),
            P(every, None),
            P(every, None),
            P(every, None),
            P(None, every),
            P(every),
            P(every, None),
            P(every, None),
            P(None, every),
            P("x", rows, None),
        ),
        out_specs=(
            P("x", rows, None),
            P("x", rows, None),
            P(every),
            P(every, None),
            P(every, None),
            P(every, None),
            P(None, every),
            P(every),
            P(every, None),
            P(every, None),
            P(None, every),
        ),
        check_vma=False,
    )
```

```python
import functools

import jax
import jax.numpy as jnp
from jax import lax
from jax.experimental import pallas as pl
from jax.experimental.pallas import tpu as pltpu
from jax.sharding import Mesh, PartitionSpec as P

WINDOW = 2048
SUB = 128
TILE = 512
epsilon = 1e-06
blocked_score = -1e30
PLANE = ("y", "c", "x")
low = jnp.bfloat16
f32 = jnp.float32
NOMINAL = pl.CostEstimate(flops=1 << 20, bytes_accessed=1 << 12, transcendentals=0)


def dot(left, right, contract, kind=f32):
    return lax.dot_general(
        left, right, ((contract[:1], contract[1:]), ((), ())), preferred_element_type=f32
    ).astype(kind)


def swap(value, axis):
    return lax.ppermute(value, axis, [(0, 1), (1, 0)])


def plane_gather(own, second=(), third=()):
    half = own.shape[0] // 2
    by_x = swap(own, "x")
    by_y = swap(own, "y")
    own_c = swap(own, "c")
    diag = (
        swap(after(by_y[:half], *second), "x"),
        swap(after(by_x[half:], *second), "y"),
    )
    by_x_c = swap(after(by_x, *second), "c")
    by_y_c = swap(after(by_y, *second), "c")
    diag_c = tuple(swap(after(part, *third), "c") for part in diag)
    return [own, by_x, own_c, by_x_c, by_y, diag, by_y_c, diag_c]


def joined_blocks(blocks):
    return [jnp.concatenate(block, 0) if isinstance(block, tuple) else block for block in blocks]


def stage(sends, work=None, given=()):
    fenced, given = lax.optimization_barrier((tuple(value for value, _ in sends), tuple(given)))
    received = tuple(
        swap(value, way) if isinstance(way, str) else way(value) for value, (_, way) in zip(fenced, sends)
    )
    return lax.optimization_barrier((received, work(*given) if work else given))


def boxed(sure, work, *given):
    shapes = jax.eval_shape(work, *given)
    return lax.cond(
        sure, work, lambda *_: jax.tree.map(lambda out: jnp.zeros(out.shape, out.dtype), shapes), *given
    )


def plane_index():
    return (lax.axis_index("y") * 2 + lax.axis_index("c")) * 2 + lax.axis_index("x")


def after(value, *earlier):
    return lax.optimization_barrier((value,) + earlier)[0]


def across(distance):
    return lambda value: lax.ppermute(value, PLANE, [(i, i ^ distance) for i in range(8)])


def behind(steps):
    count = lax.axis_size("z") * lax.axis_size("y")
    pairs = [(i, i + steps) for i in range(count) if 0 <= i + steps < count]
    return lambda value: lax.ppermute(value, ("z", "y"), pairs)


def two_heads(block, size):
    return jnp.concatenate([block[:, :size], block[:, size:]], 0)


def side_by_side(rows, size):
    half = rows.shape[0] // 2
    return jnp.concatenate([rows[:half], rows[half:]], 1)


def write_bias(bias, places, span, block):
    key = lax.broadcasted_iota(jnp.int32, (span, SUB), 0) - WINDOW
    query = lax.broadcasted_iota(jnp.int32, (span, SUB), 1)
    age = query - key
    seen = (age <= places) & (age >= 0) & (age < WINDOW)
    value = jnp.where(seen, 0.0, blocked_score).astype(f32)
    bias[:, :SUB] = value
    bias[:, SUB:] = value


def lay_window(core, blocks, window, turned, columns):
    count = blocks[0].shape[0]
    half = len(blocks) // 2
    for i in range(half):
        for which, block in ((core, blocks[i]), (1 - core, blocks[half + i])):
            at = pl.multiple_of((2 * i + which) * count, SUB)
            window[pl.ds(at, count), :] = block[...]
            turned[:, pl.ds(at, count)] = block[:, columns].T


def chunks(span, number):
    tiles = span // 128
    return [(128 * (tiles * i // number), 128 * (tiles * (i + 1) // number)) for i in range(number)]


def attend_kernel(size, scale, span, base, core, places, queries, *rest):
    blocks, (mixed, wide, logs, bias, window, turned) = rest[:-6], rest[-6:]
    block = pl.program_id(0)
    count = blocks[0].shape[0]
    start = pl.multiple_of(core[0] * count + base + block * SUB, SUB)

    @pl.when((block == 0) & (pl.program_id(1) == 0))
    def _():
        lay_window(core[0], blocks, window, turned, slice(size, 2 * size))

    @pl.when(pl.program_id(1) == 0)
    def _():
        write_bias(bias, places[...], span, block)

    query = two_heads(queries[...], size) * jnp.asarray(scale, low)
    highest = total = flat = None
    for at, end in chunks(span, 8):
        place = pl.ds(start + at, end - at)
        scores = dot(window[place, :size], query, (1, 1)) + bias[at:end]
        top = jnp.max(scores, axis=0, keepdims=True)
        if highest is not None:
            top = jnp.maximum(highest, top)
            fade = jnp.exp(highest - top)
        highest = top
        expo = jnp.exp(scores - highest)
        part = jnp.sum(expo, axis=0, keepdims=True)
        mix = dot(turned[:, place], expo.astype(low), (1, 0))
        total = part if total is None else total * fade + part
        flat = mix if flat is None else flat * fade + mix
    result = side_by_side((flat / total).T, size)
    wide[...] = result
    mixed[...] = result.astype(low)
    logs[0] = highest + jnp.log(total)


def attend_back_kernel(size, scale, span, base, core, places, queries, grads, wide, logs, *rest):
    blocks, (grad_queries, mine, theirs, bias, window, turned, total) = rest[:-7], rest[-7:]
    block = pl.program_id(0)
    count = blocks[0].shape[0]
    start = pl.multiple_of(core[0] * count + base + block * SUB, SUB)

    @pl.when((block == 0) & (pl.program_id(1) == 0))
    def _():
        lay_window(core[0], blocks, window, turned, slice(0, size))
        total[...] = jnp.zeros_like(total)

    @pl.when(pl.program_id(1) == 0)
    def _():
        write_bias(bias, places[...], span, block)

    query = two_heads(queries[...], size) * jnp.asarray(scale, low)
    grad = two_heads(grads[...], size)
    inner = jnp.sum((grad.astype(f32) * two_heads(wide[...], size)).T, axis=0, keepdims=True)
    place = pl.ds(start, span)
    keys, values = window[place, :size], window[place, size:]
    probs = jnp.exp(dot(keys, query, (1, 1)) + (bias[...] - logs[0]))
    grad_scores = (probs * (dot(values, grad, (1, 1)) - inner)).astype(low)
    total[place, size:] += dot(probs.astype(low), grad, (1, 0))
    total[place, :size] += dot(grad_scores, query, (1, 0))
    flat = dot(turned[:, place], grad_scores, (1, 0)) * scale
    grad_queries[...] = side_by_side(flat.T, size).astype(low)

    @pl.when((block == pl.num_programs(0) - 1) & (pl.program_id(1) == pl.num_programs(1) - 1))
    def _():
        for i in range(len(blocks) // 2):
            at = pl.multiple_of((2 * i + core[0]) * count, SUB)
            mine[i] = total[pl.ds(at, count), :]
            at = pl.multiple_of((2 * i + 1 - core[0]) * count, SUB)
            theirs[i] = total[pl.ds(at, count), :].astype(low)


def attend(queries, blocks, places, size, base):
    count, wide = queries.shape
    grid = (count // SUB, wide // (2 * size))
    span = WINDOW + SUB
    rows = len(blocks) * count
    core = lax.axis_index("c").astype(jnp.int32)[None]
    tile = pl.BlockSpec((SUB, 2 * size), lambda s, h, o: (s, h))
    return pl.pallas_call(
        functools.partial(attend_kernel, size, size**-0.5, span, base),
        out_shape=(
            jax.ShapeDtypeStruct((count, wide), low),
            jax.ShapeDtypeStruct((count, wide), f32),
            jax.ShapeDtypeStruct((grid[0] * grid[1], 1, 2 * SUB), f32),
        ),
        grid_spec=pltpu.PrefetchScalarGridSpec(
            num_scalar_prefetch=1,
            grid=grid,
            in_specs=[pl.BlockSpec((1, SUB), lambda s, h, o: (0, s)), tile]
            + [pl.BlockSpec(block.shape, lambda s, h, o: (0, 0)) for block in blocks],
            out_specs=[tile, tile, pl.BlockSpec((1, 1, 2 * SUB), lambda s, h, o: (s * grid[1] + h, 0, 0))],
            scratch_shapes=[
                pltpu.VMEM((span, 2 * SUB), f32),
                pltpu.VMEM((rows, 2 * size), low),
                pltpu.VMEM((size, rows), low),
            ],
        ),
        compiler_params=pltpu.CompilerParams(vmem_limit_bytes=56 << 20),
        cost_estimate=NOMINAL,
    )(core, places, queries, *blocks)


def attend_back(queries, grads, mixed, logs, blocks, places, size, base):
    count, wide = queries.shape
    grid = (count // SUB, wide // (2 * size))
    span = WINDOW + SUB
    rows = len(blocks) * count
    half = len(blocks) // 2
    core = lax.axis_index("c").astype(jnp.int32)[None]
    tile = pl.BlockSpec((SUB, 2 * size), lambda s, h, o: (s, h))
    whole = pl.BlockSpec((half, count, 2 * size), lambda s, h, o: (0, 0, 0))
    return pl.pallas_call(
        functools.partial(attend_back_kernel, size, size**-0.5, span, base),
        out_shape=(
            jax.ShapeDtypeStruct((count, wide), low),
            jax.ShapeDtypeStruct((half, count, 2 * size), f32),
            jax.ShapeDtypeStruct((half, count, 2 * size), low),
        ),
        grid_spec=pltpu.PrefetchScalarGridSpec(
            num_scalar_prefetch=1,
            grid=grid,
            in_specs=[
                pl.BlockSpec((1, SUB), lambda s, h, o: (0, s)),
                tile,
                tile,
                tile,
                pl.BlockSpec((1, 1, 2 * SUB), lambda s, h, o: (s * grid[1] + h, 0, 0)),
            ]
            + [pl.BlockSpec(block.shape, lambda s, h, o: (0, 0)) for block in blocks],
            out_specs=[tile, whole, whole],
            scratch_shapes=[
                pltpu.VMEM((span, 2 * SUB), f32),
                pltpu.VMEM((rows, 2 * size), low),
                pltpu.VMEM((size, rows), low),
                pltpu.VMEM((rows, 2 * size), f32),
            ],
        ),
        compiler_params=pltpu.CompilerParams(vmem_limit_bytes=60 << 20),
        cost_estimate=NOMINAL,
    )(core, places, queries, grads, mixed, logs, *blocks)


def lay_rows(slots, blocks, full):
    planes, rows, _ = blocks[0].shape
    for r in range(8):
        for plane in range(planes):
            at = pl.multiple_of((plane * 8 + slots[r]) * rows, 16)
            full[pl.ds(at, rows), :] = blocks[r][plane]


def apply_kernel(slots, left, *rest):
    blocks, (out, full) = rest[:8], rest[8:]
    lay_rows(slots, blocks, full)
    out[...] = dot(left[...], full[...], (1, 0), low)


def apply_turned_kernel(slots, left, *rest):
    *start, out, full = rest
    start, blocks = start[:-8], start[-8:]
    lay_rows(slots, blocks, full)

    @pl.when(pl.program_id(0) == 0)
    def _():
        out[...] = start[0][...] if start else jnp.zeros_like(out)

    out[...] += dot(left[...], full[...], (1, 1))


def whole_rows(blocks):
    planes, rows, wide = blocks[0].shape
    here = plane_index()
    whole = jnp.zeros((planes, 8, rows, wide), blocks[0].dtype)
    for r, block in enumerate(blocks):
        whole = lax.dynamic_update_slice(whole, block[:, None], (0, here ^ r, 0, 0))
    return whole.reshape(planes * 8 * rows, wide)


def apply_rows(left, blocks, turned=False, start=None):
    planes, rows, wide = blocks[0].shape
    if rows % 16 or wide % TILE:
        whole = whole_rows(blocks)
        if not turned:
            return dot(left, whole, (1, 0), low)
        return dot(left, whole, (1, 1)) + (0.0 if start is None else start)
    count, deep = left.shape[0], planes * 8 * rows
    slots = (plane_index() ^ jnp.arange(8)).astype(jnp.int32)
    pieces = [pl.BlockSpec((planes, rows, TILE), lambda n, s: (0, 0, n))] * 8
    whole = pl.BlockSpec((count, deep), lambda n, s: (0, 0))
    part = pl.BlockSpec((count, TILE), lambda n, s: (0, n))
    if not turned:
        kernel, given, specs, result = apply_kernel, [left], [whole], part
        shape = jax.ShapeDtypeStruct((count, wide), low)
    else:
        kernel, given, specs, result = apply_turned_kernel, [left], [part], whole
        if start is not None:
            given, specs = given + [start], specs + [whole]
        shape = jax.ShapeDtypeStruct((count, deep), f32)
    return pl.pallas_call(
        kernel,
        out_shape=shape,
        grid_spec=pltpu.PrefetchScalarGridSpec(
            num_scalar_prefetch=1,
            grid=(wide // TILE,),
            in_specs=specs + pieces,
            out_specs=result,
            scratch_shapes=[pltpu.VMEM((deep, TILE), low)],
        ),
        compiler_params=pltpu.CompilerParams(vmem_limit_bytes=48 << 20),
        cost_estimate=NOMINAL,
    )(slots, *given, *blocks)


def row_grads_kernel(slots, left, right, keep, send, turned):
    @pl.when(pl.program_id(1) == 0)
    def _():
        turned[...] = left[...].T

    rows = keep.shape[2]
    value = dot(turned[...], right[...], (1, 0), low)
    for i in range(8):
        place = slots[i]

        @pl.when(place < 4)
        def _():
            keep[place, 0] = value[i * rows : (i + 1) * rows]

        @pl.when(place >= 4)
        def _():
            send[place - 4, 0] = value[i * rows : (i + 1) * rows]


def row_grads(left, right):
    planes = lax.axis_size("z")
    count, deep = left.shape
    wide = right.shape[1]
    rows = deep // (planes * 8)
    places = jnp.array([3, 1, 7, 5, 2, 0, 6, 4], jnp.int32)
    slots = places[plane_index() ^ jnp.arange(8)]
    if rows % 16 or wide % TILE or (planes * 8 * rows) % (planes * 128):
        blocks = dot(left, right, (0, 0), low).reshape(planes, 8, rows, wide)
        order = jnp.argsort(slots)
        blocks = jnp.swapaxes(jnp.take(blocks, order, axis=1), 0, 1)
        return blocks[:4], blocks[4:]
    tile = wide if wide <= 5 * TILE else TILE
    group = pl.BlockSpec((4, 1, rows, tile), lambda z, n, s: (0, z, 0, n))
    shape = jax.ShapeDtypeStruct((4, planes, rows, wide), low)
    return pl.pallas_call(
        row_grads_kernel,
        out_shape=(shape, shape),
        grid_spec=pltpu.PrefetchScalarGridSpec(
            num_scalar_prefetch=1,
            grid=(planes, wide // tile),
            in_specs=[
                pl.BlockSpec((count, 8 * rows), lambda z, n, s: (0, z)),
                pl.BlockSpec((count, tile), lambda z, n, s: (0, n)),
            ],
            out_specs=[group, group],
            scratch_shapes=[pltpu.VMEM((8 * rows, count), low)],
        ),
        compiler_params=pltpu.CompilerParams(vmem_limit_bytes=48 << 20),
        cost_estimate=NOMINAL,
    )(slots, left, right)


def mlp_kernel(part, per, tiles, *rest):
    weights, rest = rest[:per], rest[per:]
    pieces = 2 * sum(tiles)
    sources, rest = rest[:pieces], rest[pieces:]
    before, rest = rest[:-8], rest[-8:]
    outs, grad_units, hidden, units, grads, arrived = rest[0:2], rest[2:4], *rest[4:]
    step = pl.program_id(0)

    def fetches(tile):
        first = 2 * sum(tiles[:tile])
        found = []
        for array, target in enumerate((units, grads)):
            at = 0
            for i in range(tiles[tile]):
                source = sources[first + array * tiles[tile] + i]
                found.append(
                    pltpu.make_async_copy(
                        source,
                        target.at[tile % 2, pl.ds(at, source.shape[0])],
                        arrived.at[tile % 2, array, i],
                    )
                )
                at += source.shape[0]
        return found

    for tile in range(len(tiles)):

        @pl.when(step == tile)
        def _():
            if tile == 0:
                for copy in fetches(0):
                    copy.start()
            if tile + 1 < len(tiles):
                for copy in fetches(tile + 1):
                    copy.start()
            for copy in fetches(tile):
                copy.wait()

    slope = 0.7978845608028654
    for j in range(per):
        both = dot(units[step % 2], weights[j][:, : 2 * part], (1, 0))
        gates, upward = both[:, :part], both[:, part:]
        grad_middle = dot(grads[step % 2], weights[j][:, 2 * part :], (1, 0))
        square = gates * gates
        half = 0.5 + 0.5 * jnp.tanh(gates * (slope + slope * 0.044715 * square))
        gelu = gates * half
        grad_gelu = half + gelu * (1.0 - half) * (2 * slope + 6 * slope * 0.044715 * square)
        at = 2 * part * j
        hidden[:, at : at + part] = (grad_middle * upward * grad_gelu).astype(low)
        hidden[:, at + part : at + 2 * part] = (grad_middle * gelu).astype(low)
        at = part * (2 * per + j)
        hidden[:, at : at + part] = (gelu * upward).astype(low)
    for which, targets in enumerate((outs, grad_units)):
        value = 0.0
        for j in range(per):
            at, width = (2 * part * j, 2 * part) if which else (part * (2 * per + j), part)
            first = 0 if which else 2 * part
            value = value + dot(hidden[:, at : at + width], weights[j][:, first : first + width], (1, 1))
        for side in range(2):

            @pl.when(step // (len(tiles) // 2) == side)
            def _():
                if before:
                    targets[side][...] = (value + before[2 * which + side][...].astype(f32)).astype(low)
                else:
                    targets[side][...] = value.astype(low)


def mlp(units, grads, weights, before):
    rows = sum(piece.shape[0] for piece in units[0])
    count, wide = rows * len(units), units[0][0].shape[1]
    per, each = len(weights), weights[0].shape[1]
    deep = per * each
    tiles = tuple(len(tile) for tile in units)
    sources = [piece for pair in zip(units, grads) for tile in pair for piece in tile]
    side = len(units) // 2
    sides = [
        pl.BlockSpec((rows, wide), lambda i: (jnp.minimum(i, side - 1), 0)),
        pl.BlockSpec((rows, wide), lambda i: (jnp.maximum(i - side, 0), 0)),
    ]
    half = jax.ShapeDtypeStruct((count // 2, wide), low)
    return pl.pallas_call(
        functools.partial(mlp_kernel, each // 3, per, tiles),
        out_shape=[half] * 4 + [jax.ShapeDtypeStruct((count, deep), low)],
        grid=(len(units),),
        in_specs=[pl.BlockSpec((wide, each), lambda i: (0, 0), pipeline_mode=pl.Buffered(1))] * per
        + [pl.BlockSpec(memory_space=pl.ANY)] * len(sources)
        + (sides * 2 if before else []),
        out_specs=sides * 2 + [pl.BlockSpec((rows, deep), lambda i: (i, 0))],
        scratch_shapes=[
            pltpu.VMEM((2, rows, wide), low),
            pltpu.VMEM((2, rows, wide), low),
            pltpu.SemaphoreType.DMA((2, 2, max(tiles))),
        ],
        compiler_params=pltpu.CompilerParams(vmem_limit_bytes=62 << 20),
        cost_estimate=NOMINAL,
    )(*weights, *sources, *before)


def mlp_grads_kernel(number, *rest):
    units, grads, hidden, rest = rest[:number], rest[number : 2 * number], rest[2 * number : 2 * number + 2], rest[2 * number + 2 :]
    *outs, turned = rest
    step = pl.program_id(0)
    part = hidden[0].shape[1] // 3
    piece = min(part, 256, *(out.shape[1] for out in outs))
    places = [(out, at) for out in outs for at in range(0, out.shape[1], piece)]

    def turn(slot, which, sources, share, shares):
        at = 0
        for i, source in enumerate(sources):
            if i * shares // len(sources) == share:
                turned[slot, which, :, at : at + source.shape[0]] = source[...].T
            at += source.shape[0]

    def multiply(slot, which, i, at):
        value, start = 0.0, 0
        for block in hidden:
            left = turned[slot, which, :, start : start + block.shape[0]]
            value = value + dot(left, block[:, at : at + piece], (1, 0))
            start += block.shape[0]
        out, place = places[i]
        out[:, place : place + piece] = value.astype(low)

    work = [(at // (2 * part), at) for at in range(0, 3 * part, piece)]

    @pl.when(step == 0)
    def _():
        turn(0, 0, units, 0, 1)
        turn(0, 1, grads, 0, 1)

    @pl.when(step > 0)
    def _():
        for i, (which, at) in enumerate(work):
            multiply((step - 1) % 2, which, i, at)
            turn(step % 2, 0, units, i, len(work))
            turn(step % 2, 1, grads, i, len(work))


def mlp_grads(units, grads, hidden, pieces=(6,)):
    wide = units[0].shape[1]
    deep = hidden[0].shape[1]
    count = sum(piece.shape[0] for piece in units)
    rows = 512
    last = wide // rows - 1
    return pl.pallas_call(
        functools.partial(mlp_grads_kernel, len(units)),
        out_shape=[jax.ShapeDtypeStruct((wide, deep // 6 * piece), low) for piece in pieces],
        grid=(last + 2,),
        in_specs=[
            pl.BlockSpec((piece.shape[0], rows), lambda s: (0, jnp.minimum(s, last))) for piece in units + grads
        ]
        + [pl.BlockSpec(piece.shape, lambda s: (0, 0), pipeline_mode=pl.Buffered(1)) for piece in hidden],
        out_specs=[
            pl.BlockSpec((rows, deep // 6 * piece), lambda s: (jnp.maximum(s - 1, 0), 0)) for piece in pieces
        ],
        scratch_shapes=[pltpu.VMEM((2, 2, rows, count), low)],
        compiler_params=pltpu.CompilerParams(vmem_limit_bytes=62 << 20),
        cost_estimate=NOMINAL,
    )(*units, *grads, *hidden)


def token_grads_kernel(number, *rest):
    units, (right, out, turned) = rest[:number], rest[number:]

    @pl.when(pl.program_id(0) == 0)
    def _():
        turned[...] = right[...].T

    value, at = 0.0, 0
    for unit in units:
        value = value + dot(turned[:, at : at + unit.shape[0]], unit[...], (1, 0))
        at += unit.shape[0]
    out[...] = value.astype(low).T


def token_grads(units, right):
    wide = units[0].shape[1]
    count, deep = right.shape
    rows = 512
    return pl.pallas_call(
        functools.partial(token_grads_kernel, len(units)),
        out_shape=jax.ShapeDtypeStruct((wide, deep), low),
        grid=(wide // rows,),
        in_specs=[pl.BlockSpec((piece.shape[0], rows), lambda s: (0, s)) for piece in units]
        + [pl.BlockSpec(right.shape, lambda s: (0, 0), pipeline_mode=pl.Buffered(1))],
        out_specs=pl.BlockSpec((rows, deep), lambda s: (s, 0)),
        scratch_shapes=[pltpu.VMEM((deep, count), low)],
        compiler_params=pltpu.CompilerParams(vmem_limit_bytes=56 << 20),
        cost_estimate=NOMINAL,
    )(*units, right)


def spread_kernel(slots, value, *outs):
    deep = outs[0].shape[1]
    for i, out in enumerate(outs):
        out[...] = value[:, pl.ds(pl.multiple_of(slots[i] * deep, 128), deep)]


def spread(value):
    count, wide = value.shape
    slots = (plane_index() ^ jnp.arange(8)).astype(jnp.int32)
    deep = wide // 8
    if deep % 128:
        return [lax.dynamic_slice(value, (0, slots[r] * deep), (count, deep)) for r in range(8)]
    return pl.pallas_call(
        spread_kernel,
        out_shape=[jax.ShapeDtypeStruct((count, deep), value.dtype)] * 8,
        grid_spec=pltpu.PrefetchScalarGridSpec(
            num_scalar_prefetch=1,
            grid=(1,),
            in_specs=[pl.BlockSpec((count, wide), lambda i, s: (0, 0))],
            out_specs=[pl.BlockSpec((count, deep), lambda i, s: (0, 0))] * 8,
        ),
        cost_estimate=NOMINAL,
    )(slots, value)


def turn_kernel(keep, found, far, diag_x, diag_y, y_bottom, x_bottom, y_top):
    half = far.shape[0]
    both = keep[...].astype(f32) + found[...].astype(f32)
    y_top[...] = (both[:half] + diag_x[...].astype(f32)).astype(low)
    y_bottom[...] = both[half:].astype(low)
    x_bottom[...] = (far[...].astype(f32) + diag_y[...].astype(f32)).astype(low)


def turn(keep, found, far, diag_x, diag_y):
    half, wide = far.shape
    part = lambda rows: pl.BlockSpec((rows, TILE), lambda n: (0, n))
    return pl.pallas_call(
        turn_kernel,
        out_shape=[jax.ShapeDtypeStruct((half, wide), low)] * 3,
        grid=(wide // TILE,),
        in_specs=[part(2 * half)] * 2 + [part(half)] * 3,
        out_specs=[part(half)] * 3,
        cost_estimate=NOMINAL,
    )(keep, found, far, diag_x, diag_y)


def halved_kernel(keep, found, *outs):
    half = outs[0].shape[0]
    for i, out in enumerate(outs):
        rows = slice(i * half, i * half + half)
        out[...] = (keep[rows].astype(f32) + found[rows].astype(f32)).astype(low)


def halved(keep, found):
    count, wide = keep.shape
    part = lambda rows: pl.BlockSpec((rows, TILE), lambda n: (0, n))
    return pl.pallas_call(
        halved_kernel,
        out_shape=[jax.ShapeDtypeStruct((count // 4, wide), low)] * 4,
        grid=(wide // TILE,),
        in_specs=[part(count)] * 2,
        out_specs=[part(count // 4)] * 4,
        cost_estimate=NOMINAL,
    )(keep, found)


def resid_kernel(steps, keep, found, x_top, x_bottom, y_top, y_bottom, resid, gift, scale, grad_out, grad_low):
    upper = pl.program_id(0) < steps
    x_part = jnp.where(upper, x_top[...].astype(f32), x_bottom[...].astype(f32))
    y_part = jnp.where(upper, y_top[...].astype(f32), y_bottom[...].astype(f32))
    grad = keep[...].astype(f32) + found[...].astype(f32) + x_part + y_part
    grad = gift[...].astype(f32) + unit_back(grad, resid[...], scale[...])
    grad_out[...] = grad
    grad_low[...] = grad.astype(low)


def resid_grads(keep, found, x_top, x_bottom, y_top, y_bottom, resid, gift, scale):
    count, wide = resid.shape
    rows = 96
    steps = count // (2 * rows)
    row = pl.BlockSpec((rows, wide), lambda i: (i, 0))
    own = pl.BlockSpec((rows, wide), lambda i: (i + 2 * steps, 0))
    first = pl.BlockSpec((rows, wide), lambda i: (jnp.minimum(i, steps - 1), 0))
    last = pl.BlockSpec((rows, wide), lambda i: (jnp.maximum(i - steps, 0), 0))
    return pl.pallas_call(
        functools.partial(resid_kernel, steps),
        out_shape=(jax.ShapeDtypeStruct((count, wide), f32), jax.ShapeDtypeStruct((count, wide), low)),
        grid=(2 * steps,),
        in_specs=[own, own, first, last, first, last, row, row, pl.BlockSpec((rows, 1), lambda i: (i, 0))],
        out_specs=(row, row),
        cost_estimate=NOMINAL,
    )(keep, found, x_top, x_bottom, y_top, y_bottom, resid, gift, scale)


def part_sums_kernel(keep, found, diag_top, diag_bottom, x_top, x_bottom, y_top, y_bottom, own):
    half = diag_top.shape[0]

    def both(place, first, rows):
        part = slice(first, first + rows)
        return (keep[place, part].astype(f32) + found[place, part].astype(f32)).astype(low)

    for place, (top, bottom) in enumerate(((diag_top, diag_bottom), (x_top, x_bottom), (y_top, y_bottom))):
        top[...] = both(place, 0, half)
        bottom[...] = both(place, half, half)
    own[...] = both(3, 0, 2 * half)


def part_sums(keep, found):
    _, planes, rows, wide = keep.shape
    four = pl.BlockSpec((4, planes, rows, TILE), lambda n: (0, 0, 0, n))
    some = lambda planes: pl.BlockSpec((planes, rows, TILE), lambda n: (0, 0, n))
    half = planes // 2
    shape = lambda planes: jax.ShapeDtypeStruct((planes, rows, wide), low)
    return pl.pallas_call(
        part_sums_kernel,
        out_shape=[shape(half)] * 6 + [shape(planes)],
        grid=(wide // TILE,),
        in_specs=[four] * 2,
        out_specs=[some(half)] * 6 + [some(planes)],
        compiler_params=pltpu.CompilerParams(vmem_limit_bytes=48 << 20),
        cost_estimate=NOMINAL,
    )(keep, found)


def pack_kernel(spans, part, gain, gate, up, down, out):
    scale = gain[...]
    share = out.shape[2] // 3
    for p, (at, n) in enumerate(spans):
        for q in range(share // part):
            width = min(part, n - q * part)
            place = slice(at + q * part, at + q * part + width)
            for which, source in enumerate((gate, up, down)):
                first = part * (3 * q + which)
                if width > 0:
                    value = source[:, place]
                    if which < 2:
                        value = (value.astype(f32) * scale).astype(low)
                    out[p, :, first : first + width] = value
                if width < part:
                    empty = max(width, 0)
                    out[p, :, first + empty : first + part] = jnp.zeros((out.shape[1], part - empty), low)


def pack(spans, part, share, gain, gate, up, down):
    rows, _ = gate.shape
    return pl.pallas_call(
        functools.partial(pack_kernel, spans, part),
        out_shape=jax.ShapeDtypeStruct((8, rows, 3 * share), low),
        compiler_params=pltpu.CompilerParams(vmem_limit_bytes=48 << 20),
        cost_estimate=NOMINAL,
    )(gain, gate, up, down)


def shares(columns):
    tiles = -(-columns // 128)
    few, more = divmod(tiles, 8)
    sizes = [128 * (few + (p < more)) for p in range(8)]
    return [(sum(sizes[:p]), size) for p, size in enumerate(sizes)], 128 * (few + (more > 0))


def finish_kernel(spans, part, per, gain, gate, up, whole, gate_out, up_out, down_out, gain_out):
    scale = gain[...]
    total = jnp.zeros_like(scale)
    for p, (at, n) in enumerate(spans):
        for q in range(-(-n // part)):
            width = min(part, n - q * part)
            start, j = 3 * part * per * (q // per), q % per
            place = slice(at + q * part, at + q * part + width)
            for which, (weight, out) in enumerate(((gate, gate_out), (up, up_out))):
                first = start + part * (2 * j + which)
                value = whole[p, :, first : first + width].astype(f32)
                total = total + jnp.sum(value * weight[:, place].astype(f32), axis=1, keepdims=True)
                out[:, place] = value * scale
            first = start + part * (2 * per + j)
            down_out[:, place] = whole[p, :, first : first + width].astype(f32)
    gain_out[...] = total


def finish(spans, part, per, gain, gate, up, whole):
    rows, columns = gate.shape
    return pl.pallas_call(
        functools.partial(finish_kernel, spans, part, per),
        out_shape=(
            jax.ShapeDtypeStruct((rows, columns), f32),
            jax.ShapeDtypeStruct((rows, columns), f32),
            jax.ShapeDtypeStruct((rows, columns), f32),
            jax.ShapeDtypeStruct((rows, 1), f32),
        ),
        compiler_params=pltpu.CompilerParams(vmem_limit_bytes=48 << 20),
        cost_estimate=NOMINAL,
    )(gain, gate, up, whole)


def unit_of(values):
    scale = lax.rsqrt(jnp.mean(values * values, axis=-1, keepdims=True) + epsilon)
    return scale, (values * scale).astype(low)


def unit_back(grad, values, scale):
    unit = values * scale
    return scale * (grad - unit * jnp.mean(grad * unit, axis=-1, keepdims=True))


def local(
    tokens,
    positions,
    attn_gain,
    query_weight,
    key_weight,
    value_weight,
    out_weight,
    mlp_gain,
    gate_weight,
    up_weight,
    down_weight,
    cotangent,
):
    count = tokens.shape[1]
    size = key_weight.shape[1]
    wide = query_weight.shape[1]
    reach = (WINDOW + count - 2) // count
    chips = (reach + 1) // 2
    base = 2 * chips * count - WINDOW
    gain_one = attn_gain[:, None]
    gain_two = mlp_gain[:, None]

    qkv_shard = jnp.concatenate([query_weight, key_weight, value_weight], 1).astype(f32) * gain_one
    qkv_shard = qkv_shard.astype(low)
    qkv_column = lax.all_gather(qkv_shard, "z", axis=0, tiled=False)
    out_column = lax.all_gather(after(out_weight.T, qkv_shard), "z", axis=0, tiled=False)

    spans, share = shares(gate_weight.shape[1])
    parts = share // 256 if share % 256 == 0 else 1
    calls = 2 if parts % 2 == 0 else 1
    per = parts // calls
    part = share // parts
    mine = pack(spans, part, share, after(gain_two, qkv_shard), gate_weight, up_weight, down_weight.T)
    gift = cotangent[0]
    mlp_column = lax.all_to_all(mine, PLANE, split_axis=0, concat_axis=0, tiled=True)
    mlp_column = mlp_column.reshape(-1, 3 * share)

    def gathered(k, *earlier):
        piece = after(mlp_column[:, k * 3 * part : (k + 1) * 3 * part], *earlier)
        return lax.all_gather(piece, "z", axis=0, tiled=True)

    mlp_full = [gathered(0)]
    sure = positions[0, 0] >= 0
    half = count // 2

    def project(qkv_column, tokens, gift):
        qkv_blocks = joined_blocks(plane_gather(qkv_column))
        scale_one, unit_one = unit_of(tokens[0].astype(f32))
        qkv = apply_rows(unit_one, qkv_blocks)
        queries, pair = qkv[:, :wide], qkv[:, wide:]
        moves = [behind(d) for d in range(chips, 0, -1)]
        found, _ = stage([(pair, move) for move in moves] + [(pair, "c"), (gift, "x"), (gift, "y"), (gift, "c")])
        *pairs, pair_c, gift_x, gift_y, gift_c = found
        found, _ = stage([(block, "c") for block in pairs])
        gifts = gift_x, gift_y, gift_c
        return qkv_blocks[1:], queries, [*pairs, pair, *found, pair_c], gifts, unit_one, scale_one

    def forward(queries, pairs, out_column, tokens, positions, gift_x, gift_y):
        inputs = tokens[0].astype(f32)
        mid = out_column.shape[0] // 2
        (out_x, out_y, out_c, gift_x_c, gift_y_c), (mixed, mixed_wide, logs) = stage(
            [(out_column, "x"), (out_column, "y"), (out_column, "c"), (gift_x, "c"), (gift_y, "c")],
            lambda *given: attend(given[0], given[1:], positions, size, base),
            [queries, *pairs],
        )
        (out_top, out_bottom, out_x_c, out_y_c), _ = stage(
            [(out_y[:mid], "x"), (out_x[mid:], "y"), (out_x, "c"), (out_y, "c")]
        )
        out_diag = jnp.concatenate([out_top, out_bottom], 0)
        (out_diag_c,), _ = stage([(out_diag, "c")])
        out_blocks = [out_column, out_x, out_c, out_x_c, out_y, out_diag, out_y_c, out_diag_c]
        resid = apply_rows(mixed, out_blocks, True, inputs)
        scale_two, unit_two = unit_of(resid)
        (unit_x, unit_y, unit_c), _ = stage([(unit_two, "x"), (unit_two, "y"), (unit_two, "c")])
        (unit_x_c, unit_y_c), _ = stage([(unit_x, "c"), (unit_y, "c")])
        unit_blocks = unit_two, unit_x, unit_c, unit_x_c, unit_y, unit_y_c
        return out_blocks[1:], mixed, mixed_wide, logs, resid, scale_two, unit_blocks, gift_x_c, gift_y_c

    qkv_column = after(qkv_column, mlp_column)
    qkv_blocks, queries, pairs, gifts, unit_one, scale_one = boxed(sure, project, qkv_column, tokens, gift)
    gift_x, gift_y, gift_c = gifts
    mlp_full += [gathered(k, pairs[0]) for k in range(1, parts)]
    out_blocks, mixed, mixed_wide, logs, resid, scale_two, unit_blocks, gift_x_c, gift_y_c = boxed(
        sure, forward, after(queries, mlp_full[0]), pairs, out_column, tokens, positions, gift_x, gift_y
    )
    qkv_blocks, out_blocks = [qkv_column, *qkv_blocks], [out_column, *out_blocks]
    grads_near = [(gift_y,), (gift,), (gift_y_c,), (gift_c,)]

    def flat(*tiles):
        return [piece for group in tiles for tile in group for piece in tile]

    def summed(keep, received):
        return keep.astype(f32) + received.astype(f32)

    def halves(value):
        middle = value.shape[0] // 2
        return value[:middle], value[middle:]

    def total(*values):
        return sum(value.astype(f32) for value in values)

    def opening(weights, blocks, gift_x, gift_x_c, grads_near, unit_one):
        unit_two, unit_x, unit_c, unit_x_c, unit_y, unit_y_c = blocks
        units_near = [(unit_y,), (unit_two,), (unit_y_c,), (unit_c,)]
        gift_y = grads_near[0][0]
        sends = [(unit_y, "x"), (gift_x, "y")]
        one_sends = [(unit_one, "x"), (unit_one, "y"), (unit_one, "c")]
        far_sums = near_sums = partial = ()
        if calls > 1:
            (unit_d, gift_d), near_sums = stage(
                sends, lambda *given: mlp([(v,) for v in given], grads_near, weights, ()), flat(units_near)
            )
        else:
            (unit_d, gift_d), _ = stage(sends)
        (unit_d_c, gift_d_c), _ = stage([(unit_d, "c"), (gift_d, "c")])
        units_far = [(unit_d,), (unit_x,), (unit_d_c,), (unit_x_c,)]
        grads_far = [(gift_d,), (gift_x,), (gift_d_c,), (gift_x_c,)]
        if calls > 1:
            (one_x, one_y, one_c), far_sums = stage(
                one_sends, lambda weights: mlp(units_far, grads_far, weights, ()), [weights]
            )
        else:
            (one_x, one_y, one_c), _ = stage(one_sends)
        one_sends = [(one_y, "x"), (one_x, "c"), (one_y, "c")]
        if calls > 1:
            (one_d, one_x_c, one_y_c), partial = stage(
                one_sends,
                lambda *given: mlp_grads(flat(units_far, units_near), flat(grads_far, grads_near), given)[0],
                [far_sums[4], near_sums[4]],
            )
        else:
            (one_d, one_x_c, one_y_c), _ = stage(one_sends)
        ones = one_x, one_c, one_x_c, one_y, one_d, one_y_c
        return (unit_d, unit_d_c), (gift_d, gift_d_c), far_sums[:4], near_sums[:4], partial, ones

    columns = []
    unit_two, unit_x, unit_c, unit_x_c, unit_y, unit_y_c = unit_blocks
    unit_far, gift_far, far_before, near_before, partial, ones = boxed(
        sure, opening, mlp_full[:per] if calls > 1 else (), unit_blocks, gift_x, gift_x_c, grads_near, unit_one
    )
    if calls > 1:
        columns.append(lax.psum_scatter(partial, "z", scatter_dimension=0, tiled=True))
    unit_d, unit_d_c = unit_far
    gift_d, gift_d_c = gift_far
    grads_far = [(gift_d,), (gift_x,), (gift_d_c,), (gift_x_c,)]
    units_far = [(unit_d,), (unit_x,), (unit_d_c,), (unit_x_c,)]
    units_near = [(unit_y,), (unit_two,), (unit_y_c,), (unit_c,)]

    def middle(weights, units_far, units_near, grads_far, grads_near, far_before, near_before, resid, scale_two, gift, ones):
        (one_d_c,), far_sums = stage(
            [(ones[4], "c")],
            lambda *weights: mlp(units_far, grads_far, weights, far_before),
            weights,
        )
        (found,), _ = stage([(far_sums[3], "c")])
        diag_top, diag_bottom, x_top, x_bottom = halved(far_sums[2], found)
        (diag_x, diag_y, x_top, far_out), near_sums = stage(
            [(diag_top, "x"), (diag_bottom, "y"), (x_top, "x"), (far_sums[1], "c")],
            lambda *given: mlp([(value,) for value in given], grads_near, weights, near_before),
            [tile[0] for tile in units_near],
        )
        (found,), _ = stage([(near_sums[3], "c")])
        y_bottom, x_bottom, y_top = turn(near_sums[2], found, x_bottom, diag_x, diag_y)
        (y_bottom, x_bottom, y_top, near_out), partial = stage(
            [(y_bottom, "y"), (x_bottom, "x"), (y_top, "y"), (near_sums[1], "c")],
            lambda *given: mlp_grads(flat(units_far, units_near), flat(grads_far, grads_near), given, cuts),
            [far_sums[4], near_sums[4]],
        )
        received = x_top, x_bottom, y_top, y_bottom
        return partial, near_sums[2], found, received, far_sums[0], far_out, near_sums[0], near_out, one_d_c

    def rest(keep, found, received, resid, gift, scale_two, far, far_out, near, near_out):
        grad_resid, grad_attn = resid_grads(keep, found, *received, resid, gift, scale_two)
        return grad_resid, grad_attn, halved(far, far_out), halved(near, near_out)

    cuts = (1, 2, 2, 1)
    partial, keep, found, received, *outs, one_d_c = boxed(
        sure,
        middle,
        mlp_full[-per:],
        units_far,
        units_near,
        grads_far,
        grads_near,
        far_before,
        near_before,
        resid,
        scale_two,
        gift,
        ones,
    )
    columns += [lax.psum_scatter(piece, "z", scatter_dimension=0, tiled=True) for piece in partial[:2]]
    grad_resid, grad_attn, out_far, out_near = boxed(
        sure, rest, after(keep, *columns[:-2]), found, received, resid, gift, scale_two, *outs
    )
    one_x, one_c, one_x_c, one_y, one_d, one_y_c = ones
    flat_ones = [unit_one, one_x, one_c, one_x_c, one_y, one_d, one_y_c, one_d_c]

    def joined(own, first, second):
        top, bottom = own if isinstance(own, tuple) else halves(own)
        return jnp.concatenate([total(top, first[2], second[1]), total(bottom, second[0], first[3])], 0)

    def backward(grad_attn, out_far, out_near, queries, pairs, mixed, mixed_wide, logs, out_blocks, positions):
        def attention(grad_attn):
            grad_mixed = apply_rows(grad_attn, out_blocks)
            return attend_back(queries, grad_mixed, mixed_wide, logs, pairs, positions, size, base)

        def out_sums(grad_attn, mixed, *given):
            keep, send = row_grads(grad_attn, mixed)
            return part_sums(keep, swap(send, "c")), given

        first, (grad_queries, mine, theirs) = stage(
            [(out_far[0], "x"), (out_far[1], "y"), (out_far[2], "x"), (out_near[1], "y")], attention, [grad_attn]
        )
        (found,), _ = stage([(theirs, "c")])
        mine = summed(mine, found)
        second = total(out_far[3], first[1]).astype(low), total(out_near[0], first[0]).astype(low)
        found, (sums, second) = stage(
            [(mine[chips - d].astype(low), behind(-d)) for d in range(chips, 0, -1)],
            out_sums,
            [grad_attn, mixed, *second],
        )
        grad_pair = total(mine[chips], *found).astype(low)
        return jnp.concatenate([grad_queries, grad_pair], 1), first, second, sums

    grad_qkv, first, second, sums = boxed(
        sure,
        backward,
        after(grad_attn, columns[-2]),
        out_far,
        out_near,
        queries,
        pairs,
        mixed,
        mixed_wide,
        logs,
        out_blocks,
        positions,
    )
    columns += [
        lax.psum_scatter(after(piece, grad_qkv), "z", scatter_dimension=0, tiled=True) for piece in partial[2:]
    ]

    def collect(grad_qkv, second, sums, grad_resid, qkv_blocks, flat_ones, scale_one, tokens):
        diag_top, diag_bottom, x_top, _, _, y_bottom, _ = sums
        own, *others = spread(grad_qkv)

        def results(grad_qkv):
            grad_unit_one = apply_rows(grad_qkv, qkv_blocks, True)
            return grad_resid + unit_back(grad_unit_one, tokens[0].astype(f32), scale_one)

        found, grad_tokens = stage(
            [(value, across(r + 1)) for r, value in enumerate(others)], results, [grad_qkv]
        )
        (*started, x_second, y_second), qkv_column = stage(
            [
                (diag_top, "x"),
                (diag_bottom, "y"),
                (x_top, "x"),
                (y_bottom, "y"),
                (second[0], "x"),
                (second[1], "y"),
            ],
            lambda *gathered: token_grads(flat_ones, jnp.concatenate(gathered, 0)),
            [own, *found],
        )
        return qkv_column, grad_tokens, started, (x_second, y_second)

    qkv_column, grad_tokens, started, second = boxed(
        sure,
        collect,
        after(grad_qkv, columns[2]),
        second,
        sums,
        grad_resid,
        qkv_blocks,
        flat_ones,
        scale_one,
        tokens,
    )
    qkv_low = lax.psum_scatter(qkv_column, "z", scatter_dimension=0, tiled=True)

    def end(sums, started, first, second, out_near, resid):
        _, _, _, x_bottom, y_top, _, own = sums
        x_bottom, y_top = total(x_bottom, started[1]).astype(low), total(y_top, started[0]).astype(low)
        received, output = stage(
            [(x_bottom, "x"), (y_top, "y")],
            lambda resid: resid + joined((out_near[2], out_near[3]), first, second),
            [resid],
        )
        column = joined(own, started, received).astype(low)
        return output, column.reshape(-1, column.shape[-1])

    output, out_column = boxed(sure, end, sums, started, first, second, out_near, after(resid, *columns[3:]))
    out_sum = lax.psum_scatter(out_column, "z", scatter_dimension=0, tiled=True).astype(f32)
    every = jnp.concatenate([*columns, qkv_low], 1)
    every = after(every, out_column).reshape(8, -1, every.shape[1])
    every = lax.all_to_all(every, PLANE, split_axis=0, concat_axis=0, tiled=True)
    deep = qkv_low.shape[1]
    qkv_sum = jnp.swapaxes(every[:, :, -deep:], 0, 1).reshape(-1, 8 * deep).astype(f32)
    query_sum = qkv_sum[:, :wide]
    key_sum = qkv_sum[:, wide : wide + size]
    value_sum = qkv_sum[:, wide + size :]
    grad_attn_gain = (
        jnp.sum(query_weight.astype(f32) * query_sum, axis=1)
        + jnp.sum(key_weight.astype(f32) * key_sum, axis=1)
        + jnp.sum(value_weight.astype(f32) * value_sum, axis=1)
    )
    grad_gate, grad_up, grad_down, grad_mlp_gain = finish(spans, part, per, gain_two, gate_weight, up_weight, every)
    return (
        output[None],
        grad_tokens[None],
        grad_attn_gain,
        query_sum * gain_one,
        key_sum * gain_one,
        value_sum * gain_one,
        out_sum.T,
        grad_mlp_gain[:, 0],
        grad_gate,
        grad_up,
        grad_down.T,
    )


def solution(mesh):
    ctx, fsdp = mesh.shape["ctx"], mesh.shape["fsdp"]
    fine = Mesh(mesh.devices.reshape(ctx // 4, 2, 2, fsdp), ("z", "y", "c", "x"))
    rows = ("z", "y", "c")
    every = ("z", "y", "c", "x")
    return jax.shard_map(
        local,
        mesh=fine,
        in_specs=(
            P("x", rows, None),
            P("x", rows),
            P(every),
            P(every, None),
            P(every, None),
            P(every, None),
            P(None, every),
            P(every),
            P(every, None),
            P(every, None),
            P(None, every),
            P("x", rows, None),
        ),
        out_specs=(
            P("x", rows, None),
            P("x", rows, None),
            P(every),
            P(every, None),
            P(every, None),
            P(every, None),
            P(None, every),
            P(every),
            P(every, None),
            P(every, None),
            P(None, every),
        ),
        check_vma=False,
    )
```

```python
import functools

import jax
import jax.numpy as jnp
from jax import lax
from jax.experimental import pallas as pl
from jax.experimental.pallas import tpu as pltpu
from jax.sharding import Mesh, PartitionSpec as P

WINDOW = 2048
SUB = 128
TILE = 512
epsilon = 1e-06
blocked_score = -1e30
PLANE = ("y", "c", "x")
low = jnp.bfloat16
f32 = jnp.float32
NOMINAL = pl.CostEstimate(flops=1 << 20, bytes_accessed=1 << 12, transcendentals=0)


def dot(left, right, contract, kind=f32):
    return lax.dot_general(
        left, right, ((contract[:1], contract[1:]), ((), ())), preferred_element_type=f32
    ).astype(kind)


def swap(value, axis):
    return lax.ppermute(value, axis, [(0, 1), (1, 0)])


def plane_gather(own, second=(), third=()):
    half = own.shape[0] // 2
    by_x = swap(own, "x")
    by_y = swap(own, "y")
    own_c = swap(own, "c")
    diag = (
        swap(after(by_y[:half], *second), "x"),
        swap(after(by_x[half:], *second), "y"),
    )
    by_x_c = swap(after(by_x, *second), "c")
    by_y_c = swap(after(by_y, *second), "c")
    diag_c = tuple(swap(after(part, *third), "c") for part in diag)
    return [own, by_x, own_c, by_x_c, by_y, diag, by_y_c, diag_c]


def joined_blocks(blocks):
    return [jnp.concatenate(block, 0) if isinstance(block, tuple) else block for block in blocks]


def stage(sends, work=None, given=()):
    fenced, given = lax.optimization_barrier((tuple(value for value, _ in sends), tuple(given)))
    received = tuple(
        swap(value, way) if isinstance(way, str) else way(value) for value, (_, way) in zip(fenced, sends)
    )
    return lax.optimization_barrier((received, work(*given) if work else given))


def boxed(sure, work, *given):
    shapes = jax.eval_shape(work, *given)
    return lax.cond(
        sure, work, lambda *_: jax.tree.map(lambda out: jnp.zeros(out.shape, out.dtype), shapes), *given
    )


def plane_index():
    return (lax.axis_index("y") * 2 + lax.axis_index("c")) * 2 + lax.axis_index("x")


def after(value, *earlier):
    return lax.optimization_barrier((value,) + earlier)[0]


def across(distance):
    return lambda value: lax.ppermute(value, PLANE, [(i, i ^ distance) for i in range(8)])


def behind(steps):
    count = lax.axis_size("z") * lax.axis_size("y")
    pairs = [(i, i + steps) for i in range(count) if 0 <= i + steps < count]
    return lambda value: lax.ppermute(value, ("z", "y"), pairs)


def two_heads(block, size):
    return jnp.concatenate([block[:, :size], block[:, size:]], 0)


def side_by_side(rows, size):
    half = rows.shape[0] // 2
    return jnp.concatenate([rows[:half], rows[half:]], 1)


def write_bias(bias, places, span, block):
    key = lax.broadcasted_iota(jnp.int32, (span, SUB), 0) - WINDOW
    query = lax.broadcasted_iota(jnp.int32, (span, SUB), 1)
    age = query - key
    seen = (age <= places) & (age >= 0) & (age < WINDOW)
    value = jnp.where(seen, 0.0, blocked_score).astype(f32)
    bias[:, :SUB] = value
    bias[:, SUB:] = value


def lay_window(core, blocks, window, turned, columns):
    count = blocks[0].shape[0]
    half = len(blocks) // 2
    for i in range(half):
        for which, block in ((core, blocks[i]), (1 - core, blocks[half + i])):
            at = pl.multiple_of((2 * i + which) * count, SUB)
            window[pl.ds(at, count), :] = block[...]
            turned[:, pl.ds(at, count)] = block[:, columns].T


def chunks(span, number):
    tiles = span // 128
    return [(128 * (tiles * i // number), 128 * (tiles * (i + 1) // number)) for i in range(number)]


def attend_kernel(size, scale, span, base, core, places, queries, *rest):
    blocks, (mixed, wide, logs, bias, window, turned) = rest[:-6], rest[-6:]
    block = pl.program_id(0)
    count = blocks[0].shape[0]
    start = pl.multiple_of(core[0] * count + base + block * SUB, SUB)

    @pl.when((block == 0) & (pl.program_id(1) == 0))
    def _():
        lay_window(core[0], blocks, window, turned, slice(size, 2 * size))

    @pl.when(pl.program_id(1) == 0)
    def _():
        write_bias(bias, places[...], span, block)

    query = two_heads(queries[...], size) * jnp.asarray(scale, low)
    highest = total = flat = None
    for at, end in chunks(span, 8):
        place = pl.ds(start + at, end - at)
        scores = dot(window[place, :size], query, (1, 1)) + bias[at:end]
        top = jnp.max(scores, axis=0, keepdims=True)
        if highest is not None:
            top = jnp.maximum(highest, top)
            fade = jnp.exp(highest - top)
        highest = top
        expo = jnp.exp(scores - highest)
        part = jnp.sum(expo, axis=0, keepdims=True)
        mix = dot(turned[:, place], expo.astype(low), (1, 0))
        total = part if total is None else total * fade + part
        flat = mix if flat is None else flat * fade + mix
    result = side_by_side((flat / total).T, size)
    wide[...] = result
    mixed[...] = result.astype(low)
    logs[0] = highest + jnp.log(total)


def attend_back_kernel(size, scale, span, base, core, places, queries, grads, wide, logs, *rest):
    blocks, (grad_queries, mine, theirs, bias, window, turned, total) = rest[:-7], rest[-7:]
    block = pl.program_id(0)
    count = blocks[0].shape[0]
    start = pl.multiple_of(core[0] * count + base + block * SUB, SUB)

    @pl.when((block == 0) & (pl.program_id(1) == 0))
    def _():
        lay_window(core[0], blocks, window, turned, slice(0, size))
        total[...] = jnp.zeros_like(total)

    @pl.when(pl.program_id(1) == 0)
    def _():
        write_bias(bias, places[...], span, block)

    query = two_heads(queries[...], size) * jnp.asarray(scale, low)
    grad = two_heads(grads[...], size)
    inner = jnp.sum((grad.astype(f32) * two_heads(wide[...], size)).T, axis=0, keepdims=True)
    place = pl.ds(start, span)
    keys, values = window[place, :size], window[place, size:]
    probs = jnp.exp(dot(keys, query, (1, 1)) + (bias[...] - logs[0]))
    grad_scores = (probs * (dot(values, grad, (1, 1)) - inner)).astype(low)
    total[place, size:] += dot(probs.astype(low), grad, (1, 0))
    total[place, :size] += dot(grad_scores, query, (1, 0))
    flat = dot(turned[:, place], grad_scores, (1, 0)) * scale
    grad_queries[...] = side_by_side(flat.T, size).astype(low)

    @pl.when((block == pl.num_programs(0) - 1) & (pl.program_id(1) == pl.num_programs(1) - 1))
    def _():
        for i in range(len(blocks) // 2):
            at = pl.multiple_of((2 * i + core[0]) * count, SUB)
            mine[i] = total[pl.ds(at, count), :]
            at = pl.multiple_of((2 * i + 1 - core[0]) * count, SUB)
            theirs[i] = total[pl.ds(at, count), :].astype(low)


def attend(queries, blocks, places, size, base):
    count, wide = queries.shape
    grid = (count // SUB, wide // (2 * size))
    span = WINDOW + SUB
    rows = len(blocks) * count
    core = lax.axis_index("c").astype(jnp.int32)[None]
    tile = pl.BlockSpec((SUB, 2 * size), lambda s, h, o: (s, h))
    return pl.pallas_call(
        functools.partial(attend_kernel, size, size**-0.5, span, base),
        out_shape=(
            jax.ShapeDtypeStruct((count, wide), low),
            jax.ShapeDtypeStruct((count, wide), f32),
            jax.ShapeDtypeStruct((grid[0] * grid[1], 1, 2 * SUB), f32),
        ),
        grid_spec=pltpu.PrefetchScalarGridSpec(
            num_scalar_prefetch=1,
            grid=grid,
            in_specs=[pl.BlockSpec((1, SUB), lambda s, h, o: (0, s)), tile]
            + [pl.BlockSpec(block.shape, lambda s, h, o: (0, 0)) for block in blocks],
            out_specs=[tile, tile, pl.BlockSpec((1, 1, 2 * SUB), lambda s, h, o: (s * grid[1] + h, 0, 0))],
            scratch_shapes=[
                pltpu.VMEM((span, 2 * SUB), f32),
                pltpu.VMEM((rows, 2 * size), low),
                pltpu.VMEM((size, rows), low),
            ],
        ),
        compiler_params=pltpu.CompilerParams(vmem_limit_bytes=56 << 20),
        cost_estimate=NOMINAL,
    )(core, places, queries, *blocks)


def attend_back(queries, grads, mixed, logs, blocks, places, size, base):
    count, wide = queries.shape
    grid = (count // SUB, wide // (2 * size))
    span = WINDOW + SUB
    rows = len(blocks) * count
    half = len(blocks) // 2
    core = lax.axis_index("c").astype(jnp.int32)[None]
    tile = pl.BlockSpec((SUB, 2 * size), lambda s, h, o: (s, h))
    whole = pl.BlockSpec((half, count, 2 * size), lambda s, h, o: (0, 0, 0))
    return pl.pallas_call(
        functools.partial(attend_back_kernel, size, size**-0.5, span, base),
        out_shape=(
            jax.ShapeDtypeStruct((count, wide), low),
            jax.ShapeDtypeStruct((half, count, 2 * size), f32),
            jax.ShapeDtypeStruct((half, count, 2 * size), low),
        ),
        grid_spec=pltpu.PrefetchScalarGridSpec(
            num_scalar_prefetch=1,
            grid=grid,
            in_specs=[
                pl.BlockSpec((1, SUB), lambda s, h, o: (0, s)),
                tile,
                tile,
                tile,
                pl.BlockSpec((1, 1, 2 * SUB), lambda s, h, o: (s * grid[1] + h, 0, 0)),
            ]
            + [pl.BlockSpec(block.shape, lambda s, h, o: (0, 0)) for block in blocks],
            out_specs=[tile, whole, whole],
            scratch_shapes=[
                pltpu.VMEM((span, 2 * SUB), f32),
                pltpu.VMEM((rows, 2 * size), low),
                pltpu.VMEM((size, rows), low),
                pltpu.VMEM((rows, 2 * size), f32),
            ],
        ),
        compiler_params=pltpu.CompilerParams(vmem_limit_bytes=60 << 20),
        cost_estimate=NOMINAL,
    )(core, places, queries, grads, mixed, logs, *blocks)


def lay_rows(slots, layout, pieces, full):
    for (r, first), piece in zip(layout, pieces):
        planes, rows, _ = piece.shape
        for plane in range(planes):
            at = pl.multiple_of(((first + plane) * 8 + slots[r]) * rows, 16)
            full[pl.ds(at, rows), :] = piece[plane]


def apply_kernel(layout, slots, left, *rest):
    *pieces, out, full = rest
    lay_rows(slots, layout, pieces, full)
    out[...] = dot(left[...], full[...], (1, 0), low)


def apply_turned_kernel(layout, slots, left, *rest):
    *start, out, full = rest
    start, pieces = start[: -len(layout)], start[-len(layout) :]
    lay_rows(slots, layout, pieces, full)

    @pl.when(pl.program_id(0) == 0)
    def _():
        out[...] = start[0][...] if start else jnp.zeros_like(out)

    out[...] += dot(left[...], full[...], (1, 1))


def whole_rows(blocks):
    planes, rows, wide = blocks[0].shape
    here = plane_index()
    whole = jnp.zeros((planes, 8, rows, wide), blocks[0].dtype)
    for r, block in enumerate(blocks):
        whole = lax.dynamic_update_slice(whole, block[:, None], (0, here ^ r, 0, 0))
    return whole.reshape(planes * 8 * rows, wide)


def apply_rows(left, blocks, turned=False, start=None):
    planes, rows, wide = blocks[0].shape
    if rows % 16 or wide % TILE:
        whole = whole_rows(joined_blocks(blocks))
        if not turned:
            return dot(left, whole, (1, 0), low)
        return dot(left, whole, (1, 1)) + (0.0 if start is None else start)
    count, deep = left.shape[0], planes * 8 * rows
    slots = (plane_index() ^ jnp.arange(8)).astype(jnp.int32)
    layout, blocks = [], [block if isinstance(block, tuple) else (block,) for block in blocks]
    for r, block in enumerate(blocks):
        layout += [(r, sum(piece.shape[0] for piece in block[:i])) for i in range(len(block))]
    blocks = [piece for block in blocks for piece in block]
    pieces = [pl.BlockSpec((piece.shape[0], rows, TILE), lambda n, s: (0, 0, n)) for piece in blocks]
    whole = pl.BlockSpec((count, deep), lambda n, s: (0, 0))
    part = pl.BlockSpec((count, TILE), lambda n, s: (0, n))
    if not turned:
        kernel, given, specs, result = apply_kernel, [left], [whole], part
        shape = jax.ShapeDtypeStruct((count, wide), low)
    else:
        kernel, given, specs, result = apply_turned_kernel, [left], [part], whole
        if start is not None:
            given, specs = given + [start], specs + [whole]
        shape = jax.ShapeDtypeStruct((count, deep), f32)
    return pl.pallas_call(
        functools.partial(kernel, layout),
        out_shape=shape,
        grid_spec=pltpu.PrefetchScalarGridSpec(
            num_scalar_prefetch=1,
            grid=(wide // TILE,),
            in_specs=specs + pieces,
            out_specs=result,
            scratch_shapes=[pltpu.VMEM((deep, TILE), low)],
        ),
        compiler_params=pltpu.CompilerParams(vmem_limit_bytes=48 << 20),
        cost_estimate=NOMINAL,
    )(slots, *given, *blocks)


def row_grads_kernel(slots, left, right, keep, send, turned):
    @pl.when(pl.program_id(1) == 0)
    def _():
        turned[...] = left[...].T

    rows = keep.shape[2]
    value = dot(turned[...], right[...], (1, 0), low)
    for i in range(8):
        place = slots[i]

        @pl.when(place < 4)
        def _():
            keep[place, 0] = value[i * rows : (i + 1) * rows]

        @pl.when(place >= 4)
        def _():
            send[place - 4, 0] = value[i * rows : (i + 1) * rows]


def row_grads(left, right):
    planes = lax.axis_size("z")
    count, deep = left.shape
    wide = right.shape[1]
    rows = deep // (planes * 8)
    places = jnp.array([3, 1, 7, 5, 2, 0, 6, 4], jnp.int32)
    slots = places[plane_index() ^ jnp.arange(8)]
    if rows % 16 or wide % TILE or (planes * 8 * rows) % (planes * 128):
        blocks = dot(left, right, (0, 0), low).reshape(planes, 8, rows, wide)
        order = jnp.argsort(slots)
        blocks = jnp.swapaxes(jnp.take(blocks, order, axis=1), 0, 1)
        return blocks[:4], blocks[4:]
    tile = wide if wide <= 5 * TILE else TILE
    group = pl.BlockSpec((4, 1, rows, tile), lambda z, n, s: (0, z, 0, n))
    shape = jax.ShapeDtypeStruct((4, planes, rows, wide), low)
    return pl.pallas_call(
        row_grads_kernel,
        out_shape=(shape, shape),
        grid_spec=pltpu.PrefetchScalarGridSpec(
            num_scalar_prefetch=1,
            grid=(planes, wide // tile),
            in_specs=[
                pl.BlockSpec((count, 8 * rows), lambda z, n, s: (0, z)),
                pl.BlockSpec((count, tile), lambda z, n, s: (0, n)),
            ],
            out_specs=[group, group],
            scratch_shapes=[pltpu.VMEM((8 * rows, count), low)],
        ),
        compiler_params=pltpu.CompilerParams(vmem_limit_bytes=48 << 20),
        cost_estimate=NOMINAL,
    )(slots, left, right)


def mlp_kernel(part, per, tiles, *rest):
    weights, rest = rest[:per], rest[per:]
    pieces = 2 * sum(tiles)
    sources, rest = rest[:pieces], rest[pieces:]
    before, rest = rest[:-8], rest[-8:]
    outs, grad_units, hidden, units, grads, arrived = rest[0:2], rest[2:4], *rest[4:]
    step = pl.program_id(0)

    def fetches(tile):
        first = 2 * sum(tiles[:tile])
        found = []
        for array, target in enumerate((units, grads)):
            at = 0
            for i in range(tiles[tile]):
                source = sources[first + array * tiles[tile] + i]
                found.append(
                    pltpu.make_async_copy(
                        source,
                        target.at[tile % 2, pl.ds(at, source.shape[0])],
                        arrived.at[tile % 2, array, i],
                    )
                )
                at += source.shape[0]
        return found

    for tile in range(len(tiles)):

        @pl.when(step == tile)
        def _():
            if tile == 0:
                for copy in fetches(0):
                    copy.start()
            if tile + 1 < len(tiles):
                for copy in fetches(tile + 1):
                    copy.start()
            for copy in fetches(tile):
                copy.wait()

    slope = 0.7978845608028654
    for j in range(per):
        both = dot(units[step % 2], weights[j][:, : 2 * part], (1, 0))
        gates, upward = both[:, :part], both[:, part:]
        grad_middle = dot(grads[step % 2], weights[j][:, 2 * part :], (1, 0))
        square = gates * gates
        half = 0.5 + 0.5 * jnp.tanh(gates * (slope + slope * 0.044715 * square))
        gelu = gates * half
        grad_gelu = half + gelu * (1.0 - half) * (2 * slope + 6 * slope * 0.044715 * square)
        at = 2 * part * j
        hidden[:, at : at + part] = (grad_middle * upward * grad_gelu).astype(low)
        hidden[:, at + part : at + 2 * part] = (grad_middle * gelu).astype(low)
        at = part * (2 * per + j)
        hidden[:, at : at + part] = (gelu * upward).astype(low)
    for which, targets in enumerate((outs, grad_units)):
        value = 0.0
        for j in range(per):
            at, width = (2 * part * j, 2 * part) if which else (part * (2 * per + j), part)
            first = 0 if which else 2 * part
            value = value + dot(hidden[:, at : at + width], weights[j][:, first : first + width], (1, 1))
        for side in range(2):

            @pl.when(step // (len(tiles) // 2) == side)
            def _():
                if before:
                    targets[side][...] = (value + before[2 * which + side][...].astype(f32)).astype(low)
                else:
                    targets[side][...] = value.astype(low)


def mlp(units, grads, weights, before):
    rows = sum(piece.shape[0] for piece in units[0])
    count, wide = rows * len(units), units[0][0].shape[1]
    per, each = len(weights), weights[0].shape[1]
    deep = per * each
    tiles = tuple(len(tile) for tile in units)
    sources = [piece for pair in zip(units, grads) for tile in pair for piece in tile]
    side = len(units) // 2
    sides = [
        pl.BlockSpec((rows, wide), lambda i: (jnp.minimum(i, side - 1), 0)),
        pl.BlockSpec((rows, wide), lambda i: (jnp.maximum(i - side, 0), 0)),
    ]
    half = jax.ShapeDtypeStruct((count // 2, wide), low)
    return pl.pallas_call(
        functools.partial(mlp_kernel, each // 3, per, tiles),
        out_shape=[half] * 4 + [jax.ShapeDtypeStruct((count, deep), low)],
        grid=(len(units),),
        in_specs=[pl.BlockSpec((wide, each), lambda i: (0, 0), pipeline_mode=pl.Buffered(1))] * per
        + [pl.BlockSpec(memory_space=pl.ANY)] * len(sources)
        + (sides * 2 if before else []),
        out_specs=sides * 2 + [pl.BlockSpec((rows, deep), lambda i: (i, 0))],
        scratch_shapes=[
            pltpu.VMEM((2, rows, wide), low),
            pltpu.VMEM((2, rows, wide), low),
            pltpu.SemaphoreType.DMA((2, 2, max(tiles))),
        ],
        compiler_params=pltpu.CompilerParams(vmem_limit_bytes=62 << 20),
        cost_estimate=NOMINAL,
    )(*weights, *sources, *before)


def mlp_grads_kernel(number, *rest):
    units, grads, hidden, rest = rest[:number], rest[number : 2 * number], rest[2 * number : 2 * number + 2], rest[2 * number + 2 :]
    *outs, turned = rest
    step = pl.program_id(0)
    part = hidden[0].shape[1] // 3
    piece = 256 if part % 256 == 0 and outs[0].shape[1] % 256 == 0 else 128
    places = [(out, at) for out in outs for at in range(0, out.shape[1], piece)]

    def turn(slot, which, sources, share, shares):
        at = 0
        for i, source in enumerate(sources):
            if i * shares // len(sources) == share:
                turned[slot, which, :, at : at + source.shape[0]] = source[...].T
            at += source.shape[0]

    def multiply(slot, which, i, at):
        value, start = 0.0, 0
        for block in hidden:
            left = turned[slot, which, :, start : start + block.shape[0]]
            value = value + dot(left, block[:, at : at + piece], (1, 0))
            start += block.shape[0]
        out, place = places[i]
        out[:, place : place + piece] = value.astype(low)

    work = [(at // (2 * part), at) for at in range(0, 3 * part, piece)]

    @pl.when(step == 0)
    def _():
        turn(0, 0, units, 0, 1)
        turn(0, 1, grads, 0, 1)

    @pl.when(step > 0)
    def _():
        for i, (which, at) in enumerate(work):
            multiply((step - 1) % 2, which, i, at)
            turn(step % 2, 0, units, i, len(work))
            turn(step % 2, 1, grads, i, len(work))


def mlp_grads(units, grads, hidden, pieces=(2,)):
    wide = units[0].shape[1]
    deep = hidden[0].shape[1]
    count = sum(piece.shape[0] for piece in units)
    rows = 512
    last = wide // rows - 1
    return pl.pallas_call(
        functools.partial(mlp_grads_kernel, len(units)),
        out_shape=[jax.ShapeDtypeStruct((wide, deep // 2 * piece), low) for piece in pieces],
        grid=(last + 2,),
        in_specs=[
            pl.BlockSpec((piece.shape[0], rows), lambda s: (0, jnp.minimum(s, last))) for piece in units + grads
        ]
        + [pl.BlockSpec(piece.shape, lambda s: (0, 0), pipeline_mode=pl.Buffered(1)) for piece in hidden],
        out_specs=[
            pl.BlockSpec((rows, deep // 2 * piece), lambda s: (jnp.maximum(s - 1, 0), 0)) for piece in pieces
        ],
        scratch_shapes=[pltpu.VMEM((2, 2, rows, count), low)],
        compiler_params=pltpu.CompilerParams(vmem_limit_bytes=62 << 20),
        cost_estimate=NOMINAL,
    )(*units, *grads, *hidden)


def token_grads_kernel(number, *rest):
    units, (right, out, turned) = rest[:number], rest[number:]

    @pl.when(pl.program_id(0) == 0)
    def _():
        turned[...] = right[...].T

    value, at = 0.0, 0
    for unit in units:
        value = value + dot(turned[:, at : at + unit.shape[0]], unit[...], (1, 0))
        at += unit.shape[0]
    out[...] = value.astype(low).T


def token_grads(units, right):
    wide = units[0].shape[1]
    count, deep = right.shape
    rows = 512
    return pl.pallas_call(
        functools.partial(token_grads_kernel, len(units)),
        out_shape=jax.ShapeDtypeStruct((wide, deep), low),
        grid=(wide // rows,),
        in_specs=[pl.BlockSpec((piece.shape[0], rows), lambda s: (0, s)) for piece in units]
        + [pl.BlockSpec(right.shape, lambda s: (0, 0), pipeline_mode=pl.Buffered(1))],
        out_specs=pl.BlockSpec((rows, deep), lambda s: (s, 0)),
        scratch_shapes=[pltpu.VMEM((deep, count), low)],
        compiler_params=pltpu.CompilerParams(vmem_limit_bytes=56 << 20),
        cost_estimate=NOMINAL,
    )(*units, right)


def spread_kernel(slots, value, *outs):
    count, deep = value.shape[0], outs[0].shape[1]
    place = 0
    for out in outs:
        for at in range(0, out.shape[0], count):
            out[at : at + count, :] = value[:, pl.ds(pl.multiple_of(slots[place] * deep, 128), deep)]
            place += 1


def spread(value):
    count, wide = value.shape
    order = (0, 2, 1, 3, 4, 6, 5, 7)
    slots = (plane_index() ^ jnp.array(order)).astype(jnp.int32)
    deep = wide // 8
    rows = (count, count, 2 * count, 2 * count, 2 * count)
    if deep % 128:
        pieces = [lax.dynamic_slice(value, (0, slots[i] * deep), (count, deep)) for i in range(8)]
        return pieces[:2] + [jnp.concatenate(pieces[i : i + 2], 0) for i in (2, 4, 6)]
    return pl.pallas_call(
        spread_kernel,
        out_shape=[jax.ShapeDtypeStruct((n, deep), value.dtype) for n in rows],
        grid_spec=pltpu.PrefetchScalarGridSpec(
            num_scalar_prefetch=1,
            grid=(1,),
            in_specs=[pl.BlockSpec((count, wide), lambda i, s: (0, 0))],
            out_specs=[pl.BlockSpec((n, deep), lambda i, s: (0, 0)) for n in rows],
        ),
        cost_estimate=NOMINAL,
    )(slots, value)


def turn_kernel(keep, found, far, diag_x, diag_y, y_bottom, x_bottom, y_top):
    half = far.shape[0]
    both = keep[...].astype(f32) + found[...].astype(f32)
    y_top[...] = (both[:half] + diag_x[...].astype(f32)).astype(low)
    y_bottom[...] = both[half:].astype(low)
    x_bottom[...] = (far[...].astype(f32) + diag_y[...].astype(f32)).astype(low)


def turn(keep, found, far, diag_x, diag_y):
    half, wide = far.shape
    part = lambda rows: pl.BlockSpec((rows, TILE), lambda n: (0, n))
    return pl.pallas_call(
        turn_kernel,
        out_shape=[jax.ShapeDtypeStruct((half, wide), low)] * 3,
        grid=(wide // TILE,),
        in_specs=[part(2 * half)] * 2 + [part(half)] * 3,
        out_specs=[part(half)] * 3,
        cost_estimate=NOMINAL,
    )(keep, found, far, diag_x, diag_y)


def halved_kernel(keep, found, *outs):
    half = outs[0].shape[0]
    for i, out in enumerate(outs):
        rows = slice(i * half, i * half + half)
        out[...] = (keep[rows].astype(f32) + found[rows].astype(f32)).astype(low)


def halved(keep, found):
    count, wide = keep.shape
    part = lambda rows: pl.BlockSpec((rows, TILE), lambda n: (0, n))
    return pl.pallas_call(
        halved_kernel,
        out_shape=[jax.ShapeDtypeStruct((count // 4, wide), low)] * 4,
        grid=(wide // TILE,),
        in_specs=[part(count)] * 2,
        out_specs=[part(count // 4)] * 4,
        cost_estimate=NOMINAL,
    )(keep, found)


def resid_kernel(steps, keep, found, x_top, x_bottom, y_top, y_bottom, resid, gift, scale, grad_out, grad_low):
    upper = pl.program_id(0) < steps
    x_part = jnp.where(upper, x_top[...].astype(f32), x_bottom[...].astype(f32))
    y_part = jnp.where(upper, y_top[...].astype(f32), y_bottom[...].astype(f32))
    grad = keep[...].astype(f32) + found[...].astype(f32) + x_part + y_part
    grad = gift[...].astype(f32) + unit_back(grad, resid[...], scale[...])
    grad_out[...] = grad
    grad_low[...] = grad.astype(low)


def resid_grads(keep, found, x_top, x_bottom, y_top, y_bottom, resid, gift, scale):
    count, wide = resid.shape
    rows = 96
    steps = count // (2 * rows)
    row = pl.BlockSpec((rows, wide), lambda i: (i, 0))
    own = pl.BlockSpec((rows, wide), lambda i: (i + 2 * steps, 0))
    first = pl.BlockSpec((rows, wide), lambda i: (jnp.minimum(i, steps - 1), 0))
    last = pl.BlockSpec((rows, wide), lambda i: (jnp.maximum(i - steps, 0), 0))
    return pl.pallas_call(
        functools.partial(resid_kernel, steps),
        out_shape=(jax.ShapeDtypeStruct((count, wide), f32), jax.ShapeDtypeStruct((count, wide), low)),
        grid=(2 * steps,),
        in_specs=[own, own, first, last, first, last, row, row, pl.BlockSpec((rows, 1), lambda i: (i, 0))],
        out_specs=(row, row),
        cost_estimate=NOMINAL,
    )(keep, found, x_top, x_bottom, y_top, y_bottom, resid, gift, scale)


def part_sums_kernel(keep, found, diag_top, diag_bottom, x_top, x_bottom, y_top, y_bottom, own):
    half = diag_top.shape[0]

    def both(place, first, rows):
        part = slice(first, first + rows)
        return (keep[place, part].astype(f32) + found[place, part].astype(f32)).astype(low)

    for place, (top, bottom) in enumerate(((diag_top, diag_bottom), (x_top, x_bottom), (y_top, y_bottom))):
        top[...] = both(place, 0, half)
        bottom[...] = both(place, half, half)
    own[...] = both(3, 0, 2 * half)


def part_sums(keep, found):
    _, planes, rows, wide = keep.shape
    four = pl.BlockSpec((4, planes, rows, TILE), lambda n: (0, 0, 0, n))
    some = lambda planes: pl.BlockSpec((planes, rows, TILE), lambda n: (0, 0, n))
    half = planes // 2
    shape = lambda planes: jax.ShapeDtypeStruct((planes, rows, wide), low)
    return pl.pallas_call(
        part_sums_kernel,
        out_shape=[shape(half)] * 6 + [shape(planes)],
        grid=(wide // TILE,),
        in_specs=[four] * 2,
        out_specs=[some(half)] * 6 + [some(planes)],
        compiler_params=pltpu.CompilerParams(vmem_limit_bytes=48 << 20),
        cost_estimate=NOMINAL,
    )(keep, found)


def pack_kernel(spans, part, gain, gate, up, down, out):
    scale = gain[...]
    share = out.shape[2] // 3
    for p, (at, n) in enumerate(spans):
        for q in range(share // part):
            width = min(part, n - q * part)
            place = slice(at + q * part, at + q * part + width)
            for which, source in enumerate((gate, up, down)):
                first = part * (3 * q + which)
                if width > 0:
                    value = source[:, place]
                    if which < 2:
                        value = (value.astype(f32) * scale).astype(low)
                    out[p, :, first : first + width] = value
                if width < part:
                    empty = max(width, 0)
                    out[p, :, first + empty : first + part] = jnp.zeros((out.shape[1], part - empty), low)


def pack(spans, part, share, gain, gate, up, down):
    rows, _ = gate.shape
    return pl.pallas_call(
        functools.partial(pack_kernel, spans, part),
        out_shape=jax.ShapeDtypeStruct((8, rows, 3 * share), low),
        compiler_params=pltpu.CompilerParams(vmem_limit_bytes=48 << 20),
        cost_estimate=NOMINAL,
    )(gain, gate, up, down)


def shares(columns):
    tiles = -(-columns // 128)
    few, more = divmod(tiles, 8)
    sizes = [128 * (few + (p < more)) for p in range(8)]
    return [(sum(sizes[:p]), size) for p, size in enumerate(sizes)], 128 * (few + (more > 0))


def finish_kernel(spans, part, per, gain, gate, up, whole, gate_out, up_out, down_out, gain_out):
    scale = gain[...]
    total = jnp.zeros_like(scale)
    for p, (at, n) in enumerate(spans):
        for q in range(-(-n // part)):
            width = min(part, n - q * part)
            start, j = 3 * part * per * (q // per), q % per
            place = slice(at + q * part, at + q * part + width)
            for which, (weight, out) in enumerate(((gate, gate_out), (up, up_out))):
                first = start + part * (2 * j + which)
                value = whole[p, :, first : first + width].astype(f32)
                total = total + jnp.sum(value * weight[:, place].astype(f32), axis=1, keepdims=True)
                out[:, place] = value * scale
            first = start + part * (2 * per + j)
            down_out[:, place] = whole[p, :, first : first + width].astype(f32)
    gain_out[...] = total


def finish(spans, part, per, gain, gate, up, whole):
    rows, columns = gate.shape
    return pl.pallas_call(
        functools.partial(finish_kernel, spans, part, per),
        out_shape=(
            jax.ShapeDtypeStruct((rows, columns), f32),
            jax.ShapeDtypeStruct((rows, columns), f32),
            jax.ShapeDtypeStruct((rows, columns), f32),
            jax.ShapeDtypeStruct((rows, 1), f32),
        ),
        compiler_params=pltpu.CompilerParams(vmem_limit_bytes=48 << 20),
        cost_estimate=NOMINAL,
    )(gain, gate, up, whole)


def unit_of(values):
    scale = lax.rsqrt(jnp.mean(values * values, axis=-1, keepdims=True) + epsilon)
    return scale, (values * scale).astype(low)


def unit_back(grad, values, scale):
    unit = values * scale
    return scale * (grad - unit * jnp.mean(grad * unit, axis=-1, keepdims=True))


def local(
    tokens,
    positions,
    attn_gain,
    query_weight,
    key_weight,
    value_weight,
    out_weight,
    mlp_gain,
    gate_weight,
    up_weight,
    down_weight,
    cotangent,
):
    count = tokens.shape[1]
    size = key_weight.shape[1]
    wide = query_weight.shape[1]
    reach = (WINDOW + count - 2) // count
    chips = (reach + 1) // 2
    base = 2 * chips * count - WINDOW
    gain_one = attn_gain[:, None]
    gain_two = mlp_gain[:, None]

    qkv_shard = jnp.concatenate([query_weight, key_weight, value_weight], 1).astype(f32) * gain_one
    qkv_shard = qkv_shard.astype(low)
    qkv_column = lax.all_gather(qkv_shard, "z", axis=0, tiled=False)
    out_column = lax.all_gather(after(out_weight.T, qkv_shard), "z", axis=0, tiled=False)

    spans, share = shares(gate_weight.shape[1])
    parts = share // 256 if share % 256 == 0 else 1
    calls = 2 if parts % 2 == 0 else 1
    per = parts // calls
    part = share // parts
    mine = pack(spans, part, share, after(gain_two, qkv_shard), gate_weight, up_weight, down_weight.T)
    gift = cotangent[0]
    mlp_column = lax.all_to_all(mine, PLANE, split_axis=0, concat_axis=0, tiled=True)
    mlp_column = mlp_column.reshape(-1, 3 * share)

    def piece_of(k, column):
        return column[:, k * 3 * part : (k + 1) * 3 * part]

    def gathered(piece):
        return lax.all_gather(piece, "z", axis=0, tiled=True)

    mlp_full = [gathered(piece_of(0, mlp_column))]
    sure = positions[0, 0] >= 0
    half = count // 2

    def project(qkv_column, tokens, gift, mlp_column):
        qkv_blocks = plane_gather(qkv_column)
        scale_one, unit_one = unit_of(tokens[0].astype(f32))
        qkv = apply_rows(unit_one, qkv_blocks)
        queries, pair = qkv[:, :wide], qkv[:, wide:]
        moves = [behind(d) for d in range(chips, 0, -1)]
        found, pieces = stage(
            [(pair, move) for move in moves] + [(pair, "c"), (gift, "x"), (gift, "y"), (gift, "c")],
            lambda column: [piece_of(k, column) for k in range(1, parts)],
            [mlp_column],
        )
        *pairs, pair_c, gift_x, gift_y, gift_c = found
        found, _ = stage([(block, "c") for block in pairs])
        gifts = gift_x, gift_y, gift_c
        return qkv_blocks[1:], queries, [*pairs, pair, *found, pair_c], gifts, unit_one, scale_one, pieces

    def forward(queries, pairs, out_column, tokens, positions, gift_x, gift_y):
        inputs = tokens[0].astype(f32)
        mid = out_column.shape[0] // 2
        (out_x, out_y, out_c, gift_x_c, gift_y_c), (mixed, mixed_wide, logs) = stage(
            [(out_column, "x"), (out_column, "y"), (out_column, "c"), (gift_x, "c"), (gift_y, "c")],
            lambda *given: attend(given[0], given[1:], positions, size, base),
            [queries, *pairs],
        )
        (out_top, out_bottom, out_x_c, out_y_c), _ = stage(
            [(out_y[:mid], "x"), (out_x[mid:], "y"), (out_x, "c"), (out_y, "c")]
        )
        out_diag_c, _ = stage([(out_top, "c"), (out_bottom, "c")])
        out_blocks = [out_column, out_x, out_c, out_x_c, out_y, (out_top, out_bottom), out_y_c, out_diag_c]
        resid = apply_rows(mixed, out_blocks, True, inputs)
        scale_two, unit_two = unit_of(resid)
        (unit_x, unit_y, unit_c), _ = stage([(unit_two, "x"), (unit_two, "y"), (unit_two, "c")])
        (unit_x_c, unit_y_c), _ = stage([(unit_x, "c"), (unit_y, "c")])
        unit_blocks = unit_two, unit_x, unit_c, unit_x_c, unit_y, unit_y_c
        return out_blocks[1:], mixed, mixed_wide, logs, resid, scale_two, unit_blocks, gift_x_c, gift_y_c

    qkv_column = after(qkv_column, mlp_column)
    qkv_blocks, queries, pairs, gifts, unit_one, scale_one, pieces = boxed(
        sure, project, qkv_column, tokens, gift, mlp_column
    )
    gift_x, gift_y, gift_c = gifts
    mlp_full += [gathered(piece) for piece in pieces]
    out_blocks, mixed, mixed_wide, logs, resid, scale_two, unit_blocks, gift_x_c, gift_y_c = boxed(
        sure, forward, after(queries, mlp_full[0]), pairs, out_column, tokens, positions, gift_x, gift_y
    )
    qkv_blocks, out_blocks = [qkv_column, *qkv_blocks], [out_column, *out_blocks]
    grads_near = [(gift_y,), (gift,), (gift_y_c,), (gift_c,)]

    def flat(*tiles):
        return [piece for group in tiles for tile in group for piece in tile]

    def summed(keep, received):
        return keep.astype(f32) + received.astype(f32)

    def halves(value):
        middle = value.shape[0] // 2
        return value[:middle], value[middle:]

    def total(*values):
        return sum(value.astype(f32) for value in values)

    def opening(weights, blocks, gift_x, gift_x_c, grads_near, unit_one):
        unit_two, unit_x, unit_c, unit_x_c, unit_y, unit_y_c = blocks
        units_near = [(unit_y,), (unit_two,), (unit_y_c,), (unit_c,)]
        gift_y = grads_near[0][0]
        sends = [(unit_y, "x"), (gift_x, "y")]
        one_sends = [(unit_one, "x"), (unit_one, "y"), (unit_one, "c")]
        far_sums = near_sums = partial = ()
        if calls > 1:
            (unit_d, gift_d), near_sums = stage(
                sends, lambda *given: mlp([(v,) for v in given], grads_near, weights, ()), flat(units_near)
            )
        else:
            (unit_d, gift_d), _ = stage(sends)
        (unit_d_c, gift_d_c), _ = stage([(unit_d, "c"), (gift_d, "c")])
        units_far = [(unit_d,), (unit_x,), (unit_d_c,), (unit_x_c,)]
        grads_far = [(gift_d,), (gift_x,), (gift_d_c,), (gift_x_c,)]
        if calls > 1:
            (one_x, one_y, one_c), far_sums = stage(
                one_sends, lambda weights: mlp(units_far, grads_far, weights, ()), [weights]
            )
        else:
            (one_x, one_y, one_c), _ = stage(one_sends)
        one_sends = [(one_y, "x"), (one_x, "c"), (one_y, "c")]
        if calls > 1:
            (one_d, one_x_c, one_y_c), partial = stage(
                one_sends,
                lambda *given: mlp_grads(flat(units_far, units_near), flat(grads_far, grads_near), given)[0],
                [far_sums[4], near_sums[4]],
            )
        else:
            (one_d, one_x_c, one_y_c), _ = stage(one_sends)
        ones = one_x, one_c, one_x_c, one_y, one_d, one_y_c
        return (unit_d, unit_d_c), (gift_d, gift_d_c), far_sums[:4], near_sums[:4], partial, ones

    columns = []
    unit_two, unit_x, unit_c, unit_x_c, unit_y, unit_y_c = unit_blocks
    unit_far, gift_far, far_before, near_before, partial, ones = boxed(
        sure, opening, mlp_full[:per] if calls > 1 else (), unit_blocks, gift_x, gift_x_c, grads_near, unit_one
    )
    if calls > 1:
        columns.append(lax.psum_scatter(partial, "z", scatter_dimension=0, tiled=True))
    unit_d, unit_d_c = unit_far
    gift_d, gift_d_c = gift_far
    grads_far = [(gift_d,), (gift_x,), (gift_d_c,), (gift_x_c,)]
    units_far = [(unit_d,), (unit_x,), (unit_d_c,), (unit_x_c,)]
    units_near = [(unit_y,), (unit_two,), (unit_y_c,), (unit_c,)]

    def middle(weights, units_far, units_near, grads_far, grads_near, far_before, near_before, resid, scale_two, gift, ones):
        (one_d_c,), far_sums = stage(
            [(ones[4], "c")],
            lambda *weights: mlp(units_far, grads_far, weights, far_before),
            weights,
        )
        (found,), _ = stage([(far_sums[3], "c")])
        diag_top, diag_bottom, x_top, x_bottom = halved(far_sums[2], found)
        (diag_x, diag_y, x_top, far_out), near_sums = stage(
            [(diag_top, "x"), (diag_bottom, "y"), (x_top, "x"), (far_sums[1], "c")],
            lambda *given: mlp([(value,) for value in given], grads_near, weights, near_before),
            [tile[0] for tile in units_near],
        )
        (found,), _ = stage([(near_sums[3], "c")])
        y_bottom, x_bottom, y_top = turn(near_sums[2], found, x_bottom, diag_x, diag_y)
        (y_bottom, x_bottom, y_top, near_out), partial = stage(
            [(y_bottom, "y"), (x_bottom, "x"), (y_top, "y"), (near_sums[1], "c")],
            lambda *given: mlp_grads(flat(units_far, units_near), flat(grads_far, grads_near), given, cuts),
            [far_sums[4], near_sums[4]],
        )
        received = x_top, x_bottom, y_top, y_bottom
        outs = far_sums[0], far_out, near_sums[0], near_out
        return partial, (near_sums[2], found, received), outs, one_d_c

    cuts = (1, 1)
    partial, own_sums, outs, one_d_c = boxed(
        sure,
        middle,
        mlp_full[-per:],
        units_far,
        units_near,
        grads_far,
        grads_near,
        far_before,
        near_before,
        resid,
        scale_two,
        gift,
        ones,
    )
    columns += [lax.psum_scatter(piece, "z", scatter_dimension=0, tiled=True) for piece in partial[:1]]
    one_x, one_c, one_x_c, one_y, one_d, one_y_c = ones
    flat_ones = [unit_one, one_x, one_y, one_d, one_c, one_x_c, one_y_c, one_d_c]

    def joined(own, first, second):
        top, bottom = own if isinstance(own, tuple) else halves(own)
        return jnp.concatenate([total(top, first[2], second[1]), total(bottom, second[0], first[3])], 0)

    def backward(
        own_sums, outs, resid, scale_two, gift, queries, pairs, mixed, mixed_wide, logs, out_blocks, positions
    ):
        keep, found, received = own_sums
        grad_resid, grad_attn = resid_grads(keep, found, *received, resid, gift, scale_two)
        out_far, out_near = halved(*outs[:2]), halved(*outs[2:])

        def attention(grad_attn):
            grad_mixed = apply_rows(grad_attn, out_blocks)
            return attend_back(queries, grad_mixed, mixed_wide, logs, pairs, positions, size, base)

        first, (grad_queries, mine, theirs) = stage(
            [(out_far[0], "x"), (out_far[1], "y"), (out_far[2], "x"), (out_near[1], "y")], attention, [grad_attn]
        )
        (found,), _ = stage([(theirs, "c")])
        mine = summed(mine, found)
        second = total(out_far[3], first[1]).astype(low), total(out_near[0], first[0]).astype(low)
        (*found, x_second, y_second), (out_keep, out_send) = stage(
            [(mine[chips - d].astype(low), behind(-d)) for d in range(chips, 0, -1)]
            + [(second[0], "x"), (second[1], "y")],
            lambda *given: row_grads(*given),
            [grad_attn, mixed],
        )
        grad_pair = total(mine[chips], *found).astype(low)
        grad_qkv = jnp.concatenate([grad_queries, grad_pair], 1)
        return grad_qkv, grad_resid, first, (x_second, y_second), out_keep, out_send, (out_near[2], out_near[3])

    grad_qkv, grad_resid, first, second, out_keep, out_send, out_own = boxed(
        sure,
        backward,
        own_sums,
        outs,
        after(resid, columns[0]),
        scale_two,
        gift,
        queries,
        pairs,
        mixed,
        mixed_wide,
        logs,
        out_blocks,
        positions,
    )
    columns += [
        lax.psum_scatter(after(piece, grad_qkv), "z", scatter_dimension=0, tiled=True) for piece in partial[1:]
    ]

    def collect(
        grad_qkv, first, second, out_own, out_keep, out_send, grad_resid, resid, qkv_blocks, flat_ones, scale_one, tokens
    ):
        own, to_c, to_x, to_y, to_d = spread(grad_qkv)

        def tokens_grads(grad_qkv):
            grad_unit_one = apply_rows(grad_qkv, qkv_blocks, True)
            return grad_resid + unit_back(grad_unit_one, tokens[0].astype(f32), scale_one)

        (by_x, by_y, by_d, out_found), grad_tokens = stage(
            [(to_x, "x"), (to_y, "y"), (to_d, across(5)), (out_send, "c")], tokens_grads, [grad_qkv]
        )
        on = jnp.concatenate([to_c, by_x[count:], by_y[count:], by_d[count:]], 0)
        (by_c,), out_parts = stage([(on, "c")], lambda *given: part_sums(*given), [out_keep, out_found])
        diag_top, diag_bottom, x_top, x_bottom, y_top, y_bottom, out_sums = out_parts

        def sums(resid, *gathered):
            gathered = jnp.concatenate(gathered, 0)
            return token_grads(flat_ones, gathered), resid + joined(out_own, first, second)

        started, (qkv_column, output) = stage(
            [(diag_top, "x"), (diag_bottom, "y"), (x_top, "x"), (y_bottom, "y")],
            sums,
            [resid, own, by_x[:count], by_y[:count], by_d[:count], by_c],
        )
        return qkv_column, grad_tokens, output, x_bottom, y_top, out_sums, started

    qkv_column, grad_tokens, output, x_bottom, y_top, out_sums, started = boxed(
        sure,
        collect,
        after(grad_qkv, columns[1]),
        first,
        second,
        out_own,
        out_keep,
        out_send,
        grad_resid,
        resid,
        qkv_blocks,
        flat_ones,
        scale_one,
        tokens,
    )
    qkv_low = lax.psum_scatter(qkv_column, "z", scatter_dimension=0, tiled=True)

    def end(x_bottom, y_top, out_sums, started):
        x_bottom, y_top = total(x_bottom, started[1]).astype(low), total(y_top, started[0]).astype(low)
        received, _ = stage([(x_bottom, "x"), (y_top, "y")])
        column = joined(out_sums, started, received).astype(low)
        return column.reshape(-1, column.shape[-1])

    out_column = boxed(sure, end, after(x_bottom, columns[-1]), y_top, out_sums, started)
    out_sum = lax.psum_scatter(out_column, "z", scatter_dimension=0, tiled=True).astype(f32)
    every = jnp.concatenate(columns, 1)
    every = after(every, out_column).reshape(8, -1, every.shape[1])
    every = lax.all_to_all(every, PLANE, split_axis=0, concat_axis=0, tiled=True)
    deep = qkv_low.shape[1]
    qkv_sum = after(qkv_low, every).reshape(8, -1, deep)
    qkv_sum = lax.all_to_all(qkv_sum, PLANE, split_axis=0, concat_axis=0, tiled=True)
    qkv_sum = jnp.swapaxes(qkv_sum, 0, 1).reshape(-1, 8 * deep).astype(f32)
    query_sum = qkv_sum[:, :wide]
    key_sum = qkv_sum[:, wide : wide + size]
    value_sum = qkv_sum[:, wide + size :]
    grad_attn_gain = (
        jnp.sum(query_weight.astype(f32) * query_sum, axis=1)
        + jnp.sum(key_weight.astype(f32) * key_sum, axis=1)
        + jnp.sum(value_weight.astype(f32) * value_sum, axis=1)
    )
    grad_gate, grad_up, grad_down, grad_mlp_gain = finish(spans, part, per, gain_two, gate_weight, up_weight, every)
    return (
        output[None],
        grad_tokens[None],
        grad_attn_gain,
        query_sum * gain_one,
        key_sum * gain_one,
        value_sum * gain_one,
        out_sum.T,
        grad_mlp_gain[:, 0],
        grad_gate,
        grad_up,
        grad_down.T,
    )


def solution(mesh):
    ctx, fsdp = mesh.shape["ctx"], mesh.shape["fsdp"]
    fine = Mesh(mesh.devices.reshape(ctx // 4, 2, 2, fsdp), ("z", "y", "c", "x"))
    rows = ("z", "y", "c")
    every = ("z", "y", "c", "x")
    return jax.shard_map(
        local,
        mesh=fine,
        in_specs=(
            P("x", rows, None),
            P("x", rows),
            P(every),
            P(every, None),
            P(every, None),
            P(every, None),
            P(None, every),
            P(every),
            P(every, None),
            P(every, None),
            P(None, every),
            P("x", rows, None),
        ),
        out_specs=(
            P("x", rows, None),
            P("x", rows, None),
            P(every),
            P(every, None),
            P(every, None),
            P(every, None),
            P(None, every),
            P(every),
            P(every, None),
            P(every, None),
            P(None, every),
        ),
        check_vma=False,
    )
```

```python
import functools

import jax
import jax.numpy as jnp
from jax import lax
from jax.experimental import pallas as pl
from jax.experimental.pallas import tpu as pltpu
from jax.sharding import Mesh, PartitionSpec as P

WINDOW = 2048
SUB = 128
TILE = 512
BROAD = 1280
epsilon = 1e-06
blocked_score = -1e30
PLANE = ("y", "c", "x")
low = jnp.bfloat16
f32 = jnp.float32
NOMINAL = pl.CostEstimate(flops=1 << 20, bytes_accessed=1 << 12, transcendentals=0)


def dot(left, right, contract, kind=f32):
    return lax.dot_general(
        left, right, ((contract[:1], contract[1:]), ((), ())), preferred_element_type=f32
    ).astype(kind)


def swap(value, axis):
    return lax.ppermute(value, axis, [(0, 1), (1, 0)])


def plane_gather(own, second=(), third=()):
    half = own.shape[0] // 2
    by_x = swap(own, "x")
    by_y = swap(own, "y")
    own_c = swap(own, "c")
    diag = (
        swap(after(by_y[:half], *second), "x"),
        swap(after(by_x[half:], *second), "y"),
    )
    by_x_c = swap(after(by_x, *second), "c")
    by_y_c = swap(after(by_y, *second), "c")
    diag_c = tuple(swap(after(part, *third), "c") for part in diag)
    return [own, by_x, own_c, by_x_c, by_y, diag, by_y_c, diag_c]


def joined_blocks(blocks):
    return [jnp.concatenate(block, 0) if isinstance(block, tuple) else block for block in blocks]


def stage(sends, work=None, given=()):
    fenced, given = lax.optimization_barrier((tuple(value for value, _ in sends), tuple(given)))
    received = tuple(
        swap(value, way) if isinstance(way, str) else way(value) for value, (_, way) in zip(fenced, sends)
    )
    return lax.optimization_barrier((received, work(*given) if work else given))


def boxed(sure, work, *given):
    shapes = jax.eval_shape(work, *given)
    return lax.cond(
        sure, work, lambda *_: jax.tree.map(lambda out: jnp.zeros(out.shape, out.dtype), shapes), *given
    )


def plane_index():
    return (lax.axis_index("y") * 2 + lax.axis_index("c")) * 2 + lax.axis_index("x")


def after(value, *earlier):
    return lax.optimization_barrier((value,) + earlier)[0]


def across(distance):
    return lambda value: lax.ppermute(value, PLANE, [(i, i ^ distance) for i in range(8)])


def behind(steps):
    count = lax.axis_size("z") * lax.axis_size("y")
    pairs = [(i, i + steps) for i in range(count) if 0 <= i + steps < count]
    return lambda value: lax.ppermute(value, ("z", "y"), pairs)


def two_heads(block, size):
    return jnp.concatenate([block[:, :size], block[:, size:]], 0)


def side_by_side(rows, size):
    half = rows.shape[0] // 2
    return jnp.concatenate([rows[:half], rows[half:]], 1)


def write_bias(bias, places, span, block):
    key = lax.broadcasted_iota(jnp.int32, (span, SUB), 0) - WINDOW
    query = lax.broadcasted_iota(jnp.int32, (span, SUB), 1)
    age = query - key
    seen = (age <= places) & (age >= 0) & (age < WINDOW)
    value = jnp.where(seen, 0.0, blocked_score).astype(f32)
    bias[:, :SUB] = value
    bias[:, SUB:] = value


def lay_window(core, blocks, window, turned, columns):
    count = blocks[0].shape[0]
    half = len(blocks) // 2
    for i in range(half):
        for which, block in ((core, blocks[i]), (1 - core, blocks[half + i])):
            at = pl.multiple_of((2 * i + which) * count, SUB)
            window[pl.ds(at, count), :] = block[...]
            turned[:, pl.ds(at, count)] = block[:, columns].T


def chunks(span, number):
    tiles = span // 128
    return [(128 * (tiles * i // number), 128 * (tiles * (i + 1) // number)) for i in range(number)]


def attend_kernel(size, scale, span, base, core, places, queries, *rest):
    blocks, (mixed, wide, logs, bias, window, turned) = rest[:-6], rest[-6:]
    block = pl.program_id(0)
    count = blocks[0].shape[0]
    start = pl.multiple_of(core[0] * count + base + block * SUB, SUB)

    @pl.when((block == 0) & (pl.program_id(1) == 0))
    def _():
        lay_window(core[0], blocks, window, turned, slice(size, 2 * size))

    @pl.when(pl.program_id(1) == 0)
    def _():
        write_bias(bias, places[...], span, block)

    query = two_heads(queries[...], size) * jnp.asarray(scale, low)
    highest = total = flat = None
    for at, end in chunks(span, 8):
        place = pl.ds(start + at, end - at)
        scores = dot(window[place, :size], query, (1, 1)) + bias[at:end]
        top = jnp.max(scores, axis=0, keepdims=True)
        if highest is not None:
            top = jnp.maximum(highest, top)
            fade = jnp.exp(highest - top)
        highest = top
        expo = jnp.exp(scores - highest)
        part = jnp.sum(expo, axis=0, keepdims=True)
        mix = dot(turned[:, place], expo.astype(low), (1, 0))
        total = part if total is None else total * fade + part
        flat = mix if flat is None else flat * fade + mix
    result = side_by_side((flat / total).T, size)
    wide[...] = result
    mixed[...] = result.astype(low)
    logs[0] = highest + jnp.log(total)


def attend_back_kernel(size, scale, span, base, core, places, queries, grads, wide, logs, *rest):
    blocks, (grad_queries, mine, theirs, bias, window, turned, total) = rest[:-7], rest[-7:]
    block = pl.program_id(0)
    count = blocks[0].shape[0]
    start = pl.multiple_of(core[0] * count + base + block * SUB, SUB)

    @pl.when((block == 0) & (pl.program_id(1) == 0))
    def _():
        lay_window(core[0], blocks, window, turned, slice(0, size))
        total[...] = jnp.zeros_like(total)

    @pl.when(pl.program_id(1) == 0)
    def _():
        write_bias(bias, places[...], span, block)

    query = two_heads(queries[...], size) * jnp.asarray(scale, low)
    grad = two_heads(grads[...], size)
    inner = jnp.sum((grad.astype(f32) * two_heads(wide[...], size)).T, axis=0, keepdims=True)
    place = pl.ds(start, span)
    keys, values = window[place, :size], window[place, size:]
    probs = jnp.exp(dot(keys, query, (1, 1)) + (bias[...] - logs[0]))
    grad_scores = (probs * (dot(values, grad, (1, 1)) - inner)).astype(low)
    total[place, size:] += dot(probs.astype(low), grad, (1, 0))
    total[place, :size] += dot(grad_scores, query, (1, 0))
    flat = dot(turned[:, place], grad_scores, (1, 0)) * scale
    grad_queries[...] = side_by_side(flat.T, size).astype(low)

    @pl.when((block == pl.num_programs(0) - 1) & (pl.program_id(1) == pl.num_programs(1) - 1))
    def _():
        for i in range(len(blocks) // 2):
            at = pl.multiple_of((2 * i + core[0]) * count, SUB)
            mine[i] = total[pl.ds(at, count), :]
            at = pl.multiple_of((2 * i + 1 - core[0]) * count, SUB)
            theirs[i] = total[pl.ds(at, count), :].astype(low)


def attend(queries, blocks, places, size, base):
    count, wide = queries.shape
    grid = (count // SUB, wide // (2 * size))
    span = WINDOW + SUB
    rows = len(blocks) * count
    core = lax.axis_index("c").astype(jnp.int32)[None]
    tile = pl.BlockSpec((SUB, 2 * size), lambda s, h, o: (s, h))
    return pl.pallas_call(
        functools.partial(attend_kernel, size, size**-0.5, span, base),
        out_shape=(
            jax.ShapeDtypeStruct((count, wide), low),
            jax.ShapeDtypeStruct((count, wide), f32),
            jax.ShapeDtypeStruct((grid[0] * grid[1], 1, 2 * SUB), f32),
        ),
        grid_spec=pltpu.PrefetchScalarGridSpec(
            num_scalar_prefetch=1,
            grid=grid,
            in_specs=[pl.BlockSpec((1, SUB), lambda s, h, o: (0, s)), tile]
            + [pl.BlockSpec(block.shape, lambda s, h, o: (0, 0)) for block in blocks],
            out_specs=[tile, tile, pl.BlockSpec((1, 1, 2 * SUB), lambda s, h, o: (s * grid[1] + h, 0, 0))],
            scratch_shapes=[
                pltpu.VMEM((span, 2 * SUB), f32),
                pltpu.VMEM((rows, 2 * size), low),
                pltpu.VMEM((size, rows), low),
            ],
        ),
        compiler_params=pltpu.CompilerParams(vmem_limit_bytes=56 << 20),
        cost_estimate=NOMINAL,
    )(core, places, queries, *blocks)


def attend_back(queries, grads, mixed, logs, blocks, places, size, base):
    count, wide = queries.shape
    grid = (count // SUB, wide // (2 * size))
    span = WINDOW + SUB
    rows = len(blocks) * count
    half = len(blocks) // 2
    core = lax.axis_index("c").astype(jnp.int32)[None]
    tile = pl.BlockSpec((SUB, 2 * size), lambda s, h, o: (s, h))
    whole = pl.BlockSpec((half, count, 2 * size), lambda s, h, o: (0, 0, 0))
    return pl.pallas_call(
        functools.partial(attend_back_kernel, size, size**-0.5, span, base),
        out_shape=(
            jax.ShapeDtypeStruct((count, wide), low),
            jax.ShapeDtypeStruct((half, count, 2 * size), f32),
            jax.ShapeDtypeStruct((half, count, 2 * size), low),
        ),
        grid_spec=pltpu.PrefetchScalarGridSpec(
            num_scalar_prefetch=1,
            grid=grid,
            in_specs=[
                pl.BlockSpec((1, SUB), lambda s, h, o: (0, s)),
                tile,
                tile,
                tile,
                pl.BlockSpec((1, 1, 2 * SUB), lambda s, h, o: (s * grid[1] + h, 0, 0)),
            ]
            + [pl.BlockSpec(block.shape, lambda s, h, o: (0, 0)) for block in blocks],
            out_specs=[tile, whole, whole],
            scratch_shapes=[
                pltpu.VMEM((span, 2 * SUB), f32),
                pltpu.VMEM((rows, 2 * size), low),
                pltpu.VMEM((size, rows), low),
                pltpu.VMEM((rows, 2 * size), f32),
            ],
        ),
        compiler_params=pltpu.CompilerParams(vmem_limit_bytes=60 << 20),
        cost_estimate=NOMINAL,
    )(core, places, queries, grads, mixed, logs, *blocks)


def lay_rows(slots, layout, pieces, full):
    for (r, first), piece in zip(layout, pieces):
        planes, rows, _ = piece.shape
        for plane in range(planes):
            at = pl.multiple_of(((first + plane) * 8 + slots[r]) * rows, 16)
            full[pl.ds(at, rows), :] = piece[plane]


def apply_kernel(layout, slots, left, *rest):
    *pieces, out, full = rest
    lay_rows(slots, layout, pieces, full)
    out[...] = dot(left[...], full[...], (1, 0), low)


def apply_turned_kernel(layout, slots, left, *rest):
    *start, out, full = rest
    start, pieces = start[: -len(layout)], start[-len(layout) :]
    lay_rows(slots, layout, pieces, full)

    @pl.when(pl.program_id(0) == 0)
    def _():
        out[...] = start[0][...] if start else jnp.zeros_like(out)

    out[...] += dot(left[...], full[...], (1, 1))


def whole_rows(blocks):
    planes, rows, wide = blocks[0].shape
    here = plane_index()
    whole = jnp.zeros((planes, 8, rows, wide), blocks[0].dtype)
    for r, block in enumerate(blocks):
        whole = lax.dynamic_update_slice(whole, block[:, None], (0, here ^ r, 0, 0))
    return whole.reshape(planes * 8 * rows, wide)


def apply_rows(left, blocks, turned=False, start=None):
    planes, rows, wide = blocks[0].shape
    if rows % 16 or wide % TILE:
        whole = whole_rows(joined_blocks(blocks))
        if not turned:
            return dot(left, whole, (1, 0), low)
        return dot(left, whole, (1, 1)) + (0.0 if start is None else start)
    count, deep = left.shape[0], planes * 8 * rows
    slots = (plane_index() ^ jnp.arange(8)).astype(jnp.int32)
    layout, blocks = [], [block if isinstance(block, tuple) else (block,) for block in blocks]
    for r, block in enumerate(blocks):
        layout += [(r, sum(piece.shape[0] for piece in block[:i])) for i in range(len(block))]
    blocks = [piece for block in blocks for piece in block]
    pieces = [pl.BlockSpec((piece.shape[0], rows, TILE), lambda n, s: (0, 0, n)) for piece in blocks]
    whole = pl.BlockSpec((count, deep), lambda n, s: (0, 0))
    part = pl.BlockSpec((count, TILE), lambda n, s: (0, n))
    if not turned:
        kernel, given, specs, result = apply_kernel, [left], [whole], part
        shape = jax.ShapeDtypeStruct((count, wide), low)
    else:
        kernel, given, specs, result = apply_turned_kernel, [left], [part], whole
        if start is not None:
            given, specs = given + [start], specs + [whole]
        shape = jax.ShapeDtypeStruct((count, deep), f32)
    return pl.pallas_call(
        functools.partial(kernel, layout),
        out_shape=shape,
        grid_spec=pltpu.PrefetchScalarGridSpec(
            num_scalar_prefetch=1,
            grid=(wide // TILE,),
            in_specs=specs + pieces,
            out_specs=result,
            scratch_shapes=[pltpu.VMEM((deep, TILE), low)],
        ),
        compiler_params=pltpu.CompilerParams(vmem_limit_bytes=48 << 20),
        cost_estimate=NOMINAL,
    )(slots, *given, *blocks)


def row_grads_kernel(slots, left, right, keep, send, turned):
    @pl.when(pl.program_id(1) == 0)
    def _():
        turned[...] = left[...].T

    rows = keep.shape[2]
    value = dot(turned[...], right[...], (1, 0), low)
    for i in range(8):
        place = slots[i]

        @pl.when(place < 4)
        def _():
            keep[place, 0] = value[i * rows : (i + 1) * rows]

        @pl.when(place >= 4)
        def _():
            send[place - 4, 0] = value[i * rows : (i + 1) * rows]


def row_grads(left, right):
    planes = lax.axis_size("z")
    count, deep = left.shape
    wide = right.shape[1]
    rows = deep // (planes * 8)
    places = jnp.array([3, 1, 7, 5, 2, 0, 6, 4], jnp.int32)
    slots = places[plane_index() ^ jnp.arange(8)]
    if rows % 16 or wide % TILE or (planes * 8 * rows) % (planes * 128):
        blocks = dot(left, right, (0, 0), low).reshape(planes, 8, rows, wide)
        order = jnp.argsort(slots)
        blocks = jnp.swapaxes(jnp.take(blocks, order, axis=1), 0, 1)
        return blocks[:4], blocks[4:]
    tile = wide if wide <= 5 * TILE else TILE
    group = pl.BlockSpec((4, 1, rows, tile), lambda z, n, s: (0, z, 0, n))
    shape = jax.ShapeDtypeStruct((4, planes, rows, wide), low)
    return pl.pallas_call(
        row_grads_kernel,
        out_shape=(shape, shape),
        grid_spec=pltpu.PrefetchScalarGridSpec(
            num_scalar_prefetch=1,
            grid=(planes, wide // tile),
            in_specs=[
                pl.BlockSpec((count, 8 * rows), lambda z, n, s: (0, z)),
                pl.BlockSpec((count, tile), lambda z, n, s: (0, n)),
            ],
            out_specs=[group, group],
            scratch_shapes=[pltpu.VMEM((8 * rows, count), low)],
        ),
        compiler_params=pltpu.CompilerParams(vmem_limit_bytes=48 << 20),
        cost_estimate=NOMINAL,
    )(slots, left, right)


def mlp_kernel(part, per, tiles, *rest):
    weights, rest = rest[:per], rest[per:]
    pieces = 2 * sum(tiles)
    sources, rest = rest[:pieces], rest[pieces:]
    before, rest = rest[:-8], rest[-8:]
    outs, grad_units, hidden, units, grads, arrived = rest[0:2], rest[2:4], *rest[4:]
    step = pl.program_id(0)

    def fetches(tile):
        first = 2 * sum(tiles[:tile])
        found = []
        for array, target in enumerate((units, grads)):
            at = 0
            for i in range(tiles[tile]):
                source = sources[first + array * tiles[tile] + i]
                found.append(
                    pltpu.make_async_copy(
                        source,
                        target.at[tile % 2, pl.ds(at, source.shape[0])],
                        arrived.at[tile % 2, array, i],
                    )
                )
                at += source.shape[0]
        return found

    for tile in range(len(tiles)):

        @pl.when(step == tile)
        def _():
            if tile == 0:
                for copy in fetches(0):
                    copy.start()
            if tile + 1 < len(tiles):
                for copy in fetches(tile + 1):
                    copy.start()
            for copy in fetches(tile):
                copy.wait()

    slope = 0.7978845608028654
    fronts = []
    for j in range(per):
        both = dot(units[step % 2], weights[j][:, : 2 * part], (1, 0))
        fronts.append((both[:, :part], both[:, part:], dot(grads[step % 2], weights[j][:, 2 * part :], (1, 0))))
    values = [0.0, 0.0]
    for j, (gates, upward, grad_middle) in enumerate(fronts):
        square = gates * gates
        half = 0.5 + 0.5 * jnp.tanh(gates * (slope + slope * 0.044715 * square))
        gelu = gates * half
        grad_gelu = half + gelu * (1.0 - half) * (2 * slope + 6 * slope * 0.044715 * square)
        at = 2 * part * j
        hidden[:, at : at + part] = (grad_middle * upward * grad_gelu).astype(low)
        hidden[:, at + part : at + 2 * part] = (grad_middle * gelu).astype(low)
        at = part * (2 * per + j)
        hidden[:, at : at + part] = (gelu * upward).astype(low)
        for which in range(2):
            at, width = (2 * part * j, 2 * part) if which else (part * (2 * per + j), part)
            first = 0 if which else 2 * part
            part_value = dot(hidden[:, at : at + width], weights[j][:, first : first + width], (1, 1))
            values[which] = values[which] + part_value
    for which, targets in enumerate((outs, grad_units)):
        value = values[which]
        for side in range(2):

            @pl.when(step // (len(tiles) // 2) == side)
            def _():
                if before:
                    targets[side][...] = (value + before[2 * which + side][...].astype(f32)).astype(low)
                else:
                    targets[side][...] = value.astype(low)


def mlp(units, grads, weights, before):
    rows = sum(piece.shape[0] for piece in units[0])
    count, wide = rows * len(units), units[0][0].shape[1]
    per, each = len(weights), weights[0].shape[1]
    deep = per * each
    tiles = tuple(len(tile) for tile in units)
    sources = [piece for pair in zip(units, grads) for tile in pair for piece in tile]
    side = len(units) // 2
    sides = [
        pl.BlockSpec((rows, wide), lambda i: (jnp.minimum(i, side - 1), 0)),
        pl.BlockSpec((rows, wide), lambda i: (jnp.maximum(i - side, 0), 0)),
    ]
    half = jax.ShapeDtypeStruct((count // 2, wide), low)
    return pl.pallas_call(
        functools.partial(mlp_kernel, each // 3, per, tiles),
        out_shape=[half] * 4 + [jax.ShapeDtypeStruct((count, deep), low)],
        grid=(len(units),),
        in_specs=[pl.BlockSpec((wide, each), lambda i: (0, 0), pipeline_mode=pl.Buffered(1))] * per
        + [pl.BlockSpec(memory_space=pl.ANY)] * len(sources)
        + (sides * 2 if before else []),
        out_specs=sides * 2 + [pl.BlockSpec((rows, deep), lambda i: (i, 0))],
        scratch_shapes=[
            pltpu.VMEM((2, rows, wide), low),
            pltpu.VMEM((2, rows, wide), low),
            pltpu.SemaphoreType.DMA((2, 2, max(tiles))),
        ],
        compiler_params=pltpu.CompilerParams(vmem_limit_bytes=62 << 20),
        cost_estimate=NOMINAL,
    )(*weights, *sources, *before)


def mlp_grads_kernel(number, *rest):
    units, grads, hidden, rest = rest[:number], rest[number : 2 * number], rest[2 * number : 2 * number + 2], rest[2 * number + 2 :]
    *outs, turned = rest
    step = pl.program_id(0)
    part = hidden[0].shape[1] // 3
    piece = 256 if part % 256 == 0 and outs[0].shape[1] % 256 == 0 else 128
    places = [(out, at) for out in outs for at in range(0, out.shape[1], piece)]

    def turn(slot, which, sources, share, shares):
        at = 0
        for i, source in enumerate(sources):
            if i * shares // len(sources) == share:
                turned[slot, which, :, at : at + source.shape[0]] = source[...].T
            at += source.shape[0]

    def multiply(slot, which, i, at):
        value, start = 0.0, 0
        for block in hidden:
            left = turned[slot, which, :, start : start + block.shape[0]]
            value = value + dot(left, block[:, at : at + piece], (1, 0))
            start += block.shape[0]
        out, place = places[i]
        out[:, place : place + piece] = value.astype(low)

    work = [(at // (2 * part), at) for at in range(0, 3 * part, piece)]

    @pl.when(step == 0)
    def _():
        turn(0, 0, units, 0, 1)
        turn(0, 1, grads, 0, 1)

    @pl.when(step > 0)
    def _():
        for i, (which, at) in enumerate(work):
            multiply((step - 1) % 2, which, i, at)
            turn(step % 2, 0, units, i, len(work))
            turn(step % 2, 1, grads, i, len(work))


def mlp_grads(units, grads, hidden, pieces=(2,)):
    wide = units[0].shape[1]
    deep = hidden[0].shape[1]
    count = sum(piece.shape[0] for piece in units)
    rows = 512
    last = wide // rows - 1
    return pl.pallas_call(
        functools.partial(mlp_grads_kernel, len(units)),
        out_shape=[jax.ShapeDtypeStruct((wide, deep // 2 * piece), low) for piece in pieces],
        grid=(last + 2,),
        in_specs=[
            pl.BlockSpec((piece.shape[0], rows), lambda s: (0, jnp.minimum(s, last))) for piece in units + grads
        ]
        + [pl.BlockSpec(piece.shape, lambda s: (0, 0), pipeline_mode=pl.Buffered(1)) for piece in hidden],
        out_specs=[
            pl.BlockSpec((rows, deep // 2 * piece), lambda s: (jnp.maximum(s - 1, 0), 0)) for piece in pieces
        ],
        scratch_shapes=[pltpu.VMEM((2, 2, rows, count), low)],
        compiler_params=pltpu.CompilerParams(vmem_limit_bytes=62 << 20),
        cost_estimate=NOMINAL,
    )(*units, *grads, *hidden)


def token_grads_kernel(number, *rest):
    units, (right, out, turned) = rest[:number], rest[number:]

    @pl.when(pl.program_id(0) == 0)
    def _():
        turned[...] = right[...].T

    value, at = 0.0, 0
    for unit in units:
        value = value + dot(turned[:, at : at + unit.shape[0]], unit[...], (1, 0))
        at += unit.shape[0]
    out[...] = value.astype(low).T


def token_grads(units, right):
    wide = units[0].shape[1]
    count, deep = right.shape
    rows = 512
    return pl.pallas_call(
        functools.partial(token_grads_kernel, len(units)),
        out_shape=jax.ShapeDtypeStruct((wide, deep), low),
        grid=(wide // rows,),
        in_specs=[pl.BlockSpec((piece.shape[0], rows), lambda s: (0, s)) for piece in units]
        + [pl.BlockSpec(right.shape, lambda s: (0, 0), pipeline_mode=pl.Buffered(1))],
        out_specs=pl.BlockSpec((rows, deep), lambda s: (s, 0)),
        scratch_shapes=[pltpu.VMEM((deep, count), low)],
        compiler_params=pltpu.CompilerParams(vmem_limit_bytes=56 << 20),
        cost_estimate=NOMINAL,
    )(*units, right)


def spread_kernel(slots, value, *outs):
    count, deep = value.shape[0], outs[0].shape[1]
    place = 0
    for out in outs:
        for at in range(0, out.shape[0], count):
            out[at : at + count, :] = value[:, pl.ds(pl.multiple_of(slots[place] * deep, 128), deep)]
            place += 1


def spread(value):
    count, wide = value.shape
    slots = (plane_index() ^ jnp.array(ORDER)).astype(jnp.int32)
    deep = wide // 8
    rows = (count, count, 2 * count, 2 * count, 2 * count)
    if deep % 128:
        pieces = [lax.dynamic_slice(value, (0, slots[i] * deep), (count, deep)) for i in range(8)]
        return pieces[:2] + [jnp.concatenate(pieces[i : i + 2], 0) for i in (2, 4, 6)]
    return pl.pallas_call(
        spread_kernel,
        out_shape=[jax.ShapeDtypeStruct((n, deep), value.dtype) for n in rows],
        grid_spec=pltpu.PrefetchScalarGridSpec(
            num_scalar_prefetch=1,
            grid=(1,),
            in_specs=[pl.BlockSpec((count, wide), lambda i, s: (0, 0))],
            out_specs=[pl.BlockSpec((n, deep), lambda i, s: (0, 0)) for n in rows],
        ),
        cost_estimate=NOMINAL,
    )(slots, value)


ORDER = (0, 2, 1, 3, 4, 6, 5, 7)


def deal_kernel(slots, value, *outs):
    place = 0
    for out in outs:
        for i in range(out.shape[0]):
            out[i] = value[slots[place]]
            place += 1


def deal(value):
    _, rows, wide = value.shape
    slots = (plane_index() ^ jnp.array(ORDER)).astype(jnp.int32)
    sizes = (1, 1, 2, 2, 2)
    return pl.pallas_call(
        deal_kernel,
        out_shape=[jax.ShapeDtypeStruct((n, rows, wide), value.dtype) for n in sizes],
        grid_spec=pltpu.PrefetchScalarGridSpec(
            num_scalar_prefetch=1,
            grid=(1,),
            in_specs=[pl.BlockSpec(value.shape, lambda i, s: (0, 0, 0))],
            out_specs=[pl.BlockSpec((n, rows, wide), lambda i, s: (0, 0, 0)) for n in sizes],
        ),
        compiler_params=pltpu.CompilerParams(vmem_limit_bytes=48 << 20),
        cost_estimate=NOMINAL,
    )(slots, value)


def turn_kernel(keep, found, far, diag_x, diag_y, y_bottom, x_bottom, y_top):
    half = far.shape[0]
    both = keep[...].astype(f32) + found[...].astype(f32)
    y_top[...] = (both[:half] + diag_x[...].astype(f32)).astype(low)
    y_bottom[...] = both[half:].astype(low)
    x_bottom[...] = (far[...].astype(f32) + diag_y[...].astype(f32)).astype(low)


def turn(keep, found, far, diag_x, diag_y):
    half, wide = far.shape
    tile = BROAD if wide % BROAD == 0 else wide
    part = lambda rows: pl.BlockSpec((rows, tile), lambda n: (0, n))
    return pl.pallas_call(
        turn_kernel,
        out_shape=[jax.ShapeDtypeStruct((half, wide), low)] * 3,
        grid=(wide // tile,),
        in_specs=[part(2 * half)] * 2 + [part(half)] * 3,
        out_specs=[part(half)] * 3,
        cost_estimate=NOMINAL,
    )(keep, found, far, diag_x, diag_y)


def halved_kernel(keep, found, *outs):
    half = outs[0].shape[0]
    for i, out in enumerate(outs):
        rows = slice(i * half, i * half + half)
        out[...] = (keep[rows].astype(f32) + found[rows].astype(f32)).astype(low)


def halved(keep, found):
    count, wide = keep.shape
    tile = BROAD if wide % BROAD == 0 else wide
    part = lambda rows: pl.BlockSpec((rows, tile), lambda n: (0, n))
    return pl.pallas_call(
        halved_kernel,
        out_shape=[jax.ShapeDtypeStruct((count // 4, wide), low)] * 4,
        grid=(wide // tile,),
        in_specs=[part(count)] * 2,
        out_specs=[part(count // 4)] * 4,
        cost_estimate=NOMINAL,
    )(keep, found)


def resid_kernel(steps, keep, found, x_top, x_bottom, y_top, y_bottom, resid, gift, scale, grad_out, grad_low):
    upper = pl.program_id(0) < steps
    x_part = jnp.where(upper, x_top[...].astype(f32), x_bottom[...].astype(f32))
    y_part = jnp.where(upper, y_top[...].astype(f32), y_bottom[...].astype(f32))
    grad = keep[...].astype(f32) + found[...].astype(f32) + x_part + y_part
    grad = gift[...].astype(f32) + unit_back(grad, resid[...], scale[...])
    grad_out[...] = grad
    grad_low[...] = grad.astype(low)


def resid_grads(keep, found, x_top, x_bottom, y_top, y_bottom, resid, gift, scale):
    count, wide = resid.shape
    rows = 96
    steps = count // (2 * rows)
    row = pl.BlockSpec((rows, wide), lambda i: (i, 0))
    own = pl.BlockSpec((rows, wide), lambda i: (i + 2 * steps, 0))
    first = pl.BlockSpec((rows, wide), lambda i: (jnp.minimum(i, steps - 1), 0))
    last = pl.BlockSpec((rows, wide), lambda i: (jnp.maximum(i - steps, 0), 0))
    return pl.pallas_call(
        functools.partial(resid_kernel, steps),
        out_shape=(jax.ShapeDtypeStruct((count, wide), f32), jax.ShapeDtypeStruct((count, wide), low)),
        grid=(2 * steps,),
        in_specs=[own, own, first, last, first, last, row, row, pl.BlockSpec((rows, 1), lambda i: (i, 0))],
        out_specs=(row, row),
        cost_estimate=NOMINAL,
    )(keep, found, x_top, x_bottom, y_top, y_bottom, resid, gift, scale)


def part_sums_kernel(keep, found, diag_top, diag_bottom, x_top, x_bottom, y_top, y_bottom, own):
    half = diag_top.shape[0]

    def both(place, first, rows):
        part = slice(first, first + rows)
        return (keep[place, part].astype(f32) + found[place, part].astype(f32)).astype(low)

    for place, (top, bottom) in enumerate(((diag_top, diag_bottom), (x_top, x_bottom), (y_top, y_bottom))):
        top[...] = both(place, 0, half)
        bottom[...] = both(place, half, half)
    own[...] = both(3, 0, 2 * half)


def part_sums(keep, found):
    _, planes, rows, wide = keep.shape
    tile = BROAD if wide % BROAD == 0 else wide
    four = pl.BlockSpec((4, planes, rows, tile), lambda n: (0, 0, 0, n))
    some = lambda planes: pl.BlockSpec((planes, rows, tile), lambda n: (0, 0, n))
    half = planes // 2
    shape = lambda planes: jax.ShapeDtypeStruct((planes, rows, wide), low)
    return pl.pallas_call(
        part_sums_kernel,
        out_shape=[shape(half)] * 6 + [shape(planes)],
        grid=(wide // tile,),
        in_specs=[four] * 2,
        out_specs=[some(half)] * 6 + [some(planes)],
        compiler_params=pltpu.CompilerParams(vmem_limit_bytes=48 << 20),
        cost_estimate=NOMINAL,
    )(keep, found)


def pack_kernel(spans, part, gain, gate, up, down, out):
    scale = gain[...]
    share = out.shape[2] // 3
    for p, (at, n) in enumerate(spans):
        for q in range(share // part):
            width = min(part, n - q * part)
            place = slice(at + q * part, at + q * part + width)
            for which, source in enumerate((gate, up, down)):
                first = part * (3 * q + which)
                if width > 0:
                    value = source[:, place]
                    if which < 2:
                        value = (value.astype(f32) * scale).astype(low)
                    out[p, :, first : first + width] = value
                if width < part:
                    empty = max(width, 0)
                    out[p, :, first + empty : first + part] = jnp.zeros((out.shape[1], part - empty), low)


def pack(spans, part, share, gain, gate, up, down):
    rows, _ = gate.shape
    return pl.pallas_call(
        functools.partial(pack_kernel, spans, part),
        out_shape=jax.ShapeDtypeStruct((8, rows, 3 * share), low),
        compiler_params=pltpu.CompilerParams(vmem_limit_bytes=48 << 20),
        cost_estimate=NOMINAL,
    )(gain, gate, up, down)


def shares(columns):
    tiles = -(-columns // 128)
    few, more = divmod(tiles, 8)
    sizes = [128 * (few + (p < more)) for p in range(8)]
    return [(sum(sizes[:p]), size) for p, size in enumerate(sizes)], 128 * (few + (more > 0))


def finish_kernel(spans, part, per, first_part, starts, gain, gate, up, whole, *rest):
    *early, gate_out, up_out, down_out, gain_out = rest
    scale = gain[...]
    total = jnp.zeros_like(scale)

    def lay(piece, start, j, place, width):
        added = jnp.zeros_like(scale)
        for which, (weight, out) in enumerate(((gate, gate_out), (up, up_out))):
            first = start + part * (2 * j + which)
            value = piece[:, first : first + width].astype(f32)
            added = added + jnp.sum(value * weight[:, place].astype(f32), axis=1, keepdims=True)
            out[:, place] = value * scale
        first = start + part * (2 * per + j)
        down_out[:, place] = piece[:, first : first + width].astype(f32)
        return added

    for p, (at, n) in enumerate(spans):
        for q in range(first_part, -(-n // part)):
            width = min(part, n - q * part)
            start = 3 * part * per * (q // per) - 3 * part * first_part
            total = total + lay(whole.at[p], start, q % per, slice(at + q * part, at + q * part + width), width)
    place = 0
    for pieces in early:
        for i in range(pieces.shape[0]):
            for q in range(first_part):
                at = pl.multiple_of(starts[place] + q * part, 128)
                total = total + lay(pieces.at[i], 0, q, pl.ds(at, part), part)
            place += 1
    gain_out[...] = total


def finish(spans, part, per, gain, gate, up, whole, early):
    rows, columns = gate.shape
    order = [r for r in (0, 1, 4, 5, 2, 3, 6, 7)]
    starts = jnp.array([at for at, _ in spans], jnp.int32)[plane_index() ^ jnp.array(order)]
    block = lambda shape: pl.BlockSpec(shape, lambda i, s: (0,) * len(shape))
    given = (gain, gate, up, whole, *early)
    shapes = ((rows, columns), (rows, columns), (rows, columns), (rows, 1))
    return pl.pallas_call(
        functools.partial(finish_kernel, spans, part, per, per if early else 0),
        out_shape=[jax.ShapeDtypeStruct(shape, f32) for shape in shapes],
        grid_spec=pltpu.PrefetchScalarGridSpec(
            num_scalar_prefetch=1,
            grid=(1,),
            in_specs=[block(value.shape) for value in given],
            out_specs=[block(shape) for shape in shapes],
        ),
        compiler_params=pltpu.CompilerParams(vmem_limit_bytes=56 << 20),
        cost_estimate=NOMINAL,
    )(starts, *given)


def unit_of(values):
    scale = lax.rsqrt(jnp.mean(values * values, axis=-1, keepdims=True) + epsilon)
    return scale, (values * scale).astype(low)


def unit_back(grad, values, scale):
    unit = values * scale
    return scale * (grad - unit * jnp.mean(grad * unit, axis=-1, keepdims=True))


def local(
    tokens,
    positions,
    attn_gain,
    query_weight,
    key_weight,
    value_weight,
    out_weight,
    mlp_gain,
    gate_weight,
    up_weight,
    down_weight,
    cotangent,
):
    count = tokens.shape[1]
    size = key_weight.shape[1]
    wide = query_weight.shape[1]
    reach = (WINDOW + count - 2) // count
    chips = (reach + 1) // 2
    base = 2 * chips * count - WINDOW
    gain_one = attn_gain[:, None]
    gain_two = mlp_gain[:, None]

    qkv_shard = jnp.concatenate([query_weight, key_weight, value_weight], 1).astype(f32) * gain_one
    qkv_shard = qkv_shard.astype(low)
    qkv_column = lax.all_gather(qkv_shard, "z", axis=0, tiled=False)
    out_column = lax.all_gather(after(out_weight.T, qkv_shard), "z", axis=0, tiled=False)

    spans, share = shares(gate_weight.shape[1])
    parts = share // 256 if share % 256 == 0 else 1
    calls = 2 if parts % 2 == 0 else 1
    per = parts // calls
    part = share // parts
    mine = pack(spans, part, share, after(gain_two, qkv_shard), gate_weight, up_weight, down_weight.T)
    gift = cotangent[0]
    mlp_column = lax.all_to_all(mine, PLANE, split_axis=0, concat_axis=0, tiled=True)
    mlp_column = mlp_column.reshape(-1, 3 * share)

    def piece_of(k, column):
        return column[:, k * 3 * part : (k + 1) * 3 * part]

    def gathered(piece):
        return lax.all_gather(piece, "z", axis=0, tiled=True)

    mlp_full = [gathered(piece_of(0, mlp_column))]
    sure = positions[0, 0] >= 0
    half = count // 2

    def project(qkv_column, tokens, gift, mlp_column):
        qkv_blocks = plane_gather(qkv_column)
        scale_one, unit_one = unit_of(tokens[0].astype(f32))
        qkv = apply_rows(unit_one, qkv_blocks)
        queries, pair = qkv[:, :wide], qkv[:, wide:]
        moves = [behind(d) for d in range(chips, 0, -1)]
        found, pieces = stage(
            [(pair, move) for move in moves] + [(pair, "c"), (gift, "x"), (gift, "y"), (gift, "c")],
            lambda column: [piece_of(k, column) for k in range(1, parts)],
            [mlp_column],
        )
        *pairs, pair_c, gift_x, gift_y, gift_c = found
        found, _ = stage([(block, "c") for block in pairs])
        gifts = gift_x, gift_y, gift_c
        return qkv_blocks[1:], queries, [*pairs, pair, *found, pair_c], gifts, unit_one, scale_one, pieces

    def forward(queries, pairs, out_column, tokens, positions, gift_x, gift_y):
        inputs = tokens[0].astype(f32)
        mid = out_column.shape[0] // 2
        (out_x, out_y, out_c, gift_x_c, gift_y_c), (mixed, mixed_wide, logs) = stage(
            [(out_column, "x"), (out_column, "y"), (out_column, "c"), (gift_x, "c"), (gift_y, "c")],
            lambda *given: attend(given[0], given[1:], positions, size, base),
            [queries, *pairs],
        )
        (out_top, out_bottom, out_x_c, out_y_c), _ = stage(
            [(out_y[:mid], "x"), (out_x[mid:], "y"), (out_x, "c"), (out_y, "c")]
        )
        out_diag_c, _ = stage([(out_top, "c"), (out_bottom, "c")])
        out_blocks = [out_column, out_x, out_c, out_x_c, out_y, (out_top, out_bottom), out_y_c, out_diag_c]
        resid = apply_rows(mixed, out_blocks, True, inputs)
        scale_two, unit_two = unit_of(resid)
        (unit_x, unit_y, unit_c), _ = stage([(unit_two, "x"), (unit_two, "y"), (unit_two, "c")])
        (unit_x_c, unit_y_c), _ = stage([(unit_x, "c"), (unit_y, "c")])
        unit_blocks = unit_two, unit_x, unit_c, unit_x_c, unit_y, unit_y_c
        return out_blocks[1:], mixed, mixed_wide, logs, resid, scale_two, unit_blocks, gift_x_c, gift_y_c

    qkv_column = after(qkv_column, mlp_column)
    qkv_blocks, queries, pairs, gifts, unit_one, scale_one, pieces = boxed(
        sure, project, qkv_column, tokens, gift, mlp_column
    )
    gift_x, gift_y, gift_c = gifts
    mlp_full += [gathered(piece) for piece in pieces]
    out_blocks, mixed, mixed_wide, logs, resid, scale_two, unit_blocks, gift_x_c, gift_y_c = boxed(
        sure, forward, after(queries, mlp_full[0]), pairs, out_column, tokens, positions, gift_x, gift_y
    )
    qkv_blocks, out_blocks = [qkv_column, *qkv_blocks], [out_column, *out_blocks]
    grads_near = [(gift_y,), (gift,), (gift_y_c,), (gift_c,)]

    def flat(*tiles):
        return [piece for group in tiles for tile in group for piece in tile]

    def summed(keep, received):
        return keep.astype(f32) + received.astype(f32)

    def halves(value):
        middle = value.shape[0] // 2
        return value[:middle], value[middle:]

    def total(*values):
        return sum(value.astype(f32) for value in values)

    def opening(weights, blocks, gift_x, gift_x_c, grads_near, unit_one):
        unit_two, unit_x, unit_c, unit_x_c, unit_y, unit_y_c = blocks
        units_near = [(unit_y,), (unit_two,), (unit_y_c,), (unit_c,)]
        gift_y = grads_near[0][0]
        sends = [(unit_y, "x"), (gift_x, "y")]
        one_sends = [(unit_one, "x"), (unit_one, "y"), (unit_one, "c")]
        far_sums = near_sums = partial = ()
        if calls > 1:
            (unit_d, gift_d), near_sums = stage(
                sends, lambda *given: mlp([(v,) for v in given], grads_near, weights, ()), flat(units_near)
            )
        else:
            (unit_d, gift_d), _ = stage(sends)
        (unit_d_c, gift_d_c), _ = stage([(unit_d, "c"), (gift_d, "c")])
        units_far = [(unit_d,), (unit_x,), (unit_d_c,), (unit_x_c,)]
        grads_far = [(gift_d,), (gift_x,), (gift_d_c,), (gift_x_c,)]
        if calls > 1:
            (one_x, one_y, one_c), far_sums = stage(
                one_sends, lambda weights: mlp(units_far, grads_far, weights, ()), [weights]
            )
        else:
            (one_x, one_y, one_c), _ = stage(one_sends)
        one_sends = [(one_y, "x"), (one_x, "c"), (one_y, "c")]
        if calls > 1:
            (one_d, one_x_c, one_y_c), partial = stage(
                one_sends,
                lambda *given: mlp_grads(flat(units_far, units_near), flat(grads_far, grads_near), given)[0],
                [far_sums[4], near_sums[4]],
            )
        else:
            (one_d, one_x_c, one_y_c), _ = stage(one_sends)
        ones = one_x, one_c, one_x_c, one_y, one_d, one_y_c
        return (unit_d, unit_d_c), (gift_d, gift_d_c), far_sums[:4], near_sums[:4], partial, ones

    columns = []
    unit_two, unit_x, unit_c, unit_x_c, unit_y, unit_y_c = unit_blocks
    unit_far, gift_far, far_before, near_before, partial, ones = boxed(
        sure, opening, mlp_full[:per] if calls > 1 else (), unit_blocks, gift_x, gift_x_c, grads_near, unit_one
    )
    if calls > 1:
        columns.append(lax.psum_scatter(partial, "z", scatter_dimension=0, tiled=True))
    unit_d, unit_d_c = unit_far
    gift_d, gift_d_c = gift_far
    grads_far = [(gift_d,), (gift_x,), (gift_d_c,), (gift_x_c,)]
    units_far = [(unit_d,), (unit_x,), (unit_d_c,), (unit_x_c,)]
    units_near = [(unit_y,), (unit_two,), (unit_y_c,), (unit_c,)]

    def middle(weights, units_far, units_near, grads_far, grads_near, far_before, near_before, resid, scale_two, gift, ones):
        (one_d_c,), far_sums = stage(
            [(ones[4], "c")],
            lambda *weights: mlp(units_far, grads_far, weights, far_before),
            weights,
        )
        (found,), _ = stage([(far_sums[3], "c")])
        diag_top, diag_bottom, x_top, x_bottom = halved(far_sums[2], found)
        (diag_x, diag_y, x_top, far_out), near_sums = stage(
            [(diag_top, "x"), (diag_bottom, "y"), (x_top, "x"), (far_sums[1], "c")],
            lambda *given: mlp([(value,) for value in given], grads_near, weights, near_before),
            [tile[0] for tile in units_near],
        )
        (found,), _ = stage([(near_sums[3], "c")])
        y_bottom, x_bottom, y_top = turn(near_sums[2], found, x_bottom, diag_x, diag_y)
        (y_bottom, x_bottom, y_top, near_out), partial = stage(
            [(y_bottom, "y"), (x_bottom, "x"), (y_top, "y"), (near_sums[1], "c")],
            lambda *given: mlp_grads(flat(units_far, units_near), flat(grads_far, grads_near), given, cuts),
            [far_sums[4], near_sums[4]],
        )
        received = x_top, x_bottom, y_top, y_bottom
        outs = far_sums[0], far_out, near_sums[0], near_out
        return partial, (near_sums[2], found, received), outs, one_d_c

    cuts = (1, 1)
    partial, own_sums, outs, one_d_c = boxed(
        sure,
        middle,
        mlp_full[-per:],
        units_far,
        units_near,
        grads_far,
        grads_near,
        far_before,
        near_before,
        resid,
        scale_two,
        gift,
        ones,
    )
    columns += [lax.psum_scatter(piece, "z", scatter_dimension=0, tiled=True) for piece in partial[:1]]
    one_x, one_c, one_x_c, one_y, one_d, one_y_c = ones
    flat_ones = [unit_one, one_x, one_y, one_d, one_c, one_x_c, one_y_c, one_d_c]

    def joined(own, first, second):
        top, bottom = own if isinstance(own, tuple) else halves(own)
        return jnp.concatenate([total(top, first[2], second[1]), total(bottom, second[0], first[3])], 0)

    def backward(
        own_sums, outs, resid, scale_two, gift, queries, pairs, mixed, mixed_wide, logs, out_blocks, positions, early
    ):
        keep, found, received = own_sums

        def remaining(keep, far, near):
            grads = resid_grads(keep, found, *received, resid, gift, scale_two)
            return grads, halved(far, outs[1]), halved(near, outs[3])

        given = keep, outs[0], outs[2]
        if early is not None:
            early_own, to_c, to_x, to_y, to_d = deal(early.reshape(8, -1, early.shape[1]))
            (by_x, by_y, by_d), results = stage([(to_x, "x"), (to_y, "y"), (to_d, across(5))], remaining, given)
            early_on = [(jnp.concatenate([to_c, by_x[1:], by_y[1:], by_d[1:]], 0), "c")]
        else:
            results, early_on = remaining(*given), []
        (grad_resid, grad_attn), out_far, out_near = results

        def attention(grad_attn):
            grad_mixed = apply_rows(grad_attn, out_blocks)
            return attend_back(queries, grad_mixed, mixed_wide, logs, pairs, positions, size, base)

        (*first, on), (grad_queries, mine, theirs) = stage(
            [(out_far[0], "x"), (out_far[1], "y"), (out_far[2], "x"), (out_near[1], "y")]
            + (early_on or [(out_near[1][:16], "c")]),
            attention,
            [grad_attn],
        )
        early = [early_own, by_x[:1], by_y[:1], by_d[:1], on] if early_on else []
        (found,), _ = stage([(theirs, "c")])
        mine = summed(mine, found)
        second = total(out_far[3], first[1]).astype(low), total(out_near[0], first[0]).astype(low)
        (*found, x_second, y_second), (out_keep, out_send) = stage(
            [(mine[chips - d].astype(low), behind(-d)) for d in range(chips, 0, -1)]
            + [(second[0], "x"), (second[1], "y")],
            lambda *given: row_grads(*given),
            [grad_attn, mixed],
        )
        grad_pair = total(mine[chips], *found).astype(low)
        grad_qkv = jnp.concatenate([grad_queries, grad_pair], 1)
        out_own = out_near[2], out_near[3]
        return grad_qkv, grad_resid, first, (x_second, y_second), out_keep, out_send, out_own, early

    ahead = calls > 1 and per * part <= min(n for _, n in spans)
    grad_qkv, grad_resid, first, second, out_keep, out_send, out_own, early = boxed(
        sure,
        backward,
        own_sums,
        outs,
        after(resid, columns[0]),
        scale_two,
        gift,
        queries,
        pairs,
        mixed,
        mixed_wide,
        logs,
        out_blocks,
        positions,
        columns[0] if ahead else None,
    )
    columns += [
        lax.psum_scatter(after(piece, grad_qkv), "z", scatter_dimension=0, tiled=True) for piece in partial[1:]
    ]

    def collect(
        grad_qkv, first, second, out_own, out_keep, out_send, grad_resid, resid, qkv_blocks, flat_ones, scale_one, tokens
    ):
        own, to_c, to_x, to_y, to_d = spread(grad_qkv)

        def tokens_grads(grad_qkv):
            grad_unit_one = apply_rows(grad_qkv, qkv_blocks, True)
            return grad_resid + unit_back(grad_unit_one, tokens[0].astype(f32), scale_one)

        (by_x, by_y, by_d, out_found), grad_tokens = stage(
            [(to_x, "x"), (to_y, "y"), (to_d, across(5)), (out_send, "c")], tokens_grads, [grad_qkv]
        )
        on = jnp.concatenate([to_c, by_x[count:], by_y[count:], by_d[count:]], 0)
        (by_c,), out_parts = stage([(on, "c")], lambda *given: part_sums(*given), [out_keep, out_found])
        diag_top, diag_bottom, x_top, x_bottom, y_top, y_bottom, out_sums = out_parts

        def sums(resid, *gathered):
            gathered = jnp.concatenate(gathered, 0)
            return token_grads(flat_ones, gathered), resid + joined(out_own, first, second)

        started, (qkv_column, output) = stage(
            [(diag_top, "x"), (diag_bottom, "y"), (x_top, "x"), (y_bottom, "y")],
            sums,
            [resid, own, by_x[:count], by_y[:count], by_d[:count], by_c],
        )
        return qkv_column, grad_tokens, output, x_bottom, y_top, out_sums, started

    qkv_column, grad_tokens, output, x_bottom, y_top, out_sums, started = boxed(
        sure,
        collect,
        after(grad_qkv, columns[1]),
        first,
        second,
        out_own,
        out_keep,
        out_send,
        grad_resid,
        resid,
        qkv_blocks,
        flat_ones,
        scale_one,
        tokens,
    )
    qkv_low = lax.psum_scatter(qkv_column, "z", scatter_dimension=0, tiled=True)

    def end(x_bottom, y_top, out_sums, started, columns):
        x_bottom, y_top = total(x_bottom, started[1]).astype(low), total(y_top, started[0]).astype(low)
        received, every = stage(
            [(x_bottom, "x"), (y_top, "y")], lambda *columns: jnp.concatenate(columns, 1), columns
        )
        column = joined(out_sums, started, received).astype(low)
        return column.reshape(-1, column.shape[-1]), every

    out_column, every = boxed(sure, end, x_bottom, y_top, out_sums, started, columns[1:] if ahead else columns)
    out_sum = lax.psum_scatter(out_column, "z", scatter_dimension=0, tiled=True).astype(f32)
    every = after(every, out_column).reshape(8, -1, every.shape[1])
    every = lax.all_to_all(every, PLANE, split_axis=0, concat_axis=0, tiled=True)
    deep = qkv_low.shape[1]
    qkv_sum = after(qkv_low, every).reshape(8, -1, deep)
    qkv_sum = lax.all_to_all(qkv_sum, PLANE, split_axis=0, concat_axis=0, tiled=True)
    qkv_sum = jnp.swapaxes(qkv_sum, 0, 1).reshape(-1, 8 * deep).astype(f32)
    query_sum = qkv_sum[:, :wide]
    key_sum = qkv_sum[:, wide : wide + size]
    value_sum = qkv_sum[:, wide + size :]
    grad_attn_gain = (
        jnp.sum(query_weight.astype(f32) * query_sum, axis=1)
        + jnp.sum(key_weight.astype(f32) * key_sum, axis=1)
        + jnp.sum(value_weight.astype(f32) * value_sum, axis=1)
    )
    grad_gate, grad_up, grad_down, grad_mlp_gain = finish(spans, part, per, gain_two, gate_weight, up_weight, every, early)
    return (
        output[None],
        grad_tokens[None],
        grad_attn_gain,
        query_sum * gain_one,
        key_sum * gain_one,
        value_sum * gain_one,
        out_sum.T,
        grad_mlp_gain[:, 0],
        grad_gate,
        grad_up,
        grad_down.T,
    )


def solution(mesh):
    ctx, fsdp = mesh.shape["ctx"], mesh.shape["fsdp"]
    fine = Mesh(mesh.devices.reshape(ctx // 4, 2, 2, fsdp), ("z", "y", "c", "x"))
    rows = ("z", "y", "c")
    every = ("z", "y", "c", "x")
    return jax.shard_map(
        local,
        mesh=fine,
        in_specs=(
            P("x", rows, None),
            P("x", rows),
            P(every),
            P(every, None),
            P(every, None),
            P(every, None),
            P(None, every),
            P(every),
            P(every, None),
            P(every, None),
            P(None, every),
            P("x", rows, None),
        ),
        out_specs=(
            P("x", rows, None),
            P("x", rows, None),
            P(every),
            P(every, None),
            P(every, None),
            P(every, None),
            P(None, every),
            P(every),
            P(every, None),
            P(every, None),
            P(None, every),
        ),
        check_vma=False,
    )
```

```python
import functools

import jax
import jax.numpy as jnp
from jax import lax
from jax.experimental import pallas as pl
from jax.experimental.pallas import tpu as pltpu
from jax.sharding import Mesh, PartitionSpec as P

WINDOW = 2048
SUB = 128
TILE = 512
BROAD = 1280
epsilon = 1e-06
blocked_score = -1e30
PLANE = ("y", "c", "x")
low = jnp.bfloat16
f32 = jnp.float32
NOMINAL = pl.CostEstimate(flops=1 << 20, bytes_accessed=1 << 12, transcendentals=0)


def dot(left, right, contract, kind=f32):
    return lax.dot_general(
        left, right, ((contract[:1], contract[1:]), ((), ())), preferred_element_type=f32
    ).astype(kind)


def swap(value, axis):
    return lax.ppermute(value, axis, [(0, 1), (1, 0)])


def plane_gather(own, second=(), third=()):
    half = own.shape[0] // 2
    by_x = swap(own, "x")
    by_y = swap(own, "y")
    own_c = swap(own, "c")
    diag = (
        swap(after(by_y[:half], *second), "x"),
        swap(after(by_x[half:], *second), "y"),
    )
    by_x_c = swap(after(by_x, *second), "c")
    by_y_c = swap(after(by_y, *second), "c")
    diag_c = tuple(swap(after(part, *third), "c") for part in diag)
    return [own, by_x, own_c, by_x_c, by_y, diag, by_y_c, diag_c]


def joined_blocks(blocks):
    return [jnp.concatenate(block, 0) if isinstance(block, tuple) else block for block in blocks]


def stage(sends, work=None, given=()):
    fenced, given = lax.optimization_barrier((tuple(value for value, _ in sends), tuple(given)))
    received = tuple(
        swap(value, way) if isinstance(way, str) else way(value) for value, (_, way) in zip(fenced, sends)
    )
    return lax.optimization_barrier((received, work(*given) if work else given))


def boxed(sure, work, *given):
    shapes = jax.eval_shape(work, *given)
    return lax.cond(
        sure, work, lambda *_: jax.tree.map(lambda out: jnp.zeros(out.shape, out.dtype), shapes), *given
    )


def plane_index():
    return (lax.axis_index("y") * 2 + lax.axis_index("c")) * 2 + lax.axis_index("x")


def after(value, *earlier):
    return lax.optimization_barrier((value,) + earlier)[0]


def across(distance):
    return lambda value: lax.ppermute(value, PLANE, [(i, i ^ distance) for i in range(8)])


def behind(steps):
    count = lax.axis_size("z") * lax.axis_size("y")
    pairs = [(i, i + steps) for i in range(count) if 0 <= i + steps < count]
    return lambda value: lax.ppermute(value, ("z", "y"), pairs)


def two_heads(block, size):
    return jnp.concatenate([block[:, :size], block[:, size:]], 0)


def side_by_side(rows, size):
    half = rows.shape[0] // 2
    return jnp.concatenate([rows[:half], rows[half:]], 1)


def write_bias(bias, places, span, block):
    key = lax.broadcasted_iota(jnp.int32, (span, SUB), 0) - WINDOW
    query = lax.broadcasted_iota(jnp.int32, (span, SUB), 1)
    age = query - key
    seen = (age <= places) & (age >= 0) & (age < WINDOW)
    value = jnp.where(seen, 0.0, blocked_score).astype(f32)
    bias[:, :SUB] = value
    bias[:, SUB:] = value


def lay_window(core, blocks, window, turned, columns):
    count = blocks[0].shape[0]
    half = len(blocks) // 2
    for i in range(half):
        for which, block in ((core, blocks[i]), (1 - core, blocks[half + i])):
            at = pl.multiple_of((2 * i + which) * count, SUB)
            window[pl.ds(at, count), :] = block[...]
            turned[:, pl.ds(at, count)] = block[:, columns].T


def chunks(span, number):
    tiles = span // 128
    return [(128 * (tiles * i // number), 128 * (tiles * (i + 1) // number)) for i in range(number)]


def attend_kernel(size, scale, span, base, core, places, queries, *rest):
    blocks, (mixed, wide, logs, bias, window, turned) = rest[:-6], rest[-6:]
    block = pl.program_id(0)
    count = blocks[0].shape[0]
    start = pl.multiple_of(core[0] * count + base + block * SUB, SUB)

    @pl.when((block == 0) & (pl.program_id(1) == 0))
    def _():
        lay_window(core[0], blocks, window, turned, slice(size, 2 * size))

    @pl.when(pl.program_id(1) == 0)
    def _():
        write_bias(bias, places[...], span, block)

    query = two_heads(queries[...], size) * jnp.asarray(scale, low)
    highest = total = flat = None
    for at, end in chunks(span, 8):
        place = pl.ds(start + at, end - at)
        scores = dot(window[place, :size], query, (1, 1)) + bias[at:end]
        top = jnp.max(scores, axis=0, keepdims=True)
        if highest is not None:
            top = jnp.maximum(highest, top)
            fade = jnp.exp(highest - top)
        highest = top
        expo = jnp.exp(scores - highest)
        part = jnp.sum(expo, axis=0, keepdims=True)
        mix = dot(turned[:, place], expo.astype(low), (1, 0))
        total = part if total is None else total * fade + part
        flat = mix if flat is None else flat * fade + mix
    result = side_by_side((flat / total).T, size)
    wide[...] = result
    mixed[...] = result.astype(low)
    logs[0] = highest + jnp.log(total)


def attend_back_kernel(size, scale, span, base, core, places, queries, grads, wide, logs, *rest):
    blocks, (grad_queries, mine, theirs, bias, window, turned, total) = rest[:-7], rest[-7:]
    block = pl.program_id(0)
    count = blocks[0].shape[0]
    start = pl.multiple_of(core[0] * count + base + block * SUB, SUB)

    @pl.when((block == 0) & (pl.program_id(1) == 0))
    def _():
        lay_window(core[0], blocks, window, turned, slice(0, size))
        total[...] = jnp.zeros_like(total)

    @pl.when(pl.program_id(1) == 0)
    def _():
        write_bias(bias, places[...], span, block)

    query = two_heads(queries[...], size) * jnp.asarray(scale, low)
    grad = two_heads(grads[...], size)
    inner = jnp.sum((grad.astype(f32) * two_heads(wide[...], size)).T, axis=0, keepdims=True)
    place = pl.ds(start, span)
    keys, values = window[place, :size], window[place, size:]
    probs = jnp.exp(dot(keys, query, (1, 1)) + (bias[...] - logs[0]))
    grad_scores = (probs * (dot(values, grad, (1, 1)) - inner)).astype(low)
    total[place, size:] += dot(probs.astype(low), grad, (1, 0))
    total[place, :size] += dot(grad_scores, query, (1, 0))
    flat = dot(turned[:, place], grad_scores, (1, 0)) * scale
    grad_queries[...] = side_by_side(flat.T, size).astype(low)

    @pl.when((block == pl.num_programs(0) - 1) & (pl.program_id(1) == pl.num_programs(1) - 1))
    def _():
        for i in range(len(blocks) // 2):
            at = pl.multiple_of((2 * i + core[0]) * count, SUB)
            mine[i] = total[pl.ds(at, count), :]
            at = pl.multiple_of((2 * i + 1 - core[0]) * count, SUB)
            theirs[i] = total[pl.ds(at, count), :].astype(low)


def attend(queries, blocks, places, size, base):
    count, wide = queries.shape
    grid = (count // SUB, wide // (2 * size))
    span = WINDOW + SUB
    rows = len(blocks) * count
    core = lax.axis_index("c").astype(jnp.int32)[None]
    tile = pl.BlockSpec((SUB, 2 * size), lambda s, h, o: (s, h))
    return pl.pallas_call(
        functools.partial(attend_kernel, size, size**-0.5, span, base),
        out_shape=(
            jax.ShapeDtypeStruct((count, wide), low),
            jax.ShapeDtypeStruct((count, wide), f32),
            jax.ShapeDtypeStruct((grid[0] * grid[1], 1, 2 * SUB), f32),
        ),
        grid_spec=pltpu.PrefetchScalarGridSpec(
            num_scalar_prefetch=1,
            grid=grid,
            in_specs=[pl.BlockSpec((1, SUB), lambda s, h, o: (0, s)), tile]
            + [pl.BlockSpec(block.shape, lambda s, h, o: (0, 0)) for block in blocks],
            out_specs=[tile, tile, pl.BlockSpec((1, 1, 2 * SUB), lambda s, h, o: (s * grid[1] + h, 0, 0))],
            scratch_shapes=[
                pltpu.VMEM((span, 2 * SUB), f32),
                pltpu.VMEM((rows, 2 * size), low),
                pltpu.VMEM((size, rows), low),
            ],
        ),
        compiler_params=pltpu.CompilerParams(vmem_limit_bytes=56 << 20),
        cost_estimate=NOMINAL,
    )(core, places, queries, *blocks)


def attend_back(queries, grads, mixed, logs, blocks, places, size, base):
    count, wide = queries.shape
    grid = (count // SUB, wide // (2 * size))
    span = WINDOW + SUB
    rows = len(blocks) * count
    half = len(blocks) // 2
    core = lax.axis_index("c").astype(jnp.int32)[None]
    tile = pl.BlockSpec((SUB, 2 * size), lambda s, h, o: (s, h))
    whole = pl.BlockSpec((half, count, 2 * size), lambda s, h, o: (0, 0, 0))
    return pl.pallas_call(
        functools.partial(attend_back_kernel, size, size**-0.5, span, base),
        out_shape=(
            jax.ShapeDtypeStruct((count, wide), low),
            jax.ShapeDtypeStruct((half, count, 2 * size), f32),
            jax.ShapeDtypeStruct((half, count, 2 * size), low),
        ),
        grid_spec=pltpu.PrefetchScalarGridSpec(
            num_scalar_prefetch=1,
            grid=grid,
            in_specs=[
                pl.BlockSpec((1, SUB), lambda s, h, o: (0, s)),
                tile,
                tile,
                tile,
                pl.BlockSpec((1, 1, 2 * SUB), lambda s, h, o: (s * grid[1] + h, 0, 0)),
            ]
            + [pl.BlockSpec(block.shape, lambda s, h, o: (0, 0)) for block in blocks],
            out_specs=[tile, whole, whole],
            scratch_shapes=[
                pltpu.VMEM((span, 2 * SUB), f32),
                pltpu.VMEM((rows, 2 * size), low),
                pltpu.VMEM((size, rows), low),
                pltpu.VMEM((rows, 2 * size), f32),
            ],
        ),
        compiler_params=pltpu.CompilerParams(vmem_limit_bytes=60 << 20),
        cost_estimate=NOMINAL,
    )(core, places, queries, grads, mixed, logs, *blocks)


def lay_rows(slots, layout, pieces, full):
    for (r, first), piece in zip(layout, pieces):
        planes, rows, _ = piece.shape
        for plane in range(planes):
            at = pl.multiple_of(((first + plane) * 8 + slots[r]) * rows, 16)
            full[pl.ds(at, rows), :] = piece[plane]


def apply_kernel(layout, slots, left, *rest):
    *pieces, out, full = rest
    lay_rows(slots, layout, pieces, full)
    out[...] = dot(left[...], full[...], (1, 0), low)


def apply_turned_kernel(layout, slots, left, *rest):
    *start, out, full = rest
    start, pieces = start[: -len(layout)], start[-len(layout) :]
    lay_rows(slots, layout, pieces, full)

    @pl.when(pl.program_id(0) == 0)
    def _():
        out[...] = start[0][...] if start else jnp.zeros_like(out)

    out[...] += dot(left[...], full[...], (1, 1))


def whole_rows(blocks):
    planes, rows, wide = blocks[0].shape
    here = plane_index()
    whole = jnp.zeros((planes, 8, rows, wide), blocks[0].dtype)
    for r, block in enumerate(blocks):
        whole = lax.dynamic_update_slice(whole, block[:, None], (0, here ^ r, 0, 0))
    return whole.reshape(planes * 8 * rows, wide)


def apply_rows(left, blocks, turned=False, start=None):
    planes, rows, wide = blocks[0].shape
    if rows % 16 or wide % TILE:
        whole = whole_rows(joined_blocks(blocks))
        if not turned:
            return dot(left, whole, (1, 0), low)
        return dot(left, whole, (1, 1)) + (0.0 if start is None else start)
    count, deep = left.shape[0], planes * 8 * rows
    slots = (plane_index() ^ jnp.arange(8)).astype(jnp.int32)
    layout, blocks = [], [block if isinstance(block, tuple) else (block,) for block in blocks]
    for r, block in enumerate(blocks):
        layout += [(r, sum(piece.shape[0] for piece in block[:i])) for i in range(len(block))]
    blocks = [piece for block in blocks for piece in block]
    pieces = [pl.BlockSpec((piece.shape[0], rows, TILE), lambda n, s: (0, 0, n)) for piece in blocks]
    whole = pl.BlockSpec((count, deep), lambda n, s: (0, 0))
    part = pl.BlockSpec((count, TILE), lambda n, s: (0, n))
    if not turned:
        kernel, given, specs, result = apply_kernel, [left], [whole], part
        shape = jax.ShapeDtypeStruct((count, wide), low)
    else:
        kernel, given, specs, result = apply_turned_kernel, [left], [part], whole
        if start is not None:
            given, specs = given + [start], specs + [whole]
        shape = jax.ShapeDtypeStruct((count, deep), f32)
    return pl.pallas_call(
        functools.partial(kernel, layout),
        out_shape=shape,
        grid_spec=pltpu.PrefetchScalarGridSpec(
            num_scalar_prefetch=1,
            grid=(wide // TILE,),
            in_specs=specs + pieces,
            out_specs=result,
            scratch_shapes=[pltpu.VMEM((deep, TILE), low)],
        ),
        compiler_params=pltpu.CompilerParams(vmem_limit_bytes=48 << 20),
        cost_estimate=NOMINAL,
    )(slots, *given, *blocks)


def row_grads_kernel(slots, left, right, keep, send, turned):
    @pl.when(pl.program_id(1) == 0)
    def _():
        turned[...] = left[...].T

    rows = keep.shape[2]
    value = dot(turned[...], right[...], (1, 0), low)
    for i in range(8):
        place = slots[i]

        @pl.when(place < 4)
        def _():
            keep[place, 0] = value[i * rows : (i + 1) * rows]

        @pl.when(place >= 4)
        def _():
            send[place - 4, 0] = value[i * rows : (i + 1) * rows]


def row_grads(left, right):
    planes = lax.axis_size("z")
    count, deep = left.shape
    wide = right.shape[1]
    rows = deep // (planes * 8)
    places = jnp.array([3, 1, 7, 5, 2, 0, 6, 4], jnp.int32)
    slots = places[plane_index() ^ jnp.arange(8)]
    if rows % 16 or wide % TILE or (planes * 8 * rows) % (planes * 128):
        blocks = dot(left, right, (0, 0), low).reshape(planes, 8, rows, wide)
        order = jnp.argsort(slots)
        blocks = jnp.swapaxes(jnp.take(blocks, order, axis=1), 0, 1)
        return blocks[:4], blocks[4:]
    tile = wide if wide <= 5 * TILE else TILE
    group = pl.BlockSpec((4, 1, rows, tile), lambda z, n, s: (0, z, 0, n))
    shape = jax.ShapeDtypeStruct((4, planes, rows, wide), low)
    return pl.pallas_call(
        row_grads_kernel,
        out_shape=(shape, shape),
        grid_spec=pltpu.PrefetchScalarGridSpec(
            num_scalar_prefetch=1,
            grid=(planes, wide // tile),
            in_specs=[
                pl.BlockSpec((count, 8 * rows), lambda z, n, s: (0, z)),
                pl.BlockSpec((count, tile), lambda z, n, s: (0, n)),
            ],
            out_specs=[group, group],
            scratch_shapes=[pltpu.VMEM((8 * rows, count), low)],
        ),
        compiler_params=pltpu.CompilerParams(vmem_limit_bytes=48 << 20),
        cost_estimate=NOMINAL,
    )(slots, left, right)


def mlp_kernel(part, per, tiles, *rest):
    weights, rest = rest[:per], rest[per:]
    pieces = 2 * sum(tiles)
    sources, rest = rest[:pieces], rest[pieces:]
    before, rest = rest[:-8], rest[-8:]
    outs, grad_units, hidden, units, grads, arrived = rest[0:2], rest[2:4], *rest[4:]
    step = pl.program_id(0)

    def fetches(tile):
        first = 2 * sum(tiles[:tile])
        found = []
        for array, target in enumerate((units, grads)):
            at = 0
            for i in range(tiles[tile]):
                source = sources[first + array * tiles[tile] + i]
                found.append(
                    pltpu.make_async_copy(
                        source,
                        target.at[tile % 2, pl.ds(at, source.shape[0])],
                        arrived.at[tile % 2, array, i],
                    )
                )
                at += source.shape[0]
        return found

    for tile in range(len(tiles)):

        @pl.when(step == tile)
        def _():
            if tile == 0:
                for copy in fetches(0):
                    copy.start()
            if tile + 1 < len(tiles):
                for copy in fetches(tile + 1):
                    copy.start()
            for copy in fetches(tile):
                copy.wait()

    slope = 0.7978845608028654
    fronts = []
    for j in range(per):
        both = dot(units[step % 2], weights[j][:, : 2 * part], (1, 0))
        fronts.append((both[:, :part], both[:, part:], dot(grads[step % 2], weights[j][:, 2 * part :], (1, 0))))
    values = [0.0, 0.0]
    for j, (gates, upward, grad_middle) in enumerate(fronts):
        square = gates * gates
        half = 0.5 + 0.5 * jnp.tanh(gates * (slope + slope * 0.044715 * square))
        gelu = gates * half
        grad_gelu = half + gelu * (1.0 - half) * (2 * slope + 6 * slope * 0.044715 * square)
        at = 2 * part * j
        hidden[:, at : at + part] = (grad_middle * upward * grad_gelu).astype(low)
        hidden[:, at + part : at + 2 * part] = (grad_middle * gelu).astype(low)
        at = part * (2 * per + j)
        hidden[:, at : at + part] = (gelu * upward).astype(low)
        for which in range(2):
            at, width = (2 * part * j, 2 * part) if which else (part * (2 * per + j), part)
            first = 0 if which else 2 * part
            part_value = dot(hidden[:, at : at + width], weights[j][:, first : first + width], (1, 1))
            values[which] = values[which] + part_value
    for which, targets in enumerate((outs, grad_units)):
        value = values[which]
        for side in range(2):

            @pl.when(step // (len(tiles) // 2) == side)
            def _():
                if before:
                    targets[side][...] = (value + before[2 * which + side][...].astype(f32)).astype(low)
                else:
                    targets[side][...] = value.astype(low)


def mlp(units, grads, weights, before):
    rows = sum(piece.shape[0] for piece in units[0])
    count, wide = rows * len(units), units[0][0].shape[1]
    per, each = len(weights), weights[0].shape[1]
    deep = per * each
    tiles = tuple(len(tile) for tile in units)
    sources = [piece for pair in zip(units, grads) for tile in pair for piece in tile]
    side = len(units) // 2
    sides = [
        pl.BlockSpec((rows, wide), lambda i: (jnp.minimum(i, side - 1), 0)),
        pl.BlockSpec((rows, wide), lambda i: (jnp.maximum(i - side, 0), 0)),
    ]
    half = jax.ShapeDtypeStruct((count // 2, wide), low)
    return pl.pallas_call(
        functools.partial(mlp_kernel, each // 3, per, tiles),
        out_shape=[half] * 4 + [jax.ShapeDtypeStruct((count, deep), low)],
        grid=(len(units),),
        in_specs=[pl.BlockSpec((wide, each), lambda i: (0, 0), pipeline_mode=pl.Buffered(1))] * per
        + [pl.BlockSpec(memory_space=pl.ANY)] * len(sources)
        + (sides * 2 if before else []),
        out_specs=sides * 2 + [pl.BlockSpec((rows, deep), lambda i: (i, 0))],
        scratch_shapes=[
            pltpu.VMEM((2, rows, wide), low),
            pltpu.VMEM((2, rows, wide), low),
            pltpu.SemaphoreType.DMA((2, 2, max(tiles))),
        ],
        compiler_params=pltpu.CompilerParams(vmem_limit_bytes=62 << 20),
        cost_estimate=NOMINAL,
    )(*weights, *sources, *before)


def mlp_grads_kernel(number, *rest):
    units, grads, hidden, rest = rest[:number], rest[number : 2 * number], rest[2 * number : 2 * number + 2], rest[2 * number + 2 :]
    *outs, turned = rest
    step = pl.program_id(0)
    part = hidden[0].shape[1] // 3
    piece = 256 if part % 256 == 0 and outs[0].shape[1] % 256 == 0 else 128
    places = [(out, at) for out in outs for at in range(0, out.shape[1], piece)]

    def turn(slot, which, sources, share, shares):
        at = 0
        for i, source in enumerate(sources):
            if i * shares // len(sources) == share:
                turned[slot, which, :, at : at + source.shape[0]] = source[...].T
            at += source.shape[0]

    def multiply(slot, which, i, at):
        value, start = 0.0, 0
        for block in hidden:
            left = turned[slot, which, :, start : start + block.shape[0]]
            value = value + dot(left, block[:, at : at + piece], (1, 0))
            start += block.shape[0]
        out, place = places[i]
        out[:, place : place + piece] = value.astype(low)

    work = [(at // (2 * part), at) for at in range(0, 3 * part, piece)]

    @pl.when(step == 0)
    def _():
        turn(0, 0, units, 0, 1)
        turn(0, 1, grads, 0, 1)

    @pl.when(step > 0)
    def _():
        for i, (which, at) in enumerate(work):
            multiply((step - 1) % 2, which, i, at)
            turn(step % 2, 0, units, i, len(work))
            turn(step % 2, 1, grads, i, len(work))


def mlp_grads(units, grads, hidden, pieces=(3,)):
    wide = units[0].shape[1]
    deep = hidden[0].shape[1]
    count = sum(piece.shape[0] for piece in units)
    rows = 512
    last = wide // rows - 1
    return pl.pallas_call(
        functools.partial(mlp_grads_kernel, len(units)),
        out_shape=[jax.ShapeDtypeStruct((wide, deep // 3 * piece), low) for piece in pieces],
        grid=(last + 2,),
        in_specs=[
            pl.BlockSpec((piece.shape[0], rows), lambda s: (0, jnp.minimum(s, last))) for piece in units + grads
        ]
        + [pl.BlockSpec(piece.shape, lambda s: (0, 0), pipeline_mode=pl.Buffered(1)) for piece in hidden],
        out_specs=[
            pl.BlockSpec((rows, deep // 3 * piece), lambda s: (jnp.maximum(s - 1, 0), 0)) for piece in pieces
        ],
        scratch_shapes=[pltpu.VMEM((2, 2, rows, count), low)],
        compiler_params=pltpu.CompilerParams(vmem_limit_bytes=62 << 20),
        cost_estimate=NOMINAL,
    )(*units, *grads, *hidden)


def token_grads_kernel(number, *rest):
    units, (right, out, turned) = rest[:number], rest[number:]

    @pl.when(pl.program_id(0) == 0)
    def _():
        turned[...] = right[...].T

    value, at = 0.0, 0
    for unit in units:
        value = value + dot(turned[:, at : at + unit.shape[0]], unit[...], (1, 0))
        at += unit.shape[0]
    out[...] = value.astype(low).T


def token_grads(units, right):
    wide = units[0].shape[1]
    count, deep = right.shape
    rows = 512
    return pl.pallas_call(
        functools.partial(token_grads_kernel, len(units)),
        out_shape=jax.ShapeDtypeStruct((wide, deep), low),
        grid=(wide // rows,),
        in_specs=[pl.BlockSpec((piece.shape[0], rows), lambda s: (0, s)) for piece in units]
        + [pl.BlockSpec(right.shape, lambda s: (0, 0), pipeline_mode=pl.Buffered(1))],
        out_specs=pl.BlockSpec((rows, deep), lambda s: (s, 0)),
        scratch_shapes=[pltpu.VMEM((deep, count), low)],
        compiler_params=pltpu.CompilerParams(vmem_limit_bytes=56 << 20),
        cost_estimate=NOMINAL,
    )(*units, right)


def spread_kernel(slots, value, *outs):
    count, deep = value.shape[0], outs[0].shape[1]
    place = 0
    for out in outs:
        for at in range(0, out.shape[0], count):
            out[at : at + count, :] = value[:, pl.ds(pl.multiple_of(slots[place] * deep, 128), deep)]
            place += 1


def spread(value):
    count, wide = value.shape
    slots = (plane_index() ^ jnp.array(ORDER)).astype(jnp.int32)
    deep = wide // 8
    rows = (count, count, 2 * count, 2 * count, 2 * count)
    if deep % 128:
        pieces = [lax.dynamic_slice(value, (0, slots[i] * deep), (count, deep)) for i in range(8)]
        return pieces[:2] + [jnp.concatenate(pieces[i : i + 2], 0) for i in (2, 4, 6)]
    return pl.pallas_call(
        spread_kernel,
        out_shape=[jax.ShapeDtypeStruct((n, deep), value.dtype) for n in rows],
        grid_spec=pltpu.PrefetchScalarGridSpec(
            num_scalar_prefetch=1,
            grid=(1,),
            in_specs=[pl.BlockSpec((count, wide), lambda i, s: (0, 0))],
            out_specs=[pl.BlockSpec((n, deep), lambda i, s: (0, 0)) for n in rows],
        ),
        cost_estimate=NOMINAL,
    )(slots, value)


ORDER = (0, 2, 1, 3, 4, 6, 5, 7)


def deal_kernel(slots, value, *outs):
    place = 0
    for out in outs:
        for i in range(out.shape[0]):
            out[i] = value[slots[place]]
            place += 1


def deal(value):
    _, rows, wide = value.shape
    slots = (plane_index() ^ jnp.array(ORDER)).astype(jnp.int32)
    sizes = (1, 1, 2, 2, 2)
    return pl.pallas_call(
        deal_kernel,
        out_shape=[jax.ShapeDtypeStruct((n, rows, wide), value.dtype) for n in sizes],
        grid_spec=pltpu.PrefetchScalarGridSpec(
            num_scalar_prefetch=1,
            grid=(1,),
            in_specs=[pl.BlockSpec(value.shape, lambda i, s: (0, 0, 0))],
            out_specs=[pl.BlockSpec((n, rows, wide), lambda i, s: (0, 0, 0)) for n in sizes],
        ),
        compiler_params=pltpu.CompilerParams(vmem_limit_bytes=48 << 20),
        cost_estimate=NOMINAL,
    )(slots, value)


def turn_kernel(keep, found, far, diag_x, diag_y, y_bottom, x_bottom, y_top):
    half = far.shape[0]
    both = keep[...].astype(f32) + found[...].astype(f32)
    y_top[...] = (both[:half] + diag_x[...].astype(f32)).astype(low)
    y_bottom[...] = both[half:].astype(low)
    x_bottom[...] = (far[...].astype(f32) + diag_y[...].astype(f32)).astype(low)


def turn(keep, found, far, diag_x, diag_y):
    half, wide = far.shape
    tile = BROAD if wide % BROAD == 0 else wide
    part = lambda rows: pl.BlockSpec((rows, tile), lambda n: (0, n))
    return pl.pallas_call(
        turn_kernel,
        out_shape=[jax.ShapeDtypeStruct((half, wide), low)] * 3,
        grid=(wide // tile,),
        in_specs=[part(2 * half)] * 2 + [part(half)] * 3,
        out_specs=[part(half)] * 3,
        cost_estimate=NOMINAL,
    )(keep, found, far, diag_x, diag_y)


def halved_kernel(keep, found, *outs):
    half = outs[0].shape[0]
    for i, out in enumerate(outs):
        rows = slice(i * half, i * half + half)
        out[...] = (keep[rows].astype(f32) + found[rows].astype(f32)).astype(low)


def halved(keep, found):
    count, wide = keep.shape
    tile = BROAD if wide % BROAD == 0 else wide
    part = lambda rows: pl.BlockSpec((rows, tile), lambda n: (0, n))
    return pl.pallas_call(
        halved_kernel,
        out_shape=[jax.ShapeDtypeStruct((count // 4, wide), low)] * 4,
        grid=(wide // tile,),
        in_specs=[part(count)] * 2,
        out_specs=[part(count // 4)] * 4,
        cost_estimate=NOMINAL,
    )(keep, found)


def resid_kernel(steps, keep, found, x_top, x_bottom, y_top, y_bottom, resid, gift, scale, grad_out, grad_low):
    upper = pl.program_id(0) < steps
    x_part = jnp.where(upper, x_top[...].astype(f32), x_bottom[...].astype(f32))
    y_part = jnp.where(upper, y_top[...].astype(f32), y_bottom[...].astype(f32))
    grad = keep[...].astype(f32) + found[...].astype(f32) + x_part + y_part
    grad = gift[...].astype(f32) + unit_back(grad, resid[...], scale[...])
    grad_out[...] = grad
    grad_low[...] = grad.astype(low)


def resid_grads(keep, found, x_top, x_bottom, y_top, y_bottom, resid, gift, scale):
    count, wide = resid.shape
    rows = 96
    steps = count // (2 * rows)
    row = pl.BlockSpec((rows, wide), lambda i: (i, 0))
    own = pl.BlockSpec((rows, wide), lambda i: (i + 2 * steps, 0))
    first = pl.BlockSpec((rows, wide), lambda i: (jnp.minimum(i, steps - 1), 0))
    last = pl.BlockSpec((rows, wide), lambda i: (jnp.maximum(i - steps, 0), 0))
    return pl.pallas_call(
        functools.partial(resid_kernel, steps),
        out_shape=(jax.ShapeDtypeStruct((count, wide), f32), jax.ShapeDtypeStruct((count, wide), low)),
        grid=(2 * steps,),
        in_specs=[own, own, first, last, first, last, row, row, pl.BlockSpec((rows, 1), lambda i: (i, 0))],
        out_specs=(row, row),
        cost_estimate=NOMINAL,
    )(keep, found, x_top, x_bottom, y_top, y_bottom, resid, gift, scale)


def part_sums_kernel(keep, found, diag_top, diag_bottom, x_top, x_bottom, y_top, y_bottom, own):
    half = diag_top.shape[0]

    def both(place, first, rows):
        part = slice(first, first + rows)
        return (keep[place, part].astype(f32) + found[place, part].astype(f32)).astype(low)

    for place, (top, bottom) in enumerate(((diag_top, diag_bottom), (x_top, x_bottom), (y_top, y_bottom))):
        top[...] = both(place, 0, half)
        bottom[...] = both(place, half, half)
    own[...] = both(3, 0, 2 * half)


def part_sums(keep, found):
    _, planes, rows, wide = keep.shape
    tile = BROAD if wide % BROAD == 0 else wide
    four = pl.BlockSpec((4, planes, rows, tile), lambda n: (0, 0, 0, n))
    some = lambda planes: pl.BlockSpec((planes, rows, tile), lambda n: (0, 0, n))
    half = planes // 2
    shape = lambda planes: jax.ShapeDtypeStruct((planes, rows, wide), low)
    return pl.pallas_call(
        part_sums_kernel,
        out_shape=[shape(half)] * 6 + [shape(planes)],
        grid=(wide // tile,),
        in_specs=[four] * 2,
        out_specs=[some(half)] * 6 + [some(planes)],
        compiler_params=pltpu.CompilerParams(vmem_limit_bytes=48 << 20),
        cost_estimate=NOMINAL,
    )(keep, found)


def pack_kernel(spans, part, gain, gate, up, down, out):
    scale = gain[...]
    share = out.shape[2] // 3
    for p, (at, n) in enumerate(spans):
        for q in range(share // part):
            width = min(part, n - q * part)
            place = slice(at + q * part, at + q * part + width)
            for which, source in enumerate((gate, up, down)):
                first = part * (3 * q + which)
                if width > 0:
                    value = source[:, place]
                    if which < 2:
                        value = (value.astype(f32) * scale).astype(low)
                    out[p, :, first : first + width] = value
                if width < part:
                    empty = max(width, 0)
                    out[p, :, first + empty : first + part] = jnp.zeros((out.shape[1], part - empty), low)


def pack(spans, part, share, gain, gate, up, down):
    rows, _ = gate.shape
    return pl.pallas_call(
        functools.partial(pack_kernel, spans, part),
        out_shape=jax.ShapeDtypeStruct((8, rows, 3 * share), low),
        compiler_params=pltpu.CompilerParams(vmem_limit_bytes=48 << 20),
        cost_estimate=NOMINAL,
    )(gain, gate, up, down)


def shares(columns):
    tiles = -(-columns // 128)
    few, more = divmod(tiles, 8)
    sizes = [128 * (few + (p < more)) for p in range(8)]
    return [(sum(sizes[:p]), size) for p, size in enumerate(sizes)], 128 * (few + (more > 0))


def finish_kernel(spans, part, per, first_part, starts, gain, gate, up, whole, *rest):
    *early, gate_out, up_out, down_out, gain_out = rest
    scale = gain[...]
    total = jnp.zeros_like(scale)

    def lay(piece, start, j, place, width):
        added = jnp.zeros_like(scale)
        for which, (weight, out) in enumerate(((gate, gate_out), (up, up_out))):
            first = start + part * (2 * j + which)
            value = piece[:, first : first + width].astype(f32)
            added = added + jnp.sum(value * weight[:, place].astype(f32), axis=1, keepdims=True)
            out[:, place] = value * scale
        first = start + part * (2 * per + j)
        down_out[:, place] = piece[:, first : first + width].astype(f32)
        return added

    for p, (at, n) in enumerate(spans):
        for q in range(first_part, -(-n // part)):
            width = min(part, n - q * part)
            start = 3 * part * per * (q // per) - 3 * part * first_part
            total = total + lay(whole.at[p], start, q % per, slice(at + q * part, at + q * part + width), width)
    place = 0
    for pieces in early:
        for i in range(pieces.shape[0]):
            for q in range(first_part):
                at = pl.multiple_of(starts[place] + q * part, 128)
                total = total + lay(pieces.at[i], 0, q, pl.ds(at, part), part)
            place += 1
    gain_out[...] = total


def finish(spans, part, per, gain, gate, up, whole, early):
    rows, columns = gate.shape
    order = [r for r in (0, 1, 4, 5, 2, 3, 6, 7)]
    starts = jnp.array([at for at, _ in spans], jnp.int32)[plane_index() ^ jnp.array(order)]
    block = lambda shape: pl.BlockSpec(shape, lambda i, s: (0,) * len(shape))
    given = (gain, gate, up, whole, *early)
    shapes = ((rows, columns), (rows, columns), (rows, columns), (rows, 1))
    return pl.pallas_call(
        functools.partial(finish_kernel, spans, part, per, per if early else 0),
        out_shape=[jax.ShapeDtypeStruct(shape, f32) for shape in shapes],
        grid_spec=pltpu.PrefetchScalarGridSpec(
            num_scalar_prefetch=1,
            grid=(1,),
            in_specs=[block(value.shape) for value in given],
            out_specs=[block(shape) for shape in shapes],
        ),
        compiler_params=pltpu.CompilerParams(vmem_limit_bytes=56 << 20),
        cost_estimate=NOMINAL,
    )(starts, *given)


def unit_of(values):
    scale = lax.rsqrt(jnp.mean(values * values, axis=-1, keepdims=True) + epsilon)
    return scale, (values * scale).astype(low)


def unit_back(grad, values, scale):
    unit = values * scale
    return scale * (grad - unit * jnp.mean(grad * unit, axis=-1, keepdims=True))


def local(
    tokens,
    positions,
    attn_gain,
    query_weight,
    key_weight,
    value_weight,
    out_weight,
    mlp_gain,
    gate_weight,
    up_weight,
    down_weight,
    cotangent,
):
    count = tokens.shape[1]
    size = key_weight.shape[1]
    wide = query_weight.shape[1]
    reach = (WINDOW + count - 2) // count
    chips = (reach + 1) // 2
    base = 2 * chips * count - WINDOW
    gain_one = attn_gain[:, None]
    gain_two = mlp_gain[:, None]

    qkv_shard = jnp.concatenate([query_weight, key_weight, value_weight], 1).astype(f32) * gain_one
    qkv_shard = qkv_shard.astype(low)
    qkv_column = lax.all_gather(qkv_shard, "z", axis=0, tiled=False)
    out_column = lax.all_gather(after(out_weight.T, qkv_shard), "z", axis=0, tiled=False)

    spans, share = shares(gate_weight.shape[1])
    parts = share // 256 if share % 256 == 0 else 1
    calls = 2 if parts % 2 == 0 else 1
    per = parts // calls
    part = share // parts
    mine = pack(spans, part, share, after(gain_two, qkv_shard), gate_weight, up_weight, down_weight.T)
    gift = cotangent[0]
    mlp_column = lax.all_to_all(mine, PLANE, split_axis=0, concat_axis=0, tiled=True)
    mlp_column = mlp_column.reshape(-1, 3 * share)

    def piece_of(k, column):
        return column[:, k * 3 * part : (k + 1) * 3 * part]

    def gathered(piece):
        return lax.all_gather(piece, "z", axis=0, tiled=True)

    mlp_full = [gathered(piece_of(0, mlp_column))]
    sure = positions[0, 0] >= 0
    half = count // 2

    def project(qkv_column, tokens, gift, mlp_column):
        qkv_blocks = plane_gather(qkv_column)
        scale_one, unit_one = unit_of(tokens[0].astype(f32))
        qkv = apply_rows(unit_one, qkv_blocks)
        queries, pair = qkv[:, :wide], qkv[:, wide:]
        moves = [behind(d) for d in range(chips, 0, -1)]
        found, pieces = stage(
            [(pair, move) for move in moves] + [(pair, "c"), (gift, "x"), (gift, "y"), (gift, "c")],
            lambda column: [piece_of(k, column) for k in range(1, parts)],
            [mlp_column],
        )
        *pairs, pair_c, gift_x, gift_y, gift_c = found
        found, _ = stage([(block, "c") for block in pairs])
        gifts = gift_x, gift_y, gift_c
        return qkv_blocks[1:], queries, [*pairs, pair, *found, pair_c], gifts, unit_one, scale_one, pieces

    def forward(queries, pairs, out_column, tokens, positions, gift_x, gift_y):
        inputs = tokens[0].astype(f32)
        mid = out_column.shape[0] // 2
        (out_x, out_y, out_c, gift_x_c, gift_y_c), (mixed, mixed_wide, logs) = stage(
            [(out_column, "x"), (out_column, "y"), (out_column, "c"), (gift_x, "c"), (gift_y, "c")],
            lambda *given: attend(given[0], given[1:], positions, size, base),
            [queries, *pairs],
        )
        (out_top, out_bottom, out_x_c, out_y_c), _ = stage(
            [(out_y[:mid], "x"), (out_x[mid:], "y"), (out_x, "c"), (out_y, "c")]
        )
        out_diag_c, _ = stage([(out_top, "c"), (out_bottom, "c")])
        out_blocks = [out_column, out_x, out_c, out_x_c, out_y, (out_top, out_bottom), out_y_c, out_diag_c]
        resid = apply_rows(mixed, out_blocks, True, inputs)
        scale_two, unit_two = unit_of(resid)
        (unit_x, unit_y, unit_c), _ = stage([(unit_two, "x"), (unit_two, "y"), (unit_two, "c")])
        (unit_x_c, unit_y_c), _ = stage([(unit_x, "c"), (unit_y, "c")])
        unit_blocks = unit_two, unit_x, unit_c, unit_x_c, unit_y, unit_y_c
        return out_blocks[1:], mixed, mixed_wide, logs, resid, scale_two, unit_blocks, gift_x_c, gift_y_c

    qkv_column = after(qkv_column, mlp_column)
    qkv_blocks, queries, pairs, gifts, unit_one, scale_one, pieces = boxed(
        sure, project, qkv_column, tokens, gift, mlp_column
    )
    gift_x, gift_y, gift_c = gifts
    mlp_full += [gathered(piece) for piece in pieces]
    out_blocks, mixed, mixed_wide, logs, resid, scale_two, unit_blocks, gift_x_c, gift_y_c = boxed(
        sure, forward, after(queries, mlp_full[0]), pairs, out_column, tokens, positions, gift_x, gift_y
    )
    qkv_blocks, out_blocks = [qkv_column, *qkv_blocks], [out_column, *out_blocks]
    grads_near = [(gift_y,), (gift,), (gift_y_c,), (gift_c,)]

    def flat(*tiles):
        return [piece for group in tiles for tile in group for piece in tile]

    def summed(keep, received):
        return keep.astype(f32) + received.astype(f32)

    def halves(value):
        middle = value.shape[0] // 2
        return value[:middle], value[middle:]

    def total(*values):
        return sum(value.astype(f32) for value in values)

    def opening(weights, blocks, gift_x, gift_x_c, grads_near, unit_one):
        unit_two, unit_x, unit_c, unit_x_c, unit_y, unit_y_c = blocks
        units_near = [(unit_y,), (unit_two,), (unit_y_c,), (unit_c,)]
        gift_y = grads_near[0][0]
        sends = [(unit_y, "x"), (gift_x, "y")]
        one_sends = [(unit_one, "x"), (unit_one, "y"), (unit_one, "c")]
        far_sums = near_sums = partial = ()
        if calls > 1:
            (unit_d, gift_d), near_sums = stage(
                sends, lambda *given: mlp([(v,) for v in given], grads_near, weights, ()), flat(units_near)
            )
        else:
            (unit_d, gift_d), _ = stage(sends)
        (unit_d_c, gift_d_c), _ = stage([(unit_d, "c"), (gift_d, "c")])
        units_far = [(unit_d,), (unit_x,), (unit_d_c,), (unit_x_c,)]
        grads_far = [(gift_d,), (gift_x,), (gift_d_c,), (gift_x_c,)]
        if calls > 1:
            (one_x, one_y, one_c), far_sums = stage(
                one_sends, lambda weights: mlp(units_far, grads_far, weights, ()), [weights]
            )
        else:
            (one_x, one_y, one_c), _ = stage(one_sends)
        one_sends = [(one_y, "x"), (one_x, "c"), (one_y, "c")]
        if calls > 1:
            (one_d, one_x_c, one_y_c), partial = stage(
                one_sends,
                lambda *given: mlp_grads(flat(units_far, units_near), flat(grads_far, grads_near), given)[0],
                [far_sums[4], near_sums[4]],
            )
        else:
            (one_d, one_x_c, one_y_c), _ = stage(one_sends)
        ones = one_x, one_c, one_x_c, one_y, one_d, one_y_c
        return (unit_d, unit_d_c), (gift_d, gift_d_c), far_sums[:4], near_sums[:4], partial, ones

    columns = []
    unit_two, unit_x, unit_c, unit_x_c, unit_y, unit_y_c = unit_blocks
    unit_far, gift_far, far_before, near_before, partial, ones = boxed(
        sure, opening, mlp_full[:per] if calls > 1 else (), unit_blocks, gift_x, gift_x_c, grads_near, unit_one
    )
    if calls > 1:
        columns.append(lax.psum_scatter(partial, "z", scatter_dimension=0, tiled=True))
    unit_d, unit_d_c = unit_far
    gift_d, gift_d_c = gift_far
    grads_far = [(gift_d,), (gift_x,), (gift_d_c,), (gift_x_c,)]
    units_far = [(unit_d,), (unit_x,), (unit_d_c,), (unit_x_c,)]
    units_near = [(unit_y,), (unit_two,), (unit_y_c,), (unit_c,)]

    def middle(weights, units_far, units_near, grads_far, grads_near, far_before, near_before, resid, scale_two, gift, ones):
        (one_d_c,), far_sums = stage(
            [(ones[4], "c")],
            lambda *weights: mlp(units_far, grads_far, weights, far_before),
            weights,
        )
        (found,), _ = stage([(far_sums[3], "c")])
        diag_top, diag_bottom, x_top, x_bottom = halved(far_sums[2], found)
        (diag_x, diag_y, x_top, far_out), near_sums = stage(
            [(diag_top, "x"), (diag_bottom, "y"), (x_top, "x"), (far_sums[1], "c")],
            lambda *given: mlp([(value,) for value in given], grads_near, weights, near_before),
            [tile[0] for tile in units_near],
        )
        (found,), _ = stage([(near_sums[3], "c")])
        y_bottom, x_bottom, y_top = turn(near_sums[2], found, x_bottom, diag_x, diag_y)
        (y_bottom, x_bottom, y_top, near_out), partial = stage(
            [(y_bottom, "y"), (x_bottom, "x"), (y_top, "y"), (near_sums[1], "c")],
            lambda *given: mlp_grads(flat(units_far, units_near), flat(grads_far, grads_near), given, cuts),
            [far_sums[4], near_sums[4]],
        )
        received = x_top, x_bottom, y_top, y_bottom
        outs = far_sums[0], far_out, near_sums[0], near_out
        return partial, (near_sums[2], found, received), outs, one_d_c

    cuts = (2, 1)
    partial, own_sums, outs, one_d_c = boxed(
        sure,
        middle,
        mlp_full[-per:],
        units_far,
        units_near,
        grads_far,
        grads_near,
        far_before,
        near_before,
        resid,
        scale_two,
        gift,
        ones,
    )
    columns += [lax.psum_scatter(piece, "z", scatter_dimension=0, tiled=True) for piece in partial[:1]]
    one_x, one_c, one_x_c, one_y, one_d, one_y_c = ones
    flat_ones = [unit_one, one_x, one_y, one_d, one_c, one_x_c, one_y_c, one_d_c]

    def joined(own, first, second):
        top, bottom = own if isinstance(own, tuple) else halves(own)
        return jnp.concatenate([total(top, first[2], second[1]), total(bottom, second[0], first[3])], 0)

    def backward(
        own_sums, outs, resid, scale_two, gift, queries, pairs, mixed, mixed_wide, logs, out_blocks, positions, early
    ):
        keep, found, received = own_sums

        def remaining(keep, far, near):
            grads = resid_grads(keep, found, *received, resid, gift, scale_two)
            return grads, halved(far, outs[1]), halved(near, outs[3])

        given = keep, outs[0], outs[2]
        if early is not None:
            early_own, to_c, to_x, to_y, to_d = deal(early.reshape(8, -1, early.shape[1]))
            (by_x, by_y, by_d), results = stage([(to_x, "x"), (to_y, "y"), (to_d, across(5))], remaining, given)
        else:
            results = remaining(*given)
        (grad_resid, grad_attn), out_far, out_near = results

        def attention(grad_attn):
            grad_mixed = apply_rows(grad_attn, out_blocks)
            return attend_back(queries, grad_mixed, mixed_wide, logs, pairs, positions, size, base)

        first, (grad_queries, mine, theirs) = stage(
            [(out_far[0], "x"), (out_far[1], "y"), (out_far[2], "x"), (out_near[1], "y")], attention, [grad_attn]
        )
        (found,), _ = stage([(theirs, "c")])
        mine = summed(mine, found)
        second = total(out_far[3], first[1]).astype(low), total(out_near[0], first[0]).astype(low)
        on = [] if early is None else [(value, "c") for value in (to_c, by_x[1:], by_y[1:], by_d[1:])]
        (*found, x_second, y_second), (out_keep, out_send) = stage(
            [(mine[chips - d].astype(low), behind(-d)) for d in range(chips, 0, -1)]
            + [(second[0], "x"), (second[1], "y")],
            lambda *given: row_grads(*given),
            [grad_attn, mixed],
        )
        grad_pair = total(mine[chips], *found).astype(low)
        grad_qkv = jnp.concatenate([grad_queries, grad_pair], 1)
        out_own = out_near[2], out_near[3]
        if early is not None:
            on, _ = stage(on)
            early = [early_own, by_x[:1], by_y[:1], by_d[:1], *on]
        return grad_qkv, grad_resid, first, (x_second, y_second), out_keep, out_send, out_own, early

    ahead = calls > 1 and per * part <= min(n for _, n in spans)
    grad_qkv, grad_resid, first, second, out_keep, out_send, out_own, early = boxed(
        sure,
        backward,
        own_sums,
        outs,
        after(resid, columns[0]),
        scale_two,
        gift,
        queries,
        pairs,
        mixed,
        mixed_wide,
        logs,
        out_blocks,
        positions,
        columns[0] if ahead else None,
    )
    columns += [
        lax.psum_scatter(after(piece, grad_qkv), "z", scatter_dimension=0, tiled=True) for piece in partial[1:]
    ]

    def collect(
        grad_qkv, first, second, out_own, out_keep, out_send, grad_resid, resid, qkv_blocks, flat_ones, scale_one, tokens
    ):
        own, to_c, to_x, to_y, to_d = spread(grad_qkv)

        def tokens_grads(grad_qkv):
            grad_unit_one = apply_rows(grad_qkv, qkv_blocks, True)
            return grad_resid + unit_back(grad_unit_one, tokens[0].astype(f32), scale_one)

        (by_x, by_y, by_d, out_found), grad_tokens = stage(
            [(to_x, "x"), (to_y, "y"), (to_d, across(5)), (out_send, "c")], tokens_grads, [grad_qkv]
        )
        on = jnp.concatenate([to_c, by_x[count:], by_y[count:], by_d[count:]], 0)
        (by_c,), out_parts = stage([(on, "c")], lambda *given: part_sums(*given), [out_keep, out_found])
        diag_top, diag_bottom, x_top, x_bottom, y_top, y_bottom, out_sums = out_parts

        def sums(resid, *gathered):
            gathered = jnp.concatenate(gathered, 0)
            return token_grads(flat_ones, gathered), resid + joined(out_own, first, second)

        started, (qkv_column, output) = stage(
            [(diag_top, "x"), (diag_bottom, "y"), (x_top, "x"), (y_bottom, "y")],
            sums,
            [resid, own, by_x[:count], by_y[:count], by_d[:count], by_c],
        )
        return qkv_column, grad_tokens, output, x_bottom, y_top, out_sums, started

    qkv_column, grad_tokens, output, x_bottom, y_top, out_sums, started = boxed(
        sure,
        collect,
        after(grad_qkv, columns[1]),
        first,
        second,
        out_own,
        out_keep,
        out_send,
        grad_resid,
        resid,
        qkv_blocks,
        flat_ones,
        scale_one,
        tokens,
    )
    qkv_low = lax.psum_scatter(qkv_column, "z", scatter_dimension=0, tiled=True)

    def end(x_bottom, y_top, out_sums, started, columns):
        x_bottom, y_top = total(x_bottom, started[1]).astype(low), total(y_top, started[0]).astype(low)
        received, every = stage(
            [(x_bottom, "x"), (y_top, "y")], lambda *columns: jnp.concatenate(columns, 1), columns
        )
        column = joined(out_sums, started, received).astype(low)
        return column.reshape(-1, column.shape[-1]), every

    out_column, every = boxed(sure, end, x_bottom, y_top, out_sums, started, columns[1:] if ahead else columns)
    out_sum = lax.psum_scatter(out_column, "z", scatter_dimension=0, tiled=True).astype(f32)
    every = after(every, out_column).reshape(8, -1, every.shape[1])
    every = lax.all_to_all(every, PLANE, split_axis=0, concat_axis=0, tiled=True)
    deep = qkv_low.shape[1]
    qkv_sum = after(qkv_low, every).reshape(8, -1, deep)
    qkv_sum = lax.all_to_all(qkv_sum, PLANE, split_axis=0, concat_axis=0, tiled=True)
    qkv_sum = jnp.swapaxes(qkv_sum, 0, 1).reshape(-1, 8 * deep).astype(f32)
    query_sum = qkv_sum[:, :wide]
    key_sum = qkv_sum[:, wide : wide + size]
    value_sum = qkv_sum[:, wide + size :]
    grad_attn_gain = (
        jnp.sum(query_weight.astype(f32) * query_sum, axis=1)
        + jnp.sum(key_weight.astype(f32) * key_sum, axis=1)
        + jnp.sum(value_weight.astype(f32) * value_sum, axis=1)
    )
    grad_gate, grad_up, grad_down, grad_mlp_gain = finish(spans, part, per, gain_two, gate_weight, up_weight, every, early)
    return (
        output[None],
        grad_tokens[None],
        grad_attn_gain,
        query_sum * gain_one,
        key_sum * gain_one,
        value_sum * gain_one,
        out_sum.T,
        grad_mlp_gain[:, 0],
        grad_gate,
        grad_up,
        grad_down.T,
    )


def solution(mesh):
    ctx, fsdp = mesh.shape["ctx"], mesh.shape["fsdp"]
    fine = Mesh(mesh.devices.reshape(ctx // 4, 2, 2, fsdp), ("z", "y", "c", "x"))
    rows = ("z", "y", "c")
    every = ("z", "y", "c", "x")
    return jax.shard_map(
        local,
        mesh=fine,
        in_specs=(
            P("x", rows, None),
            P("x", rows),
            P(every),
            P(every, None),
            P(every, None),
            P(every, None),
            P(None, every),
            P(every),
            P(every, None),
            P(every, None),
            P(None, every),
            P("x", rows, None),
        ),
        out_specs=(
            P("x", rows, None),
            P("x", rows, None),
            P(every),
            P(every, None),
            P(every, None),
            P(every, None),
            P(None, every),
            P(every),
            P(every, None),
            P(every, None),
            P(None, every),
        ),
        check_vma=False,
    )
```

```python
import functools

import jax
import jax.numpy as jnp
from jax import lax
from jax.experimental import pallas as pl
from jax.experimental.pallas import tpu as pltpu
from jax.sharding import Mesh, PartitionSpec as P

WINDOW = 2048
SUB = 128
TILE = 512
BROAD = 1280
epsilon = 1e-06
blocked_score = -1e30
PLANE = ("y", "c", "x")
low = jnp.bfloat16
f32 = jnp.float32
NOMINAL = pl.CostEstimate(flops=1 << 20, bytes_accessed=1 << 12, transcendentals=0)


def dot(left, right, contract, kind=f32):
    return lax.dot_general(
        left, right, ((contract[:1], contract[1:]), ((), ())), preferred_element_type=f32
    ).astype(kind)


def swap(value, axis):
    return lax.ppermute(value, axis, [(0, 1), (1, 0)])


def plane_gather(own, second=(), third=()):
    half = own.shape[0] // 2
    by_x = swap(own, "x")
    by_y = swap(own, "y")
    own_c = swap(own, "c")
    diag = (
        swap(after(by_y[:half], *second), "x"),
        swap(after(by_x[half:], *second), "y"),
    )
    by_x_c = swap(after(by_x, *second), "c")
    by_y_c = swap(after(by_y, *second), "c")
    diag_c = tuple(swap(after(part, *third), "c") for part in diag)
    return [own, by_x, own_c, by_x_c, by_y, diag, by_y_c, diag_c]


def joined_blocks(blocks):
    return [jnp.concatenate(block, 0) if isinstance(block, tuple) else block for block in blocks]


def stage(sends, work=None, given=()):
    fenced, given = lax.optimization_barrier((tuple(value for value, _ in sends), tuple(given)))
    received = tuple(
        swap(value, way) if isinstance(way, str) else way(value) for value, (_, way) in zip(fenced, sends)
    )
    return lax.optimization_barrier((received, work(*given) if work else given))


def boxed(sure, work, *given):
    shapes = jax.eval_shape(work, *given)
    return lax.cond(
        sure, work, lambda *_: jax.tree.map(lambda out: jnp.zeros(out.shape, out.dtype), shapes), *given
    )


def plane_index():
    return (lax.axis_index("y") * 2 + lax.axis_index("c")) * 2 + lax.axis_index("x")


def after(value, *earlier):
    return lax.optimization_barrier((value,) + earlier)[0]


def across(distance):
    return lambda value: lax.ppermute(value, PLANE, [(i, i ^ distance) for i in range(8)])


def behind(steps):
    count = lax.axis_size("z") * lax.axis_size("y")
    pairs = [(i, i + steps) for i in range(count) if 0 <= i + steps < count]
    return lambda value: lax.ppermute(value, ("z", "y"), pairs)


def two_heads(block, size):
    return jnp.concatenate([block[:, :size], block[:, size:]], 0)


def side_by_side(rows, size):
    half = rows.shape[0] // 2
    return jnp.concatenate([rows[:half], rows[half:]], 1)


def write_bias(bias, places, span, block):
    key = lax.broadcasted_iota(jnp.int32, (span, SUB), 0) - WINDOW
    query = lax.broadcasted_iota(jnp.int32, (span, SUB), 1)
    age = query - key
    seen = (age <= places) & (age >= 0) & (age < WINDOW)
    value = jnp.where(seen, 0.0, blocked_score).astype(f32)
    bias[:, :SUB] = value
    bias[:, SUB:] = value


def lay_window(core, blocks, window, turned, columns):
    count = blocks[0].shape[0]
    half = len(blocks) // 2
    for i in range(half):
        for which, block in ((core, blocks[i]), (1 - core, blocks[half + i])):
            at = pl.multiple_of((2 * i + which) * count, SUB)
            window[pl.ds(at, count), :] = block[...]
            turned[:, pl.ds(at, count)] = block[:, columns].T


def chunks(span, number):
    tiles = span // 128
    return [(128 * (tiles * i // number), 128 * (tiles * (i + 1) // number)) for i in range(number)]


def attend_kernel(size, scale, span, base, core, places, queries, *rest):
    blocks, (mixed, wide, logs, bias, window, turned) = rest[:-6], rest[-6:]
    block = pl.program_id(0)
    count = blocks[0].shape[0]
    start = pl.multiple_of(core[0] * count + base + block * SUB, SUB)

    @pl.when((block == 0) & (pl.program_id(1) == 0))
    def _():
        lay_window(core[0], blocks, window, turned, slice(size, 2 * size))

    @pl.when(pl.program_id(1) == 0)
    def _():
        write_bias(bias, places[...], span, block)

    query = two_heads(queries[...], size) * jnp.asarray(scale, low)
    highest = total = flat = None
    for at, end in chunks(span, 8):
        place = pl.ds(start + at, end - at)
        scores = dot(window[place, :size], query, (1, 1)) + bias[at:end]
        top = jnp.max(scores, axis=0, keepdims=True)
        if highest is not None:
            top = jnp.maximum(highest, top)
            fade = jnp.exp(highest - top)
        highest = top
        expo = jnp.exp(scores - highest)
        part = jnp.sum(expo, axis=0, keepdims=True)
        mix = dot(turned[:, place], expo.astype(low), (1, 0))
        total = part if total is None else total * fade + part
        flat = mix if flat is None else flat * fade + mix
    result = side_by_side((flat / total).T, size)
    wide[...] = result
    mixed[...] = result.astype(low)
    logs[0] = highest + jnp.log(total)


def attend_back_kernel(size, scale, span, base, core, places, queries, grads, wide, logs, *rest):
    blocks, (grad_queries, mine, theirs, bias, window, turned, total) = rest[:-7], rest[-7:]
    block = pl.program_id(0)
    count = blocks[0].shape[0]
    start = pl.multiple_of(core[0] * count + base + block * SUB, SUB)

    @pl.when((block == 0) & (pl.program_id(1) == 0))
    def _():
        lay_window(core[0], blocks, window, turned, slice(0, size))
        total[...] = jnp.zeros_like(total)

    @pl.when(pl.program_id(1) == 0)
    def _():
        write_bias(bias, places[...], span, block)

    query = two_heads(queries[...], size) * jnp.asarray(scale, low)
    grad = two_heads(grads[...], size)
    inner = jnp.sum((grad.astype(f32) * two_heads(wide[...], size)).T, axis=0, keepdims=True)
    place = pl.ds(start, span)
    keys, values = window[place, :size], window[place, size:]
    probs = jnp.exp(dot(keys, query, (1, 1)) + (bias[...] - logs[0]))
    grad_scores = (probs * (dot(values, grad, (1, 1)) - inner)).astype(low)
    total[place, size:] += dot(probs.astype(low), grad, (1, 0))
    total[place, :size] += dot(grad_scores, query, (1, 0))
    flat = dot(turned[:, place], grad_scores, (1, 0)) * scale
    grad_queries[...] = side_by_side(flat.T, size).astype(low)

    @pl.when((block == pl.num_programs(0) - 1) & (pl.program_id(1) == pl.num_programs(1) - 1))
    def _():
        for i in range(len(blocks) // 2):
            at = pl.multiple_of((2 * i + core[0]) * count, SUB)
            mine[i] = total[pl.ds(at, count), :]
            at = pl.multiple_of((2 * i + 1 - core[0]) * count, SUB)
            theirs[i] = total[pl.ds(at, count), :].astype(low)


def attend(queries, blocks, places, size, base):
    count, wide = queries.shape
    grid = (count // SUB, wide // (2 * size))
    span = WINDOW + SUB
    rows = len(blocks) * count
    core = lax.axis_index("c").astype(jnp.int32)[None]
    tile = pl.BlockSpec((SUB, 2 * size), lambda s, h, o: (s, h))
    return pl.pallas_call(
        functools.partial(attend_kernel, size, size**-0.5, span, base),
        out_shape=(
            jax.ShapeDtypeStruct((count, wide), low),
            jax.ShapeDtypeStruct((count, wide), f32),
            jax.ShapeDtypeStruct((grid[0] * grid[1], 1, 2 * SUB), f32),
        ),
        grid_spec=pltpu.PrefetchScalarGridSpec(
            num_scalar_prefetch=1,
            grid=grid,
            in_specs=[pl.BlockSpec((1, SUB), lambda s, h, o: (0, s)), tile]
            + [pl.BlockSpec(block.shape, lambda s, h, o: (0, 0)) for block in blocks],
            out_specs=[tile, tile, pl.BlockSpec((1, 1, 2 * SUB), lambda s, h, o: (s * grid[1] + h, 0, 0))],
            scratch_shapes=[
                pltpu.VMEM((span, 2 * SUB), f32),
                pltpu.VMEM((rows, 2 * size), low),
                pltpu.VMEM((size, rows), low),
            ],
        ),
        compiler_params=pltpu.CompilerParams(vmem_limit_bytes=56 << 20),
        cost_estimate=NOMINAL,
    )(core, places, queries, *blocks)


def attend_back(queries, grads, mixed, logs, blocks, places, size, base):
    count, wide = queries.shape
    grid = (count // SUB, wide // (2 * size))
    span = WINDOW + SUB
    rows = len(blocks) * count
    half = len(blocks) // 2
    core = lax.axis_index("c").astype(jnp.int32)[None]
    tile = pl.BlockSpec((SUB, 2 * size), lambda s, h, o: (s, h))
    whole = pl.BlockSpec((half, count, 2 * size), lambda s, h, o: (0, 0, 0))
    return pl.pallas_call(
        functools.partial(attend_back_kernel, size, size**-0.5, span, base),
        out_shape=(
            jax.ShapeDtypeStruct((count, wide), low),
            jax.ShapeDtypeStruct((half, count, 2 * size), f32),
            jax.ShapeDtypeStruct((half, count, 2 * size), low),
        ),
        grid_spec=pltpu.PrefetchScalarGridSpec(
            num_scalar_prefetch=1,
            grid=grid,
            in_specs=[
                pl.BlockSpec((1, SUB), lambda s, h, o: (0, s)),
                tile,
                tile,
                tile,
                pl.BlockSpec((1, 1, 2 * SUB), lambda s, h, o: (s * grid[1] + h, 0, 0)),
            ]
            + [pl.BlockSpec(block.shape, lambda s, h, o: (0, 0)) for block in blocks],
            out_specs=[tile, whole, whole],
            scratch_shapes=[
                pltpu.VMEM((span, 2 * SUB), f32),
                pltpu.VMEM((rows, 2 * size), low),
                pltpu.VMEM((size, rows), low),
                pltpu.VMEM((rows, 2 * size), f32),
            ],
        ),
        compiler_params=pltpu.CompilerParams(vmem_limit_bytes=60 << 20),
        cost_estimate=NOMINAL,
    )(core, places, queries, grads, mixed, logs, *blocks)


def lay_rows(slots, layout, pieces, full):
    for (r, first), piece in zip(layout, pieces):
        planes, rows, _ = piece.shape
        for plane in range(planes):
            at = pl.multiple_of(((first + plane) * 8 + slots[r]) * rows, 16)
            full[pl.ds(at, rows), :] = piece[plane]


def apply_kernel(layout, slots, left, *rest):
    *pieces, out, full = rest
    lay_rows(slots, layout, pieces, full)
    out[...] = dot(left[...], full[...], (1, 0), low)


def apply_turned_kernel(layout, slots, left, *rest):
    *start, out, full = rest
    start, pieces = start[: -len(layout)], start[-len(layout) :]
    lay_rows(slots, layout, pieces, full)

    @pl.when(pl.program_id(0) == 0)
    def _():
        out[...] = start[0][...] if start else jnp.zeros_like(out)

    out[...] += dot(left[...], full[...], (1, 1))


def whole_rows(blocks):
    planes, rows, wide = blocks[0].shape
    here = plane_index()
    whole = jnp.zeros((planes, 8, rows, wide), blocks[0].dtype)
    for r, block in enumerate(blocks):
        whole = lax.dynamic_update_slice(whole, block[:, None], (0, here ^ r, 0, 0))
    return whole.reshape(planes * 8 * rows, wide)


def apply_rows(left, blocks, turned=False, start=None):
    planes, rows, wide = blocks[0].shape
    if rows % 16 or wide % TILE:
        whole = whole_rows(joined_blocks(blocks))
        if not turned:
            return dot(left, whole, (1, 0), low)
        return dot(left, whole, (1, 1)) + (0.0 if start is None else start)
    count, deep = left.shape[0], planes * 8 * rows
    slots = (plane_index() ^ jnp.arange(8)).astype(jnp.int32)
    layout, blocks = [], [block if isinstance(block, tuple) else (block,) for block in blocks]
    for r, block in enumerate(blocks):
        layout += [(r, sum(piece.shape[0] for piece in block[:i])) for i in range(len(block))]
    blocks = [piece for block in blocks for piece in block]
    pieces = [pl.BlockSpec((piece.shape[0], rows, TILE), lambda n, s: (0, 0, n)) for piece in blocks]
    whole = pl.BlockSpec((count, deep), lambda n, s: (0, 0))
    part = pl.BlockSpec((count, TILE), lambda n, s: (0, n))
    if not turned:
        kernel, given, specs, result = apply_kernel, [left], [whole], part
        shape = jax.ShapeDtypeStruct((count, wide), low)
    else:
        kernel, given, specs, result = apply_turned_kernel, [left], [part], whole
        if start is not None:
            given, specs = given + [start], specs + [whole]
        shape = jax.ShapeDtypeStruct((count, deep), f32)
    return pl.pallas_call(
        functools.partial(kernel, layout),
        out_shape=shape,
        grid_spec=pltpu.PrefetchScalarGridSpec(
            num_scalar_prefetch=1,
            grid=(wide // TILE,),
            in_specs=specs + pieces,
            out_specs=result,
            scratch_shapes=[pltpu.VMEM((deep, TILE), low)],
        ),
        compiler_params=pltpu.CompilerParams(vmem_limit_bytes=48 << 20),
        cost_estimate=NOMINAL,
    )(slots, *given, *blocks)


def row_grads_kernel(slots, left, right, keep, send, turned):
    @pl.when(pl.program_id(1) == 0)
    def _():
        turned[...] = left[...].T

    rows = keep.shape[2]
    value = dot(turned[...], right[...], (1, 0), low)
    for i in range(8):
        place = slots[i]

        @pl.when(place < 4)
        def _():
            keep[place, 0] = value[i * rows : (i + 1) * rows]

        @pl.when(place >= 4)
        def _():
            send[place - 4, 0] = value[i * rows : (i + 1) * rows]


def row_grads(left, right):
    planes = lax.axis_size("z")
    count, deep = left.shape
    wide = right.shape[1]
    rows = deep // (planes * 8)
    places = jnp.array([3, 1, 7, 5, 2, 0, 6, 4], jnp.int32)
    slots = places[plane_index() ^ jnp.arange(8)]
    if rows % 16 or wide % TILE or (planes * 8 * rows) % (planes * 128):
        blocks = dot(left, right, (0, 0), low).reshape(planes, 8, rows, wide)
        order = jnp.argsort(slots)
        blocks = jnp.swapaxes(jnp.take(blocks, order, axis=1), 0, 1)
        return blocks[:4], blocks[4:]
    tile = wide if wide <= 5 * TILE else TILE
    group = pl.BlockSpec((4, 1, rows, tile), lambda z, n, s: (0, z, 0, n))
    shape = jax.ShapeDtypeStruct((4, planes, rows, wide), low)
    return pl.pallas_call(
        row_grads_kernel,
        out_shape=(shape, shape),
        grid_spec=pltpu.PrefetchScalarGridSpec(
            num_scalar_prefetch=1,
            grid=(planes, wide // tile),
            in_specs=[
                pl.BlockSpec((count, 8 * rows), lambda z, n, s: (0, z)),
                pl.BlockSpec((count, tile), lambda z, n, s: (0, n)),
            ],
            out_specs=[group, group],
            scratch_shapes=[pltpu.VMEM((8 * rows, count), low)],
        ),
        compiler_params=pltpu.CompilerParams(vmem_limit_bytes=48 << 20),
        cost_estimate=NOMINAL,
    )(slots, left, right)


def mlp_kernel(part, per, tiles, *rest):
    weights, rest = rest[:per], rest[per:]
    pieces = 2 * sum(tiles)
    sources, rest = rest[:pieces], rest[pieces:]
    before, rest = rest[:-8], rest[-8:]
    outs, grad_units, hidden, units, grads, arrived = rest[0:2], rest[2:4], *rest[4:]
    step = pl.program_id(0)

    def fetches(tile):
        first = 2 * sum(tiles[:tile])
        found = []
        for array, target in enumerate((units, grads)):
            at = 0
            for i in range(tiles[tile]):
                source = sources[first + array * tiles[tile] + i]
                found.append(
                    pltpu.make_async_copy(
                        source,
                        target.at[tile % 2, pl.ds(at, source.shape[0])],
                        arrived.at[tile % 2, array, i],
                    )
                )
                at += source.shape[0]
        return found

    for tile in range(len(tiles)):

        @pl.when(step == tile)
        def _():
            if tile == 0:
                for copy in fetches(0):
                    copy.start()
            if tile + 1 < len(tiles):
                for copy in fetches(tile + 1):
                    copy.start()
            for copy in fetches(tile):
                copy.wait()

    slope = 0.7978845608028654
    fronts = []
    for j in range(per):
        both = dot(units[step % 2], weights[j][:, : 2 * part], (1, 0))
        fronts.append((both[:, :part], both[:, part:], dot(grads[step % 2], weights[j][:, 2 * part :], (1, 0))))
    values = [0.0, 0.0]
    for j, (gates, upward, grad_middle) in enumerate(fronts):
        square = gates * gates
        half = 0.5 + 0.5 * jnp.tanh(gates * (slope + slope * 0.044715 * square))
        gelu = gates * half
        grad_gelu = half + gelu * (1.0 - half) * (2 * slope + 6 * slope * 0.044715 * square)
        at = 2 * part * j
        hidden[:, at : at + part] = (grad_middle * upward * grad_gelu).astype(low)
        hidden[:, at + part : at + 2 * part] = (grad_middle * gelu).astype(low)
        at = part * (2 * per + j)
        hidden[:, at : at + part] = (gelu * upward).astype(low)
        for which in range(2):
            at, width = (2 * part * j, 2 * part) if which else (part * (2 * per + j), part)
            first = 0 if which else 2 * part
            part_value = dot(hidden[:, at : at + width], weights[j][:, first : first + width], (1, 1))
            values[which] = values[which] + part_value
    for which, targets in enumerate((outs, grad_units)):
        value = values[which]
        for side in range(2):

            @pl.when(step // (len(tiles) // 2) == side)
            def _():
                if before:
                    targets[side][...] = (value + before[2 * which + side][...].astype(f32)).astype(low)
                else:
                    targets[side][...] = value.astype(low)


def mlp(units, grads, weights, before):
    rows = sum(piece.shape[0] for piece in units[0])
    count, wide = rows * len(units), units[0][0].shape[1]
    per, each = len(weights), weights[0].shape[1]
    deep = per * each
    tiles = tuple(len(tile) for tile in units)
    sources = [piece for pair in zip(units, grads) for tile in pair for piece in tile]
    side = len(units) // 2
    sides = [
        pl.BlockSpec((rows, wide), lambda i: (jnp.minimum(i, side - 1), 0)),
        pl.BlockSpec((rows, wide), lambda i: (jnp.maximum(i - side, 0), 0)),
    ]
    half = jax.ShapeDtypeStruct((count // 2, wide), low)
    return pl.pallas_call(
        functools.partial(mlp_kernel, each // 3, per, tiles),
        out_shape=[half] * 4 + [jax.ShapeDtypeStruct((count, deep), low)],
        grid=(len(units),),
        in_specs=[pl.BlockSpec((wide, each), lambda i: (0, 0), pipeline_mode=pl.Buffered(1))] * per
        + [pl.BlockSpec(memory_space=pl.ANY)] * len(sources)
        + (sides * 2 if before else []),
        out_specs=sides * 2 + [pl.BlockSpec((rows, deep), lambda i: (i, 0))],
        scratch_shapes=[
            pltpu.VMEM((2, rows, wide), low),
            pltpu.VMEM((2, rows, wide), low),
            pltpu.SemaphoreType.DMA((2, 2, max(tiles))),
        ],
        compiler_params=pltpu.CompilerParams(vmem_limit_bytes=62 << 20),
        cost_estimate=NOMINAL,
    )(*weights, *sources, *before)


def mlp_grads_kernel(number, *rest):
    units, grads, hidden, rest = rest[:number], rest[number : 2 * number], rest[2 * number : 2 * number + 2], rest[2 * number + 2 :]
    *outs, turned = rest
    step = pl.program_id(0)
    part = hidden[0].shape[1] // 3
    piece = 256 if part % 256 == 0 and outs[0].shape[1] % 256 == 0 else 128
    places = [(out, at) for out in outs for at in range(0, out.shape[1], piece)]

    def turn(slot, which, sources, share, shares):
        at = 0
        for i, source in enumerate(sources):
            if i * shares // len(sources) == share:
                turned[slot, which, :, at : at + source.shape[0]] = source[...].T
            at += source.shape[0]

    def multiply(slot, which, i, at):
        value, start = 0.0, 0
        for block in hidden:
            left = turned[slot, which, :, start : start + block.shape[0]]
            value = value + dot(left, block[:, at : at + piece], (1, 0))
            start += block.shape[0]
        out, place = places[i]
        out[:, place : place + piece] = value.astype(low)

    work = [(at // (2 * part), at) for at in range(0, 3 * part, piece)]

    @pl.when(step == 0)
    def _():
        turn(0, 0, units, 0, 1)
        turn(0, 1, grads, 0, 1)

    @pl.when(step > 0)
    def _():
        for i, (which, at) in enumerate(work):
            multiply((step - 1) % 2, which, i, at)
            turn(step % 2, 0, units, i, len(work))
            turn(step % 2, 1, grads, i, len(work))


def mlp_grads(units, grads, hidden, pieces=(3,)):
    wide = units[0].shape[1]
    deep = hidden[0].shape[1]
    count = sum(piece.shape[0] for piece in units)
    rows = 512
    last = wide // rows - 1
    return pl.pallas_call(
        functools.partial(mlp_grads_kernel, len(units)),
        out_shape=[jax.ShapeDtypeStruct((wide, deep // 3 * piece), low) for piece in pieces],
        grid=(last + 2,),
        in_specs=[
            pl.BlockSpec((piece.shape[0], rows), lambda s: (0, jnp.minimum(s, last))) for piece in units + grads
        ]
        + [pl.BlockSpec(piece.shape, lambda s: (0, 0), pipeline_mode=pl.Buffered(1)) for piece in hidden],
        out_specs=[
            pl.BlockSpec((rows, deep // 3 * piece), lambda s: (jnp.maximum(s - 1, 0), 0)) for piece in pieces
        ],
        scratch_shapes=[pltpu.VMEM((2, 2, rows, count), low)],
        compiler_params=pltpu.CompilerParams(vmem_limit_bytes=62 << 20),
        cost_estimate=NOMINAL,
    )(*units, *grads, *hidden)


def token_grads_kernel(number, *rest):
    units, (right, out, turned) = rest[:number], rest[number:]

    @pl.when(pl.program_id(0) == 0)
    def _():
        turned[...] = right[...].T

    value, at = 0.0, 0
    for unit in units:
        value = value + dot(turned[:, at : at + unit.shape[0]], unit[...], (1, 0))
        at += unit.shape[0]
    out[...] = value.astype(low).T


def token_grads(units, right):
    wide = units[0].shape[1]
    count, deep = right.shape
    rows = 512
    return pl.pallas_call(
        functools.partial(token_grads_kernel, len(units)),
        out_shape=jax.ShapeDtypeStruct((wide, deep), low),
        grid=(wide // rows,),
        in_specs=[pl.BlockSpec((piece.shape[0], rows), lambda s: (0, s)) for piece in units]
        + [pl.BlockSpec(right.shape, lambda s: (0, 0), pipeline_mode=pl.Buffered(1))],
        out_specs=pl.BlockSpec((rows, deep), lambda s: (s, 0)),
        scratch_shapes=[pltpu.VMEM((deep, count), low)],
        compiler_params=pltpu.CompilerParams(vmem_limit_bytes=56 << 20),
        cost_estimate=NOMINAL,
    )(*units, right)


def spread_kernel(slots, value, *outs):
    count, deep = value.shape[0], outs[0].shape[1]
    place = 0
    for out in outs:
        for at in range(0, out.shape[0], count):
            out[at : at + count, :] = value[:, pl.ds(pl.multiple_of(slots[place] * deep, 128), deep)]
            place += 1


def spread(value):
    count, wide = value.shape
    slots = (plane_index() ^ jnp.array(ORDER)).astype(jnp.int32)
    deep = wide // 8
    rows = (count, count, 2 * count, 2 * count, 2 * count)
    if deep % 128:
        pieces = [lax.dynamic_slice(value, (0, slots[i] * deep), (count, deep)) for i in range(8)]
        return pieces[:2] + [jnp.concatenate(pieces[i : i + 2], 0) for i in (2, 4, 6)]
    return pl.pallas_call(
        spread_kernel,
        out_shape=[jax.ShapeDtypeStruct((n, deep), value.dtype) for n in rows],
        grid_spec=pltpu.PrefetchScalarGridSpec(
            num_scalar_prefetch=1,
            grid=(1,),
            in_specs=[pl.BlockSpec((count, wide), lambda i, s: (0, 0))],
            out_specs=[pl.BlockSpec((n, deep), lambda i, s: (0, 0)) for n in rows],
        ),
        cost_estimate=NOMINAL,
    )(slots, value)


ORDER = (0, 2, 1, 3, 4, 6, 5, 7)


def deal_kernel(slots, value, *outs):
    place = 0
    for out in outs:
        for i in range(out.shape[0]):
            out[i] = value[slots[place]]
            place += 1


def deal(value):
    _, rows, wide = value.shape
    slots = (plane_index() ^ jnp.array(ORDER)).astype(jnp.int32)
    sizes = (1, 1, 2, 2, 2)
    return pl.pallas_call(
        deal_kernel,
        out_shape=[jax.ShapeDtypeStruct((n, rows, wide), value.dtype) for n in sizes],
        grid_spec=pltpu.PrefetchScalarGridSpec(
            num_scalar_prefetch=1,
            grid=(1,),
            in_specs=[pl.BlockSpec(value.shape, lambda i, s: (0, 0, 0))],
            out_specs=[pl.BlockSpec((n, rows, wide), lambda i, s: (0, 0, 0)) for n in sizes],
        ),
        compiler_params=pltpu.CompilerParams(vmem_limit_bytes=48 << 20),
        cost_estimate=NOMINAL,
    )(slots, value)


def turn_kernel(keep, found, far, diag_x, diag_y, y_bottom, x_bottom, y_top):
    half = far.shape[0]
    both = keep[...].astype(f32) + found[...].astype(f32)
    y_top[...] = (both[:half] + diag_x[...].astype(f32)).astype(low)
    y_bottom[...] = both[half:].astype(low)
    x_bottom[...] = (far[...].astype(f32) + diag_y[...].astype(f32)).astype(low)


def turn(keep, found, far, diag_x, diag_y):
    half, wide = far.shape
    tile = BROAD if wide % BROAD == 0 else wide
    part = lambda rows: pl.BlockSpec((rows, tile), lambda n: (0, n))
    return pl.pallas_call(
        turn_kernel,
        out_shape=[jax.ShapeDtypeStruct((half, wide), low)] * 3,
        grid=(wide // tile,),
        in_specs=[part(2 * half)] * 2 + [part(half)] * 3,
        out_specs=[part(half)] * 3,
        cost_estimate=NOMINAL,
    )(keep, found, far, diag_x, diag_y)


def halved_kernel(keep, found, *outs):
    half = outs[0].shape[0]
    for i, out in enumerate(outs):
        rows = slice(i * half, i * half + half)
        out[...] = (keep[rows].astype(f32) + found[rows].astype(f32)).astype(low)


def halved(keep, found):
    count, wide = keep.shape
    tile = BROAD if wide % BROAD == 0 else wide
    part = lambda rows: pl.BlockSpec((rows, tile), lambda n: (0, n))
    return pl.pallas_call(
        halved_kernel,
        out_shape=[jax.ShapeDtypeStruct((count // 4, wide), low)] * 4,
        grid=(wide // tile,),
        in_specs=[part(count)] * 2,
        out_specs=[part(count // 4)] * 4,
        cost_estimate=NOMINAL,
    )(keep, found)


def resid_kernel(steps, keep, found, x_top, x_bottom, y_top, y_bottom, resid, gift, scale, grad_out, grad_low):
    upper = pl.program_id(0) < steps
    x_part = jnp.where(upper, x_top[...].astype(f32), x_bottom[...].astype(f32))
    y_part = jnp.where(upper, y_top[...].astype(f32), y_bottom[...].astype(f32))
    grad = keep[...].astype(f32) + found[...].astype(f32) + x_part + y_part
    grad = gift[...].astype(f32) + unit_back(grad, resid[...], scale[...])
    grad_out[...] = grad
    grad_low[...] = grad.astype(low)


def resid_grads(keep, found, x_top, x_bottom, y_top, y_bottom, resid, gift, scale):
    count, wide = resid.shape
    rows = 96
    steps = count // (2 * rows)
    row = pl.BlockSpec((rows, wide), lambda i: (i, 0))
    own = pl.BlockSpec((rows, wide), lambda i: (i + 2 * steps, 0))
    first = pl.BlockSpec((rows, wide), lambda i: (jnp.minimum(i, steps - 1), 0))
    last = pl.BlockSpec((rows, wide), lambda i: (jnp.maximum(i - steps, 0), 0))
    return pl.pallas_call(
        functools.partial(resid_kernel, steps),
        out_shape=(jax.ShapeDtypeStruct((count, wide), f32), jax.ShapeDtypeStruct((count, wide), low)),
        grid=(2 * steps,),
        in_specs=[own, own, first, last, first, last, row, row, pl.BlockSpec((rows, 1), lambda i: (i, 0))],
        out_specs=(row, row),
        cost_estimate=NOMINAL,
    )(keep, found, x_top, x_bottom, y_top, y_bottom, resid, gift, scale)


def part_sums_kernel(keep, found, diag_top, diag_bottom, x_top, x_bottom, y_top, y_bottom, own):
    half = diag_top.shape[0]

    def both(place, first, rows):
        part = slice(first, first + rows)
        return (keep[place, part].astype(f32) + found[place, part].astype(f32)).astype(low)

    for place, (top, bottom) in enumerate(((diag_top, diag_bottom), (x_top, x_bottom), (y_top, y_bottom))):
        top[...] = both(place, 0, half)
        bottom[...] = both(place, half, half)
    own[...] = both(3, 0, 2 * half)


def part_sums(keep, found):
    _, planes, rows, wide = keep.shape
    tile = BROAD if wide % BROAD == 0 else wide
    four = pl.BlockSpec((4, planes, rows, tile), lambda n: (0, 0, 0, n))
    some = lambda planes: pl.BlockSpec((planes, rows, tile), lambda n: (0, 0, n))
    half = planes // 2
    shape = lambda planes: jax.ShapeDtypeStruct((planes, rows, wide), low)
    return pl.pallas_call(
        part_sums_kernel,
        out_shape=[shape(half)] * 6 + [shape(planes)],
        grid=(wide // tile,),
        in_specs=[four] * 2,
        out_specs=[some(half)] * 6 + [some(planes)],
        compiler_params=pltpu.CompilerParams(vmem_limit_bytes=48 << 20),
        cost_estimate=NOMINAL,
    )(keep, found)


def pack_kernel(spans, part, gain, gate, up, down, out):
    scale = gain[...]
    share = out.shape[2] // 3
    for p, (at, n) in enumerate(spans):
        for q in range(share // part):
            width = min(part, n - q * part)
            place = slice(at + q * part, at + q * part + width)
            for which, source in enumerate((gate, up, down)):
                first = part * (3 * q + which)
                if width > 0:
                    value = source[:, place]
                    if which < 2:
                        value = (value.astype(f32) * scale).astype(low)
                    out[p, :, first : first + width] = value
                if width < part:
                    empty = max(width, 0)
                    out[p, :, first + empty : first + part] = jnp.zeros((out.shape[1], part - empty), low)


def pack(spans, part, share, gain, gate, up, down):
    rows, _ = gate.shape
    return pl.pallas_call(
        functools.partial(pack_kernel, spans, part),
        out_shape=jax.ShapeDtypeStruct((8, rows, 3 * share), low),
        compiler_params=pltpu.CompilerParams(vmem_limit_bytes=48 << 20),
        cost_estimate=NOMINAL,
    )(gain, gate, up, down)


def shares(columns):
    tiles = -(-columns // 128)
    few, more = divmod(tiles, 8)
    sizes = [128 * (few + (p < more)) for p in range(8)]
    return [(sum(sizes[:p]), size) for p, size in enumerate(sizes)], 128 * (few + (more > 0))


def finish_kernel(spans, part, per, first_part, starts, gain, gate, up, whole, *rest):
    *early, gate_out, up_out, down_out, gain_out = rest
    scale = gain[...]
    total = jnp.zeros_like(scale)

    def lay(piece, start, j, place, width):
        added = jnp.zeros_like(scale)
        for which, (weight, out) in enumerate(((gate, gate_out), (up, up_out))):
            first = start + part * (2 * j + which)
            value = piece[:, first : first + width].astype(f32)
            added = added + jnp.sum(value * weight[:, place].astype(f32), axis=1, keepdims=True)
            out[:, place] = value * scale
        first = start + part * (2 * per + j)
        down_out[:, place] = piece[:, first : first + width].astype(f32)
        return added

    for p, (at, n) in enumerate(spans):
        for q in range(first_part, -(-n // part)):
            width = min(part, n - q * part)
            start = 3 * part * per * (q // per) - 3 * part * first_part
            total = total + lay(whole.at[p], start, q % per, slice(at + q * part, at + q * part + width), width)
    place = 0
    for pieces in early:
        for i in range(pieces.shape[0]):
            for q in range(first_part):
                at = pl.multiple_of(starts[place] + q * part, 128)
                total = total + lay(pieces.at[i], 0, q, pl.ds(at, part), part)
            place += 1
    gain_out[...] = total


def finish(spans, part, per, gain, gate, up, whole, early):
    rows, columns = gate.shape
    order = [r for r in (0, 1, 4, 5, 2, 3, 6, 7)]
    starts = jnp.array([at for at, _ in spans], jnp.int32)[plane_index() ^ jnp.array(order)]
    block = lambda shape: pl.BlockSpec(shape, lambda i, s: (0,) * len(shape))
    given = (gain, gate, up, whole, *early)
    shapes = ((rows, columns), (rows, columns), (rows, columns), (rows, 1))
    return pl.pallas_call(
        functools.partial(finish_kernel, spans, part, per, per if early else 0),
        out_shape=[jax.ShapeDtypeStruct(shape, f32) for shape in shapes],
        grid_spec=pltpu.PrefetchScalarGridSpec(
            num_scalar_prefetch=1,
            grid=(1,),
            in_specs=[block(value.shape) for value in given],
            out_specs=[block(shape) for shape in shapes],
        ),
        compiler_params=pltpu.CompilerParams(vmem_limit_bytes=56 << 20),
        cost_estimate=NOMINAL,
    )(starts, *given)


def unit_of(values):
    scale = lax.rsqrt(jnp.mean(values * values, axis=-1, keepdims=True) + epsilon)
    return scale, (values * scale).astype(low)


def unit_back(grad, values, scale):
    unit = values * scale
    return scale * (grad - unit * jnp.mean(grad * unit, axis=-1, keepdims=True))


def local(
    tokens,
    positions,
    attn_gain,
    query_weight,
    key_weight,
    value_weight,
    out_weight,
    mlp_gain,
    gate_weight,
    up_weight,
    down_weight,
    cotangent,
):
    count = tokens.shape[1]
    size = key_weight.shape[1]
    wide = query_weight.shape[1]
    reach = (WINDOW + count - 2) // count
    chips = (reach + 1) // 2
    base = 2 * chips * count - WINDOW
    gain_one = attn_gain[:, None]
    gain_two = mlp_gain[:, None]

    qkv_shard = jnp.concatenate([query_weight, key_weight, value_weight], 1).astype(f32) * gain_one
    qkv_shard = qkv_shard.astype(low)
    qkv_column = lax.all_gather(qkv_shard, "z", axis=0, tiled=False)
    out_column = lax.all_gather(after(out_weight.T, qkv_shard), "z", axis=0, tiled=False)

    spans, share = shares(gate_weight.shape[1])
    parts = share // 256 if share % 256 == 0 else 1
    calls = 2 if parts % 2 == 0 else 1
    per = parts // calls
    part = share // parts
    mine = pack(spans, part, share, after(gain_two, qkv_shard), gate_weight, up_weight, down_weight.T)
    gift = cotangent[0]
    mlp_column = lax.all_to_all(mine, PLANE, split_axis=0, concat_axis=0, tiled=True)
    mlp_column = mlp_column.reshape(-1, 3 * share)

    def piece_of(k, column):
        return column[:, k * 3 * part : (k + 1) * 3 * part]

    def gathered(piece):
        return lax.all_gather(piece, "z", axis=0, tiled=True)

    mlp_full = [gathered(piece_of(0, mlp_column))]
    sure = positions[0, 0] >= 0
    half = count // 2

    def project(qkv_column, tokens, gift, mlp_column):
        qkv_blocks = plane_gather(qkv_column)
        scale_one, unit_one = unit_of(tokens[0].astype(f32))
        qkv = apply_rows(unit_one, qkv_blocks)
        queries, pair = qkv[:, :wide], qkv[:, wide:]
        moves = [behind(d) for d in range(chips, 0, -1)]
        found, pieces = stage(
            [(pair, move) for move in moves] + [(pair, "c"), (gift, "x"), (gift, "y"), (gift, "c")],
            lambda column: [piece_of(k, column) for k in range(1, parts)],
            [mlp_column],
        )
        *pairs, pair_c, gift_x, gift_y, gift_c = found
        found, _ = stage([(block, "c") for block in pairs])
        gifts = gift_x, gift_y, gift_c
        return qkv_blocks[1:], queries, [*pairs, pair, *found, pair_c], gifts, unit_one, scale_one, pieces

    def forward(queries, pairs, out_column, tokens, positions, gift_x, gift_y):
        inputs = tokens[0].astype(f32)
        mid = out_column.shape[0] // 2
        (out_x, out_y, out_c, gift_x_c, gift_y_c), (mixed, mixed_wide, logs) = stage(
            [(out_column, "x"), (out_column, "y"), (out_column, "c"), (gift_x, "c"), (gift_y, "c")],
            lambda *given: attend(given[0], given[1:], positions, size, base),
            [queries, *pairs],
        )
        (out_top, out_bottom, out_x_c, out_y_c), _ = stage(
            [(out_y[:mid], "x"), (out_x[mid:], "y"), (out_x, "c"), (out_y, "c")]
        )
        out_diag_c, _ = stage([(out_top, "c"), (out_bottom, "c")])
        out_blocks = [out_column, out_x, out_c, out_x_c, out_y, (out_top, out_bottom), out_y_c, out_diag_c]
        resid = apply_rows(mixed, out_blocks, True, inputs)
        scale_two, unit_two = unit_of(resid)
        (unit_x, unit_y, unit_c), _ = stage([(unit_two, "x"), (unit_two, "y"), (unit_two, "c")])
        (unit_x_c, unit_y_c), _ = stage([(unit_x, "c"), (unit_y, "c")])
        unit_blocks = unit_two, unit_x, unit_c, unit_x_c, unit_y, unit_y_c
        return out_blocks[1:], mixed, mixed_wide, logs, resid, scale_two, unit_blocks, gift_x_c, gift_y_c

    qkv_column = after(qkv_column, mlp_column)
    qkv_blocks, queries, pairs, gifts, unit_one, scale_one, pieces = boxed(
        sure, project, qkv_column, tokens, gift, mlp_column
    )
    gift_x, gift_y, gift_c = gifts
    mlp_full += [gathered(piece) for piece in pieces]
    out_blocks, mixed, mixed_wide, logs, resid, scale_two, unit_blocks, gift_x_c, gift_y_c = boxed(
        sure, forward, after(queries, mlp_full[0]), pairs, out_column, tokens, positions, gift_x, gift_y
    )
    qkv_blocks, out_blocks = [qkv_column, *qkv_blocks], [out_column, *out_blocks]
    grads_near = [(gift_y,), (gift,), (gift_y_c,), (gift_c,)]

    def flat(*tiles):
        return [piece for group in tiles for tile in group for piece in tile]

    def summed(keep, received):
        return keep.astype(f32) + received.astype(f32)

    def halves(value):
        middle = value.shape[0] // 2
        return value[:middle], value[middle:]

    def total(*values):
        return sum(value.astype(f32) for value in values)

    def opening(weights, blocks, gift_x, gift_x_c, grads_near, unit_one):
        unit_two, unit_x, unit_c, unit_x_c, unit_y, unit_y_c = blocks
        units_near = [(unit_y,), (unit_two,), (unit_y_c,), (unit_c,)]
        gift_y = grads_near[0][0]
        sends = [(unit_y, "x"), (gift_x, "y")]
        one_sends = [(unit_one, "x"), (unit_one, "y"), (unit_one, "c")]
        far_sums = near_sums = partial = ()
        if calls > 1:
            (unit_d, gift_d), near_sums = stage(
                sends, lambda *given: mlp([(v,) for v in given], grads_near, weights, ()), flat(units_near)
            )
        else:
            (unit_d, gift_d), _ = stage(sends)
        (unit_d_c, gift_d_c), _ = stage([(unit_d, "c"), (gift_d, "c")])
        units_far = [(unit_d,), (unit_x,), (unit_d_c,), (unit_x_c,)]
        grads_far = [(gift_d,), (gift_x,), (gift_d_c,), (gift_x_c,)]
        if calls > 1:
            (one_x, one_y, one_c), far_sums = stage(
                one_sends, lambda weights: mlp(units_far, grads_far, weights, ()), [weights]
            )
        else:
            (one_x, one_y, one_c), _ = stage(one_sends)
        one_sends = [(one_y, "x"), (one_x, "c"), (one_y, "c")]
        if calls > 1:
            (one_d, one_x_c, one_y_c), partial = stage(
                one_sends,
                lambda *given: mlp_grads(flat(units_far, units_near), flat(grads_far, grads_near), given)[0],
                [far_sums[4], near_sums[4]],
            )
        else:
            (one_d, one_x_c, one_y_c), _ = stage(one_sends)
        ones = one_x, one_c, one_x_c, one_y, one_d, one_y_c
        return (unit_d, unit_d_c), (gift_d, gift_d_c), far_sums[:4], near_sums[:4], partial, ones

    columns = []
    unit_two, unit_x, unit_c, unit_x_c, unit_y, unit_y_c = unit_blocks
    unit_far, gift_far, far_before, near_before, partial, ones = boxed(
        sure, opening, mlp_full[:per] if calls > 1 else (), unit_blocks, gift_x, gift_x_c, grads_near, unit_one
    )
    if calls > 1:
        columns.append(lax.psum_scatter(partial, "z", scatter_dimension=0, tiled=True))
    unit_d, unit_d_c = unit_far
    gift_d, gift_d_c = gift_far
    grads_far = [(gift_d,), (gift_x,), (gift_d_c,), (gift_x_c,)]
    units_far = [(unit_d,), (unit_x,), (unit_d_c,), (unit_x_c,)]
    units_near = [(unit_y,), (unit_two,), (unit_y_c,), (unit_c,)]

    def middle(weights, units_far, units_near, grads_far, grads_near, far_before, near_before, resid, scale_two, gift, ones):
        (one_d_c,), far_sums = stage(
            [(ones[4], "c")],
            lambda *weights: mlp(units_far, grads_far, weights, far_before),
            weights,
        )
        (found,), _ = stage([(far_sums[3], "c")])
        diag_top, diag_bottom, x_top, x_bottom = halved(far_sums[2], found)
        (diag_x, diag_y, x_top, far_out), near_sums = stage(
            [(diag_top, "x"), (diag_bottom, "y"), (x_top, "x"), (far_sums[1], "c")],
            lambda *given: mlp([(value,) for value in given], grads_near, weights, near_before),
            [tile[0] for tile in units_near],
        )
        (found,), _ = stage([(near_sums[3], "c")])
        y_bottom, x_bottom, y_top = turn(near_sums[2], found, x_bottom, diag_x, diag_y)
        (y_bottom, x_bottom, y_top, near_out), partial = stage(
            [(y_bottom, "y"), (x_bottom, "x"), (y_top, "y"), (near_sums[1], "c")],
            lambda *given: mlp_grads(flat(units_far, units_near), flat(grads_far, grads_near), given, cuts),
            [far_sums[4], near_sums[4]],
        )
        received = x_top, x_bottom, y_top, y_bottom
        outs = far_sums[0], far_out, near_sums[0], near_out
        return partial, (near_sums[2], found, received), outs, one_d_c

    cuts = (2, 1)
    partial, own_sums, outs, one_d_c = boxed(
        sure,
        middle,
        mlp_full[-per:],
        units_far,
        units_near,
        grads_far,
        grads_near,
        far_before,
        near_before,
        resid,
        scale_two,
        gift,
        ones,
    )
    columns += [lax.psum_scatter(piece, "z", scatter_dimension=0, tiled=True) for piece in partial[:1]]
    one_x, one_c, one_x_c, one_y, one_d, one_y_c = ones
    flat_ones = [unit_one, one_x, one_y, one_d, one_c, one_x_c, one_y_c, one_d_c]

    def joined(own, first, second):
        top, bottom = own if isinstance(own, tuple) else halves(own)
        return jnp.concatenate([total(top, first[2], second[1]), total(bottom, second[0], first[3])], 0)

    def backward(
        own_sums, outs, resid, scale_two, gift, queries, pairs, mixed, mixed_wide, logs, out_blocks, positions, early
    ):
        keep, found, received = own_sums

        def remaining(keep, far, near):
            grads = resid_grads(keep, found, *received, resid, gift, scale_two)
            return grads, halved(far, outs[1]), halved(near, outs[3])

        given = keep, outs[0], outs[2]
        if early is not None:
            early_own, to_c, to_x, to_y, to_d = deal(early.reshape(8, -1, early.shape[1]))
            (by_x, by_y, by_d), results = stage([(to_x, "x"), (to_y, "y"), (to_d, across(5))], remaining, given)
        else:
            results = remaining(*given)
        (grad_resid, grad_attn), out_far, out_near = results

        def attention(grad_attn):
            grad_mixed = apply_rows(grad_attn, out_blocks)
            return attend_back(queries, grad_mixed, mixed_wide, logs, pairs, positions, size, base)

        first, (grad_queries, mine, theirs) = stage(
            [(out_far[0], "x"), (out_far[1], "y"), (out_far[2], "x"), (out_near[1], "y")], attention, [grad_attn]
        )
        (found,), _ = stage([(theirs, "c")])
        mine = summed(mine, found)
        second = total(out_far[3], first[1]).astype(low), total(out_near[0], first[0]).astype(low)
        on = [] if early is None else [(value, "c") for value in (to_c, by_x[1:], by_y[1:], by_d[1:])]
        (*found, x_second, y_second), (out_keep, out_send) = stage(
            [(mine[chips - d].astype(low), behind(-d)) for d in range(chips, 0, -1)]
            + [(second[0], "x"), (second[1], "y")],
            lambda *given: row_grads(*given),
            [grad_attn, mixed],
        )
        grad_pair = total(mine[chips], *found).astype(low)
        grad_qkv = jnp.concatenate([grad_queries, grad_pair], 1)
        out_own = out_near[2], out_near[3]
        if early is not None:
            on, _ = stage(on)
            early = [early_own, by_x[:1], by_y[:1], by_d[:1], *on]
        return grad_qkv, grad_resid, first, (x_second, y_second), out_keep, out_send, out_own, early

    ahead = calls > 1 and per * part <= min(n for _, n in spans)
    grad_qkv, grad_resid, first, second, out_keep, out_send, out_own, early = boxed(
        sure,
        backward,
        own_sums,
        outs,
        after(resid, columns[0]),
        scale_two,
        gift,
        queries,
        pairs,
        mixed,
        mixed_wide,
        logs,
        out_blocks,
        positions,
        columns[0] if ahead else None,
    )
    columns += [
        lax.psum_scatter(after(piece, grad_qkv), "z", scatter_dimension=0, tiled=True) for piece in partial[1:]
    ]

    def collect(
        grad_qkv, out_keep, out_send, grad_resid, qkv_blocks, flat_ones, scale_one, tokens
    ):
        own, to_c, to_x, to_y, to_d = spread(grad_qkv)

        def tokens_grads(grad_qkv):
            grad_unit_one = apply_rows(grad_qkv, qkv_blocks, True)
            return grad_resid + unit_back(grad_unit_one, tokens[0].astype(f32), scale_one)

        (by_x, by_y, by_d, out_found), grad_tokens = stage(
            [(to_x, "x"), (to_y, "y"), (to_d, across(5)), (out_send, "c")], tokens_grads, [grad_qkv]
        )
        on = jnp.concatenate([to_c, by_x[count:], by_y[count:], by_d[count:]], 0)
        (by_c,), out_parts = stage([(on, "c")], lambda *given: part_sums(*given), [out_keep, out_found])
        diag_top, diag_bottom, x_top, x_bottom, y_top, y_bottom, out_sums = out_parts

        started, qkv_column = stage(
            [(diag_top, "x"), (diag_bottom, "y"), (x_top, "x"), (y_bottom, "y")],
            lambda *gathered: token_grads(flat_ones, jnp.concatenate(gathered, 0)),
            [own, by_x[:count], by_y[:count], by_d[:count], by_c],
        )
        return qkv_column, grad_tokens, x_bottom, y_top, out_sums, started

    qkv_column, grad_tokens, x_bottom, y_top, out_sums, started = boxed(
        sure,
        collect,
        after(grad_qkv, columns[1]),
        out_keep,
        out_send,
        grad_resid,
        qkv_blocks,
        flat_ones,
        scale_one,
        tokens,
    )
    qkv_low = lax.psum_scatter(qkv_column, "z", scatter_dimension=0, tiled=True)

    def end(x_bottom, y_top, out_sums, started, columns, first, second, out_own, resid):
        x_bottom, y_top = total(x_bottom, started[1]).astype(low), total(y_top, started[0]).astype(low)
        def last(resid, *columns):
            return jnp.concatenate(columns, 1), resid + joined(out_own, first, second)

        received, (every, output) = stage([(x_bottom, "x"), (y_top, "y")], last, [resid, *columns])
        column = joined(out_sums, started, received).astype(low)
        return column.reshape(-1, column.shape[-1]), every, output

    out_column, every, output = boxed(
        sure,
        end,
        x_bottom,
        y_top,
        out_sums,
        started,
        columns[1:] if ahead else columns,
        first,
        second,
        out_own,
        resid,
    )
    out_sum = lax.psum_scatter(out_column, "z", scatter_dimension=0, tiled=True).astype(f32)
    every = after(every, out_column).reshape(8, -1, every.shape[1])
    every = lax.all_to_all(every, PLANE, split_axis=0, concat_axis=0, tiled=True)
    deep = qkv_low.shape[1]
    qkv_sum = after(qkv_low, every).reshape(8, -1, deep)
    qkv_sum = lax.all_to_all(qkv_sum, PLANE, split_axis=0, concat_axis=0, tiled=True)
    qkv_sum = jnp.swapaxes(qkv_sum, 0, 1).reshape(-1, 8 * deep).astype(f32)
    query_sum = qkv_sum[:, :wide]
    key_sum = qkv_sum[:, wide : wide + size]
    value_sum = qkv_sum[:, wide + size :]
    grad_attn_gain = (
        jnp.sum(query_weight.astype(f32) * query_sum, axis=1)
        + jnp.sum(key_weight.astype(f32) * key_sum, axis=1)
        + jnp.sum(value_weight.astype(f32) * value_sum, axis=1)
    )
    grad_gate, grad_up, grad_down, grad_mlp_gain = finish(spans, part, per, gain_two, gate_weight, up_weight, every, early)
    return (
        output[None],
        grad_tokens[None],
        grad_attn_gain,
        query_sum * gain_one,
        key_sum * gain_one,
        value_sum * gain_one,
        out_sum.T,
        grad_mlp_gain[:, 0],
        grad_gate,
        grad_up,
        grad_down.T,
    )


def solution(mesh):
    ctx, fsdp = mesh.shape["ctx"], mesh.shape["fsdp"]
    fine = Mesh(mesh.devices.reshape(ctx // 4, 2, 2, fsdp), ("z", "y", "c", "x"))
    rows = ("z", "y", "c")
    every = ("z", "y", "c", "x")
    return jax.shard_map(
        local,
        mesh=fine,
        in_specs=(
            P("x", rows, None),
            P("x", rows),
            P(every),
            P(every, None),
            P(every, None),
            P(every, None),
            P(None, every),
            P(every),
            P(every, None),
            P(every, None),
            P(None, every),
            P("x", rows, None),
        ),
        out_specs=(
            P("x", rows, None),
            P("x", rows, None),
            P(every),
            P(every, None),
            P(every, None),
            P(every, None),
            P(None, every),
            P(every),
            P(every, None),
            P(every, None),
            P(None, every),
        ),
        check_vma=False,
    )
```

```python
import functools

import jax
import jax.numpy as jnp
from jax import lax
from jax.experimental import pallas as pl
from jax.experimental.pallas import tpu as pltpu
from jax.sharding import Mesh, PartitionSpec as P

WINDOW = 2048
SUB = 128
TILE = 512
BROAD = 1280
epsilon = 1e-06
blocked_score = -1e30
PLANE = ("y", "c", "x")
low = jnp.bfloat16
f32 = jnp.float32
NOMINAL = pl.CostEstimate(flops=1 << 20, bytes_accessed=1 << 12, transcendentals=0)


def dot(left, right, contract, kind=f32):
    return lax.dot_general(
        left, right, ((contract[:1], contract[1:]), ((), ())), preferred_element_type=f32
    ).astype(kind)


def swap(value, axis):
    return lax.ppermute(value, axis, [(0, 1), (1, 0)])


def plane_gather(own, second=(), third=()):
    half = own.shape[0] // 2
    by_x = swap(own, "x")
    by_y = swap(own, "y")
    own_c = swap(own, "c")
    diag = (
        swap(after(by_y[:half], *second), "x"),
        swap(after(by_x[half:], *second), "y"),
    )
    by_x_c = swap(after(by_x, *second), "c")
    by_y_c = swap(after(by_y, *second), "c")
    diag_c = tuple(swap(after(part, *third), "c") for part in diag)
    return [own, by_x, own_c, by_x_c, by_y, diag, by_y_c, diag_c]


def joined_blocks(blocks):
    return [jnp.concatenate(block, 0) if isinstance(block, tuple) else block for block in blocks]


def stage(sends, work=None, given=()):
    fenced, given = lax.optimization_barrier((tuple(value for value, _ in sends), tuple(given)))
    received = tuple(
        swap(value, way) if isinstance(way, str) else way(value) for value, (_, way) in zip(fenced, sends)
    )
    return lax.optimization_barrier((received, work(*given) if work else given))


def boxed(sure, work, *given):
    shapes = jax.eval_shape(work, *given)
    return lax.cond(
        sure, work, lambda *_: jax.tree.map(lambda out: jnp.zeros(out.shape, out.dtype), shapes), *given
    )


def plane_index():
    return (lax.axis_index("y") * 2 + lax.axis_index("c")) * 2 + lax.axis_index("x")


def after(value, *earlier):
    return lax.optimization_barrier((value,) + earlier)[0]


def across(distance):
    return lambda value: lax.ppermute(value, PLANE, [(i, i ^ distance) for i in range(8)])


def behind(steps):
    count = lax.axis_size("z") * lax.axis_size("y")
    pairs = [(i, i + steps) for i in range(count) if 0 <= i + steps < count]
    return lambda value: lax.ppermute(value, ("z", "y"), pairs)


def two_heads(block, size):
    return jnp.concatenate([block[:, :size], block[:, size:]], 0)


def side_by_side(rows, size):
    half = rows.shape[0] // 2
    return jnp.concatenate([rows[:half], rows[half:]], 1)


def write_bias(bias, places, span, block):
    key = lax.broadcasted_iota(jnp.int32, (span, SUB), 0) - WINDOW
    query = lax.broadcasted_iota(jnp.int32, (span, SUB), 1)
    age = query - key
    seen = (age <= places) & (age >= 0) & (age < WINDOW)
    value = jnp.where(seen, 0.0, blocked_score).astype(f32)
    bias[:, :SUB] = value
    bias[:, SUB:] = value


def lay_window(core, blocks, window, turned, columns):
    count = blocks[0].shape[0]
    half = len(blocks) // 2
    for i in range(half):
        for which, block in ((core, blocks[i]), (1 - core, blocks[half + i])):
            at = pl.multiple_of((2 * i + which) * count, SUB)
            window[pl.ds(at, count), :] = block[...]
            turned[:, pl.ds(at, count)] = block[:, columns].T


def chunks(span, number):
    tiles = span // 128
    return [(128 * (tiles * i // number), 128 * (tiles * (i + 1) // number)) for i in range(number)]


def attend_kernel(size, scale, span, base, core, places, queries, *rest):
    blocks, (mixed, wide, logs, bias, window, turned) = rest[:-6], rest[-6:]
    block = pl.program_id(0)
    count = blocks[0].shape[0]
    start = pl.multiple_of(core[0] * count + base + block * SUB, SUB)

    @pl.when((block == 0) & (pl.program_id(1) == 0))
    def _():
        lay_window(core[0], blocks, window, turned, slice(size, 2 * size))

    @pl.when(pl.program_id(1) == 0)
    def _():
        write_bias(bias, places[...], span, block)

    query = two_heads(queries[...], size) * jnp.asarray(scale, low)
    highest = total = flat = None
    for at, end in chunks(span, 8):
        place = pl.ds(start + at, end - at)
        scores = dot(window[place, :size], query, (1, 1)) + bias[at:end]
        top = jnp.max(scores, axis=0, keepdims=True)
        if highest is not None:
            top = jnp.maximum(highest, top)
            fade = jnp.exp(highest - top)
        highest = top
        expo = jnp.exp(scores - highest)
        part = jnp.sum(expo, axis=0, keepdims=True)
        mix = dot(turned[:, place], expo.astype(low), (1, 0))
        total = part if total is None else total * fade + part
        flat = mix if flat is None else flat * fade + mix
    result = side_by_side((flat / total).T, size)
    wide[...] = result
    mixed[...] = result.astype(low)
    logs[0] = highest + jnp.log(total)


def attend_back_kernel(size, scale, span, base, core, places, queries, grads, wide, logs, *rest):
    blocks, (grad_queries, mine, theirs, bias, window, turned, total) = rest[:-7], rest[-7:]
    block = pl.program_id(0)
    count = blocks[0].shape[0]
    start = pl.multiple_of(core[0] * count + base + block * SUB, SUB)

    @pl.when((block == 0) & (pl.program_id(1) == 0))
    def _():
        lay_window(core[0], blocks, window, turned, slice(0, size))
        total[...] = jnp.zeros_like(total)

    @pl.when(pl.program_id(1) == 0)
    def _():
        write_bias(bias, places[...], span, block)

    query = two_heads(queries[...], size) * jnp.asarray(scale, low)
    grad = two_heads(grads[...], size)
    inner = jnp.sum((grad.astype(f32) * two_heads(wide[...], size)).T, axis=0, keepdims=True)
    place = pl.ds(start, span)
    keys, values = window[place, :size], window[place, size:]
    probs = jnp.exp(dot(keys, query, (1, 1)) + (bias[...] - logs[0]))
    grad_scores = (probs * (dot(values, grad, (1, 1)) - inner)).astype(low)
    total[place, size:] += dot(probs.astype(low), grad, (1, 0))
    total[place, :size] += dot(grad_scores, query, (1, 0))
    flat = dot(turned[:, place], grad_scores, (1, 0)) * scale
    grad_queries[...] = side_by_side(flat.T, size).astype(low)

    @pl.when((block == pl.num_programs(0) - 1) & (pl.program_id(1) == pl.num_programs(1) - 1))
    def _():
        for i in range(len(blocks) // 2):
            at = pl.multiple_of((2 * i + core[0]) * count, SUB)
            mine[i] = total[pl.ds(at, count), :]
            at = pl.multiple_of((2 * i + 1 - core[0]) * count, SUB)
            theirs[i] = total[pl.ds(at, count), :].astype(low)


def attend(queries, blocks, places, size, base):
    count, wide = queries.shape
    grid = (count // SUB, wide // (2 * size))
    span = WINDOW + SUB
    rows = len(blocks) * count
    core = lax.axis_index("c").astype(jnp.int32)[None]
    tile = pl.BlockSpec((SUB, 2 * size), lambda s, h, o: (s, h))
    return pl.pallas_call(
        functools.partial(attend_kernel, size, size**-0.5, span, base),
        out_shape=(
            jax.ShapeDtypeStruct((count, wide), low),
            jax.ShapeDtypeStruct((count, wide), f32),
            jax.ShapeDtypeStruct((grid[0] * grid[1], 1, 2 * SUB), f32),
        ),
        grid_spec=pltpu.PrefetchScalarGridSpec(
            num_scalar_prefetch=1,
            grid=grid,
            in_specs=[pl.BlockSpec((1, SUB), lambda s, h, o: (0, s)), tile]
            + [pl.BlockSpec(block.shape, lambda s, h, o: (0, 0)) for block in blocks],
            out_specs=[tile, tile, pl.BlockSpec((1, 1, 2 * SUB), lambda s, h, o: (s * grid[1] + h, 0, 0))],
            scratch_shapes=[
                pltpu.VMEM((span, 2 * SUB), f32),
                pltpu.VMEM((rows, 2 * size), low),
                pltpu.VMEM((size, rows), low),
            ],
        ),
        compiler_params=pltpu.CompilerParams(vmem_limit_bytes=56 << 20),
        cost_estimate=NOMINAL,
    )(core, places, queries, *blocks)


def attend_back(queries, grads, mixed, logs, blocks, places, size, base):
    count, wide = queries.shape
    grid = (count // SUB, wide // (2 * size))
    span = WINDOW + SUB
    rows = len(blocks) * count
    half = len(blocks) // 2
    core = lax.axis_index("c").astype(jnp.int32)[None]
    tile = pl.BlockSpec((SUB, 2 * size), lambda s, h, o: (s, h))
    whole = pl.BlockSpec((half, count, 2 * size), lambda s, h, o: (0, 0, 0))
    return pl.pallas_call(
        functools.partial(attend_back_kernel, size, size**-0.5, span, base),
        out_shape=(
            jax.ShapeDtypeStruct((count, wide), low),
            jax.ShapeDtypeStruct((half, count, 2 * size), f32),
            jax.ShapeDtypeStruct((half, count, 2 * size), low),
        ),
        grid_spec=pltpu.PrefetchScalarGridSpec(
            num_scalar_prefetch=1,
            grid=grid,
            in_specs=[
                pl.BlockSpec((1, SUB), lambda s, h, o: (0, s)),
                tile,
                tile,
                tile,
                pl.BlockSpec((1, 1, 2 * SUB), lambda s, h, o: (s * grid[1] + h, 0, 0)),
            ]
            + [pl.BlockSpec(block.shape, lambda s, h, o: (0, 0)) for block in blocks],
            out_specs=[tile, whole, whole],
            scratch_shapes=[
                pltpu.VMEM((span, 2 * SUB), f32),
                pltpu.VMEM((rows, 2 * size), low),
                pltpu.VMEM((size, rows), low),
                pltpu.VMEM((rows, 2 * size), f32),
            ],
        ),
        compiler_params=pltpu.CompilerParams(vmem_limit_bytes=60 << 20),
        cost_estimate=NOMINAL,
    )(core, places, queries, grads, mixed, logs, *blocks)


def lay_rows(slots, layout, pieces, full):
    for (r, first), piece in zip(layout, pieces):
        planes, rows, _ = piece.shape
        for plane in range(planes):
            at = pl.multiple_of(((first + plane) * 8 + slots[r]) * rows, 16)
            full[pl.ds(at, rows), :] = piece[plane]


def apply_kernel(layout, slots, left, *rest):
    *pieces, out, full = rest
    lay_rows(slots, layout, pieces, full)
    out[...] = dot(left[...], full[...], (1, 0), low)


def apply_turned_kernel(layout, slots, left, *rest):
    *start, out, full = rest
    start, pieces = start[: -len(layout)], start[-len(layout) :]
    lay_rows(slots, layout, pieces, full)

    @pl.when(pl.program_id(0) == 0)
    def _():
        out[...] = start[0][...] if start else jnp.zeros_like(out)

    out[...] += dot(left[...], full[...], (1, 1))


def whole_rows(blocks):
    planes, rows, wide = blocks[0].shape
    here = plane_index()
    whole = jnp.zeros((planes, 8, rows, wide), blocks[0].dtype)
    for r, block in enumerate(blocks):
        whole = lax.dynamic_update_slice(whole, block[:, None], (0, here ^ r, 0, 0))
    return whole.reshape(planes * 8 * rows, wide)


def apply_rows(left, blocks, turned=False, start=None):
    planes, rows, wide = blocks[0].shape
    if rows % 16 or wide % TILE:
        whole = whole_rows(joined_blocks(blocks))
        if not turned:
            return dot(left, whole, (1, 0), low)
        return dot(left, whole, (1, 1)) + (0.0 if start is None else start)
    count, deep = left.shape[0], planes * 8 * rows
    slots = (plane_index() ^ jnp.arange(8)).astype(jnp.int32)
    layout, blocks = [], [block if isinstance(block, tuple) else (block,) for block in blocks]
    for r, block in enumerate(blocks):
        layout += [(r, sum(piece.shape[0] for piece in block[:i])) for i in range(len(block))]
    blocks = [piece for block in blocks for piece in block]
    pieces = [pl.BlockSpec((piece.shape[0], rows, TILE), lambda n, s: (0, 0, n)) for piece in blocks]
    whole = pl.BlockSpec((count, deep), lambda n, s: (0, 0))
    part = pl.BlockSpec((count, TILE), lambda n, s: (0, n))
    if not turned:
        kernel, given, specs, result = apply_kernel, [left], [whole], part
        shape = jax.ShapeDtypeStruct((count, wide), low)
    else:
        kernel, given, specs, result = apply_turned_kernel, [left], [part], whole
        if start is not None:
            given, specs = given + [start], specs + [whole]
        shape = jax.ShapeDtypeStruct((count, deep), f32)
    return pl.pallas_call(
        functools.partial(kernel, layout),
        out_shape=shape,
        grid_spec=pltpu.PrefetchScalarGridSpec(
            num_scalar_prefetch=1,
            grid=(wide // TILE,),
            in_specs=specs + pieces,
            out_specs=result,
            scratch_shapes=[pltpu.VMEM((deep, TILE), low)],
        ),
        compiler_params=pltpu.CompilerParams(vmem_limit_bytes=48 << 20),
        cost_estimate=NOMINAL,
    )(slots, *given, *blocks)


def row_grads_kernel(slots, left, right, keep, send, turned):
    @pl.when(pl.program_id(1) == 0)
    def _():
        turned[...] = left[...].T

    rows = keep.shape[2]
    value = dot(turned[...], right[...], (1, 0), low)
    for i in range(8):
        place = slots[i]

        @pl.when(place < 4)
        def _():
            keep[place, 0] = value[i * rows : (i + 1) * rows]

        @pl.when(place >= 4)
        def _():
            send[place - 4, 0] = value[i * rows : (i + 1) * rows]


def row_grads(left, right):
    planes = lax.axis_size("z")
    count, deep = left.shape
    wide = right.shape[1]
    rows = deep // (planes * 8)
    places = jnp.array([3, 1, 7, 5, 2, 0, 6, 4], jnp.int32)
    slots = places[plane_index() ^ jnp.arange(8)]
    if rows % 16 or wide % TILE or (planes * 8 * rows) % (planes * 128):
        blocks = dot(left, right, (0, 0), low).reshape(planes, 8, rows, wide)
        order = jnp.argsort(slots)
        blocks = jnp.swapaxes(jnp.take(blocks, order, axis=1), 0, 1)
        return blocks[:4], blocks[4:]
    tile = wide if wide <= 5 * TILE else TILE
    group = pl.BlockSpec((4, 1, rows, tile), lambda z, n, s: (0, z, 0, n))
    shape = jax.ShapeDtypeStruct((4, planes, rows, wide), low)
    return pl.pallas_call(
        row_grads_kernel,
        out_shape=(shape, shape),
        grid_spec=pltpu.PrefetchScalarGridSpec(
            num_scalar_prefetch=1,
            grid=(planes, wide // tile),
            in_specs=[
                pl.BlockSpec((count, 8 * rows), lambda z, n, s: (0, z)),
                pl.BlockSpec((count, tile), lambda z, n, s: (0, n)),
            ],
            out_specs=[group, group],
            scratch_shapes=[pltpu.VMEM((8 * rows, count), low)],
        ),
        compiler_params=pltpu.CompilerParams(vmem_limit_bytes=48 << 20),
        cost_estimate=NOMINAL,
    )(slots, left, right)


def mlp_kernel(part, per, tiles, *rest):
    weights, rest = rest[:per], rest[per:]
    pieces = 2 * sum(tiles)
    sources, rest = rest[:pieces], rest[pieces:]
    before, rest = rest[:-8], rest[-8:]
    outs, grad_units, hidden, units, grads, arrived = rest[0:2], rest[2:4], *rest[4:]
    step = pl.program_id(0)

    def fetches(tile):
        first = 2 * sum(tiles[:tile])
        found = []
        for array, target in enumerate((units, grads)):
            at = 0
            for i in range(tiles[tile]):
                source = sources[first + array * tiles[tile] + i]
                found.append(
                    pltpu.make_async_copy(
                        source,
                        target.at[tile % 2, pl.ds(at, source.shape[0])],
                        arrived.at[tile % 2, array, i],
                    )
                )
                at += source.shape[0]
        return found

    for tile in range(len(tiles)):

        @pl.when(step == tile)
        def _():
            if tile == 0:
                for copy in fetches(0):
                    copy.start()
            if tile + 1 < len(tiles):
                for copy in fetches(tile + 1):
                    copy.start()
            for copy in fetches(tile):
                copy.wait()

    slope = 0.7978845608028654
    fronts = []
    for j in range(per):
        both = dot(units[step % 2], weights[j][:, : 2 * part], (1, 0))
        fronts.append((both[:, :part], both[:, part:], dot(grads[step % 2], weights[j][:, 2 * part :], (1, 0))))
    values = [0.0, 0.0]
    for j, (gates, upward, grad_middle) in enumerate(fronts):
        square = gates * gates
        half = 0.5 + 0.5 * jnp.tanh(gates * (slope + slope * 0.044715 * square))
        gelu = gates * half
        grad_gelu = half + gelu * (1.0 - half) * (2 * slope + 6 * slope * 0.044715 * square)
        at = 2 * part * j
        hidden[:, at : at + part] = (grad_middle * upward * grad_gelu).astype(low)
        hidden[:, at + part : at + 2 * part] = (grad_middle * gelu).astype(low)
        at = part * (2 * per + j)
        hidden[:, at : at + part] = (gelu * upward).astype(low)
        for which in range(2):
            at, width = (2 * part * j, 2 * part) if which else (part * (2 * per + j), part)
            first = 0 if which else 2 * part
            part_value = dot(hidden[:, at : at + width], weights[j][:, first : first + width], (1, 1))
            values[which] = values[which] + part_value
    for which, targets in enumerate((outs, grad_units)):
        value = values[which]
        for side in range(2):

            @pl.when(step // (len(tiles) // 2) == side)
            def _():
                if before:
                    targets[side][...] = (value + before[2 * which + side][...].astype(f32)).astype(low)
                else:
                    targets[side][...] = value.astype(low)


def mlp(units, grads, weights, before):
    rows = sum(piece.shape[0] for piece in units[0])
    count, wide = rows * len(units), units[0][0].shape[1]
    per, each = len(weights), weights[0].shape[1]
    deep = per * each
    tiles = tuple(len(tile) for tile in units)
    sources = [piece for pair in zip(units, grads) for tile in pair for piece in tile]
    side = len(units) // 2
    sides = [
        pl.BlockSpec((rows, wide), lambda i: (jnp.minimum(i, side - 1), 0)),
        pl.BlockSpec((rows, wide), lambda i: (jnp.maximum(i - side, 0), 0)),
    ]
    half = jax.ShapeDtypeStruct((count // 2, wide), low)
    return pl.pallas_call(
        functools.partial(mlp_kernel, each // 3, per, tiles),
        out_shape=[half] * 4 + [jax.ShapeDtypeStruct((count, deep), low)],
        grid=(len(units),),
        in_specs=[pl.BlockSpec((wide, each), lambda i: (0, 0), pipeline_mode=pl.Buffered(1))] * per
        + [pl.BlockSpec(memory_space=pl.ANY)] * len(sources)
        + (sides * 2 if before else []),
        out_specs=sides * 2 + [pl.BlockSpec((rows, deep), lambda i: (i, 0))],
        scratch_shapes=[
            pltpu.VMEM((2, rows, wide), low),
            pltpu.VMEM((2, rows, wide), low),
            pltpu.SemaphoreType.DMA((2, 2, max(tiles))),
        ],
        compiler_params=pltpu.CompilerParams(vmem_limit_bytes=62 << 20),
        cost_estimate=NOMINAL,
    )(*weights, *sources, *before)


def mlp_grads_kernel(number, *rest):
    units, grads, hidden, rest = rest[:number], rest[number : 2 * number], rest[2 * number : 2 * number + 2], rest[2 * number + 2 :]
    *outs, turned = rest
    step = pl.program_id(0)
    part = hidden[0].shape[1] // 3
    piece = 256 if part % 256 == 0 and outs[0].shape[1] % 256 == 0 else 128
    places = [(out, at) for out in outs for at in range(0, out.shape[1], piece)]

    def turn(slot, which, sources, share, shares):
        at = 0
        for i, source in enumerate(sources):
            if i * shares // len(sources) == share:
                turned[slot, which, :, at : at + source.shape[0]] = source[...].T
            at += source.shape[0]

    def multiply(slot, which, i, at):
        value, start = 0.0, 0
        for block in hidden:
            left = turned[slot, which, :, start : start + block.shape[0]]
            value = value + dot(left, block[:, at : at + piece], (1, 0))
            start += block.shape[0]
        out, place = places[i]
        out[:, place : place + piece] = value.astype(low)

    work = [(at // (2 * part), at) for at in range(0, 3 * part, piece)]

    @pl.when(step == 0)
    def _():
        turn(0, 0, units, 0, 1)
        turn(0, 1, grads, 0, 1)

    @pl.when(step > 0)
    def _():
        for i, (which, at) in enumerate(work):
            multiply((step - 1) % 2, which, i, at)
            turn(step % 2, 0, units, i, len(work))
            turn(step % 2, 1, grads, i, len(work))


def mlp_grads(units, grads, hidden, pieces=(3,)):
    wide = units[0].shape[1]
    deep = hidden[0].shape[1]
    count = sum(piece.shape[0] for piece in units)
    rows = 512
    last = wide // rows - 1
    return pl.pallas_call(
        functools.partial(mlp_grads_kernel, len(units)),
        out_shape=[jax.ShapeDtypeStruct((wide, deep // 3 * piece), low) for piece in pieces],
        grid=(last + 2,),
        in_specs=[
            pl.BlockSpec((piece.shape[0], rows), lambda s: (0, jnp.minimum(s, last))) for piece in units + grads
        ]
        + [pl.BlockSpec(piece.shape, lambda s: (0, 0), pipeline_mode=pl.Buffered(1)) for piece in hidden],
        out_specs=[
            pl.BlockSpec((rows, deep // 3 * piece), lambda s: (jnp.maximum(s - 1, 0), 0)) for piece in pieces
        ],
        scratch_shapes=[pltpu.VMEM((2, 2, rows, count), low)],
        compiler_params=pltpu.CompilerParams(vmem_limit_bytes=62 << 20),
        cost_estimate=NOMINAL,
    )(*units, *grads, *hidden)


def token_grads_kernel(number, *rest):
    units, (*rights, out, turned) = rest[:number], rest[number:]

    @pl.when(pl.program_id(0) == 0)
    def _():
        at = 0
        for right in rights:
            turned[:, at : at + right.shape[0]] = right[...].T
            at += right.shape[0]

    value, at = 0.0, 0
    for unit in units:
        value = value + dot(turned[:, at : at + unit.shape[0]], unit[...], (1, 0))
        at += unit.shape[0]
    out[...] = value.astype(low).T


def token_grads(units, rights, sizes):
    wide = units[0].shape[1]
    count, deep = sum(sizes), rights[0].shape[1]
    rows = 512
    return pl.pallas_call(
        functools.partial(token_grads_kernel, len(units)),
        out_shape=jax.ShapeDtypeStruct((wide, deep), low),
        grid=(wide // rows,),
        in_specs=[pl.BlockSpec((piece.shape[0], rows), lambda s: (0, s)) for piece in units]
        + [pl.BlockSpec((size, deep), lambda s: (0, 0), pipeline_mode=pl.Buffered(1)) for size in sizes],
        out_specs=pl.BlockSpec((rows, deep), lambda s: (s, 0)),
        scratch_shapes=[pltpu.VMEM((deep, count), low)],
        compiler_params=pltpu.CompilerParams(vmem_limit_bytes=56 << 20),
        cost_estimate=NOMINAL,
    )(*units, *rights)


def spread_kernel(slots, value, *outs):
    count, deep = value.shape[0], outs[0].shape[1]
    place = 0
    for out in outs:
        for at in range(0, out.shape[0], count):
            out[at : at + count, :] = value[:, pl.ds(pl.multiple_of(slots[place] * deep, 128), deep)]
            place += 1


def spread(value):
    count, wide = value.shape
    slots = (plane_index() ^ jnp.array(ORDER)).astype(jnp.int32)
    deep = wide // 8
    rows = (count, count, 2 * count, 2 * count, 2 * count)
    if deep % 128:
        pieces = [lax.dynamic_slice(value, (0, slots[i] * deep), (count, deep)) for i in range(8)]
        return pieces[:2] + [jnp.concatenate(pieces[i : i + 2], 0) for i in (2, 4, 6)]
    return pl.pallas_call(
        spread_kernel,
        out_shape=[jax.ShapeDtypeStruct((n, deep), value.dtype) for n in rows],
        grid_spec=pltpu.PrefetchScalarGridSpec(
            num_scalar_prefetch=1,
            grid=(1,),
            in_specs=[pl.BlockSpec((count, wide), lambda i, s: (0, 0))],
            out_specs=[pl.BlockSpec((n, deep), lambda i, s: (0, 0)) for n in rows],
        ),
        cost_estimate=NOMINAL,
    )(slots, value)


ORDER = (0, 2, 1, 3, 4, 6, 5, 7)


def deal_kernel(slots, value, *outs):
    place = 0
    for out in outs:
        for i in range(out.shape[0]):
            out[i] = value[slots[place]]
            place += 1


def deal(value):
    _, rows, wide = value.shape
    slots = (plane_index() ^ jnp.array(ORDER)).astype(jnp.int32)
    sizes = (1, 1, 2, 2, 2)
    return pl.pallas_call(
        deal_kernel,
        out_shape=[jax.ShapeDtypeStruct((n, rows, wide), value.dtype) for n in sizes],
        grid_spec=pltpu.PrefetchScalarGridSpec(
            num_scalar_prefetch=1,
            grid=(1,),
            in_specs=[pl.BlockSpec(value.shape, lambda i, s: (0, 0, 0))],
            out_specs=[pl.BlockSpec((n, rows, wide), lambda i, s: (0, 0, 0)) for n in sizes],
        ),
        compiler_params=pltpu.CompilerParams(vmem_limit_bytes=48 << 20),
        cost_estimate=NOMINAL,
    )(slots, value)


def turn_kernel(keep, found, far, diag_x, diag_y, y_bottom, x_bottom, y_top):
    half = far.shape[0]
    both = keep[...].astype(f32) + found[...].astype(f32)
    y_top[...] = (both[:half] + diag_x[...].astype(f32)).astype(low)
    y_bottom[...] = both[half:].astype(low)
    x_bottom[...] = (far[...].astype(f32) + diag_y[...].astype(f32)).astype(low)


def turn(keep, found, far, diag_x, diag_y):
    half, wide = far.shape
    tile = BROAD if wide % BROAD == 0 else wide
    part = lambda rows: pl.BlockSpec((rows, tile), lambda n: (0, n))
    return pl.pallas_call(
        turn_kernel,
        out_shape=[jax.ShapeDtypeStruct((half, wide), low)] * 3,
        grid=(wide // tile,),
        in_specs=[part(2 * half)] * 2 + [part(half)] * 3,
        out_specs=[part(half)] * 3,
        cost_estimate=NOMINAL,
    )(keep, found, far, diag_x, diag_y)


def halved_kernel(keep, found, *outs):
    half = outs[0].shape[0]
    for i, out in enumerate(outs):
        rows = slice(i * half, i * half + half)
        out[...] = (keep[rows].astype(f32) + found[rows].astype(f32)).astype(low)


def halved(keep, found):
    count, wide = keep.shape
    tile = BROAD if wide % BROAD == 0 else wide
    part = lambda rows: pl.BlockSpec((rows, tile), lambda n: (0, n))
    return pl.pallas_call(
        halved_kernel,
        out_shape=[jax.ShapeDtypeStruct((count // 4, wide), low)] * 4,
        grid=(wide // tile,),
        in_specs=[part(count)] * 2,
        out_specs=[part(count // 4)] * 4,
        cost_estimate=NOMINAL,
    )(keep, found)


def resid_kernel(steps, keep, found, x_top, x_bottom, y_top, y_bottom, resid, gift, scale, grad_out, grad_low):
    upper = pl.program_id(0) < steps
    x_part = jnp.where(upper, x_top[...].astype(f32), x_bottom[...].astype(f32))
    y_part = jnp.where(upper, y_top[...].astype(f32), y_bottom[...].astype(f32))
    grad = keep[...].astype(f32) + found[...].astype(f32) + x_part + y_part
    grad = gift[...].astype(f32) + unit_back(grad, resid[...], scale[...])
    grad_out[...] = grad
    grad_low[...] = grad.astype(low)


def resid_grads(keep, found, x_top, x_bottom, y_top, y_bottom, resid, gift, scale):
    count, wide = resid.shape
    rows = 96
    steps = count // (2 * rows)
    row = pl.BlockSpec((rows, wide), lambda i: (i, 0))
    own = pl.BlockSpec((rows, wide), lambda i: (i + 2 * steps, 0))
    first = pl.BlockSpec((rows, wide), lambda i: (jnp.minimum(i, steps - 1), 0))
    last = pl.BlockSpec((rows, wide), lambda i: (jnp.maximum(i - steps, 0), 0))
    return pl.pallas_call(
        functools.partial(resid_kernel, steps),
        out_shape=(jax.ShapeDtypeStruct((count, wide), f32), jax.ShapeDtypeStruct((count, wide), low)),
        grid=(2 * steps,),
        in_specs=[own, own, first, last, first, last, row, row, pl.BlockSpec((rows, 1), lambda i: (i, 0))],
        out_specs=(row, row),
        cost_estimate=NOMINAL,
    )(keep, found, x_top, x_bottom, y_top, y_bottom, resid, gift, scale)


def part_sums_kernel(keep, found, diag_top, diag_bottom, x_top, x_bottom, y_top, y_bottom, own):
    half = diag_top.shape[0]

    def both(place, first, rows):
        part = slice(first, first + rows)
        return (keep[place, part].astype(f32) + found[place, part].astype(f32)).astype(low)

    for place, (top, bottom) in enumerate(((diag_top, diag_bottom), (x_top, x_bottom), (y_top, y_bottom))):
        top[...] = both(place, 0, half)
        bottom[...] = both(place, half, half)
    own[...] = both(3, 0, 2 * half)


def part_sums(keep, found):
    _, planes, rows, wide = keep.shape
    tile = BROAD if wide % BROAD == 0 else wide
    four = pl.BlockSpec((4, planes, rows, tile), lambda n: (0, 0, 0, n))
    some = lambda planes: pl.BlockSpec((planes, rows, tile), lambda n: (0, 0, n))
    half = planes // 2
    shape = lambda planes: jax.ShapeDtypeStruct((planes, rows, wide), low)
    return pl.pallas_call(
        part_sums_kernel,
        out_shape=[shape(half)] * 6 + [shape(planes)],
        grid=(wide // tile,),
        in_specs=[four] * 2,
        out_specs=[some(half)] * 6 + [some(planes)],
        compiler_params=pltpu.CompilerParams(vmem_limit_bytes=48 << 20),
        cost_estimate=NOMINAL,
    )(keep, found)


def pack_kernel(spans, part, gain, gate, up, down, out):
    scale = gain[...]
    share = out.shape[2] // 3
    for p, (at, n) in enumerate(spans):
        for q in range(share // part):
            width = min(part, n - q * part)
            place = slice(at + q * part, at + q * part + width)
            for which, source in enumerate((gate, up, down)):
                first = part * (3 * q + which)
                if width > 0:
                    value = source[:, place]
                    if which < 2:
                        value = (value.astype(f32) * scale).astype(low)
                    out[p, :, first : first + width] = value
                if width < part:
                    empty = max(width, 0)
                    out[p, :, first + empty : first + part] = jnp.zeros((out.shape[1], part - empty), low)


def pack(spans, part, share, gain, gate, up, down):
    rows, _ = gate.shape
    return pl.pallas_call(
        functools.partial(pack_kernel, spans, part),
        out_shape=jax.ShapeDtypeStruct((8, rows, 3 * share), low),
        compiler_params=pltpu.CompilerParams(vmem_limit_bytes=48 << 20),
        cost_estimate=NOMINAL,
    )(gain, gate, up, down)


def shares(columns):
    tiles = -(-columns // 128)
    few, more = divmod(tiles, 8)
    sizes = [128 * (few + (p < more)) for p in range(8)]
    return [(sum(sizes[:p]), size) for p, size in enumerate(sizes)], 128 * (few + (more > 0))


def finish_kernel(spans, part, per, first_part, starts, gain, gate, up, whole, *rest):
    *early, gate_out, up_out, down_out, gain_out = rest
    scale = gain[...]
    total = jnp.zeros_like(scale)

    def lay(piece, start, j, place, width):
        added = jnp.zeros_like(scale)
        for which, (weight, out) in enumerate(((gate, gate_out), (up, up_out))):
            first = start + part * (2 * j + which)
            value = piece[:, first : first + width].astype(f32)
            added = added + jnp.sum(value * weight[:, place].astype(f32), axis=1, keepdims=True)
            out[:, place] = value * scale
        first = start + part * (2 * per + j)
        down_out[:, place] = piece[:, first : first + width].astype(f32)
        return added

    for p, (at, n) in enumerate(spans):
        for q in range(first_part, -(-n // part)):
            width = min(part, n - q * part)
            start = 3 * part * per * (q // per) - 3 * part * first_part
            total = total + lay(whole.at[p], start, q % per, slice(at + q * part, at + q * part + width), width)
    place = 0
    for pieces in early:
        for i in range(pieces.shape[0]):
            for q in range(first_part):
                at = pl.multiple_of(starts[place] + q * part, 128)
                total = total + lay(pieces.at[i], 0, q, pl.ds(at, part), part)
            place += 1
    gain_out[...] = total


def finish(spans, part, per, gain, gate, up, whole, early):
    rows, columns = gate.shape
    order = [r for r in (0, 1, 4, 5, 2, 3, 6, 7)]
    starts = jnp.array([at for at, _ in spans], jnp.int32)[plane_index() ^ jnp.array(order)]
    block = lambda shape: pl.BlockSpec(shape, lambda i, s: (0,) * len(shape))
    given = (gain, gate, up, whole, *early)
    shapes = ((rows, columns), (rows, columns), (rows, columns), (rows, 1))
    return pl.pallas_call(
        functools.partial(finish_kernel, spans, part, per, per if early else 0),
        out_shape=[jax.ShapeDtypeStruct(shape, f32) for shape in shapes],
        grid_spec=pltpu.PrefetchScalarGridSpec(
            num_scalar_prefetch=1,
            grid=(1,),
            in_specs=[block(value.shape) for value in given],
            out_specs=[block(shape) for shape in shapes],
        ),
        compiler_params=pltpu.CompilerParams(vmem_limit_bytes=56 << 20),
        cost_estimate=NOMINAL,
    )(starts, *given)


def unit_of(values):
    scale = lax.rsqrt(jnp.mean(values * values, axis=-1, keepdims=True) + epsilon)
    return scale, (values * scale).astype(low)


def unit_back(grad, values, scale):
    unit = values * scale
    return scale * (grad - unit * jnp.mean(grad * unit, axis=-1, keepdims=True))


def local(
    tokens,
    positions,
    attn_gain,
    query_weight,
    key_weight,
    value_weight,
    out_weight,
    mlp_gain,
    gate_weight,
    up_weight,
    down_weight,
    cotangent,
):
    count = tokens.shape[1]
    size = key_weight.shape[1]
    wide = query_weight.shape[1]
    reach = (WINDOW + count - 2) // count
    chips = (reach + 1) // 2
    base = 2 * chips * count - WINDOW
    gain_one = attn_gain[:, None]
    gain_two = mlp_gain[:, None]

    qkv_shard = jnp.concatenate([query_weight, key_weight, value_weight], 1).astype(f32) * gain_one
    qkv_shard = qkv_shard.astype(low)
    qkv_column = lax.all_gather(qkv_shard, "z", axis=0, tiled=False)
    out_column = lax.all_gather(after(out_weight.T, qkv_shard), "z", axis=0, tiled=False)

    spans, share = shares(gate_weight.shape[1])
    parts = share // 256 if share % 256 == 0 else 1
    calls = 2 if parts % 2 == 0 else 1
    per = parts // calls
    part = share // parts
    mine = pack(spans, part, share, after(gain_two, qkv_shard), gate_weight, up_weight, down_weight.T)
    gift = cotangent[0]
    mlp_column = lax.all_to_all(mine, PLANE, split_axis=0, concat_axis=0, tiled=True)
    mlp_column = mlp_column.reshape(-1, 3 * share)

    def piece_of(k, column):
        return column[:, k * 3 * part : (k + 1) * 3 * part]

    def gathered(piece):
        return lax.all_gather(piece, "z", axis=0, tiled=True)

    mlp_full = [gathered(piece_of(0, mlp_column))]
    sure = positions[0, 0] >= 0
    half = count // 2

    def project(qkv_column, tokens, gift, mlp_column):
        qkv_blocks = plane_gather(qkv_column)
        scale_one, unit_one = unit_of(tokens[0].astype(f32))
        qkv = apply_rows(unit_one, qkv_blocks)
        queries, pair = qkv[:, :wide], qkv[:, wide:]
        moves = [behind(d) for d in range(chips, 0, -1)]
        found, pieces = stage(
            [(pair, move) for move in moves] + [(pair, "c"), (gift, "x"), (gift, "y"), (gift, "c")],
            lambda column: [piece_of(k, column) for k in range(1, parts)],
            [mlp_column],
        )
        *pairs, pair_c, gift_x, gift_y, gift_c = found
        found, _ = stage([(block, "c") for block in pairs])
        gifts = gift_x, gift_y, gift_c
        return qkv_blocks[1:], queries, [*pairs, pair, *found, pair_c], gifts, unit_one, scale_one, pieces

    def forward(queries, pairs, out_column, tokens, positions, gift_x, gift_y):
        inputs = tokens[0].astype(f32)
        mid = out_column.shape[0] // 2
        (out_x, out_y, out_c, gift_x_c, gift_y_c), (mixed, mixed_wide, logs) = stage(
            [(out_column, "x"), (out_column, "y"), (out_column, "c"), (gift_x, "c"), (gift_y, "c")],
            lambda *given: attend(given[0], given[1:], positions, size, base),
            [queries, *pairs],
        )
        (out_top, out_bottom, out_x_c, out_y_c), _ = stage(
            [(out_y[:mid], "x"), (out_x[mid:], "y"), (out_x, "c"), (out_y, "c")]
        )
        out_diag_c, _ = stage([(out_top, "c"), (out_bottom, "c")])
        out_blocks = [out_column, out_x, out_c, out_x_c, out_y, (out_top, out_bottom), out_y_c, out_diag_c]
        resid = apply_rows(mixed, out_blocks, True, inputs)
        scale_two, unit_two = unit_of(resid)
        (unit_x, unit_y, unit_c), _ = stage([(unit_two, "x"), (unit_two, "y"), (unit_two, "c")])
        (unit_x_c, unit_y_c), _ = stage([(unit_x, "c"), (unit_y, "c")])
        unit_blocks = unit_two, unit_x, unit_c, unit_x_c, unit_y, unit_y_c
        return out_blocks[1:], mixed, mixed_wide, logs, resid, scale_two, unit_blocks, gift_x_c, gift_y_c

    qkv_column = after(qkv_column, mlp_column)
    qkv_blocks, queries, pairs, gifts, unit_one, scale_one, pieces = boxed(
        sure, project, qkv_column, tokens, gift, mlp_column
    )
    gift_x, gift_y, gift_c = gifts
    mlp_full += [gathered(piece) for piece in pieces]
    out_blocks, mixed, mixed_wide, logs, resid, scale_two, unit_blocks, gift_x_c, gift_y_c = boxed(
        sure, forward, after(queries, mlp_full[0]), pairs, out_column, tokens, positions, gift_x, gift_y
    )
    qkv_blocks, out_blocks = [qkv_column, *qkv_blocks], [out_column, *out_blocks]
    grads_near = [(gift_y,), (gift,), (gift_y_c,), (gift_c,)]

    def flat(*tiles):
        return [piece for group in tiles for tile in group for piece in tile]

    def summed(keep, received):
        return keep.astype(f32) + received.astype(f32)

    def halves(value):
        middle = value.shape[0] // 2
        return value[:middle], value[middle:]

    def total(*values):
        return sum(value.astype(f32) for value in values)

    def opening(weights, blocks, gift_x, gift_x_c, grads_near, unit_one):
        unit_two, unit_x, unit_c, unit_x_c, unit_y, unit_y_c = blocks
        units_near = [(unit_y,), (unit_two,), (unit_y_c,), (unit_c,)]
        gift_y = grads_near[0][0]
        sends = [(unit_y, "x"), (gift_x, "y")]
        one_sends = [(unit_one, "x"), (unit_one, "y"), (unit_one, "c")]
        far_sums = near_sums = partial = ()
        if calls > 1:
            (unit_d, gift_d), near_sums = stage(
                sends, lambda *given: mlp([(v,) for v in given], grads_near, weights, ()), flat(units_near)
            )
        else:
            (unit_d, gift_d), _ = stage(sends)
        (unit_d_c, gift_d_c), _ = stage([(unit_d, "c"), (gift_d, "c")])
        units_far = [(unit_d,), (unit_x,), (unit_d_c,), (unit_x_c,)]
        grads_far = [(gift_d,), (gift_x,), (gift_d_c,), (gift_x_c,)]
        if calls > 1:
            (one_x, one_y, one_c), far_sums = stage(
                one_sends, lambda weights: mlp(units_far, grads_far, weights, ()), [weights]
            )
        else:
            (one_x, one_y, one_c), _ = stage(one_sends)
        one_sends = [(one_y, "x"), (one_x, "c"), (one_y, "c")]
        if calls > 1:
            (one_d, one_x_c, one_y_c), partial = stage(
                one_sends,
                lambda *given: mlp_grads(flat(units_far, units_near), flat(grads_far, grads_near), given)[0],
                [far_sums[4], near_sums[4]],
            )
        else:
            (one_d, one_x_c, one_y_c), _ = stage(one_sends)
        ones = one_x, one_c, one_x_c, one_y, one_d, one_y_c
        return (unit_d, unit_d_c), (gift_d, gift_d_c), far_sums[:4], near_sums[:4], partial, ones

    columns = []
    unit_two, unit_x, unit_c, unit_x_c, unit_y, unit_y_c = unit_blocks
    unit_far, gift_far, far_before, near_before, partial, ones = boxed(
        sure, opening, mlp_full[:per] if calls > 1 else (), unit_blocks, gift_x, gift_x_c, grads_near, unit_one
    )
    if calls > 1:
        columns.append(lax.psum_scatter(partial, "z", scatter_dimension=0, tiled=True))
    unit_d, unit_d_c = unit_far
    gift_d, gift_d_c = gift_far
    grads_far = [(gift_d,), (gift_x,), (gift_d_c,), (gift_x_c,)]
    units_far = [(unit_d,), (unit_x,), (unit_d_c,), (unit_x_c,)]
    units_near = [(unit_y,), (unit_two,), (unit_y_c,), (unit_c,)]

    def middle(weights, units_far, units_near, grads_far, grads_near, far_before, near_before, resid, scale_two, gift, ones):
        (one_d_c,), far_sums = stage(
            [(ones[4], "c")],
            lambda *weights: mlp(units_far, grads_far, weights, far_before),
            weights,
        )
        (found,), _ = stage([(far_sums[3], "c")])
        diag_top, diag_bottom, x_top, x_bottom = halved(far_sums[2], found)
        (diag_x, diag_y, x_top, far_out), near_sums = stage(
            [(diag_top, "x"), (diag_bottom, "y"), (x_top, "x"), (far_sums[1], "c")],
            lambda *given: mlp([(value,) for value in given], grads_near, weights, near_before),
            [tile[0] for tile in units_near],
        )
        (found,), _ = stage([(near_sums[3], "c")])
        y_bottom, x_bottom, y_top = turn(near_sums[2], found, x_bottom, diag_x, diag_y)
        (y_bottom, x_bottom, y_top, near_out), partial = stage(
            [(y_bottom, "y"), (x_bottom, "x"), (y_top, "y"), (near_sums[1], "c")],
            lambda *given: mlp_grads(flat(units_far, units_near), flat(grads_far, grads_near), given, cuts),
            [far_sums[4], near_sums[4]],
        )
        received = x_top, x_bottom, y_top, y_bottom
        outs = far_sums[0], far_out, near_sums[0], near_out
        return partial, (near_sums[2], found, received), outs, one_d_c

    cuts = (2, 1)
    partial, own_sums, outs, one_d_c = boxed(
        sure,
        middle,
        mlp_full[-per:],
        units_far,
        units_near,
        grads_far,
        grads_near,
        far_before,
        near_before,
        resid,
        scale_two,
        gift,
        ones,
    )
    columns += [lax.psum_scatter(piece, "z", scatter_dimension=0, tiled=True) for piece in partial[:1]]
    one_x, one_c, one_x_c, one_y, one_d, one_y_c = ones
    flat_ones = [unit_one, one_x, one_y, one_d, one_c, one_x_c, one_y_c, one_d_c]

    def joined(own, first, second):
        top, bottom = own if isinstance(own, tuple) else halves(own)
        return jnp.concatenate([total(top, first[2], second[1]), total(bottom, second[0], first[3])], 0)

    def backward(
        own_sums, outs, resid, scale_two, gift, queries, pairs, mixed, mixed_wide, logs, out_blocks, positions, early
    ):
        keep, found, received = own_sums

        def remaining(keep, far, near):
            grads = resid_grads(keep, found, *received, resid, gift, scale_two)
            return grads, halved(far, outs[1]), halved(near, outs[3])

        given = keep, outs[0], outs[2]
        if early is not None:
            early_own, to_c, to_x, to_y, to_d = deal(early.reshape(8, -1, early.shape[1]))
            (by_x, by_y, by_d), results = stage([(to_x, "x"), (to_y, "y"), (to_d, across(5))], remaining, given)
        else:
            results = remaining(*given)
        (grad_resid, grad_attn), out_far, out_near = results

        def attention(grad_attn):
            grad_mixed = apply_rows(grad_attn, out_blocks)
            return attend_back(queries, grad_mixed, mixed_wide, logs, pairs, positions, size, base)

        first, (grad_queries, mine, theirs) = stage(
            [(out_far[0], "x"), (out_far[1], "y"), (out_far[2], "x"), (out_near[1], "y")], attention, [grad_attn]
        )
        (found,), _ = stage([(theirs, "c")])
        mine = summed(mine, found)
        second = total(out_far[3], first[1]).astype(low), total(out_near[0], first[0]).astype(low)
        on = [] if early is None else [(value, "c") for value in (to_c, by_x[1:], by_y[1:], by_d[1:])]
        (*found, x_second, y_second), (out_keep, out_send) = stage(
            [(mine[chips - d].astype(low), behind(-d)) for d in range(chips, 0, -1)]
            + [(second[0], "x"), (second[1], "y")],
            lambda *given: row_grads(*given),
            [grad_attn, mixed],
        )
        grad_pair = total(mine[chips], *found).astype(low)
        grad_qkv = jnp.concatenate([grad_queries, grad_pair], 1)
        out_own = out_near[2], out_near[3]
        if early is not None:
            on, _ = stage(on)
            early = [early_own, by_x[:1], by_y[:1], by_d[:1], *on]
        return grad_qkv, grad_resid, first, (x_second, y_second), out_keep, out_send, out_own, early

    ahead = calls > 1 and per * part <= min(n for _, n in spans)
    grad_qkv, grad_resid, first, second, out_keep, out_send, out_own, early = boxed(
        sure,
        backward,
        own_sums,
        outs,
        after(resid, columns[0]),
        scale_two,
        gift,
        queries,
        pairs,
        mixed,
        mixed_wide,
        logs,
        out_blocks,
        positions,
        columns[0] if ahead else None,
    )
    columns += [
        lax.psum_scatter(after(piece, grad_qkv), "z", scatter_dimension=0, tiled=True) for piece in partial[1:]
    ]

    def collect(
        grad_qkv, out_keep, out_send, grad_resid, qkv_blocks, flat_ones, scale_one, tokens
    ):
        own, to_c, to_x, to_y, to_d = spread(grad_qkv)

        def tokens_grads(grad_qkv):
            grad_unit_one = apply_rows(grad_qkv, qkv_blocks, True)
            return grad_resid + unit_back(grad_unit_one, tokens[0].astype(f32), scale_one)

        (by_x, by_y, by_d, out_found), grad_tokens = stage(
            [(to_x, "x"), (to_y, "y"), (to_d, across(5)), (out_send, "c")], tokens_grads, [grad_qkv]
        )
        on = jnp.concatenate([to_c, by_x[count:], by_y[count:], by_d[count:]], 0)
        (by_c,), out_parts = stage([(on, "c")], lambda *given: part_sums(*given), [out_keep, out_found])
        diag_top, diag_bottom, x_top, x_bottom, y_top, y_bottom, out_sums = out_parts

        started, qkv_column = stage(
            [(diag_top, "x"), (diag_bottom, "y"), (x_top, "x"), (y_bottom, "y")],
            lambda *gathered: token_grads(flat_ones, gathered, [count] * 4 + [4 * count]),
            [own, by_x, by_y, by_d, by_c],
        )
        return qkv_column, grad_tokens, x_bottom, y_top, out_sums, started

    qkv_column, grad_tokens, x_bottom, y_top, out_sums, started = boxed(
        sure,
        collect,
        after(grad_qkv, columns[1]),
        out_keep,
        out_send,
        grad_resid,
        qkv_blocks,
        flat_ones,
        scale_one,
        tokens,
    )
    qkv_low = lax.psum_scatter(qkv_column, "z", scatter_dimension=0, tiled=True)

    def end(x_bottom, y_top, out_sums, started, columns, first, second, out_own, resid):
        x_bottom, y_top = total(x_bottom, started[1]).astype(low), total(y_top, started[0]).astype(low)
        def last(resid, *columns):
            return jnp.concatenate(columns, 1), resid + joined(out_own, first, second)

        received, (every, output) = stage([(x_bottom, "x"), (y_top, "y")], last, [resid, *columns])
        column = joined(out_sums, started, received).astype(low)
        return column.reshape(-1, column.shape[-1]), every, output

    out_column, every, output = boxed(
        sure,
        end,
        x_bottom,
        y_top,
        out_sums,
        started,
        columns[1:] if ahead else columns,
        first,
        second,
        out_own,
        resid,
    )
    out_sum = lax.psum_scatter(out_column, "z", scatter_dimension=0, tiled=True).astype(f32)
    every = after(every, out_column).reshape(8, -1, every.shape[1])
    every = lax.all_to_all(every, PLANE, split_axis=0, concat_axis=0, tiled=True)
    deep = qkv_low.shape[1]
    qkv_sum = after(qkv_low, every).reshape(8, -1, deep)
    qkv_sum = lax.all_to_all(qkv_sum, PLANE, split_axis=0, concat_axis=0, tiled=True)
    qkv_sum = jnp.swapaxes(qkv_sum, 0, 1).reshape(-1, 8 * deep).astype(f32)
    query_sum = qkv_sum[:, :wide]
    key_sum = qkv_sum[:, wide : wide + size]
    value_sum = qkv_sum[:, wide + size :]
    grad_attn_gain = (
        jnp.sum(query_weight.astype(f32) * query_sum, axis=1)
        + jnp.sum(key_weight.astype(f32) * key_sum, axis=1)
        + jnp.sum(value_weight.astype(f32) * value_sum, axis=1)
    )
    grad_gate, grad_up, grad_down, grad_mlp_gain = finish(spans, part, per, gain_two, gate_weight, up_weight, every, early)
    return (
        output[None],
        grad_tokens[None],
        grad_attn_gain,
        query_sum * gain_one,
        key_sum * gain_one,
        value_sum * gain_one,
        out_sum.T,
        grad_mlp_gain[:, 0],
        grad_gate,
        grad_up,
        grad_down.T,
    )


def solution(mesh):
    ctx, fsdp = mesh.shape["ctx"], mesh.shape["fsdp"]
    fine = Mesh(mesh.devices.reshape(ctx // 4, 2, 2, fsdp), ("z", "y", "c", "x"))
    rows = ("z", "y", "c")
    every = ("z", "y", "c", "x")
    return jax.shard_map(
        local,
        mesh=fine,
        in_specs=(
            P("x", rows, None),
            P("x", rows),
            P(every),
            P(every, None),
            P(every, None),
            P(every, None),
            P(None, every),
            P(every),
            P(every, None),
            P(every, None),
            P(None, every),
            P("x", rows, None),
        ),
        out_specs=(
            P("x", rows, None),
            P("x", rows, None),
            P(every),
            P(every, None),
            P(every, None),
            P(every, None),
            P(None, every),
            P(every),
            P(every, None),
            P(every, None),
            P(None, every),
        ),
        check_vma=False,
    )
```
